32 devices in a mesh: parts: 2 (over y), gz: 16 (over z, x, core).
Axes of the slice: x: 2, y: 2, z: 4, core: 2. Of those that a mesh axis runs over, the one named last changes fastest.
Arguments:
- state: float32 [16, 64, 16, 512], P('parts', 'gz'), parts along dimension 0, may hold values from -6 to 6
- target: float32 [128, 16, 512], P(('parts', 'gz')), parts along dimension 0, may hold values from -6 to 6
- rock_type: int32 [16, 64, 16, 512], P('parts', 'gz'), parts along dimension 0, may hold values from 0 to 7
- log_table: float32 [16, 8], P('parts'), parts along dimension 0, may hold values from -1.5 to 1.5
- obs_scale: float32 [16], P('parts'), parts along dimension 0, may hold values from 0.25 to 1
Outputs:
- adjoint: float32 [16, 64, 16, 512], P('parts', 'gz'), parts along dimension 0
- control_gradient: float32 [1024, 512], P(('parts', 'gz')), parts along dimension 0
- moments: float32 [4], P('parts'), parts along dimension 0
The draws below stay inside these ranges and needn't reach their ends.
There are 2 independent parts, one for each index of `parts`. The reference program is written for one: setup_inputs(seed, part) draws one part's arguments, and reference() takes and returns one part's arrays. A program takes and returns all parts, laid end to end along the dimension named above; each array names one. Nothing has to cross between parts.
All inputs are finite; a program needn't handle non-finite values.
Results may differ from the reference program's by a relative error of at most 0.0003.
Values sent between devices are 32-bit elements; how exact they have to be, the bound alone decides.
No kernel may reach another device: no remote copies, remote signals or barrier semaphores. Data moves between devices by JAX's collectives and lax.ppermute only.
A program may use at most 64 MiB of HBM per device.

```python
import math
import jax
import jax.numpy as jnp
from jax import lax

S = 8
NR = 8
NX = 512
NY = 16
DEGREE = 4
SWEEPS = 2
MA = 512
MB = 512
NZ = 64


def plant(entries, rng, low, largest):
    shape = entries.shape
    place = [jax.random.randint(jax.random.fold_in(rng, axis), (), 0, shape[axis]) for axis in range(len(shape))]
    entries = entries.at[tuple(place)].set(low)
    longest = shape.index(max(shape))
    place[longest] = (place[longest] + 1) % shape[longest]
    return entries.at[tuple(place)].set(largest)


def shard_levels(own_key, shape, pieces, low, top_value):
    factor_of = 1.0
    for axis_at, parts in pieces:
        heights = jax.random.uniform(jax.random.fold_in(jax.random.fold_in(own_key, 6), axis_at), (parts,), jnp.float32, low / len(pieces), top_value / len(pieces))
        factor_of = factor_of * jnp.repeat(jnp.exp(heights), shape[axis_at] // parts).reshape((-1,) + (1,) * (len(shape) - 1 - axis_at))
    return factor_of


def gaussian(rng, dims, scale, reach, pieces=(), kind=jnp.bfloat16):
    factor_of = shard_levels(rng, dims, pieces, -0.22, 0.18) if pieces else 1.0
    array = jax.random.normal(rng, dims, jnp.float32) * scale * factor_of
    return jnp.minimum(jnp.maximum(array, -reach), reach).astype(kind)


def setup_inputs(seed: int = 0, part: int = 0) -> dict:
    key_of = jax.random.split(jax.random.key(seed), 6)
    part_keys = jax.random.split(jax.random.fold_in(key_of[5], part), 6)
    state = gaussian(part_keys[0], (S, NZ, NY, NX), 1.0, 6.0, ((1, 16),), jnp.float32)
    target = gaussian(part_keys[1], (NZ, NY, NX), 1.0, 6.0, ((0, 16),), jnp.float32)
    rock_type = plant(jax.random.randint(part_keys[2], (S, NZ, NY, NX), 0, NR), jax.random.fold_in(part_keys[2], 1), 0, NR - 1).astype(jnp.int32)
    log_table = jnp.clip(jax.random.uniform(part_keys[3], (S, NR), jnp.float32, -1.5, 1.5), -1.5, 1.5)
    obs_scale = jnp.clip(jnp.exp(jax.random.uniform(part_keys[4], (S,), jnp.float32, math.log(0.25), math.log(1.0))), 0.25, 1.0)
    return dict(state=state, target=target, rock_type=rock_type, log_table=log_table, obs_scale=obs_scale)


STORAGE = 0.05
BETA_RISK = 0.5
LOWER_EIGEN = 0.05
UPPER_EIGEN = 2.0

def harmonic(left_side, right_side):
    summed = left_side + right_side
    guarded = jnp.where(summed > 0, summed, 1.0)
    return jnp.where(summed > 0, 2.0 * left_side * right_side / guarded, 0.0)

def shift_ahead(values, dimension):
    length_dim = values.shape[dimension]
    zero_plane = jnp.zeros_like(lax.slice_in_dim(values, 0, 1, axis=dimension))
    return jnp.concatenate([lax.slice_in_dim(values, 1, length_dim, axis=dimension), zero_plane], axis=dimension)

def shift_behind(values, dimension):
    length_dim = values.shape[dimension]
    zero_plane = jnp.zeros_like(lax.slice_in_dim(values, 0, 1, axis=dimension))
    return jnp.concatenate([zero_plane, lax.slice_in_dim(values, 0, length_dim - 1, axis=dimension)], axis=dimension)

def face_weights(conduct, first_dim):
    return tuple((harmonic(conduct, shift_ahead(conduct, first_dim + offset)) for offset in range(3)))

def diagonal_of(weights, first_dim):
    summed = weights[0] + shift_behind(weights[0], first_dim)
    summed = summed + (weights[1] + shift_behind(weights[1], first_dim + 1))
    summed = summed + (weights[2] + shift_behind(weights[2], first_dim + 2))
    return summed + STORAGE

def apply_operator(values, weights, first_dim):
    result = STORAGE * values
    for offset in range(3):
        flux_term = weights[offset] * (shift_ahead(values, first_dim + offset) - values)
        result = result + (shift_behind(flux_term, first_dim + offset) - flux_term)
    return result

def chebyshev_constants(number_steps):
    centre = (UPPER_EIGEN + LOWER_EIGEN) / 2
    spread = (UPPER_EIGEN - LOWER_EIGEN) / 2
    quotient = centre / spread
    rho_now = 1.0 / quotient
    coefficients = []
    for position in range(number_steps):
        rho_next = 1.0 / (2.0 * quotient - rho_now)
        coefficients.append((rho_next * rho_now, 2.0 * rho_next / spread))
        rho_now = rho_next
    return (centre, coefficients)

def cosine_basis(positions, mode_index, length_total):
    product_index = jnp.remainder((2 * positions[:, None] + 1) * (2 * mode_index[None, :] + 1), 8 * length_total)
    angle = product_index.astype(jnp.float32) * (math.pi / (4 * length_total))
    return math.sqrt(2.0 / length_total) * jnp.cos(angle)

def reference(state, target, rock_type, log_table, obs_scale):
    depth_index = jnp.arange(NZ, dtype=jnp.int32).astype(jnp.float32)
    depth_weight = 1.0 + 2.0 * depth_index / (NZ - 1)
    centre, coefficients = chebyshev_constants(DEGREE)

    def one_sample(inputs):
        state_field, rock_codes, table_row, scale_value = inputs
        conduct = jnp.zeros(state_field.shape, jnp.float32)
        for code_index in range(NR):
            conduct = conduct + jnp.where(rock_codes == code_index, jnp.exp(table_row[code_index]), 0.0)
        weights = face_weights(conduct, 0)
        diagonal = diagonal_of(weights, 0)
        misfit_gap = state_field - target
        weighted = depth_weight[:, None, None] * misfit_gap
        misfit_sum = jnp.sum(weighted * misfit_gap)
        residual = scale_value * weighted
        iterate = jnp.zeros(state_field.shape, jnp.float32)
        for sweep_index in range(SWEEPS):
            search = residual / diagonal / centre
            for position in range(DEGREE):
                iterate = iterate + search
                residual = residual - apply_operator(search, weights, 0)
                if position + 1 < DEGREE:
                    first_mix, second_mix = coefficients[position]
                    search = first_mix * search + second_mix * (residual / diagonal)
        return (iterate, misfit_sum)
    adjoint, misfit_sums = lax.map(one_sample, (state, rock_type, log_table, obs_scale))
    misfit = obs_scale * misfit_sums / (2.0 * NZ * NY * NX)
    mean_value = jnp.mean(misfit)
    deviation = misfit - mean_value
    variance = jnp.mean(deviation * deviation)
    risk_weight = 1.0 + 2.0 * BETA_RISK * deviation
    face_values = lax.optimization_barrier(jnp.sum(risk_weight[:, None, None] * adjoint[:, :, 0, :], axis=0))
    basis_x = cosine_basis(jnp.arange(NX, dtype=jnp.int32), jnp.arange(MB, dtype=jnp.int32), NX)
    basis_z = cosine_basis(jnp.arange(NZ, dtype=jnp.int32), jnp.arange(MA, dtype=jnp.int32), NZ)
    projected = jnp.dot(face_values, basis_x, precision=lax.Precision.HIGHEST)
    gradient = jnp.dot(basis_z.T, projected, precision=lax.Precision.HIGHEST)
    moments = jnp.stack([mean_value, variance])
    return (adjoint, gradient, moments)
```

```python
import math

import jax
import jax.numpy as jnp
from jax import lax
from jax.sharding import PartitionSpec as P

NR = 8
DEGREE = 4
SWEEPS = 2
MA = 512
MB = 512

STORAGE = 0.05
BETA_RISK = 0.5
LOWER_EIGEN = 0.05
UPPER_EIGEN = 2.0

HALO = DEGREE * SWEEPS


def harmonic(left_side, right_side):
    summed = left_side + right_side
    guarded = jnp.where(summed > 0, summed, 1.0)
    return jnp.where(summed > 0, 2.0 * left_side * right_side / guarded, 0.0)


def shift_ahead(values, dimension):
    length_dim = values.shape[dimension]
    zero_plane = jnp.zeros_like(lax.slice_in_dim(values, 0, 1, axis=dimension))
    return jnp.concatenate(
        [lax.slice_in_dim(values, 1, length_dim, axis=dimension), zero_plane], axis=dimension
    )


def shift_behind(values, dimension):
    length_dim = values.shape[dimension]
    zero_plane = jnp.zeros_like(lax.slice_in_dim(values, 0, 1, axis=dimension))
    return jnp.concatenate(
        [zero_plane, lax.slice_in_dim(values, 0, length_dim - 1, axis=dimension)], axis=dimension
    )


def face_weights(conduct):
    return tuple(harmonic(conduct, shift_ahead(conduct, dim)) for dim in range(3))


def diagonal_of(weights):
    summed = weights[0] + shift_behind(weights[0], 0)
    summed = summed + (weights[1] + shift_behind(weights[1], 1))
    summed = summed + (weights[2] + shift_behind(weights[2], 2))
    return summed + STORAGE


def apply_operator(values, weights):
    result = STORAGE * values
    for dim in range(3):
        flux_term = weights[dim] * (shift_ahead(values, dim) - values)
        result = result + (shift_behind(flux_term, dim) - flux_term)
    return result


def chebyshev_constants(number_steps):
    centre = (UPPER_EIGEN + LOWER_EIGEN) / 2
    spread = (UPPER_EIGEN - LOWER_EIGEN) / 2
    quotient = centre / spread
    rho_now = 1.0 / quotient
    coefficients = []
    for position in range(number_steps):
        rho_next = 1.0 / (2.0 * quotient - rho_now)
        coefficients.append((rho_next * rho_now, 2.0 * rho_next / spread))
        rho_now = rho_next
    return (centre, coefficients)


def cosine_basis(positions, mode_index, length_total):
    product_index = jnp.remainder(
        (2 * positions[:, None] + 1) * (2 * mode_index[None, :] + 1), 8 * length_total
    )
    angle = product_index.astype(jnp.float32) * (math.pi / (4 * length_total))
    return math.sqrt(2.0 / length_total) * jnp.cos(angle)


def on_device(state, target, rock_type, log_table, obs_scale):
    samples, planes, rows_y, columns = state.shape
    slabs = lax.axis_size("gz")
    teams = slabs // samples
    depth = samples * planes
    groups = [[team * samples + i for i in range(samples)] for team in range(teams)]
    rank = lax.axis_index("gz")
    sample = lax.rem(rank, samples)
    depth_total = planes * slabs
    plane_index = rank * planes + jnp.arange(planes, dtype=jnp.int32)
    depth_weight = 1.0 + 2.0 * plane_index.astype(jnp.float32) / (depth_total - 1)

    def deal(field):
        return lax.all_to_all(
            field, "gz", split_axis=0, concat_axis=0, axis_index_groups=groups, tiled=True
        )

    def widen(field):
        ahead = [(i, i + samples) for i in range(slabs - samples)]
        behind = [(i + samples, i) for i in range(slabs - samples)]
        before = lax.ppermute(field[depth - HALO :], "gz", ahead)
        after = lax.ppermute(field[:HALO], "gz", behind)
        return jnp.concatenate([before, field, after], axis=0)

    codes = deal(rock_type).reshape(depth, rows_y, columns)

    misfit_gap = state - target[None]
    weighted = depth_weight[None, :, None, None] * misfit_gap
    local_sums = jnp.sum(weighted * misfit_gap, axis=(1, 2, 3))
    all_sums = lax.all_gather(local_sums, "gz")
    source = deal(obs_scale[:, None, None, None] * weighted).reshape(depth, rows_y, columns)

    table_row = jnp.exp(lax.dynamic_index_in_dim(log_table, sample, 0, keepdims=False))
    conduct = jnp.zeros(codes.shape, jnp.float32)
    for code_index in range(NR):
        conduct = conduct + jnp.where(codes == code_index, table_row[code_index], 0.0)
    weights = face_weights(widen(conduct))
    diagonal = diagonal_of(weights)
    residual = widen(source)
    iterate = jnp.zeros(residual.shape, jnp.float32)
    centre, coefficients = chebyshev_constants(DEGREE)
    for sweep_index in range(SWEEPS):
        search = residual / diagonal / centre
        for position in range(DEGREE):
            iterate = iterate + search
            residual = residual - apply_operator(search, weights)
            if position + 1 < DEGREE:
                first_mix, second_mix = coefficients[position]
                search = first_mix * search + second_mix * (residual / diagonal)
    own = iterate[HALO : HALO + depth]
    adjoint = deal(own.reshape(samples, planes, rows_y, columns))

    misfit = obs_scale * jnp.sum(all_sums, axis=0) / (2.0 * depth_total * rows_y * columns)
    mean_value = jnp.mean(misfit)
    deviation = misfit - mean_value
    variance = jnp.mean(deviation * deviation)
    risk_weight = 1.0 + 2.0 * BETA_RISK * deviation
    own_face = lax.dynamic_index_in_dim(risk_weight, sample, 0, keepdims=False) * own[:, 0, :]
    faces = lax.all_gather(own_face, "gz")
    face_values = jnp.sum(faces.reshape(teams, samples, depth, columns), axis=1)
    face_values = face_values.reshape(depth_total, columns)
    basis_x = cosine_basis(
        jnp.arange(columns, dtype=jnp.int32), jnp.arange(MB, dtype=jnp.int32), columns
    )
    own_count = MA // slabs
    mode_index = rank * own_count + jnp.arange(own_count, dtype=jnp.int32)
    basis_z = cosine_basis(jnp.arange(depth_total, dtype=jnp.int32), mode_index, depth_total)
    along_z = jnp.dot(basis_z.T, face_values, precision=lax.Precision.HIGHEST)
    gradient = jnp.dot(along_z, basis_x, precision=lax.Precision.HIGHEST)
    moments = jnp.stack([mean_value, variance])
    return (adjoint, gradient, moments)


def solution(mesh):
    return jax.shard_map(
        on_device,
        mesh=mesh,
        in_specs=(
            P("parts", "gz", None, None),
            P(("parts", "gz"), None, None),
            P("parts", "gz", None, None),
            P("parts", None),
            P("parts"),
        ),
        out_specs=(P("parts", "gz", None, None), P(("parts", "gz"), None), P("parts")),
        check_vma=False,
    )
```

```python
import math

import jax
import jax.numpy as jnp
import numpy as np
from jax import lax
from jax.experimental import pallas as pl
from jax.experimental.pallas import tpu as pltpu
from jax.sharding import PartitionSpec as P

NR = 8
DEGREE = 4
SWEEPS = 2
MA = 512
MB = 512

STORAGE = 0.05
BETA_RISK = 0.5
LOWER_EIGEN = 0.05
UPPER_EIGEN = 2.0

TEAM = 4
STEPS = DEGREE * SWEEPS
F32 = jnp.float32
MIB = 1024 * 1024


def chebyshev_constants(number_steps):
    centre = (UPPER_EIGEN + LOWER_EIGEN) / 2
    spread = (UPPER_EIGEN - LOWER_EIGEN) / 2
    quotient = centre / spread
    rho_now = 1.0 / quotient
    coefficients = []
    for position in range(number_steps):
        rho_next = 1.0 / (2.0 * quotient - rho_now)
        coefficients.append((rho_next * rho_now, 2.0 * rho_next / spread))
        rho_now = rho_next
    return (centre, coefficients)


def cosine_basis(length_total, modes):
    positions = np.arange(length_total, dtype=np.int64)
    mode_index = np.arange(modes, dtype=np.int64)
    product_index = ((2 * positions[:, None] + 1) * (2 * mode_index[None, :] + 1)) % (
        8 * length_total
    )
    angle = product_index.astype(np.float64) * (math.pi / (4 * length_total))
    return (math.sqrt(2.0 / length_total) * np.cos(angle)).astype(np.float32)


def team_place():
    return lax.rem(lax.axis_index("gz"), TEAM)


def prepare(slot, state, target, rock_type, log_table, obs_scale, depth_total):
    samples, planes, rows_y, columns = state.shape
    slots = samples // TEAM
    block = (planes, rows_y, columns)
    order = (2, 3, 1, 0)

    def kernel(table, scale, state_ref, target_ref, rock_ref, *rest):
        outs, sums_ref = rest[:TEAM], rest[TEAM]
        state_buf, rock_buf, target_buf, sems = rest[TEAM + 1 :]
        place = team_place()
        first_plane = lax.axis_index("gz") * planes
        members = [slots * (place ^ m) + slot for m in range(TEAM)]
        target_copy = pltpu.make_async_copy(target_ref, target_buf, sems.at[2, 0])
        target_copy.start()
        copies = {}
        for m in order:
            copies[m] = (
                pltpu.make_async_copy(state_ref.at[members[m]], state_buf.at[m], sems.at[0, m]),
                pltpu.make_async_copy(rock_ref.at[members[m]], rock_buf.at[m], sems.at[1, m]),
            )
            for copy in copies[m]:
                copy.start()
        sums_ref[...] = jnp.zeros(sums_ref.shape, F32)
        target_copy.wait()
        for m in order:
            for copy in copies[m]:
                copy.wait()
            values = [
                jnp.exp(jnp.full((1, columns), table[members[m], code], F32))
                for code in range(NR)
            ]
            own_scale = scale[members[m]]

            def one_plane(p, total):
                codes = rock_buf[m, p]
                low, mid, high = ((codes & bit) != 0 for bit in (1, 2, 4))
                pairs = [
                    jnp.where(low, values[2 * i + 1], values[2 * i]) for i in range(NR // 2)
                ]
                halves = [jnp.where(mid, pairs[2 * i + 1], pairs[2 * i]) for i in range(2)]
                outs[m][0, p] = jnp.where(high, halves[1], halves[0])
                depth_weight = 1.0 + (2.0 / (depth_total - 1)) * (first_plane + p).astype(F32)
                gap = state_buf[m, p] - target_buf[p]
                source = (own_scale * depth_weight) * gap
                outs[m][1, p] = source
                return total + source * gap

            total = lax.fori_loop(0, planes, one_plane, jnp.zeros((rows_y, columns), F32))
            summed = jnp.sum(total, keepdims=True)
            sums_ref[pl.ds(members[m], 1), :] = jnp.broadcast_to(summed, (1, 128))

    any_space = pl.BlockSpec(memory_space=pl.ANY)
    smem = pl.BlockSpec(memory_space=pltpu.SMEM)
    vmem = pl.BlockSpec(memory_space=pltpu.VMEM)
    results = pl.pallas_call(
        kernel,
        out_shape=[jax.ShapeDtypeStruct((2,) + block, F32)] * TEAM
        + [jax.ShapeDtypeStruct((samples, 128), F32)],
        in_specs=[smem, smem, any_space, any_space, any_space],
        out_specs=[vmem] * (TEAM + 1),
        scratch_shapes=[
            pltpu.VMEM((TEAM,) + block, F32),
            pltpu.VMEM((TEAM,) + block, jnp.int32),
            pltpu.VMEM(block, F32),
            pltpu.SemaphoreType.DMA((3, TEAM)),
        ],
        compiler_params=pltpu.CompilerParams(vmem_limit_bytes=16 * MIB),
        name=f"prepare{slot}",
    )(log_table, obs_scale, state, target, rock_type)
    return results[:TEAM], results[TEAM]


def solve(slot, blocks, near, far):
    _, planes, rows_y, columns = blocks[0].shape
    halo = 2 * planes
    own = TEAM * planes
    span = own + 2 * halo
    plane_shape = (rows_y, columns)
    centre, coefficients = chebyshev_constants(DEGREE)
    assert halo >= STEPS

    def kernel(*refs):
        inputs, outs = refs[:8], refs[8:12]
        cond, u, s_a, s_b, zp, zm, yp, ym, xp, xm, total, sems = refs[12:]
        place = team_place()
        column, side = lax.rem(place, 2), place // 2
        copies = []
        for m in range(TEAM):
            copies.append((inputs[m], halo + planes * (place ^ m)))
        upper, lower = halo + own, 0
        near_base = jnp.where(side == 0, upper, lower)
        far_base = jnp.where(side == 0, lower, upper)
        copies.append((inputs[4], near_base + planes * column))
        copies.append((inputs[5], near_base + planes * (1 - column)))
        copies.append((inputs[6], far_base + planes * column))
        copies.append((inputs[7], far_base + planes * (1 - column)))
        started = []
        for i, (source, place_at) in enumerate(copies):
            for j, held in enumerate((cond, u)):
                copy = pltpu.make_async_copy(
                    source.at[j], held.at[pl.ds(place_at, planes)], sems.at[i, j]
                )
                copy.start()
                started.append(copy)
        for copy in started:
            copy.wait()

        row_index = lax.broadcasted_iota(jnp.int32, plane_shape, 0)
        column_index = lax.broadcasted_iota(jnp.int32, plane_shape, 1)
        last_row = row_index == rows_y - 1
        last_column = column_index == columns - 1

        def ahead_y(v):
            return pltpu.roll(v, rows_y - 1, 0)

        def behind_y(v):
            return pltpu.roll(v, 1, 0)

        def ahead_x(v):
            return pltpu.roll(v, columns - 1, 1)

        def behind_x(v):
            return pltpu.roll(v, 1, 1)

        def harmonic(a, b):
            return 2.0 * a * b / jnp.maximum(a + b, 1e-30)

        def setup(p, w_behind):
            here = cond[p]
            w_z = harmonic(here, cond[p + 1])
            w_y = jnp.where(last_row, 0.0, harmonic(here, ahead_y(here)))
            w_x = jnp.where(last_column, 0.0, harmonic(here, ahead_x(here)))
            w_y_behind, w_x_behind = behind_y(w_y), behind_x(w_x)
            diagonal = (w_z + w_behind) + (w_y + w_y_behind) + (w_x + w_x_behind) + STORAGE
            inverse = 1.0 / diagonal
            zp[p] = w_z * inverse
            zm[p] = w_behind * inverse
            yp[p] = w_y * inverse
            ym[p] = w_y_behind * inverse
            xp[p] = w_x * inverse
            xm[p] = w_x_behind * inverse
            scaled = u[p] * inverse
            u[p] = scaled
            s_a[p] = scaled * (1.0 / centre)
            return w_z

        lax.fori_loop(1, span - 1, setup, harmonic(cond[0], cond[1]))

        here, there = s_a, s_b
        for step in range(STEPS - 1):
            position = step % DEGREE
            if position + 1 < DEGREE:
                keep, mix = coefficients[position]
            else:
                keep, mix = 0.0, 1.0 / centre
            last = step == STEPS - 2

            def advance(p, inside, here=here, there=there, step=step, keep=keep, mix=mix, last=last):
                s = here[p]
                moved = zp[p] * here[p + 1] + zm[p] * here[p - 1]
                moved += yp[p] * ahead_y(s) + ym[p] * behind_y(s)
                moved += xp[p] * ahead_x(s) + xm[p] * behind_x(s)
                new_u = (u[p] - s) + moved
                new_s = mix * new_u if keep == 0.0 else keep * s + mix * new_u
                if last:
                    total[p - halo] = (total[p - halo] + s) + new_s
                else:
                    u[p] = new_u
                    there[p] = new_s
                    if inside:
                        total[p - halo] = s if step == 0 else total[p - halo] + s
                return inside

            def run(start, stop, inside):
                if start < stop:
                    lax.fori_loop(
                        start, stop, lambda p, c: (advance(p, inside), c)[1], 0, unroll=2
                    )

            margin = halo - (STEPS - 2 - step)
            run(margin, halo, False)
            run(halo, halo + own, True)
            run(halo + own, span - margin, False)
            here, there = there, here

        for m in range(TEAM):
            outs[m][...] = total[pl.ds(planes * (place ^ m), planes)]

    any_space = pl.BlockSpec(memory_space=pl.ANY)
    vmem = pl.BlockSpec(memory_space=pltpu.VMEM)
    field = pltpu.VMEM((span,) + plane_shape, F32)
    return pl.pallas_call(
        kernel,
        out_shape=[jax.ShapeDtypeStruct((planes,) + plane_shape, F32)] * TEAM,
        in_specs=[any_space] * 8,
        out_specs=[vmem] * TEAM,
        scratch_shapes=[field] * 10
        + [pltpu.VMEM((own,) + plane_shape, F32), pltpu.SemaphoreType.DMA((8, 2))],
        compiler_params=pltpu.CompilerParams(vmem_limit_bytes=32 * MIB),
        name=f"solve{slot}",
    )(*blocks, *near, *far)


def weigh_faces(pieces, sums, cells):
    slots = len(pieces)
    planes, rows_y, columns = pieces[0][0].shape
    slabs, samples, _ = sums.shape

    def kernel(sums_ref, *refs):
        faces = refs[: slots * TEAM]
        face_ref, moments_ref, buf, weights, sems = refs[slots * TEAM :]
        place = team_place()
        copies = []
        for i, piece in enumerate(faces):
            copy = pltpu.make_async_copy(
                piece.at[:, pl.ds(0, 8), :], buf.at[i], sems.at[i]
            )
            copy.start()
            copies.append(copy)
        misfit = jnp.sum(sums_ref[...], axis=0) * (1.0 / (2.0 * cells))
        mean = jnp.sum(misfit, axis=0, keepdims=True) * (1.0 / samples)
        deviation = misfit - mean
        variance = jnp.sum(deviation * deviation, axis=0, keepdims=True) * (1.0 / samples)
        moments_ref[0:1, :] = mean
        moments_ref[1:2, :] = variance
        weights[...] = 1.0 + 2.0 * BETA_RISK * deviation
        for copy in copies:
            copy.wait()
        face = jnp.zeros((planes, columns), F32)
        for slot in range(slots):
            for m in range(TEAM):
                row = weights[pl.ds(slots * (place ^ m) + slot, 1), :]
                wide = jnp.concatenate([row] * (columns // 128), axis=1)
                face = face + wide * buf[slot * TEAM + m, :, 0, :]
        face_ref[...] = jnp.broadcast_to(face[None], face_ref.shape)

    any_space = pl.BlockSpec(memory_space=pl.ANY)
    vmem = pl.BlockSpec(memory_space=pltpu.VMEM)
    return pl.pallas_call(
        kernel,
        out_shape=[
            jax.ShapeDtypeStruct((slabs, planes, columns), F32),
            jax.ShapeDtypeStruct((2, 128), F32),
        ],
        in_specs=[vmem] + [any_space] * (slots * TEAM),
        out_specs=[vmem, vmem],
        scratch_shapes=[
            pltpu.VMEM((slots * TEAM, planes, 8, columns), F32),
            pltpu.VMEM((samples, 128), F32),
            pltpu.SemaphoreType.DMA((slots * TEAM,)),
        ],
        name="weigh_faces",
    )(sums, *[piece for group in pieces for piece in group])


def gather_adjoint(pieces):
    slots = len(pieces)
    block = pieces[0][0].shape

    def kernel(*refs):
        blocks, out, sems = refs[: slots * TEAM], refs[slots * TEAM], refs[slots * TEAM + 1]
        place = team_place()
        copies = []
        for slot in range(slots):
            for m in range(TEAM):
                i = slot * TEAM + m
                copy = pltpu.make_async_copy(
                    blocks[i], out.at[slots * (place ^ m) + slot], sems.at[i]
                )
                copy.start()
                copies.append(copy)
        for copy in copies:
            copy.wait()

    any_space = pl.BlockSpec(memory_space=pl.ANY)
    return pl.pallas_call(
        kernel,
        out_shape=jax.ShapeDtypeStruct((slots * TEAM,) + block, F32),
        in_specs=[any_space] * (slots * TEAM),
        out_specs=any_space,
        scratch_shapes=[pltpu.SemaphoreType.DMA((slots * TEAM,))],
        name="gather_adjoint",
    )(*[piece for group in pieces for piece in group])


def control(faces, basis_z, basis_x, own_count):
    depth_total, columns = faces.shape

    def kernel(face_ref, z_ref, x_ref, out_ref):
        own_modes = z_ref[lax.axis_index("gz")]
        along_z = jnp.dot(
            own_modes, face_ref[...], precision=lax.Precision.HIGHEST, preferred_element_type=F32
        )
        out_ref[...] = jnp.dot(
            along_z, x_ref[...], precision=lax.Precision.HIGHEST, preferred_element_type=F32
        )

    vmem = pl.BlockSpec(memory_space=pltpu.VMEM)
    return pl.pallas_call(
        kernel,
        out_shape=jax.ShapeDtypeStruct((own_count, basis_x.shape[1]), F32),
        in_specs=[vmem] * 3,
        out_specs=vmem,
        compiler_params=pltpu.CompilerParams(vmem_limit_bytes=16 * MIB),
        name="control",
    )(faces, basis_z, basis_x)


def on_device(state, target, rock_type, log_table, obs_scale):
    samples, planes, rows_y, columns = state.shape
    slabs = lax.axis_size("gz")
    slots = samples // TEAM
    depth_total = planes * slabs

    def swap(value, m):
        return lax.ppermute(value, "gz", [(i, i ^ m) for i in range(slabs)])

    def along(value, outward):
        pairs = []
        for i in range(slabs):
            side = (i % TEAM) // 2
            to = i + TEAM if (side == 1) == outward else i - TEAM
            if 0 <= to < slabs:
                pairs.append((i, to))
        return lax.ppermute(value, "gz", pairs)

    received, sums = [], []
    for slot in range(slots):
        blocks, slot_sums = prepare(
            slot, state, target, rock_type, log_table, obs_scale, depth_total
        )
        sums.append(slot_sums)
        far = [swap(blocks[m], m) for m in (2, 3)]
        received.append([blocks[0], swap(blocks[1], 1)] + far)
    pieces = []
    for slot in range(slots):
        blocks = received[slot]
        near = [along(blocks[m], True) for m in (0, 1)]
        far = [along(blocks[m], False) for m in (2, 3)]
        solved = solve(slot, blocks, near, far)
        pieces.append([solved[0]] + [swap(solved[m], m) for m in (1, 2, 3)])

    local_sums = sum(sums[1:], sums[0])
    spread_sums = jnp.broadcast_to(local_sums[None], (slabs,) + local_sums.shape)
    all_sums = lax.all_to_all(spread_sums, "gz", split_axis=0, concat_axis=0, tiled=True)

    faces, moments = weigh_faces(pieces, all_sums, depth_total * rows_y * columns)
    faces = lax.all_to_all(faces, "gz", split_axis=0, concat_axis=0, tiled=True)
    adjoint = gather_adjoint(pieces)
    gradient = control(
        faces.reshape(depth_total, columns),
        jnp.asarray(cosine_basis(depth_total, MA).T.reshape(slabs, MA // slabs, depth_total)),
        jnp.asarray(cosine_basis(columns, MB)),
        MA // slabs,
    )
    return (adjoint, gradient, moments[:, 0])


def solution(mesh):
    return jax.shard_map(
        on_device,
        mesh=mesh,
        in_specs=(
            P("parts", "gz", None, None),
            P(("parts", "gz"), None, None),
            P("parts", "gz", None, None),
            P("parts", None),
            P("parts"),
        ),
        out_specs=(P("parts", "gz", None, None), P(("parts", "gz"), None), P("parts")),
        check_vma=False,
    )
```

```python
import math

import jax
import jax.numpy as jnp
import numpy as np
from jax import lax
from jax.experimental import pallas as pl
from jax.experimental.pallas import tpu as pltpu
from jax.sharding import PartitionSpec as P

NR = 8
DEGREE = 4
SWEEPS = 2
MA = 512
MB = 512

STORAGE = 0.05
BETA_RISK = 0.5
LOWER_EIGEN = 0.05
UPPER_EIGEN = 2.0

TEAM = 4
STEPS = DEGREE * SWEEPS
F32 = jnp.float32
MIB = 1024 * 1024
SUM_LANES = 256


def chebyshev_constants(number_steps):
    centre = (UPPER_EIGEN + LOWER_EIGEN) / 2
    spread = (UPPER_EIGEN - LOWER_EIGEN) / 2
    quotient = centre / spread
    rho_now = 1.0 / quotient
    coefficients = []
    for position in range(number_steps):
        rho_next = 1.0 / (2.0 * quotient - rho_now)
        coefficients.append((rho_next * rho_now, 2.0 * rho_next / spread))
        rho_now = rho_next
    return (centre, coefficients)


def cosine_basis(length_total, modes):
    positions = np.arange(length_total, dtype=np.int64)
    mode_index = np.arange(modes, dtype=np.int64)
    product_index = ((2 * positions[:, None] + 1) * (2 * mode_index[None, :] + 1)) % (
        8 * length_total
    )
    angle = product_index.astype(np.float64) * (math.pi / (4 * length_total))
    return (math.sqrt(2.0 / length_total) * np.cos(angle)).astype(np.float32)


def team_place():
    return lax.rem(lax.axis_index("gz"), TEAM)


def prepare(jobs, fields):
    state, target, rock_type, log_table, obs_scale, depth_total = fields
    samples, planes, rows_y, columns = state.shape
    slots = samples // TEAM
    block = (planes, rows_y, columns)
    half, tiles = rows_y // 2, columns // 128
    flat = [(o, i, job) for o, group in enumerate(jobs) for i, job in enumerate(group)]
    count = len(flat)

    def kernel(table_ref, scale_ref, state_ref, target_ref, rock_ref, *rest):
        outs, sums_ref = rest[: len(jobs)], rest[len(jobs)]
        table, scale, state_buf, rock_buf, target_buf, mixed, sems = rest[len(jobs) + 1 :]
        place = team_place()
        first_plane = lax.axis_index("gz") * planes
        members = [slots * (place ^ m) + slot for _, _, (slot, m) in flat]
        small = [
            pltpu.make_async_copy(table_ref, table, sems.at[2, 0]),
            pltpu.make_async_copy(scale_ref, scale, sems.at[2, 1]),
            pltpu.make_async_copy(target_ref, target_buf, sems.at[2, 2]),
        ]
        for copy in small:
            copy.start()
        copies = []
        for n, member in enumerate(members):
            pair = (
                pltpu.make_async_copy(rock_ref.at[member], rock_buf.at[n], sems.at[1, n]),
                pltpu.make_async_copy(state_ref.at[member], state_buf.at[n], sems.at[0, n]),
            )
            for copy in pair:
                copy.start()
            copies.append(pair)
        sums_ref[...] = jnp.zeros(sums_ref.shape, F32)
        for copy in small:
            copy.wait()
        for n, (o, i, _) in enumerate(flat):
            for copy in copies[n]:
                copy.wait()
            member = members[n]
            values = [
                jnp.exp(jnp.full((8, columns), table[member, code], F32)) for code in range(NR)
            ]
            own_scale = scale[member]
            total = jnp.zeros((8, columns), F32)
            for p in range(planes):
                depth_weight = 1.0 + (2.0 / (depth_total - 1)) * (first_plane + p).astype(F32)
                factor = own_scale * depth_weight
                for first in range(0, rows_y, 8):
                    rows = slice(first, first + 8)
                    codes = rock_buf[n, p, rows]
                    low, mid, high = ((codes & bit) != 0 for bit in (1, 2, 4))
                    pairs = [
                        jnp.where(low, values[2 * k + 1], values[2 * k]) for k in range(NR // 2)
                    ]
                    halves = [jnp.where(mid, pairs[2 * k + 1], pairs[2 * k]) for k in range(2)]
                    gap = state_buf[n, p, rows] - target_buf[p, rows]
                    source = factor * gap
                    total = total + source * gap
                    made = (jnp.where(high, halves[1], halves[0]), source)
                    for a in range(2):
                        for c in range(tiles):
                            mixed[n % 2, p, a, c, rows] = made[a][:, c * 128 : (c + 1) * 128]
                for a in range(2):
                    for t in range(2):
                        for c in range(tiles):
                            outs[o][i, a, p, t, :, c * 128 : (c + 1) * 128] = mixed[
                                n % 2, p, a, c, pl.ds(t, half, stride=2), :
                            ]
            summed = jnp.sum(total, keepdims=True)
            sums_ref[pl.ds(member, 1), :] = jnp.broadcast_to(summed, (1, sums_ref.shape[1]))

    hbm = pl.BlockSpec(memory_space=pltpu.HBM)
    vmem = pl.BlockSpec(memory_space=pltpu.VMEM)
    results = pl.pallas_call(
        kernel,
        out_shape=[jax.ShapeDtypeStruct((len(group), 2, planes, 2, half, columns), F32) for group in jobs]
        + [jax.ShapeDtypeStruct((samples, SUM_LANES), F32)],
        in_specs=[hbm] * 5,
        out_specs=[vmem] * (len(jobs) + 1),
        scratch_shapes=[
            pltpu.SMEM(log_table.shape, F32),
            pltpu.SMEM(obs_scale.shape, F32),
            pltpu.VMEM((count,) + block, F32),
            pltpu.VMEM((count,) + block, jnp.int32),
            pltpu.VMEM(block, F32),
            pltpu.VMEM((2, planes, 2, tiles, rows_y, 128), F32),
            pltpu.SemaphoreType.DMA((3, max(count, 3))),
        ],
        compiler_params=pltpu.CompilerParams(vmem_limit_bytes=16 * MIB),
        cost_estimate=pl.CostEstimate(flops=0, bytes_accessed=count * MIB, transcendentals=0),
        name="prepare",
    )(log_table, obs_scale, state, target, rock_type)
    return results[:-1], results[-1]


def reciprocal(x):
    guess = pl.reciprocal(x, approx=True)
    return guess * (2.0 - x * guess)


def harmonic(a, b):
    return (a * b) * (2.0 * reciprocal(a + b))


def each(start, stop, body, width):
    whole = (stop - start) // width

    def group(n, carry):
        for k in range(width):
            body(start + n * width + k)
        return carry

    lax.fori_loop(0, whole, group, 0)
    for p in range(start + whole * width, stop):
        body(p)


def solve(slot, blocks, halos):
    inputs = list(blocks) + list(halos)
    planes, _, half, columns = blocks[0].shape[2:]
    near = [0, 1, 4, 5]
    halo = 2 * planes
    own = TEAM * planes
    span = own + 2 * halo
    centre, coefficients = chebyshev_constants(DEGREE)
    assert halo >= STEPS

    def kernel(*refs):
        ins, outs = refs[:8], refs[8:12]
        cond, u_a, u_b, s_a, s_b, zp, zm, yp, ym, xp, xm, t_a, t_b = refs[12:]
        place = team_place()
        column, side = lax.rem(place, 2), place // 2
        upper, lower = halo + own, 0
        near_base = jnp.where(side == 0, upper, lower)
        far_base = jnp.where(side == 0, lower, upper)
        bases = [halo + planes * (place ^ m) for m in range(TEAM)]
        bases += [near_base + planes * column, near_base + planes * (1 - column)]
        bases += [far_base + planes * column, far_base + planes * (1 - column)]
        for n, base in enumerate(bases):
            item = slot if n in near else 0
            for j in range(planes):
                for t in range(2):
                    cond[base + j, t] = jnp.maximum(ins[n][item, 0, j, t], 1e-30)
                    t_a[base + j, t] = ins[n][item, 1, j, t]

        last_row = lax.broadcasted_iota(jnp.int32, (half, columns), 0) == half - 1
        last_column = lax.broadcasted_iota(jnp.int32, (half, columns), 1) == columns - 1

        def ahead_x(v):
            return pltpu.roll(v, columns - 1, 1)

        def behind_x(v):
            return pltpu.roll(v, 1, 1)

        def ahead_y(v):
            return pltpu.roll(v, half - 1, 0)

        def behind_y(v):
            return pltpu.roll(v, 1, 0)

        def setup(p):
            even, odd = cond[p, 0], cond[p, 1]
            w_pair = harmonic(even, odd)
            w_next = jnp.where(last_row, 0.0, harmonic(odd, ahead_y(even)))
            for t, here in enumerate((even, odd)):
                w_z = harmonic(here, cond[p + 1, t])
                w_z_behind = harmonic(here, cond[p - 1, t])
                w_y = w_next if t else w_pair
                w_y_behind = w_pair if t else behind_y(w_next)
                w_x = jnp.where(last_column, 0.0, harmonic(here, ahead_x(here)))
                w_x_behind = behind_x(w_x)
                diagonal = (w_z + w_z_behind) + (w_y + w_y_behind) + (w_x + w_x_behind) + STORAGE
                inverse = reciprocal(diagonal)
                zp[p, t] = w_z * inverse
                zm[p, t] = w_z_behind * inverse
                yp[p, t] = w_y * inverse
                ym[p, t] = w_y_behind * inverse
                xp[p, t] = w_x * inverse
                xm[p, t] = w_x_behind * inverse
                scaled = t_a[p, t] * inverse
                u_a[p, t] = scaled
                s_a[p, t] = scaled * (1.0 / centre)

        each(1, span - 1, setup, 2)

        s_now, s_next, u_now, u_next, t_now, t_next = s_a, s_b, u_a, u_b, t_a, t_b
        for step in range(STEPS - 1):
            position = step % DEGREE
            if position + 1 < DEGREE:
                keep, mix = coefficients[position]
            else:
                keep, mix = 0.0, 1.0 / centre
            last = step == STEPS - 2

            def advance(p):
                even, odd = s_now[p, 0], s_now[p, 1]
                for t, s in enumerate((even, odd)):
                    ahead = ahead_y(even) if t else odd
                    behind = even if t else behind_y(odd)
                    moved = zp[p, t] * s_now[p + 1, t] + zm[p, t] * s_now[p - 1, t]
                    moved += yp[p, t] * ahead + ym[p, t] * behind
                    moved += xp[p, t] * ahead_x(s) + xm[p, t] * behind_x(s)
                    new_u = (u_now[p, t] - s) + moved
                    new_s = mix * new_u if keep == 0.0 else keep * s + mix * new_u
                    if not last:
                        u_next[p, t] = new_u
                        s_next[p, t] = new_s
                    if step == 0:
                        t_next[p, t] = s + new_s
                    elif step % 2 == 0:
                        t_next[p, t] = t_now[p, t] + (s + new_s)

            margin = halo - (STEPS - 2 - step)
            each(margin, span - margin, advance, 4)
            s_now, s_next, u_now, u_next = s_next, s_now, u_next, u_now
            if step % 2 == 0:
                t_now, t_next = t_next, t_now

        for m in range(TEAM):
            base = halo + planes * (place ^ m)
            for j in range(planes):
                for t in range(2):
                    outs[m][j, t] = t_now[base + j, t]

    vmem = pl.BlockSpec(memory_space=pltpu.VMEM)
    field = pltpu.VMEM((span, 2, half, columns), F32)
    return pl.pallas_call(
        kernel,
        out_shape=[jax.ShapeDtypeStruct((planes, 2, half, columns), F32)] * TEAM,
        in_specs=[vmem] * 8,
        out_specs=[vmem] * TEAM,
        scratch_shapes=[field] * 13,
        compiler_params=pltpu.CompilerParams(vmem_limit_bytes=32 * MIB),
        cost_estimate=pl.CostEstimate(flops=0, bytes_accessed=22 * MIB, transcendentals=0),
        name=f"solve{slot}",
    )(*inputs)


def weigh_faces(pieces, sums, cells):
    slots = len(pieces)
    planes, _, _, columns = pieces[0][0].shape
    slabs, samples, _ = sums.shape

    def kernel(sums_ref, *refs):
        faces = refs[: slots * TEAM]
        face_ref, moments_ref, weights = refs[slots * TEAM :]
        place = team_place()
        misfit = jnp.sum(sums_ref[...], axis=0)[:, :128] * (1.0 / (2.0 * cells))
        mean = jnp.sum(misfit, axis=0, keepdims=True) * (1.0 / samples)
        deviation = misfit - mean
        variance = jnp.sum(deviation * deviation, axis=0, keepdims=True) * (1.0 / samples)
        lane = lax.broadcasted_iota(jnp.int32, (1, 128), 1)
        moments_ref[...] = jnp.where(lane == 0, mean, variance)
        weights[...] = 1.0 + 2.0 * BETA_RISK * deviation
        for j in range(planes):
            face = jnp.zeros((1, columns), F32)
            for slot in range(slots):
                for m in range(TEAM):
                    row = weights[pl.ds(slots * (place ^ m) + slot, 1), :]
                    wide = jnp.concatenate([row] * (columns // 128), axis=1)
                    face = face + wide * faces[slot * TEAM + m][j, 0, 0:1, :]
            for d in range(slabs):
                face_ref[d, j : j + 1, :] = face

    vmem = pl.BlockSpec(memory_space=pltpu.VMEM)
    return pl.pallas_call(
        kernel,
        out_shape=[
            jax.ShapeDtypeStruct((slabs, planes, columns), F32),
            jax.ShapeDtypeStruct((1, 128), F32),
        ],
        in_specs=[vmem] * (1 + slots * TEAM),
        out_specs=[vmem, vmem],
        scratch_shapes=[pltpu.VMEM((samples, 128), F32)],
        compiler_params=pltpu.CompilerParams(vmem_limit_bytes=24 * MIB),
        name="weigh_faces",
    )(sums, *[piece for group in pieces for piece in group])


def gather_adjoint(pieces):
    slots = len(pieces)
    planes, _, half, columns = pieces[0][0].shape
    tiles = columns // 128
    block = (planes, 2 * half, columns)

    def kernel(*refs):
        blocks, out, held, mixed, sems = refs[: slots * TEAM], *refs[slots * TEAM :]
        place = team_place()
        copies = []
        for slot in range(slots):
            for m in range(TEAM):
                i = slot * TEAM + m
                for j in range(planes):
                    for t in range(2):
                        for c in range(tiles):
                            mixed[i % 2, j, c, pl.ds(t, half, stride=2), :] = blocks[i][
                                j, t, :, c * 128 : (c + 1) * 128
                            ]
                    for c in range(tiles):
                        held[i, j, :, c * 128 : (c + 1) * 128] = mixed[i % 2, j, c]
                copy = pltpu.make_async_copy(
                    held.at[i], out.at[slots * (place ^ m) + slot], sems.at[i]
                )
                copy.start()
                copies.append(copy)
        for copy in copies:
            copy.wait()

    return pl.pallas_call(
        kernel,
        out_shape=jax.ShapeDtypeStruct((slots * TEAM,) + block, F32),
        in_specs=[pl.BlockSpec(memory_space=pltpu.VMEM)] * (slots * TEAM),
        out_specs=pl.BlockSpec(memory_space=pltpu.HBM),
        scratch_shapes=[
            pltpu.VMEM((slots * TEAM,) + block, F32),
            pltpu.VMEM((2, planes, tiles, 2 * half, 128), F32),
            pltpu.SemaphoreType.DMA((slots * TEAM,)),
        ],
        compiler_params=pltpu.CompilerParams(vmem_limit_bytes=16 * MIB),
        cost_estimate=pl.CostEstimate(flops=0, bytes_accessed=4 * MIB, transcendentals=0),
        name="gather_adjoint",
    )(*[piece for group in pieces for piece in group])


def control(faces, basis_z, basis_x, own_count):
    depth_total, columns = faces.shape

    def kernel(face_ref, z_ref, x_ref, out_ref):
        own_modes = z_ref[lax.axis_index("gz")]
        along_z = jnp.dot(
            own_modes, face_ref[...], precision=lax.Precision.HIGHEST, preferred_element_type=F32
        )
        out_ref[...] = jnp.dot(
            along_z, x_ref[...], precision=lax.Precision.HIGHEST, preferred_element_type=F32
        )

    vmem = pl.BlockSpec(memory_space=pltpu.VMEM)
    return pl.pallas_call(
        kernel,
        out_shape=jax.ShapeDtypeStruct((own_count, basis_x.shape[1]), F32),
        in_specs=[vmem] * 3,
        out_specs=vmem,
        compiler_params=pltpu.CompilerParams(vmem_limit_bytes=16 * MIB),
        name="control",
    )(faces, basis_z, basis_x)


def on_device(state, target, rock_type, log_table, obs_scale):
    samples, planes, rows_y, columns = state.shape
    slabs = lax.axis_size("gz")
    slots = samples // TEAM
    depth_total = planes * slabs

    def swap(value, m):
        return lax.ppermute(value, "gz", [(i, i ^ m) for i in range(slabs)])

    def along(value, outward):
        pairs = []
        for i in range(slabs):
            side = (i % TEAM) // 2
            to = i + TEAM if (side == 1) == outward else i - TEAM
            if 0 <= to < slabs:
                pairs.append((i, to))
        return lax.ppermute(value, "gz", pairs)

    fields = (state, target, rock_type, log_table, obs_scale, depth_total)
    sums, far = [], []
    for slot in range(slots):
        blocks, slot_sums = prepare([[(slot, 2)], [(slot, 3)]], fields)
        sums.append(slot_sums)
        far.append([swap(blocks[0], 2), swap(blocks[1], 3)])
    blocks, near_sums = prepare(
        [[(slot, m) for slot in range(slots)] for m in range(2)], fields
    )
    sums.append(near_sums)
    near = [blocks[0], swap(blocks[1], 1)]
    near_halo = [along(block, True) for block in near]
    pieces = []
    for slot in range(slots):
        far_halo = [along(block, False) for block in far[slot]]
        solved = solve(slot, near + far[slot], near_halo + far_halo)
        pieces.append([solved[0]] + [swap(solved[m], m) for m in (1, 2, 3)])

    local_sums = sum(sums[1:], sums[0])
    spread_sums = jnp.broadcast_to(local_sums[None], (slabs,) + local_sums.shape)
    all_sums = lax.all_to_all(spread_sums, "gz", split_axis=0, concat_axis=0, tiled=True)

    faces, moments = weigh_faces(pieces, all_sums, depth_total * rows_y * columns)
    faces = lax.all_to_all(faces, "gz", split_axis=0, concat_axis=0, tiled=True)
    adjoint = gather_adjoint(pieces)
    gradient = control(
        faces.reshape(depth_total, columns),
        jnp.asarray(cosine_basis(depth_total, MA).T.reshape(slabs, MA // slabs, depth_total)),
        jnp.asarray(cosine_basis(columns, MB)),
        MA // slabs,
    )
    return (adjoint, gradient, moments[0, :2])


def solution(mesh):
    return jax.shard_map(
        on_device,
        mesh=mesh,
        in_specs=(
            P("parts", "gz", None, None),
            P(("parts", "gz"), None, None),
            P("parts", "gz", None, None),
            P("parts", None),
            P("parts"),
        ),
        out_specs=(P("parts", "gz", None, None), P(("parts", "gz"), None), P("parts")),
        check_vma=False,
    )
```

```python
import math

import jax
import jax.numpy as jnp
import numpy as np
from jax import lax
from jax.experimental import pallas as pl
from jax.experimental.pallas import tpu as pltpu
from jax.sharding import PartitionSpec as P

NR = 8
DEGREE = 4
SWEEPS = 2
MA = 512
MB = 512

STORAGE = 0.05
BETA_RISK = 0.5
LOWER_EIGEN = 0.05
UPPER_EIGEN = 2.0

TEAM = 4
STEPS = DEGREE * SWEEPS
F32 = jnp.float32
MIB = 1024 * 1024
LANES = 128


def chebyshev_constants(number_steps):
    centre = (UPPER_EIGEN + LOWER_EIGEN) / 2
    spread = (UPPER_EIGEN - LOWER_EIGEN) / 2
    quotient = centre / spread
    rho_now = 1.0 / quotient
    coefficients = []
    for position in range(number_steps):
        rho_next = 1.0 / (2.0 * quotient - rho_now)
        coefficients.append((rho_next * rho_now, 2.0 * rho_next / spread))
        rho_now = rho_next
    return (centre, coefficients)


def cosine_basis(length_total, modes):
    positions = np.arange(length_total, dtype=np.int64)
    mode_index = np.arange(modes, dtype=np.int64)
    product_index = ((2 * positions[:, None] + 1) * (2 * mode_index[None, :] + 1)) % (
        8 * length_total
    )
    angle = product_index.astype(np.float64) * (math.pi / (4 * length_total))
    return (math.sqrt(2.0 / length_total) * np.cos(angle)).astype(np.float32)


def team_place():
    return lax.rem(lax.axis_index("gz"), TEAM)


def prepare(jobs, fields, sums_before):
    state, target, rock_type, log_table, obs_scale = fields
    samples, planes, rows_y, columns = state.shape
    slots = samples // TEAM
    block = (planes, rows_y, columns)
    half, tiles = rows_y // 2, columns // 128
    depth_total = planes * lax.axis_size("gz")
    flat = [(o, i, job) for o, group in enumerate(jobs) for i, job in enumerate(group)]
    count = len(flat)

    def kernel(before_ref, table_ref, scale_ref, state_ref, target_ref, rock_ref, *rest):
        outs, sums_ref = rest[: len(jobs)], rest[len(jobs)]
        table, scale, state_buf, rock_buf, target_buf, mixed, sems = rest[len(jobs) + 1 :]
        place = team_place()
        first_plane = lax.axis_index("gz") * planes
        members = [slots * (place ^ m) + slot for _, _, (slot, m) in flat]
        small = [
            pltpu.make_async_copy(table_ref, table, sems.at[2, 0]),
            pltpu.make_async_copy(scale_ref, scale, sems.at[2, 1]),
            pltpu.make_async_copy(target_ref, target_buf, sems.at[2, 2]),
        ]
        for copy in small:
            copy.start()
        copies = []
        for n, member in enumerate(members):
            pair = (
                pltpu.make_async_copy(rock_ref.at[member], rock_buf.at[n], sems.at[1, n]),
                pltpu.make_async_copy(state_ref.at[member], state_buf.at[n], sems.at[0, n]),
            )
            for copy in pair:
                copy.start()
            copies.append(pair)
        sums_ref[...] = before_ref[...]
        for copy in small:
            copy.wait()
        for n, (o, i, _) in enumerate(flat):
            for copy in copies[n]:
                copy.wait()
            member = members[n]
            values = [
                jnp.exp(jnp.full((8, columns), table[member, code], F32)) for code in range(NR)
            ]
            own_scale = scale[member]
            total = jnp.zeros((8, columns), F32)
            for p in range(planes):
                depth_weight = 1.0 + (2.0 / (depth_total - 1)) * (first_plane + p).astype(F32)
                factor = own_scale * depth_weight
                for first in range(0, rows_y, 8):
                    rows = slice(first, first + 8)
                    codes = rock_buf[n, p, rows]
                    low, mid, high = ((codes & bit) != 0 for bit in (1, 2, 4))
                    pairs = [
                        jnp.where(low, values[2 * k + 1], values[2 * k]) for k in range(NR // 2)
                    ]
                    halves = [jnp.where(mid, pairs[2 * k + 1], pairs[2 * k]) for k in range(2)]
                    gap = state_buf[n, p, rows] - target_buf[p, rows]
                    source = factor * gap
                    total = total + source * gap
                    made = (jnp.where(high, halves[1], halves[0]), source)
                    for a in range(2):
                        for c in range(tiles):
                            mixed[n % 2, p, a, c, rows] = made[a][:, c * 128 : (c + 1) * 128]
                for a in range(2):
                    for t in range(2):
                        for c in range(tiles):
                            outs[o][i, a, p, t, :, c * 128 : (c + 1) * 128] = mixed[
                                n % 2, p, a, c, pl.ds(t, half, stride=2), :
                            ]
            summed = jnp.sum(total, keepdims=True)
            sums_ref[pl.ds(member, 1), :] = jnp.broadcast_to(summed, (1, sums_ref.shape[1]))

    hbm = pl.BlockSpec(memory_space=pltpu.HBM)
    vmem = pl.BlockSpec(memory_space=pltpu.VMEM)
    results = pl.pallas_call(
        kernel,
        out_shape=[jax.ShapeDtypeStruct((len(group), 2, planes, 2, half, columns), F32) for group in jobs]
        + [jax.ShapeDtypeStruct((samples, LANES), F32)],
        in_specs=[vmem] + [hbm] * 5,
        out_specs=[vmem] * (len(jobs) + 1),
        scratch_shapes=[
            pltpu.SMEM(log_table.shape, F32),
            pltpu.SMEM(obs_scale.shape, F32),
            pltpu.VMEM((count,) + block, F32),
            pltpu.VMEM((count,) + block, jnp.int32),
            pltpu.VMEM(block, F32),
            pltpu.VMEM((2, planes, 2, tiles, rows_y, 128), F32),
            pltpu.SemaphoreType.DMA((3, max(count, 3))),
        ],
        compiler_params=pltpu.CompilerParams(vmem_limit_bytes=16 * MIB),
        cost_estimate=pl.CostEstimate(flops=0, bytes_accessed=count * MIB, transcendentals=0),
        name="prepare",
    )(sums_before, log_table, obs_scale, state, target, rock_type)
    return results[:-1], results[-1]


def reciprocal(x):
    guess = pl.reciprocal(x, approx=True)
    return guess * (2.0 - x * guess)


def harmonic(a, b):
    return (a * b) * (2.0 * reciprocal(a + b))


def each(start, stop, body, width):
    whole = (stop - start) // width

    def group(n, carry):
        for k in range(width):
            body(start + n * width + k)
        return carry

    lax.fori_loop(0, whole, group, 0)
    for p in range(start + whole * width, stop):
        body(p)


def risk(sums, cells):
    misfit = sums * (1.0 / (2.0 * cells))
    mean = jnp.mean(misfit, axis=0, keepdims=True)
    deviation = misfit - mean
    variance = jnp.mean(deviation * deviation, axis=0, keepdims=True)
    return 1.0 + 2.0 * BETA_RISK * deviation, mean, variance


def solve(slot, blocks, halos, sums=None, faces=()):
    inputs = list(blocks) + list(halos)
    weigh = sums is not None
    extra = [sums, *faces] if weigh else []
    slots = len(faces) + 1
    planes, _, half, columns = blocks[0].shape[2:]
    near = [0, 1, 4, 5]
    halo = 2 * planes
    own = TEAM * planes
    span = own + 2 * halo
    cells = planes * lax.axis_size("gz") * 2 * half * columns
    centre, coefficients = chebyshev_constants(DEGREE)
    assert halo >= STEPS

    def kernel(*refs):
        ins, refs = refs[:8], refs[8:]
        given, refs = refs[: len(extra)], refs[len(extra) :]
        outs, face_ref, refs = refs[:TEAM], refs[TEAM], refs[TEAM + 1 :]
        if weigh:
            moments_ref, weights, refs = refs[0], refs[-1], refs[1:-1]
        cond, u_a, u_b, s_a, s_b, zp, zm, yp, ym, xp, xm, t_a, t_b = refs
        place = team_place()
        column, side = lax.rem(place, 2), place // 2
        upper, lower = halo + own, 0
        near_base = jnp.where(side == 0, upper, lower)
        far_base = jnp.where(side == 0, lower, upper)
        bases = [halo + planes * (place ^ m) for m in range(TEAM)]
        bases += [near_base + planes * column, near_base + planes * (1 - column)]
        bases += [far_base + planes * column, far_base + planes * (1 - column)]
        for n, base in enumerate(bases):
            item = slot if n in near else 0
            for j in range(planes):
                for t in range(2):
                    cond[base + j, t] = jnp.maximum(ins[n][item, 0, j, t], 1e-30)
                    t_a[base + j, t] = ins[n][item, 1, j, t]

        last_row = lax.broadcasted_iota(jnp.int32, (half, columns), 0) == half - 1
        last_column = lax.broadcasted_iota(jnp.int32, (half, columns), 1) == columns - 1

        def ahead_x(v):
            return pltpu.roll(v, columns - 1, 1)

        def behind_x(v):
            return pltpu.roll(v, 1, 1)

        def ahead_y(v):
            return pltpu.roll(v, half - 1, 0)

        def behind_y(v):
            return pltpu.roll(v, 1, 0)

        def setup(p):
            even, odd = cond[p, 0], cond[p, 1]
            w_pair = harmonic(even, odd)
            w_next = jnp.where(last_row, 0.0, harmonic(odd, ahead_y(even)))
            for t, here in enumerate((even, odd)):
                w_z = harmonic(here, cond[p + 1, t])
                w_z_behind = harmonic(here, cond[p - 1, t])
                w_y = w_next if t else w_pair
                w_y_behind = w_pair if t else behind_y(w_next)
                w_x = jnp.where(last_column, 0.0, harmonic(here, ahead_x(here)))
                w_x_behind = behind_x(w_x)
                diagonal = (w_z + w_z_behind) + (w_y + w_y_behind) + (w_x + w_x_behind) + STORAGE
                inverse = reciprocal(diagonal)
                zp[p, t] = w_z * inverse
                zm[p, t] = w_z_behind * inverse
                yp[p, t] = w_y * inverse
                ym[p, t] = w_y_behind * inverse
                xp[p, t] = w_x * inverse
                xm[p, t] = w_x_behind * inverse
                scaled = t_a[p, t] * inverse
                u_a[p, t] = scaled
                s_a[p, t] = scaled * (1.0 / centre)

        each(1, span - 1, setup, 2)

        s_now, s_next, u_now, u_next, t_now, t_next = s_a, s_b, u_a, u_b, t_a, t_b
        for step in range(STEPS - 1):
            position = step % DEGREE
            if position + 1 < DEGREE:
                keep, mix = coefficients[position]
            else:
                keep, mix = 0.0, 1.0 / centre
            last = step == STEPS - 2

            def advance(p):
                even, odd = s_now[p, 0], s_now[p, 1]
                for t, s in enumerate((even, odd)):
                    ahead = ahead_y(even) if t else odd
                    behind = even if t else behind_y(odd)
                    moved = zp[p, t] * s_now[p + 1, t] + zm[p, t] * s_now[p - 1, t]
                    moved += yp[p, t] * ahead + ym[p, t] * behind
                    moved += xp[p, t] * ahead_x(s) + xm[p, t] * behind_x(s)
                    new_u = (u_now[p, t] - s) + moved
                    new_s = mix * new_u if keep == 0.0 else keep * s + mix * new_u
                    if not last:
                        u_next[p, t] = new_u
                        s_next[p, t] = new_s
                    if step == 0:
                        t_next[p, t] = s + new_s
                    elif step % 2 == 0:
                        t_next[p, t] = t_now[p, t] + (s + new_s)

            margin = halo - (STEPS - 2 - step)
            each(margin, span - margin, advance, 4)
            s_now, s_next, u_now, u_next = s_next, s_now, u_next, u_now
            if step % 2 == 0:
                t_now, t_next = t_next, t_now

        for m in range(TEAM):
            base = halo + planes * (place ^ m)
            for j in range(planes):
                for t in range(2):
                    outs[m][j, t] = t_now[base + j, t]
        face = jnp.concatenate([t_now[halo + p, 0, 0:1, :] for p in range(own)], axis=0)
        if weigh:
            weights[...], mean, variance = risk(given[0][...], cells)
            lane = lax.broadcasted_iota(jnp.int32, (1, LANES), 1)
            moments_ref[...] = jnp.where(lane == 0, mean, variance)
            total = jnp.zeros((own, columns), F32)
            for n, values in enumerate([ref[...] for ref in given[1:]] + [face]):
                row = weights[pl.ds(slots * place + n, 1), :]
                total = total + values * jnp.concatenate([row] * (columns // LANES), axis=1)
            face_ref[...] = total
        else:
            face_ref[...] = face

    vmem = pl.BlockSpec(memory_space=pltpu.VMEM)
    field = pltpu.VMEM((span, 2, half, columns), F32)
    return pl.pallas_call(
        kernel,
        out_shape=[jax.ShapeDtypeStruct((planes, 2, half, columns), F32)] * TEAM
        + [jax.ShapeDtypeStruct((own, columns), F32)]
        + [jax.ShapeDtypeStruct((1, LANES), F32)] * weigh,
        in_specs=[vmem] * (8 + len(extra)),
        out_specs=[vmem] * (TEAM + 1 + weigh),
        scratch_shapes=[field] * 13 + ([pltpu.VMEM(sums.shape, F32)] if weigh else []),
        compiler_params=pltpu.CompilerParams(vmem_limit_bytes=32 * MIB),
        cost_estimate=pl.CostEstimate(flops=0, bytes_accessed=22 * MIB, transcendentals=0),
        name=f"solve{slot}",
    )(*inputs, *extra)


def gather_adjoint(pieces):
    slots = len(pieces)
    planes, _, half, columns = pieces[0][0].shape
    tiles = columns // 128
    block = (planes, 2 * half, columns)

    def kernel(*refs):
        blocks, out, held, mixed, sems = refs[: slots * TEAM], *refs[slots * TEAM :]
        place = team_place()
        copies = []
        for slot in range(slots):
            for m in range(TEAM):
                i = slot * TEAM + m
                for j in range(planes):
                    for t in range(2):
                        for c in range(tiles):
                            mixed[i % 2, j, c, pl.ds(t, half, stride=2), :] = blocks[i][
                                j, t, :, c * 128 : (c + 1) * 128
                            ]
                    for c in range(tiles):
                        held[i, j, :, c * 128 : (c + 1) * 128] = mixed[i % 2, j, c]
                copy = pltpu.make_async_copy(
                    held.at[i], out.at[slots * (place ^ m) + slot], sems.at[i]
                )
                copy.start()
                copies.append(copy)
        for copy in copies:
            copy.wait()

    return pl.pallas_call(
        kernel,
        out_shape=jax.ShapeDtypeStruct((slots * TEAM,) + block, F32),
        in_specs=[pl.BlockSpec(memory_space=pltpu.VMEM)] * (slots * TEAM),
        out_specs=pl.BlockSpec(memory_space=pltpu.HBM),
        scratch_shapes=[
            pltpu.VMEM((slots * TEAM,) + block, F32),
            pltpu.VMEM((2, planes, tiles, 2 * half, 128), F32),
            pltpu.SemaphoreType.DMA((slots * TEAM,)),
        ],
        compiler_params=pltpu.CompilerParams(vmem_limit_bytes=16 * MIB),
        cost_estimate=pl.CostEstimate(flops=0, bytes_accessed=4 * MIB, transcendentals=0),
        name="gather_adjoint",
    )(*[piece for group in pieces for piece in group])


def control(faces, radices, basis_z, basis_x):
    slabs, own_count, depth_total = basis_z.shape
    own, columns = faces[0].shape[1:]
    teams = depth_total // own

    def kernel(*refs):
        parts, (z_ref, x_ref, out_ref, whole) = refs[: len(faces)], refs[len(faces) :]
        rank = lax.axis_index("gz")
        team = rank // TEAM
        for n in range(teams):
            at, left, stride = 0, n, 1
            for radix in radices:
                digit = lax.rem(team // stride + left % radix, radix)
                at, left, stride = at + digit * stride, left // radix, stride * radix
            inner = teams // len(faces)
            whole[at] = parts[n // inner][n % inner]
        along_z = jnp.dot(
            z_ref[rank],
            whole[...].reshape(depth_total, columns),
            precision=lax.Precision.HIGHEST,
            preferred_element_type=F32,
        )
        out_ref[...] = jnp.dot(
            along_z, x_ref[...], precision=lax.Precision.HIGHEST, preferred_element_type=F32
        )

    vmem = pl.BlockSpec(memory_space=pltpu.VMEM)
    return pl.pallas_call(
        kernel,
        out_shape=jax.ShapeDtypeStruct((own_count, basis_x.shape[1]), F32),
        in_specs=[vmem] * (len(faces) + 2),
        out_specs=vmem,
        scratch_shapes=[pltpu.VMEM((teams, own, columns), F32)],
        compiler_params=pltpu.CompilerParams(vmem_limit_bytes=16 * MIB),
        name="control",
    )(*faces, basis_z, basis_x)


def radices_of(teams):
    radices = []
    while teams > 1:
        radix = next(r for r in (4, 2, 3, *range(5, teams + 1)) if teams % r == 0)
        radices.append(radix)
        teams //= radix
    return radices


def on_device(state, target, rock_type, log_table, obs_scale):
    samples, planes, rows_y, columns = state.shape
    slabs = lax.axis_size("gz")
    slots = samples // TEAM
    depth_total = planes * slabs
    radices = radices_of(slabs // TEAM)

    def swap(value, m):
        return lax.ppermute(value, "gz", [(i, i ^ m) for i in range(slabs)])

    def along(value, outward):
        pairs = []
        for i in range(slabs):
            side = (i % TEAM) // 2
            to = i + TEAM if (side == 1) == outward else i - TEAM
            if 0 <= to < slabs:
                pairs.append((i, to))
        return lax.ppermute(value, "gz", pairs)

    def from_teams(value, stride, radix):
        heard = []
        for k in range(1, radix):
            pairs = []
            for i in range(slabs):
                digit = i // (TEAM * stride) % radix
                pairs.append((i + ((digit + k) % radix - digit) * stride * TEAM, i))
            heard.append(lax.ppermute(value, "gz", pairs))
        return heard

    def team_sum(value):
        return sum((swap(value, m) for m in (2, 3, 1)), value)

    fields = [
        pltpu.with_memory_space_constraint(field, pltpu.HBM)
        for field in (state, target, rock_type, log_table, obs_scale)
    ]
    sums = jnp.zeros((samples, LANES), F32)
    far = []
    for slot in range(slots):
        blocks, sums = prepare([[(slot, 2)], [(slot, 3)]], fields, sums)
        far.append([swap(blocks[0], 2), swap(blocks[1], 3)])
    blocks, sums = prepare([[(slot, m) for slot in range(slots)] for m in range(2)], fields, sums)
    near = [blocks[0], swap(blocks[1], 1)]
    near_halo = [along(block, True) for block in near]

    sums = team_sum(sums)
    stride = 1
    for radix in radices:
        sums = sum(from_teams(sums, stride, radix), sums)
        stride *= radix

    pieces, faces = [], []
    for slot in range(slots):
        last = slot == slots - 1
        far_halo = [along(block, False) for block in far[slot]]
        solved = solve(
            slot, near + far[slot], near_halo + far_halo, *((sums, faces) if last else ())
        )
        pieces.append([solved[0]] + [swap(solved[m], m) for m in (1, 2, 3)])
        faces.append(solved[TEAM])
    moments = solved[TEAM + 1]

    heard = [team_sum(faces[-1])[None]]
    stride = 1
    for radix in radices:
        held = heard[0] if len(heard) == 1 else jnp.concatenate(heard)
        heard = [held] + from_teams(held, stride, radix)
        stride *= radix
    adjoint = gather_adjoint(pieces)
    own_count = MA // slabs
    gradient = control(
        heard,
        radices,
        jnp.asarray(cosine_basis(depth_total, MA).T.reshape(slabs, own_count, depth_total)),
        jnp.asarray(cosine_basis(columns, MB)),
    )
    return (adjoint, gradient, moments[0, :2])


def solution(mesh):
    return jax.shard_map(
        on_device,
        mesh=mesh,
        in_specs=(
            P("parts", "gz", None, None),
            P(("parts", "gz"), None, None),
            P("parts", "gz", None, None),
            P("parts", None),
            P("parts"),
        ),
        out_specs=(P("parts", "gz", None, None), P(("parts", "gz"), None), P("parts")),
        check_vma=False,
    )
```

```python
import math

import jax
import jax.numpy as jnp
import numpy as np
from jax import lax
from jax.experimental import pallas as pl
from jax.experimental.pallas import tpu as pltpu
from jax.sharding import PartitionSpec as P

NR = 8
DEGREE = 4
SWEEPS = 2
MA = 512
MB = 512

STORAGE = 0.05
BETA_RISK = 0.5
LOWER_EIGEN = 0.05
UPPER_EIGEN = 2.0

TEAM = 4
STEPS = DEGREE * SWEEPS
F32 = jnp.float32
MIB = 1024 * 1024
LANES = 128


def chebyshev_constants(number_steps):
    centre = (UPPER_EIGEN + LOWER_EIGEN) / 2
    spread = (UPPER_EIGEN - LOWER_EIGEN) / 2
    quotient = centre / spread
    rho_now = 1.0 / quotient
    coefficients = []
    for position in range(number_steps):
        rho_next = 1.0 / (2.0 * quotient - rho_now)
        coefficients.append((rho_next * rho_now, 2.0 * rho_next / spread))
        rho_now = rho_next
    return (centre, coefficients)


def cosine_basis(length_total, modes):
    positions = np.arange(length_total, dtype=np.int64)
    mode_index = np.arange(modes, dtype=np.int64)
    product_index = ((2 * positions[:, None] + 1) * (2 * mode_index[None, :] + 1)) % (
        8 * length_total
    )
    angle = product_index.astype(np.float64) * (math.pi / (4 * length_total))
    return (math.sqrt(2.0 / length_total) * np.cos(angle)).astype(np.float32)


def team_place():
    return lax.rem(lax.axis_index("gz"), TEAM)


def prepare(jobs, fields, sums_before, by_core=False):
    state, target, rock_type, log_table, obs_scale = fields
    samples, planes, rows_y, columns = state.shape
    slots = samples // TEAM
    block = (planes, rows_y, columns)
    half, tiles = rows_y // 2, columns // 128
    depth_total = planes * lax.axis_size("gz")
    flat = [(o, i, job) for o, group in enumerate(jobs) for i, job in enumerate(group)]
    count = len(flat)
    shapes = [(len(group), 2, planes, 2, half, columns) for group in jobs]
    if by_core:
        shapes = [(len(jobs),) + shapes[0]]

    def kernel(before_ref, table_ref, scale_ref, state_ref, target_ref, rock_ref, *rest):
        outs, sums_ref = rest[: len(shapes)], rest[len(shapes)]
        table, scale, state_buf, rock_buf, target_buf, mixed, sems = rest[len(shapes) + 1 :]
        place = team_place()
        first_plane = lax.axis_index("gz") * planes
        members = [slots * (place ^ m) + slot for _, _, (slot, m) in flat]
        small = [
            pltpu.make_async_copy(table_ref, table, sems.at[2, 0]),
            pltpu.make_async_copy(scale_ref, scale, sems.at[2, 1]),
            pltpu.make_async_copy(target_ref, target_buf, sems.at[2, 2]),
        ]
        for copy in small:
            copy.start()
        copies = []
        for n, member in enumerate(members):
            pair = (
                pltpu.make_async_copy(rock_ref.at[member], rock_buf.at[n], sems.at[1, n]),
                pltpu.make_async_copy(state_ref.at[member], state_buf.at[n], sems.at[0, n]),
            )
            for copy in pair:
                copy.start()
            copies.append(pair)
        sums_ref[...] = before_ref[...]
        for copy in small:
            copy.wait()
        for n, (o, i, _) in enumerate(flat):
            for copy in copies[n]:
                copy.wait()
            member = members[n]
            values = [
                jnp.exp(jnp.full((8, columns), table[member, code], F32)) for code in range(NR)
            ]
            own_scale = scale[member]
            at = (lax.rem(place, 2) ^ o, i) if by_core else (i,)
            out_ref = outs[0 if by_core else o]
            total = jnp.zeros((8, columns), F32)
            for p in range(planes):
                depth_weight = 1.0 + (2.0 / (depth_total - 1)) * (first_plane + p).astype(F32)
                factor = own_scale * depth_weight
                for first in range(0, rows_y, 8):
                    rows = slice(first, first + 8)
                    codes = rock_buf[n, p, rows]
                    low, mid, high = ((codes & bit) != 0 for bit in (1, 2, 4))
                    pairs = [
                        jnp.where(low, values[2 * k + 1], values[2 * k]) for k in range(NR // 2)
                    ]
                    halves = [jnp.where(mid, pairs[2 * k + 1], pairs[2 * k]) for k in range(2)]
                    gap = state_buf[n, p, rows] - target_buf[p, rows]
                    source = factor * gap
                    total = total + source * gap
                    made = (jnp.where(high, halves[1], halves[0]), source)
                    for a in range(2):
                        for c in range(tiles):
                            mixed[n % 2, p, a, c, rows] = made[a][:, c * 128 : (c + 1) * 128]
                for a in range(2):
                    for t in range(2):
                        for c in range(tiles):
                            out_ref[*at, a, p, t, :, c * 128 : (c + 1) * 128] = mixed[
                                n % 2, p, a, c, pl.ds(t, half, stride=2), :
                            ]
            summed = jnp.sum(total, keepdims=True)
            sums_ref[pl.ds(member, 1), :] = jnp.broadcast_to(summed, (1, sums_ref.shape[1]))

    hbm = pl.BlockSpec(memory_space=pltpu.HBM)
    vmem = pl.BlockSpec(memory_space=pltpu.VMEM)
    results = pl.pallas_call(
        kernel,
        out_shape=[jax.ShapeDtypeStruct(shape, F32) for shape in shapes]
        + [jax.ShapeDtypeStruct(sums_before.shape, F32)],
        in_specs=[vmem] + [hbm] * 5,
        out_specs=[vmem] * (len(shapes) + 1),
        scratch_shapes=[
            pltpu.SMEM(log_table.shape, F32),
            pltpu.SMEM(obs_scale.shape, F32),
            pltpu.VMEM((count,) + block, F32),
            pltpu.VMEM((count,) + block, jnp.int32),
            pltpu.VMEM(block, F32),
            pltpu.VMEM((2, planes, 2, tiles, rows_y, 128), F32),
            pltpu.SemaphoreType.DMA((3, max(count, 3))),
        ],
        compiler_params=pltpu.CompilerParams(vmem_limit_bytes=16 * MIB),
        cost_estimate=pl.CostEstimate(flops=0, bytes_accessed=count * MIB, transcendentals=0),
        name="prepare",
    )(sums_before, log_table, obs_scale, state, target, rock_type)
    return results[:-1], results[-1]


def reciprocal(x):
    guess = pl.reciprocal(x, approx=True)
    return guess * (2.0 - x * guess)


def harmonic(a, b):
    return (a * b) * (2.0 * reciprocal(a + b))


def each(start, stop, body, width):
    whole = (stop - start) // width

    def group(n, carry):
        for k in range(width):
            body(start + n * width + k)
        return carry

    lax.fori_loop(0, whole, group, 0)
    for p in range(start + whole * width, stop):
        body(p)


def team_sums(first):
    def kernel(*refs):
        last = first[0].shape[0] - 1
        total = refs[0][last]
        for ref in refs[1:TEAM]:
            total = total + ref[last]
        refs[TEAM][...] = total[:, :LANES]

    vmem = pl.BlockSpec(memory_space=pltpu.VMEM)
    return pl.pallas_call(
        kernel,
        out_shape=jax.ShapeDtypeStruct((first[0].shape[1], LANES), F32),
        in_specs=[vmem] * TEAM,
        out_specs=vmem,
        name="team_sums",
    )(*first)


def weigh(sums, first, faces, planes, cells):
    own = TEAM * planes
    half, columns = faces[0].shape[1:]
    slots = 2
    samples = sums[0].shape[0]

    def kernel(*refs):
        sum_refs, refs = refs[: len(sums)], refs[len(sums) :]
        first_refs, face_refs, refs = refs[:TEAM], refs[TEAM : 2 * TEAM], refs[2 * TEAM :]
        out_ref, moments_ref, weights = refs
        place = team_place()
        summed = sum_refs[0][...]
        for ref in sum_refs[1:]:
            summed = summed + ref[...]
        misfit = summed * (1.0 / (2.0 * cells))
        mean = jnp.sum(misfit, axis=0, keepdims=True) * (1.0 / samples)
        deviation = misfit - mean
        variance = jnp.sum(deviation * deviation, axis=0, keepdims=True) * (1.0 / samples)
        lane = lax.broadcasted_iota(jnp.int32, (1, LANES), 1)
        moments_ref[...] = jnp.where(lane == 0, mean, variance)
        weights[...] = 1.0 + 2.0 * BETA_RISK * deviation
        for tile in range(own // half):
            total = jnp.zeros((half, columns), F32)
            for slot in range(slots):
                for m in range(TEAM):
                    row = weights[pl.ds(slots * (place ^ m) + slot, 1), :]
                    wide = jnp.concatenate([row] * (columns // LANES), axis=1)
                    face = face_refs[m][tile] if slot else first_refs[m][2 * planes + tile]
                    total = total + wide * face
            out_ref[0, tile * half : (tile + 1) * half, :] = total

    vmem = pl.BlockSpec(memory_space=pltpu.VMEM)
    return pl.pallas_call(
        kernel,
        out_shape=[
            jax.ShapeDtypeStruct((1, own, columns), F32),
            jax.ShapeDtypeStruct((1, LANES), F32),
        ],
        in_specs=[vmem] * (len(sums) + 2 * TEAM),
        out_specs=[vmem, vmem],
        scratch_shapes=[pltpu.VMEM((samples, LANES), F32)],
        compiler_params=pltpu.CompilerParams(vmem_limit_bytes=16 * MIB),
        name="weigh",
    )(*sums, *first, *faces)


def solve(slot, near, far, near_halo, far_halo, sums=None):
    inputs = [near, near_halo, *far, *far_halo]
    extra = [] if sums is None else [sums]
    planes, _, half, columns = far[0].shape[2:]
    halo = 2 * planes
    own = TEAM * planes
    span = own + 2 * halo
    centre, coefficients = chebyshev_constants(DEGREE)
    assert halo >= STEPS
    tail = (own + sums.shape[0]) // half if extra else 0

    def kernel(*refs):
        ins, refs = refs[:6], refs[6:]
        given, refs = refs[: len(extra)], refs[len(extra) :]
        outs, face_ref, refs = refs[:TEAM], refs[TEAM], refs[TEAM + 1 :]
        cond, u_a, u_b, s_a, s_b, zp, zm, yp, ym, xp, xm, t_a, t_b = refs
        place = team_place()
        column, side = lax.rem(place, 2), place // 2
        upper, lower = halo + own, 0
        near_base = jnp.where(side == 0, upper, lower)
        far_base = jnp.where(side == 0, lower, upper)
        blocks = [(ins[0].at[core, slot], halo + planes * (2 * side + core)) for core in range(2)]
        blocks += [(ins[1].at[core, slot], near_base + planes * core) for core in range(2)]
        blocks += [(ins[m].at[0], halo + planes * (place ^ m)) for m in (2, 3)]
        blocks += [(ins[4].at[0], far_base + planes * column)]
        blocks += [(ins[5].at[0], far_base + planes * (1 - column))]
        for block, base in blocks:
            for j in range(planes):
                for t in range(2):
                    cond[base + j, t] = jnp.maximum(block[0, j, t], 1e-30)
                    t_a[base + j, t] = block[1, j, t]

        last_row = lax.broadcasted_iota(jnp.int32, (half, columns), 0) == half - 1
        last_column = lax.broadcasted_iota(jnp.int32, (half, columns), 1) == columns - 1

        def ahead_x(v):
            return pltpu.roll(v, columns - 1, 1)

        def behind_x(v):
            return pltpu.roll(v, 1, 1)

        def ahead_y(v):
            return pltpu.roll(v, half - 1, 0)

        def behind_y(v):
            return pltpu.roll(v, 1, 0)

        def setup(p):
            even, odd = cond[p, 0], cond[p, 1]
            w_pair = harmonic(even, odd)
            w_next = jnp.where(last_row, 0.0, harmonic(odd, ahead_y(even)))
            for t, here in enumerate((even, odd)):
                w_z = harmonic(here, cond[p + 1, t])
                w_z_behind = harmonic(here, cond[p - 1, t])
                w_y = w_next if t else w_pair
                w_y_behind = w_pair if t else behind_y(w_next)
                w_x = jnp.where(last_column, 0.0, harmonic(here, ahead_x(here)))
                w_x_behind = behind_x(w_x)
                diagonal = (w_z + w_z_behind) + (w_y + w_y_behind) + (w_x + w_x_behind) + STORAGE
                inverse = reciprocal(diagonal)
                zp[p, t] = w_z * inverse
                zm[p, t] = w_z_behind * inverse
                yp[p, t] = w_y * inverse
                ym[p, t] = w_y_behind * inverse
                xp[p, t] = w_x * inverse
                xm[p, t] = w_x_behind * inverse
                scaled = t_a[p, t] * inverse
                u_a[p, t] = scaled
                s_a[p, t] = scaled * (1.0 / centre)

        each(1, span - 1, setup, 2)

        s_now, s_next, u_now, u_next, t_now, t_next = s_a, s_b, u_a, u_b, t_a, t_b
        for step in range(STEPS - 1):
            position = step % DEGREE
            if position + 1 < DEGREE:
                keep, mix = coefficients[position]
            else:
                keep, mix = 0.0, 1.0 / centre
            last = step == STEPS - 2

            def advance(p):
                even, odd = s_now[p, 0], s_now[p, 1]
                for t, s in enumerate((even, odd)):
                    ahead = ahead_y(even) if t else odd
                    behind = even if t else behind_y(odd)
                    moved = zp[p, t] * s_now[p + 1, t] + zm[p, t] * s_now[p - 1, t]
                    moved += yp[p, t] * ahead + ym[p, t] * behind
                    moved += xp[p, t] * ahead_x(s) + xm[p, t] * behind_x(s)
                    new_u = (u_now[p, t] - s) + moved
                    new_s = mix * new_u if keep == 0.0 else keep * s + mix * new_u
                    if not last:
                        u_next[p, t] = new_u
                        s_next[p, t] = new_s
                    if step == 0:
                        t_next[p, t] = s + new_s
                    elif step % 2 == 0:
                        t_next[p, t] = t_now[p, t] + (s + new_s)

            margin = halo - (STEPS - 2 - step)
            each(margin, span - margin, advance, 4)
            s_now, s_next, u_now, u_next = s_next, s_now, u_next, u_now
            if step % 2 == 0:
                t_now, t_next = t_next, t_now

        for m in range(TEAM):
            base = halo + planes * (place ^ m)
            for j in range(planes):
                for t in range(2):
                    outs[m][2 * j + t] = t_now[base + j, t]
        for p in range(own):
            face_ref[p // half, p % half : p % half + 1, :] = t_now[halo + p, 0, 0:1, :]
        for m in range(TEAM if extra else 0):
            outs[m][2 * planes : 2 * planes + own // half] = face_ref[...]
            outs[m][2 * planes + own // half] = given[0][...]

    vmem = pl.BlockSpec(memory_space=pltpu.VMEM)
    field = pltpu.VMEM((span, 2, half, columns), F32)
    return pl.pallas_call(
        kernel,
        out_shape=[jax.ShapeDtypeStruct((2 * planes + tail, half, columns), F32)] * TEAM
        + [jax.ShapeDtypeStruct((own // half, half, columns), F32)],
        in_specs=[vmem] * (6 + len(extra)),
        out_specs=[vmem] * (TEAM + 1),
        scratch_shapes=[field] * 13,
        compiler_params=pltpu.CompilerParams(vmem_limit_bytes=32 * MIB),
        cost_estimate=pl.CostEstimate(flops=0, bytes_accessed=22 * MIB, transcendentals=0),
        name=f"solve{slot}",
    )(*inputs, *extra)


def gather_adjoint(pieces, planes):
    slots = len(pieces)
    _, half, columns = pieces[0][0].shape
    tiles = columns // 128
    block = (planes, 2 * half, columns)

    def kernel(*refs):
        blocks, out, held, mixed, sems = refs[: slots * TEAM], *refs[slots * TEAM :]
        place = team_place()
        copies = []
        for slot in range(slots):
            for m in range(TEAM):
                i = slot * TEAM + m
                for j in range(planes):
                    for t in range(2):
                        for c in range(tiles):
                            mixed[i % 2, j, c, pl.ds(t, half, stride=2), :] = blocks[i][
                                2 * j + t, :, c * 128 : (c + 1) * 128
                            ]
                    for c in range(tiles):
                        held[i, j, :, c * 128 : (c + 1) * 128] = mixed[i % 2, j, c]
                copy = pltpu.make_async_copy(
                    held.at[i], out.at[slots * (place ^ m) + slot], sems.at[i]
                )
                copy.start()
                copies.append(copy)
        for copy in copies:
            copy.wait()

    return pl.pallas_call(
        kernel,
        out_shape=jax.ShapeDtypeStruct((slots * TEAM,) + block, F32),
        in_specs=[pl.BlockSpec(memory_space=pltpu.VMEM)] * (slots * TEAM),
        out_specs=pl.BlockSpec(memory_space=pltpu.HBM),
        scratch_shapes=[
            pltpu.VMEM((slots * TEAM,) + block, F32),
            pltpu.VMEM((2, planes, tiles, 2 * half, 128), F32),
            pltpu.SemaphoreType.DMA((slots * TEAM,)),
        ],
        compiler_params=pltpu.CompilerParams(vmem_limit_bytes=16 * MIB),
        cost_estimate=pl.CostEstimate(flops=0, bytes_accessed=4 * MIB, transcendentals=0),
        name="gather_adjoint",
    )(*[piece for group in pieces for piece in group])


def control(faces, radices, basis_z, basis_x):
    slabs, own_count, depth_total = basis_z.shape
    own, columns = faces[0].shape[1:]
    teams = depth_total // own

    def kernel(*refs):
        parts, (z_ref, x_ref, out_ref, whole) = refs[: len(faces)], refs[len(faces) :]
        rank = lax.axis_index("gz")
        team = rank // TEAM
        for n in range(teams):
            at, left, stride = 0, n, 1
            for radix in radices:
                digit = lax.rem(team // stride + left % radix, radix)
                at, left, stride = at + digit * stride, left // radix, stride * radix
            inner = teams // len(faces)
            whole[at] = parts[n // inner][n % inner]
        along_z = jnp.dot(
            z_ref[rank],
            whole[...].reshape(depth_total, columns),
            precision=lax.Precision.HIGHEST,
            preferred_element_type=F32,
        )
        out_ref[...] = jnp.dot(
            along_z, x_ref[...], precision=lax.Precision.HIGHEST, preferred_element_type=F32
        )

    vmem = pl.BlockSpec(memory_space=pltpu.VMEM)
    return pl.pallas_call(
        kernel,
        out_shape=jax.ShapeDtypeStruct((own_count, basis_x.shape[1]), F32),
        in_specs=[vmem] * (len(faces) + 2),
        out_specs=vmem,
        scratch_shapes=[pltpu.VMEM((teams, own, columns), F32)],
        compiler_params=pltpu.CompilerParams(vmem_limit_bytes=16 * MIB),
        name="control",
    )(*faces, basis_z, basis_x)


def radices_of(teams):
    radices = []
    while teams > 1:
        radix = next(r for r in (4, 2, 3, *range(5, teams + 1)) if teams % r == 0)
        radices.append(radix)
        teams //= radix
    return radices


def on_device(state, target, rock_type, log_table, obs_scale):
    samples, planes, rows_y, columns = state.shape
    slabs = lax.axis_size("gz")
    slots = samples // TEAM
    depth_total = planes * slabs
    radices = radices_of(slabs // TEAM)

    def swap(value, m):
        return lax.ppermute(value, "gz", [(i, i ^ m) for i in range(slabs)])

    def along(value, outward):
        pairs = []
        for i in range(slabs):
            side = (i % TEAM) // 2
            to = i + TEAM if (side == 1) == outward else i - TEAM
            if 0 <= to < slabs:
                pairs.append((i, to))
        return lax.ppermute(value, "gz", pairs)

    def from_teams(value, stride, radix):
        heard = []
        for k in range(1, radix):
            pairs = []
            for i in range(slabs):
                digit = i // (TEAM * stride) % radix
                pairs.append((i + ((digit + k) % radix - digit) * stride * TEAM, i))
            heard.append(lax.ppermute(value, "gz", pairs))
        return heard

    fields = [
        pltpu.with_memory_space_constraint(field, pltpu.HBM)
        for field in (state, target, rock_type, log_table, obs_scale)
    ]
    sums = jnp.zeros((samples, columns), F32)
    jobs = [[(slot, m) for slot in range(slots)] for m in range(2)]
    far = [None] * slots
    blocks, sums = prepare([[(0, 2)], [(0, 3)]], fields, sums)
    far[0] = [swap(blocks[0], 2), swap(blocks[1], 3)]
    (near_blocks,), sums = prepare(jobs, fields, sums, by_core=True)
    for slot in range(1, slots):
        blocks, sums = prepare([[(slot, 2)], [(slot, 3)]], fields, sums)
        far[slot] = [swap(blocks[0], 2), swap(blocks[1], 3)]
    blocks = near_blocks
    chips = [[i, i + 1] for i in range(0, slabs, 2)]
    near = lax.all_to_all(
        blocks, "gz", split_axis=0, concat_axis=0, axis_index_groups=chips, tiled=True
    )
    near_halo = along(near, True)

    pieces = []
    for slot in range(slots):
        far_halo = [along(block, False) for block in far[slot]]
        solved = solve(slot, near, far[slot], near_halo, far_halo, None if slot else sums)
        pieces.append([solved[0]] + [swap(solved[m], m) for m in (1, 2, 3)])
    faces = [solved[TEAM]] + [swap(solved[TEAM], m) for m in (1, 2, 3)]

    sums = [team_sums(pieces[0])]
    stride = 1
    for radix in radices:
        held = sum(sums[1:], sums[0])
        sums = [held] + from_teams(held, stride, radix)
        stride *= radix
    heard, moments = weigh(sums, pieces[0], faces, planes, depth_total * rows_y * columns)
    heard = [heard]
    stride = 1
    for radix in radices:
        held = heard[0] if len(heard) == 1 else jnp.concatenate(heard)
        heard = [held] + from_teams(held, stride, radix)
        stride *= radix
    adjoint = gather_adjoint(pieces, planes)
    own_count = MA // slabs
    gradient = control(
        heard,
        radices,
        jnp.asarray(cosine_basis(depth_total, MA).T.reshape(slabs, own_count, depth_total)),
        jnp.asarray(cosine_basis(columns, MB)),
    )
    return (adjoint, gradient, moments[0, :2])


def solution(mesh):
    return jax.shard_map(
        on_device,
        mesh=mesh,
        in_specs=(
            P("parts", "gz", None, None),
            P(("parts", "gz"), None, None),
            P("parts", "gz", None, None),
            P("parts", None),
            P("parts"),
        ),
        out_specs=(P("parts", "gz", None, None), P(("parts", "gz"), None), P("parts")),
        check_vma=False,
    )
```

```python
import math

import jax
import jax.numpy as jnp
import numpy as np
from jax import lax
from jax.experimental import pallas as pl
from jax.experimental.pallas import tpu as pltpu
from jax.sharding import PartitionSpec as P

NR = 8
DEGREE = 4
SWEEPS = 2
MA = 512
MB = 512

STORAGE = 0.05
BETA_RISK = 0.5
LOWER_EIGEN = 0.05
UPPER_EIGEN = 2.0

TEAM = 4
STEPS = DEGREE * SWEEPS
F32 = jnp.float32
MIB = 1024 * 1024
LANES = 128


def chebyshev_constants(number_steps):
    centre = (UPPER_EIGEN + LOWER_EIGEN) / 2
    spread = (UPPER_EIGEN - LOWER_EIGEN) / 2
    quotient = centre / spread
    rho_now = 1.0 / quotient
    coefficients = []
    for position in range(number_steps):
        rho_next = 1.0 / (2.0 * quotient - rho_now)
        coefficients.append((rho_next * rho_now, 2.0 * rho_next / spread))
        rho_now = rho_next
    return (centre, coefficients)


def cosine_basis(length_total, modes):
    positions = np.arange(length_total, dtype=np.int64)
    mode_index = np.arange(modes, dtype=np.int64)
    product_index = ((2 * positions[:, None] + 1) * (2 * mode_index[None, :] + 1)) % (
        8 * length_total
    )
    angle = product_index.astype(np.float64) * (math.pi / (4 * length_total))
    return (math.sqrt(2.0 / length_total) * np.cos(angle)).astype(np.float32)


def team_place():
    return lax.rem(lax.axis_index("gz"), TEAM)


def prepare(jobs, fields, sums=None):
    state, target, rock_type, log_table, obs_scale = fields
    samples, planes, rows_y, columns = state.shape
    slots = samples // TEAM
    block = (planes, rows_y, columns)
    half, tiles = rows_y // 2, columns // 128
    size = 2 * 2 * planes
    depth_total = planes * lax.axis_size("gz")
    flat = [(o, i, job) for o, group in enumerate(jobs) for i, job in enumerate(group)]
    count = len(flat)
    shapes = [(len(group) * size + 1, half, columns) for group in jobs]
    given = [] if sums is None else [sums]
    states = count if given else samples

    def kernel(*refs):
        before, refs = refs[: len(given)], refs[len(given) :]
        (table_ref, scale_ref, state_ref, target_ref, rock_ref), refs = refs[:5], refs[5:]
        outs, refs = refs[: len(jobs)], refs[len(jobs) :]
        if not given:
            sums_ref, refs = refs[0], refs[1:]
        table, scale, state_buf, rock_buf, target_buf, mixed, sems = refs
        place = team_place()
        first_plane = lax.axis_index("gz") * planes
        members = [slots * (place ^ m) + slot for _, _, (slot, m) in flat]
        small = [
            pltpu.make_async_copy(table_ref, table, sems.at[2, 0]),
            pltpu.make_async_copy(scale_ref, scale, sems.at[2, 1]),
            pltpu.make_async_copy(target_ref, target_buf, sems.at[2, 2]),
        ]
        for copy in small:
            copy.start()
        rocks = [
            pltpu.make_async_copy(rock_ref.at[member], rock_buf.at[n], sems.at[1, n])
            for n, member in enumerate(members)
        ]
        loads = [
            pltpu.make_async_copy(
                state_ref.at[members[n] if given else n], state_buf.at[n], sems.at[0, n]
            )
            for n in range(states)
        ]
        for copy in rocks + loads:
            copy.start()
        depth_weights = [
            1.0 + (2.0 / (depth_total - 1)) * (first_plane + p).astype(F32) for p in range(planes)
        ]
        for copy in small:
            copy.wait()
        if not given:
            for copy in loads:
                copy.wait()
            for n in range(samples):
                total = jnp.zeros((8, columns), F32)
                for p in range(planes):
                    part = jnp.zeros((8, columns), F32)
                    for first in range(0, rows_y, 8):
                        rows = slice(first, first + 8)
                        gap = state_buf[n, p, rows] - target_buf[p, rows]
                        part = part + gap * gap
                    total = total + (scale[n] * depth_weights[p]) * part
                summed = jnp.sum(total, keepdims=True)
                sums_ref[n : n + 1, :] = jnp.broadcast_to(summed, (1, columns))
        for n, (o, i, _) in enumerate(flat):
            rocks[n].wait()
            if given:
                loads[n].wait()
            member = members[n]
            own_state = n if given else member
            values = [
                jnp.exp(jnp.full((8, columns), table[member, code], F32)) for code in range(NR)
            ]
            for p in range(planes):
                factor = scale[member] * depth_weights[p]
                for first in range(0, rows_y, 8):
                    rows = slice(first, first + 8)
                    codes = rock_buf[n, p, rows]
                    low, mid, high = ((codes & bit) != 0 for bit in (1, 2, 4))
                    pairs = [
                        jnp.where(low, values[2 * k + 1], values[2 * k]) for k in range(NR // 2)
                    ]
                    halves = [jnp.where(mid, pairs[2 * k + 1], pairs[2 * k]) for k in range(2)]
                    gap = state_buf[own_state, p, rows] - target_buf[p, rows]
                    made = (jnp.where(high, halves[1], halves[0]), factor * gap)
                    for a in range(2):
                        for c in range(tiles):
                            mixed[n % 2, p, a, c, rows] = made[a][:, c * 128 : (c + 1) * 128]
                for a in range(2):
                    for t in range(2):
                        for c in range(tiles):
                            at = i * size + (a * planes + p) * 2 + t
                            outs[o][at, :, c * 128 : (c + 1) * 128] = mixed[
                                n % 2, p, a, c, pl.ds(t, half, stride=2), :
                            ]
        for o, group in enumerate(jobs):
            outs[o][len(group) * size] = before[0][...] if given else sums_ref[...]

    hbm = pl.BlockSpec(memory_space=pltpu.HBM)
    vmem = pl.BlockSpec(memory_space=pltpu.VMEM)
    sums_shape = (samples, columns)
    return pl.pallas_call(
        kernel,
        out_shape=[jax.ShapeDtypeStruct(shape, F32) for shape in shapes]
        + ([] if given else [jax.ShapeDtypeStruct(sums_shape, F32)]),
        in_specs=[vmem] * len(given) + [hbm] * 5,
        out_specs=[vmem] * (len(shapes) + 1 - len(given)),
        scratch_shapes=[
            pltpu.SMEM(log_table.shape, F32),
            pltpu.SMEM(obs_scale.shape, F32),
            pltpu.VMEM((states,) + block, F32),
            pltpu.VMEM((count,) + block, jnp.int32),
            pltpu.VMEM(block, F32),
            pltpu.VMEM((2, planes, 2, tiles, rows_y, 128), F32),
            pltpu.SemaphoreType.DMA((3, max(states, 3))),
        ],
        compiler_params=pltpu.CompilerParams(vmem_limit_bytes=6 * MIB),
        cost_estimate=pl.CostEstimate(flops=0, bytes_accessed=count * MIB, transcendentals=0),
        name="prepare",
    )(*given, log_table, obs_scale, state, target, rock_type)


def merge(mine, theirs, slots, after):
    size = (mine.shape[0] - 1) // slots

    def kernel(mine_ref, theirs_ref, _, out_ref):
        core = lax.rem(team_place(), 2)
        for ref, at in ((mine_ref, core), (theirs_ref, 1 - core)):
            for slot in range(slots):
                for n in range(size):
                    out_ref[at, slot, n] = ref[slot * size + n]

    vmem = pl.BlockSpec(memory_space=pltpu.VMEM)
    return pl.pallas_call(
        kernel,
        out_shape=jax.ShapeDtypeStruct((2, slots, size) + mine.shape[1:], F32),
        in_specs=[vmem] * 2 + [pl.BlockSpec(memory_space=pl.ANY)],
        out_specs=vmem,
        compiler_params=pltpu.CompilerParams(vmem_limit_bytes=4 * MIB),
        name="merge",
    )(mine, theirs, after)


def reciprocal(x):
    guess = pl.reciprocal(x, approx=True)
    return guess * (2.0 - x * guess)


def harmonic(a, b):
    return (a * b) * (2.0 * reciprocal(a + b))


def each(start, stop, body, width):
    whole = (stop - start) // width

    def group(n, carry):
        for k in range(width):
            body(start + n * width + k)
        return carry

    lax.fori_loop(0, whole, group, 0)
    for p in range(start + whole * width, stop):
        body(p)


def solve(slot, near, far, near_halo, far_halo, sums, planes):
    inputs = [near, near_halo, *far, *far_halo, *sums]
    half, columns = far[0].shape[1:]
    halo = 2 * planes
    own = TEAM * planes
    span = own + 2 * halo
    centre, coefficients = chebyshev_constants(DEGREE)
    assert halo >= STEPS

    def kernel(*refs):
        ins, refs = refs[:6], refs[6:]
        sum_refs, refs = refs[: len(sums)], refs[len(sums) :]
        outs, face_ref, refs = refs[:TEAM], refs[TEAM], refs[TEAM + 1 :]
        if sums:
            summed_ref, refs = refs[0], refs[1:]
            summed = sum_refs[0][sums[0].shape[0] - 1]
            for n, ref in enumerate(sum_refs[1:], 1):
                summed = summed + ref[sums[n].shape[0] - 1]
            summed_ref[...] = summed
        cond, u_a, u_b, s_a, s_b, zp, zm, yp, ym, xp, xm, t_a, t_b = refs
        place = team_place()
        column, side = lax.rem(place, 2), place // 2
        upper, lower = halo + own, 0
        near_base = jnp.where(side == 0, upper, lower)
        far_base = jnp.where(side == 0, lower, upper)
        blocks = [(ins[0].at[core, slot], halo + planes * (2 * side + core)) for core in range(2)]
        blocks += [(ins[1].at[core, slot], near_base + planes * core) for core in range(2)]
        blocks += [(ins[m], halo + planes * (place ^ m)) for m in (2, 3)]
        blocks += [(ins[4], far_base + planes * column)]
        blocks += [(ins[5], far_base + planes * (1 - column))]
        for block, base in blocks:
            for j in range(planes):
                for t in range(2):
                    cond[base + j, t] = jnp.maximum(block[2 * j + t], 1e-30)
                    t_a[base + j, t] = block[2 * (planes + j) + t]

        last_row = lax.broadcasted_iota(jnp.int32, (half, columns), 0) == half - 1
        last_column = lax.broadcasted_iota(jnp.int32, (half, columns), 1) == columns - 1

        def ahead_x(v):
            return pltpu.roll(v, columns - 1, 1)

        def behind_x(v):
            return pltpu.roll(v, 1, 1)

        def ahead_y(v):
            return pltpu.roll(v, half - 1, 0)

        def behind_y(v):
            return pltpu.roll(v, 1, 0)

        def setup(p):
            even, odd = cond[p, 0], cond[p, 1]
            w_pair = harmonic(even, odd)
            w_next = jnp.where(last_row, 0.0, harmonic(odd, ahead_y(even)))
            for t, here in enumerate((even, odd)):
                w_z = harmonic(here, cond[p + 1, t])
                w_z_behind = harmonic(here, cond[p - 1, t])
                w_y = w_next if t else w_pair
                w_y_behind = w_pair if t else behind_y(w_next)
                w_x = jnp.where(last_column, 0.0, harmonic(here, ahead_x(here)))
                w_x_behind = behind_x(w_x)
                diagonal = (w_z + w_z_behind) + (w_y + w_y_behind) + (w_x + w_x_behind) + STORAGE
                inverse = reciprocal(diagonal)
                zp[p, t] = w_z * inverse
                zm[p, t] = w_z_behind * inverse
                yp[p, t] = w_y * inverse
                ym[p, t] = w_y_behind * inverse
                xp[p, t] = w_x * inverse
                xm[p, t] = w_x_behind * inverse
                scaled = t_a[p, t] * inverse
                u_a[p, t] = scaled
                s_a[p, t] = scaled * (1.0 / centre)

        each(1, span - 1, setup, 2)

        s_now, s_next, u_now, u_next, t_now, t_next = s_a, s_b, u_a, u_b, t_a, t_b
        for step in range(STEPS - 1):
            position = step % DEGREE
            if position + 1 < DEGREE:
                keep, mix = coefficients[position]
            else:
                keep, mix = 0.0, 1.0 / centre
            last = step == STEPS - 2

            def advance(p):
                even, odd = s_now[p, 0], s_now[p, 1]
                for t, s in enumerate((even, odd)):
                    ahead = ahead_y(even) if t else odd
                    behind = even if t else behind_y(odd)
                    moved = zp[p, t] * s_now[p + 1, t] + zm[p, t] * s_now[p - 1, t]
                    moved += yp[p, t] * ahead + ym[p, t] * behind
                    moved += xp[p, t] * ahead_x(s) + xm[p, t] * behind_x(s)
                    new_u = (u_now[p, t] - s) + moved
                    new_s = mix * new_u if keep == 0.0 else keep * s + mix * new_u
                    if not last:
                        u_next[p, t] = new_u
                        s_next[p, t] = new_s
                    if step == 0:
                        t_next[p, t] = s + new_s
                    elif step % 2 == 0:
                        t_next[p, t] = t_now[p, t] + (s + new_s)

            margin = halo - (STEPS - 2 - step)
            each(margin, span - margin, advance, 4)
            s_now, s_next, u_now, u_next = s_next, s_now, u_next, u_now
            if step % 2 == 0:
                t_now, t_next = t_next, t_now

        for m in range(TEAM):
            base = halo + planes * (place ^ m)
            for j in range(planes):
                for t in range(2):
                    outs[m][2 * j + t] = t_now[base + j, t]
        for p in range(own):
            face_ref[p : p + 1, :] = t_now[halo + p, 0, 0:1, :]

    vmem = pl.BlockSpec(memory_space=pltpu.VMEM)
    field = pltpu.VMEM((span, 2, half, columns), F32)
    return pl.pallas_call(
        kernel,
        out_shape=[jax.ShapeDtypeStruct((2 * planes, half, columns), F32)] * TEAM
        + [jax.ShapeDtypeStruct((own, columns), F32)]
        + [jax.ShapeDtypeStruct(sums[0].shape[1:], F32) for _ in sums[:1]],
        in_specs=[vmem] * len(inputs),
        out_specs=[vmem] * (TEAM + 1 + len(sums[:1])),
        scratch_shapes=[field] * 13,
        compiler_params=pltpu.CompilerParams(vmem_limit_bytes=16 * MIB),
        cost_estimate=pl.CostEstimate(flops=0, bytes_accessed=22 * MIB, transcendentals=0),
        name=f"solve{slot}",
    )(*inputs)


def weigh(sums, faces, cells, after):
    slots = len(faces)
    samples, columns = sums[0].shape

    def kernel(*refs):
        sum_refs, refs = refs[: len(sums)], refs[len(sums) :]
        face_refs, (out_ref, moments_ref, weights) = refs[:slots], refs[slots + len(after) :]
        place = team_place()
        summed = sum_refs[0][...]
        for ref in sum_refs[1:]:
            summed = summed + ref[...]
        misfit = summed * (1.0 / (2.0 * cells))
        mean = jnp.sum(misfit, axis=0, keepdims=True) * (1.0 / samples)
        deviation = misfit - mean
        variance = jnp.sum(deviation * deviation, axis=0, keepdims=True) * (1.0 / samples)
        lane = lax.broadcasted_iota(jnp.int32, (1, columns), 1)
        moments_ref[...] = jnp.where(lane == 0, mean, variance)
        weights[...] = 1.0 + 2.0 * BETA_RISK * deviation
        total = weights[pl.ds(slots * place, 1), :] * face_refs[0][...]
        for n in range(1, slots):
            total = total + weights[pl.ds(slots * place + n, 1), :] * face_refs[n][...]
        out_ref[...] = total

    vmem = pl.BlockSpec(memory_space=pltpu.VMEM)
    return pl.pallas_call(
        kernel,
        out_shape=[
            jax.ShapeDtypeStruct(faces[0].shape, F32),
            jax.ShapeDtypeStruct((1, columns), F32),
        ],
        in_specs=[vmem] * (len(sums) + slots)
        + [pl.BlockSpec(memory_space=pl.ANY)] * len(after),
        out_specs=[vmem, vmem],
        scratch_shapes=[pltpu.VMEM((samples, columns), F32)],
        compiler_params=pltpu.CompilerParams(vmem_limit_bytes=2 * MIB),
        name="weigh",
    )(*sums, *faces, *after)


def gather_adjoint(pieces, planes):
    slots = len(pieces)
    _, half, columns = pieces[0][0].shape
    tiles = columns // 128
    block = (planes, 2 * half, columns)

    def kernel(*refs):
        blocks, out, held, mixed, sems = refs[: slots * TEAM], *refs[slots * TEAM :]
        place = team_place()
        copies = []
        for slot in range(slots):
            for m in range(TEAM):
                i = slot * TEAM + m
                for j in range(planes):
                    for t in range(2):
                        for c in range(tiles):
                            mixed[i % 2, j, c, pl.ds(t, half, stride=2), :] = blocks[i][
                                2 * j + t, :, c * 128 : (c + 1) * 128
                            ]
                    for c in range(tiles):
                        held[i, j, :, c * 128 : (c + 1) * 128] = mixed[i % 2, j, c]
                copy = pltpu.make_async_copy(
                    held.at[i], out.at[slots * (place ^ m) + slot], sems.at[i]
                )
                copy.start()
                copies.append(copy)
        for copy in copies:
            copy.wait()

    return pl.pallas_call(
        kernel,
        out_shape=jax.ShapeDtypeStruct((slots * TEAM,) + block, F32),
        in_specs=[pl.BlockSpec(memory_space=pltpu.VMEM)] * (slots * TEAM),
        out_specs=pl.BlockSpec(memory_space=pltpu.HBM),
        scratch_shapes=[
            pltpu.VMEM((slots * TEAM,) + block, F32),
            pltpu.VMEM((2, planes, tiles, 2 * half, 128), F32),
            pltpu.SemaphoreType.DMA((slots * TEAM,)),
        ],
        compiler_params=pltpu.CompilerParams(vmem_limit_bytes=4 * MIB),
        cost_estimate=pl.CostEstimate(flops=0, bytes_accessed=4 * MIB, transcendentals=0),
        name="gather_adjoint",
    )(*[piece for group in pieces for piece in group])


def control(faces, radices, basis_z, basis_x):
    slabs, own_count, depth_total = basis_z.shape
    own, columns = faces[0].shape[1:]
    teams = depth_total // own

    def kernel(*refs):
        parts, (z_ref, x_ref, out_ref, whole) = refs[: len(faces)], refs[len(faces) :]
        rank = lax.axis_index("gz")
        team = rank // TEAM
        for n in range(teams):
            at, left, stride = 0, n, 1
            for radix in radices:
                digit = lax.rem(team // stride + left % radix, radix)
                at, left, stride = at + digit * stride, left // radix, stride * radix
            inner = teams // len(faces)
            whole[at] = parts[n // inner][n % inner]
        along_z = jnp.dot(
            z_ref[rank],
            whole[...].reshape(depth_total, columns),
            precision=lax.Precision.HIGHEST,
            preferred_element_type=F32,
        )
        out_ref[...] = jnp.dot(
            along_z, x_ref[...], precision=lax.Precision.HIGHEST, preferred_element_type=F32
        )

    vmem = pl.BlockSpec(memory_space=pltpu.VMEM)
    return pl.pallas_call(
        kernel,
        out_shape=jax.ShapeDtypeStruct((own_count, basis_x.shape[1]), F32),
        in_specs=[vmem] * (len(faces) + 2),
        out_specs=vmem,
        scratch_shapes=[pltpu.VMEM((teams, own, columns), F32)],
        compiler_params=pltpu.CompilerParams(vmem_limit_bytes=8 * MIB),
        name="control",
    )(*faces, basis_z, basis_x)


def radices_of(teams):
    radices = []
    while teams > 1:
        radix = next(r for r in (4, 2, 3, *range(5, teams + 1)) if teams % r == 0)
        radices.append(radix)
        teams //= radix
    return radices


def on_device(state, target, rock_type, log_table, obs_scale):
    samples, planes, rows_y, columns = state.shape
    slabs = lax.axis_size("gz")
    slots = samples // TEAM
    depth_total = planes * slabs
    radices = radices_of(slabs // TEAM)

    def swap(value, m):
        return lax.ppermute(value, "gz", [(i, i ^ m) for i in range(slabs)])

    def along(value, outward):
        pairs = []
        for i in range(slabs):
            side = (i % TEAM) // 2
            to = i + TEAM if (side == 1) == outward else i - TEAM
            if 0 <= to < slabs:
                pairs.append((i, to))
        return lax.ppermute(value, "gz", pairs)

    def from_teams(value, stride, radix):
        heard = []
        for k in range(1, radix):
            pairs = []
            for i in range(slabs):
                digit = i // (TEAM * stride) % radix
                pairs.append((i + ((digit + k) % radix - digit) * stride * TEAM, i))
            heard.append(lax.ppermute(value, "gz", pairs))
        return heard

    fields = [
        pltpu.with_memory_space_constraint(field, pltpu.HBM)
        for field in (state, target, rock_type, log_table, obs_scale)
    ]
    jobs = [[(slot, m) for slot in range(slots)] for m in range(2)]
    mine, theirs, sums = prepare(jobs, fields)
    theirs = swap(theirs, 1)
    far = []
    for slot in range(slots):
        blocks = prepare([[(slot, 2)], [(slot, 3)]], fields, sums)
        far.append([swap(blocks[0], 2), swap(blocks[1], 3)])
        if slot == 0:
            near = merge(mine, theirs, slots, blocks[0])
    near_halo = along(near, True)

    pieces, faces = [], []
    for slot in range(slots):
        far_halo = [along(block, False) for block in far[slot]]
        known = [mine, theirs, *far[0]] if slot == 0 else []
        solved = solve(slot, near, far[slot], near_halo, far_halo, known, planes)
        pieces.append([solved[0]] + [swap(solved[m], m) for m in (1, 2, 3)])
        faces.append(solved[TEAM])
        if slot == 0:
            sums = [solved[TEAM + 1]]
            stride = 1
            for radix in radices:
                held = sum(sums[1:], sums[0])
                sums = [held] + from_teams(held, stride, radix)
                stride *= radix

    face, moments = weigh(sums, faces, depth_total * rows_y * columns, pieces[0][1:])
    heard = [sum((swap(face, m) for m in (2, 3, 1)), face)[None]]
    stride = 1
    for radix in radices:
        held = heard[0] if len(heard) == 1 else jnp.concatenate(heard)
        heard = [held] + from_teams(held, stride, radix)
        stride *= radix
    adjoint = gather_adjoint(pieces, planes)
    own_count = MA // slabs
    gradient = control(
        heard,
        radices,
        jnp.asarray(cosine_basis(depth_total, MA).T.reshape(slabs, own_count, depth_total)),
        jnp.asarray(cosine_basis(columns, MB)),
    )
    return (adjoint, gradient, moments[0, :2])


def solution(mesh):
    return jax.shard_map(
        on_device,
        mesh=mesh,
        in_specs=(
            P("parts", "gz", None, None),
            P(("parts", "gz"), None, None),
            P("parts", "gz", None, None),
            P("parts", None),
            P("parts"),
        ),
        out_specs=(P("parts", "gz", None, None), P(("parts", "gz"), None), P("parts")),
        check_vma=False,
    )
```

```python
import math

import jax
import jax.numpy as jnp
import numpy as np
from jax import lax
from jax.experimental import pallas as pl
from jax.experimental.pallas import tpu as pltpu
from jax.sharding import PartitionSpec as P

NR = 8
DEGREE = 4
SWEEPS = 2
MA = 512
MB = 512

STORAGE = 0.05
BETA_RISK = 0.5
LOWER_EIGEN = 0.05
UPPER_EIGEN = 2.0

TEAM = 4
STEPS = DEGREE * SWEEPS
F32 = jnp.float32
MIB = 1024 * 1024
LANES = 128


def chebyshev_constants(number_steps):
    centre = (UPPER_EIGEN + LOWER_EIGEN) / 2
    spread = (UPPER_EIGEN - LOWER_EIGEN) / 2
    quotient = centre / spread
    rho_now = 1.0 / quotient
    coefficients = []
    for position in range(number_steps):
        rho_next = 1.0 / (2.0 * quotient - rho_now)
        coefficients.append((rho_next * rho_now, 2.0 * rho_next / spread))
        rho_now = rho_next
    return (centre, coefficients)


def cosine_basis(length_total, modes):
    positions = np.arange(length_total, dtype=np.int64)
    mode_index = np.arange(modes, dtype=np.int64)
    product_index = ((2 * positions[:, None] + 1) * (2 * mode_index[None, :] + 1)) % (
        8 * length_total
    )
    angle = product_index.astype(np.float64) * (math.pi / (4 * length_total))
    return (math.sqrt(2.0 / length_total) * np.cos(angle)).astype(np.float32)


def team_place():
    return lax.rem(lax.axis_index("gz"), TEAM)


def prepare(jobs, fields, sums=None):
    state, target, rock_type, log_table, obs_scale = fields
    samples, planes, rows_y, columns = state.shape
    slots = samples // TEAM
    block = (planes, rows_y, columns)
    half, tiles = rows_y // 2, columns // 128
    size = 2 * 2 * planes
    depth_total = planes * lax.axis_size("gz")
    flat = [(o, i, job) for o, group in enumerate(jobs) for i, job in enumerate(group)]
    count = len(flat)
    shapes = [(len(group) * size + 1, half, columns) for group in jobs]
    given = [] if sums is None else [sums]
    states = count if given else samples

    def kernel(*refs):
        before, refs = refs[: len(given)], refs[len(given) :]
        (table_ref, scale_ref, state_ref, target_ref, rock_ref), refs = refs[:5], refs[5:]
        outs, refs = refs[: len(jobs)], refs[len(jobs) :]
        if not given:
            sums_ref, refs = refs[0], refs[1:]
        table, scale, state_buf, rock_buf, target_buf, mixed, sems = refs
        place = team_place()
        first_plane = lax.axis_index("gz") * planes
        members = [slots * (place ^ m) + slot for _, _, (slot, m) in flat]
        small = [
            pltpu.make_async_copy(table_ref, table, sems.at[2, 0]),
            pltpu.make_async_copy(scale_ref, scale, sems.at[2, 1]),
            pltpu.make_async_copy(target_ref, target_buf, sems.at[2, 2]),
        ]
        for copy in small:
            copy.start()
        rocks = [
            pltpu.make_async_copy(rock_ref.at[member], rock_buf.at[n], sems.at[1, n])
            for n, member in enumerate(members)
        ]
        loads = [
            pltpu.make_async_copy(
                state_ref.at[members[n] if given else n], state_buf.at[n], sems.at[0, n]
            )
            for n in range(states)
        ]
        for copy in rocks + loads:
            copy.start()
        depth_weights = [
            1.0 + (2.0 / (depth_total - 1)) * (first_plane + p).astype(F32) for p in range(planes)
        ]
        for copy in small:
            copy.wait()
        if not given:
            for copy in loads:
                copy.wait()
            for n in range(samples):
                total = jnp.zeros((8, columns), F32)
                for p in range(planes):
                    part = jnp.zeros((8, columns), F32)
                    for first in range(0, rows_y, 8):
                        rows = slice(first, first + 8)
                        gap = state_buf[n, p, rows] - target_buf[p, rows]
                        part = part + gap * gap
                    total = total + (scale[n] * depth_weights[p]) * part
                summed = jnp.sum(total, keepdims=True)
                sums_ref[n : n + 1, :] = jnp.broadcast_to(summed, (1, columns))
        for n, (o, i, _) in enumerate(flat):
            rocks[n].wait()
            if given:
                loads[n].wait()
            member = members[n]
            own_state = n if given else member
            values = [
                jnp.exp(jnp.full((8, columns), table[member, code], F32)) for code in range(NR)
            ]
            for p in range(planes):
                factor = scale[member] * depth_weights[p]
                for first in range(0, rows_y, 8):
                    rows = slice(first, first + 8)
                    codes = rock_buf[n, p, rows]
                    low, mid, high = ((codes & bit) != 0 for bit in (1, 2, 4))
                    pairs = [
                        jnp.where(low, values[2 * k + 1], values[2 * k]) for k in range(NR // 2)
                    ]
                    halves = [jnp.where(mid, pairs[2 * k + 1], pairs[2 * k]) for k in range(2)]
                    gap = state_buf[own_state, p, rows] - target_buf[p, rows]
                    made = (jnp.where(high, halves[1], halves[0]), factor * gap)
                    for a in range(2):
                        for c in range(tiles):
                            mixed[n % 2, p, a, c, rows] = made[a][:, c * 128 : (c + 1) * 128]
                for a in range(2):
                    for t in range(2):
                        for c in range(tiles):
                            at = i * size + (a * planes + p) * 2 + t
                            outs[o][at, :, c * 128 : (c + 1) * 128] = mixed[
                                n % 2, p, a, c, pl.ds(t, half, stride=2), :
                            ]
        for o, group in enumerate(jobs):
            outs[o][len(group) * size] = before[0][...] if given else sums_ref[...]

    hbm = pl.BlockSpec(memory_space=pltpu.HBM)
    vmem = pl.BlockSpec(memory_space=pltpu.VMEM)
    sums_shape = (samples, columns)
    return pl.pallas_call(
        kernel,
        out_shape=[jax.ShapeDtypeStruct(shape, F32) for shape in shapes]
        + ([] if given else [jax.ShapeDtypeStruct(sums_shape, F32)]),
        in_specs=[vmem] * len(given) + [hbm] * 5,
        out_specs=[vmem] * (len(shapes) + 1 - len(given)),
        scratch_shapes=[
            pltpu.SMEM(log_table.shape, F32),
            pltpu.SMEM(obs_scale.shape, F32),
            pltpu.VMEM((states,) + block, F32),
            pltpu.VMEM((count,) + block, jnp.int32),
            pltpu.VMEM(block, F32),
            pltpu.VMEM((2, planes, 2, tiles, rows_y, 128), F32),
            pltpu.SemaphoreType.DMA((3, max(states, 3))),
        ],
        compiler_params=pltpu.CompilerParams(vmem_limit_bytes=6 * MIB),
        cost_estimate=pl.CostEstimate(flops=0, bytes_accessed=count * MIB, transcendentals=0),
        name="prepare",
    )(*given, log_table, obs_scale, state, target, rock_type)


def merge(mine, theirs, slots, after):
    size = (mine.shape[0] - 1) // slots

    def kernel(mine_ref, theirs_ref, _, out_ref):
        core = lax.rem(team_place(), 2)
        for ref, at in ((mine_ref, core), (theirs_ref, 1 - core)):
            for slot in range(slots):
                for n in range(size):
                    out_ref[at, slot, n] = ref[slot * size + n]

    vmem = pl.BlockSpec(memory_space=pltpu.VMEM)
    return pl.pallas_call(
        kernel,
        out_shape=jax.ShapeDtypeStruct((2, slots, size) + mine.shape[1:], F32),
        in_specs=[vmem] * 2 + [pl.BlockSpec(memory_space=pl.ANY)],
        out_specs=vmem,
        compiler_params=pltpu.CompilerParams(vmem_limit_bytes=4 * MIB),
        name="merge",
    )(mine, theirs, after)


def reciprocal(x):
    guess = pl.reciprocal(x, approx=True)
    return guess * (2.0 - x * guess)


def harmonic(a, b):
    return (a * b) * (2.0 * reciprocal(a + b))


def each(start, stop, body, width):
    whole = (stop - start) // width

    def group(n, carry):
        for k in range(width):
            body(start + n * width + k)
        return carry

    lax.fori_loop(0, whole, group, 0)
    for p in range(start + whole * width, stop):
        body(p)


def solve(slot, near, far, near_halo, far_halo, sums, planes):
    inputs = [near, near_halo, *far, *far_halo, *sums]
    half, columns = far[0].shape[1:]
    halo = 2 * planes
    own = TEAM * planes
    span = own + 2 * halo
    centre, coefficients = chebyshev_constants(DEGREE)
    assert halo >= STEPS

    def kernel(*refs):
        ins, refs = refs[:6], refs[6:]
        sum_refs, refs = refs[: len(sums)], refs[len(sums) :]
        outs, face_ref, refs = refs[:TEAM], refs[TEAM], refs[TEAM + 1 :]
        if sums:
            summed_ref, refs = refs[0], refs[1:]
            summed = sum_refs[0][sums[0].shape[0] - 1]
            for n, ref in enumerate(sum_refs[1:], 1):
                summed = summed + ref[sums[n].shape[0] - 1]
            summed_ref[...] = summed
        cond, u_a, u_b, s_a, s_b, zp, zm, yp, ym, xp, xm, t_a, t_b = refs
        place = team_place()
        column, side = lax.rem(place, 2), place // 2
        upper, lower = halo + own, 0
        near_base = jnp.where(side == 0, upper, lower)
        far_base = jnp.where(side == 0, lower, upper)
        blocks = [(ins[0].at[core, slot], halo + planes * (2 * side + core)) for core in range(2)]
        blocks += [(ins[1].at[core, slot], near_base + planes * core) for core in range(2)]
        blocks += [(ins[m], halo + planes * (place ^ m)) for m in (2, 3)]
        blocks += [(ins[4], far_base + planes * column)]
        blocks += [(ins[5], far_base + planes * (1 - column))]
        for block, base in blocks:
            for j in range(planes):
                for t in range(2):
                    cond[base + j, t] = jnp.maximum(block[2 * j + t], 1e-30)
                    t_a[base + j, t] = block[2 * (planes + j) + t]

        last_row = lax.broadcasted_iota(jnp.int32, (half, columns), 0) == half - 1
        last_column = lax.broadcasted_iota(jnp.int32, (half, columns), 1) == columns - 1

        def ahead_x(v):
            return pltpu.roll(v, columns - 1, 1)

        def behind_x(v):
            return pltpu.roll(v, 1, 1)

        def ahead_y(v):
            return pltpu.roll(v, half - 1, 0)

        def behind_y(v):
            return pltpu.roll(v, 1, 0)

        def setup(p):
            even, odd = cond[p, 0], cond[p, 1]
            w_pair = harmonic(even, odd)
            w_next = jnp.where(last_row, 0.0, harmonic(odd, ahead_y(even)))
            for t, here in enumerate((even, odd)):
                w_z = harmonic(here, cond[p + 1, t])
                w_z_behind = harmonic(here, cond[p - 1, t])
                w_y = w_next if t else w_pair
                w_y_behind = w_pair if t else behind_y(w_next)
                w_x = jnp.where(last_column, 0.0, harmonic(here, ahead_x(here)))
                w_x_behind = behind_x(w_x)
                diagonal = (w_z + w_z_behind) + (w_y + w_y_behind) + (w_x + w_x_behind) + STORAGE
                inverse = reciprocal(diagonal)
                zp[p, t] = w_z * inverse
                zm[p, t] = w_z_behind * inverse
                yp[p, t] = w_y * inverse
                ym[p, t] = w_y_behind * inverse
                xp[p, t] = w_x * inverse
                xm[p, t] = w_x_behind * inverse
                scaled = t_a[p, t] * inverse
                u_a[p, t] = scaled
                s_a[p, t] = scaled * (1.0 / centre)

        each(1, span - 1, setup, 5)

        s_now, s_next, u_now, u_next, t_now, t_next = s_a, s_b, u_a, u_b, t_a, t_b
        for step in range(STEPS - 1):
            position = step % DEGREE
            if position + 1 < DEGREE:
                keep, mix = coefficients[position]
            else:
                keep, mix = 0.0, 1.0 / centre
            last = step == STEPS - 2

            def advance(p):
                even, odd = s_now[p, 0], s_now[p, 1]
                for t, s in enumerate((even, odd)):
                    ahead = ahead_y(even) if t else odd
                    behind = even if t else behind_y(odd)
                    moved = zp[p, t] * s_now[p + 1, t] + zm[p, t] * s_now[p - 1, t]
                    moved += yp[p, t] * ahead + ym[p, t] * behind
                    moved += xp[p, t] * ahead_x(s) + xm[p, t] * behind_x(s)
                    new_u = (u_now[p, t] - s) + moved
                    new_s = mix * new_u if keep == 0.0 else keep * s + mix * new_u
                    if not last:
                        u_next[p, t] = new_u
                        s_next[p, t] = new_s
                    if step == 0:
                        t_next[p, t] = s + new_s
                    elif step % 2 == 0:
                        t_next[p, t] = t_now[p, t] + (s + new_s)

            margin = halo - (STEPS - 2 - step)
            each(margin, span - margin, advance, 8)
            s_now, s_next, u_now, u_next = s_next, s_now, u_next, u_now
            if step % 2 == 0:
                t_now, t_next = t_next, t_now

        for m in range(TEAM):
            base = halo + planes * (place ^ m)
            for j in range(planes):
                for t in range(2):
                    outs[m][2 * j + t] = t_now[base + j, t]
        for p in range(own):
            face_ref[p : p + 1, :] = t_now[halo + p, 0, 0:1, :]

    vmem = pl.BlockSpec(memory_space=pltpu.VMEM)
    field = pltpu.VMEM((span, 2, half, columns), F32)
    return pl.pallas_call(
        kernel,
        out_shape=[jax.ShapeDtypeStruct((2 * planes, half, columns), F32)] * TEAM
        + [jax.ShapeDtypeStruct((own, columns), F32)]
        + [jax.ShapeDtypeStruct(sums[0].shape[1:], F32) for _ in sums[:1]],
        in_specs=[vmem] * len(inputs),
        out_specs=[vmem] * (TEAM + 1 + len(sums[:1])),
        scratch_shapes=[field] * 13,
        compiler_params=pltpu.CompilerParams(vmem_limit_bytes=16 * MIB),
        cost_estimate=pl.CostEstimate(flops=0, bytes_accessed=22 * MIB, transcendentals=0),
        name=f"solve{slot}",
    )(*inputs)


def weigh(sums, faces, cells, after):
    slots = len(faces)
    samples, columns = sums[0].shape

    def kernel(*refs):
        sum_refs, refs = refs[: len(sums)], refs[len(sums) :]
        face_refs, (out_ref, moments_ref, weights) = refs[:slots], refs[slots + len(after) :]
        place = team_place()
        summed = sum_refs[0][...]
        for ref in sum_refs[1:]:
            summed = summed + ref[...]
        misfit = summed * (1.0 / (2.0 * cells))
        mean = jnp.sum(misfit, axis=0, keepdims=True) * (1.0 / samples)
        deviation = misfit - mean
        variance = jnp.sum(deviation * deviation, axis=0, keepdims=True) * (1.0 / samples)
        lane = lax.broadcasted_iota(jnp.int32, (1, columns), 1)
        moments_ref[...] = jnp.where(lane == 0, mean, variance)
        weights[...] = 1.0 + 2.0 * BETA_RISK * deviation
        total = weights[pl.ds(slots * place, 1), :] * face_refs[0][...]
        for n in range(1, slots):
            total = total + weights[pl.ds(slots * place + n, 1), :] * face_refs[n][...]
        out_ref[...] = total

    vmem = pl.BlockSpec(memory_space=pltpu.VMEM)
    return pl.pallas_call(
        kernel,
        out_shape=[
            jax.ShapeDtypeStruct(faces[0].shape, F32),
            jax.ShapeDtypeStruct((1, columns), F32),
        ],
        in_specs=[vmem] * (len(sums) + slots)
        + [pl.BlockSpec(memory_space=pl.ANY)] * len(after),
        out_specs=[vmem, vmem],
        scratch_shapes=[pltpu.VMEM((samples, columns), F32)],
        compiler_params=pltpu.CompilerParams(vmem_limit_bytes=2 * MIB),
        name="weigh",
    )(*sums, *faces, *after)


def gather_adjoint(pieces, planes):
    slots = len(pieces)
    _, half, columns = pieces[0][0].shape
    tiles = columns // 128
    block = (planes, 2 * half, columns)

    def kernel(*refs):
        blocks, out, held, mixed, sems = refs[: slots * TEAM], *refs[slots * TEAM :]
        place = team_place()
        copies = []
        for slot in range(slots):
            for m in range(TEAM):
                i = slot * TEAM + m
                for j in range(planes):
                    for t in range(2):
                        for c in range(tiles):
                            mixed[i % 2, j, c, pl.ds(t, half, stride=2), :] = blocks[i][
                                2 * j + t, :, c * 128 : (c + 1) * 128
                            ]
                    for c in range(tiles):
                        held[i, j, :, c * 128 : (c + 1) * 128] = mixed[i % 2, j, c]
                copy = pltpu.make_async_copy(
                    held.at[i], out.at[slots * (place ^ m) + slot], sems.at[i]
                )
                copy.start()
                copies.append(copy)
        for copy in copies:
            copy.wait()

    return pl.pallas_call(
        kernel,
        out_shape=jax.ShapeDtypeStruct((slots * TEAM,) + block, F32),
        in_specs=[pl.BlockSpec(memory_space=pltpu.VMEM)] * (slots * TEAM),
        out_specs=pl.BlockSpec(memory_space=pltpu.HBM),
        scratch_shapes=[
            pltpu.VMEM((slots * TEAM,) + block, F32),
            pltpu.VMEM((2, planes, tiles, 2 * half, 128), F32),
            pltpu.SemaphoreType.DMA((slots * TEAM,)),
        ],
        compiler_params=pltpu.CompilerParams(vmem_limit_bytes=4 * MIB),
        cost_estimate=pl.CostEstimate(flops=0, bytes_accessed=4 * MIB, transcendentals=0),
        name="gather_adjoint",
    )(*[piece for group in pieces for piece in group])


def control(faces, radices, basis_z, basis_x):
    slabs, own_count, depth_total = basis_z.shape
    own, columns = faces[0].shape[1:]
    teams = depth_total // own

    def kernel(*refs):
        parts, (z_ref, x_ref, out_ref, whole) = refs[: len(faces)], refs[len(faces) :]
        rank = lax.axis_index("gz")
        team = rank // TEAM
        for n in range(teams):
            at, left, stride = 0, n, 1
            for radix in radices:
                digit = lax.rem(team // stride + left % radix, radix)
                at, left, stride = at + digit * stride, left // radix, stride * radix
            inner = teams // len(faces)
            whole[at] = parts[n // inner][n % inner]
        along_z = jnp.dot(
            z_ref[rank],
            whole[...].reshape(depth_total, columns),
            precision=lax.Precision.HIGHEST,
            preferred_element_type=F32,
        )
        out_ref[...] = jnp.dot(
            along_z, x_ref[...], precision=lax.Precision.HIGHEST, preferred_element_type=F32
        )

    vmem = pl.BlockSpec(memory_space=pltpu.VMEM)
    return pl.pallas_call(
        kernel,
        out_shape=jax.ShapeDtypeStruct((own_count, basis_x.shape[1]), F32),
        in_specs=[vmem] * (len(faces) + 2),
        out_specs=vmem,
        scratch_shapes=[pltpu.VMEM((teams, own, columns), F32)],
        compiler_params=pltpu.CompilerParams(vmem_limit_bytes=8 * MIB),
        name="control",
    )(*faces, basis_z, basis_x)


def radices_of(teams):
    radices = []
    while teams > 1:
        radix = next(r for r in (4, 2, 3, *range(5, teams + 1)) if teams % r == 0)
        radices.append(radix)
        teams //= radix
    return radices


def on_device(state, target, rock_type, log_table, obs_scale):
    samples, planes, rows_y, columns = state.shape
    slabs = lax.axis_size("gz")
    slots = samples // TEAM
    depth_total = planes * slabs
    radices = radices_of(slabs // TEAM)

    def swap(value, m):
        return lax.ppermute(value, "gz", [(i, i ^ m) for i in range(slabs)])

    def along(value, outward):
        pairs = []
        for i in range(slabs):
            side = (i % TEAM) // 2
            to = i + TEAM if (side == 1) == outward else i - TEAM
            if 0 <= to < slabs:
                pairs.append((i, to))
        return lax.ppermute(value, "gz", pairs)

    def from_teams(value, stride, radix):
        heard = []
        for k in range(1, radix):
            pairs = []
            for i in range(slabs):
                digit = i // (TEAM * stride) % radix
                pairs.append((i + ((digit + k) % radix - digit) * stride * TEAM, i))
            heard.append(lax.ppermute(value, "gz", pairs))
        return heard

    fields = [
        pltpu.with_memory_space_constraint(field, pltpu.HBM)
        for field in (state, target, rock_type, log_table, obs_scale)
    ]
    jobs = [[(slot, m) for slot in range(slots)] for m in range(2)]
    mine, theirs, sums = prepare(jobs, fields)
    theirs = swap(theirs, 1)
    far = []
    for slot in range(slots):
        blocks = prepare([[(slot, 2)], [(slot, 3)]], fields, sums)
        far.append([swap(blocks[0], 2), swap(blocks[1], 3)])
        if slot == 0:
            near = merge(mine, theirs, slots, blocks[0])
    near_halo = along(near, True)

    pieces, faces = [], []
    for slot in range(slots):
        far_halo = [along(block, False) for block in far[slot]]
        known = [mine, theirs, *far[0]] if slot == 0 else []
        solved = solve(slot, near, far[slot], near_halo, far_halo, known, planes)
        pieces.append([solved[0]] + [swap(solved[m], m) for m in (1, 2, 3)])
        faces.append(solved[TEAM])
        if slot == 0:
            sums = [solved[TEAM + 1]]
            stride = 1
            for radix in radices:
                held = sum(sums[1:], sums[0])
                sums = [held] + from_teams(held, stride, radix)
                stride *= radix

    face, moments = weigh(sums, faces, depth_total * rows_y * columns, pieces[0][1:])
    heard = [sum((swap(face, m) for m in (2, 3, 1)), face)[None]]
    stride = 1
    for radix in radices:
        held = heard[0] if len(heard) == 1 else jnp.concatenate(heard)
        heard = [held] + from_teams(held, stride, radix)
        stride *= radix
    adjoint = gather_adjoint(pieces, planes)
    own_count = MA // slabs
    gradient = control(
        heard,
        radices,
        jnp.asarray(cosine_basis(depth_total, MA).T.reshape(slabs, own_count, depth_total)),
        jnp.asarray(cosine_basis(columns, MB)),
    )
    return (adjoint, gradient, moments[0, :2])


def solution(mesh):
    return jax.shard_map(
        on_device,
        mesh=mesh,
        in_specs=(
            P("parts", "gz", None, None),
            P(("parts", "gz"), None, None),
            P("parts", "gz", None, None),
            P("parts", None),
            P("parts"),
        ),
        out_specs=(P("parts", "gz", None, None), P(("parts", "gz"), None), P("parts")),
        check_vma=False,
    )
```

```python
import math

import jax
import jax.numpy as jnp
import numpy as np
from jax import lax
from jax.experimental import pallas as pl
from jax.experimental.pallas import tpu as pltpu
from jax.sharding import PartitionSpec as P

NR = 8
DEGREE = 4
SWEEPS = 2
MA = 512
MB = 512

STORAGE = 0.05
BETA_RISK = 0.5
LOWER_EIGEN = 0.05
UPPER_EIGEN = 2.0

TEAM = 4
STEPS = DEGREE * SWEEPS
F32 = jnp.float32
MIB = 1024 * 1024
LANES = 128


def chebyshev_constants(number_steps):
    centre = (UPPER_EIGEN + LOWER_EIGEN) / 2
    spread = (UPPER_EIGEN - LOWER_EIGEN) / 2
    quotient = centre / spread
    rho_now = 1.0 / quotient
    coefficients = []
    for position in range(number_steps):
        rho_next = 1.0 / (2.0 * quotient - rho_now)
        coefficients.append((rho_next * rho_now, 2.0 * rho_next / spread))
        rho_now = rho_next
    return (centre, coefficients)


def cosine_basis(length_total, modes):
    positions = np.arange(length_total, dtype=np.int64)
    mode_index = np.arange(modes, dtype=np.int64)
    product_index = ((2 * positions[:, None] + 1) * (2 * mode_index[None, :] + 1)) % (
        8 * length_total
    )
    angle = product_index.astype(np.float64) * (math.pi / (4 * length_total))
    return (math.sqrt(2.0 / length_total) * np.cos(angle)).astype(np.float32)


def team_place():
    return lax.rem(lax.axis_index("gz"), TEAM)


def prepare(jobs, fields, sums=None):
    state, target, rock_type, log_table, obs_scale = fields
    samples, planes, rows_y, columns = state.shape
    slots = samples // TEAM
    block = (planes, rows_y, columns)
    half, tiles = rows_y // 2, columns // 128
    size = 2 * 2 * planes
    depth_total = planes * lax.axis_size("gz")
    flat = [(o, i, job) for o, group in enumerate(jobs) for i, job in enumerate(group)]
    count = len(flat)
    given = [] if sums is None else [sums]
    shapes = [(len(group) * size + 1 - len(given), half, columns) for group in jobs]
    states = count if given else samples

    def kernel(*refs):
        refs = refs[len(given) :]
        (table_ref, scale_ref, state_ref, target_ref, rock_ref), refs = refs[:5], refs[5:]
        outs, refs = refs[: len(jobs)], refs[len(jobs) :]
        if not given:
            sums_ref, refs = refs[0], refs[1:]
        table, scale, state_buf, rock_buf, target_buf, mixed, sems = refs
        place = team_place()
        first_plane = lax.axis_index("gz") * planes
        members = [slots * (place ^ m) + slot for _, _, (slot, m) in flat]
        small = [
            pltpu.make_async_copy(table_ref, table, sems.at[2, 0]),
            pltpu.make_async_copy(scale_ref, scale, sems.at[2, 1]),
            pltpu.make_async_copy(target_ref, target_buf, sems.at[2, 2]),
        ]
        for copy in small:
            copy.start()
        rocks = [
            pltpu.make_async_copy(rock_ref.at[member], rock_buf.at[n], sems.at[1, n])
            for n, member in enumerate(members)
        ]
        loads = [
            pltpu.make_async_copy(
                state_ref.at[members[n] if given else n], state_buf.at[n], sems.at[0, n]
            )
            for n in range(states)
        ]
        for copy in rocks + loads:
            copy.start()
        depth_weights = [
            1.0 + (2.0 / (depth_total - 1)) * (first_plane + p).astype(F32) for p in range(planes)
        ]
        for copy in small:
            copy.wait()
        if not given:
            for copy in loads:
                copy.wait()
            for n in range(samples):
                total = jnp.zeros((8, columns), F32)
                for p in range(planes):
                    part = jnp.zeros((8, columns), F32)
                    for first in range(0, rows_y, 8):
                        rows = slice(first, first + 8)
                        gap = state_buf[n, p, rows] - target_buf[p, rows]
                        part = part + gap * gap
                    total = total + (scale[n] * depth_weights[p]) * part
                summed = jnp.sum(total, keepdims=True)
                sums_ref[n : n + 1, :] = jnp.broadcast_to(summed, (1, columns))
        for n, (o, i, _) in enumerate(flat):
            rocks[n].wait()
            if given:
                loads[n].wait()
            member = members[n]
            own_state = n if given else member
            values = [
                jnp.exp(jnp.full((8, columns), table[member, code], F32)) for code in range(NR)
            ]
            for p in range(planes):
                factor = scale[member] * depth_weights[p]
                for first in range(0, rows_y, 8):
                    rows = slice(first, first + 8)
                    codes = rock_buf[n, p, rows]
                    low, mid, high = ((codes & bit) != 0 for bit in (1, 2, 4))
                    pairs = [
                        jnp.where(low, values[2 * k + 1], values[2 * k]) for k in range(NR // 2)
                    ]
                    halves = [jnp.where(mid, pairs[2 * k + 1], pairs[2 * k]) for k in range(2)]
                    gap = state_buf[own_state, p, rows] - target_buf[p, rows]
                    made = (jnp.where(high, halves[1], halves[0]), factor * gap)
                    for a in range(2):
                        for c in range(tiles):
                            mixed[n % 2, p, a, c, rows] = made[a][:, c * 128 : (c + 1) * 128]
                for a in range(2):
                    for t in range(2):
                        for c in range(tiles):
                            at = i * size + (a * planes + p) * 2 + t
                            outs[o][at, :, c * 128 : (c + 1) * 128] = mixed[
                                n % 2, p, a, c, pl.ds(t, half, stride=2), :
                            ]
        for o, group in enumerate([] if given else jobs):
            outs[o][len(group) * size] = sums_ref[...]

    hbm = pl.BlockSpec(memory_space=pltpu.HBM)
    vmem = pl.BlockSpec(memory_space=pltpu.VMEM)
    sums_shape = (samples, columns)
    return pl.pallas_call(
        kernel,
        out_shape=[jax.ShapeDtypeStruct(shape, F32) for shape in shapes]
        + ([] if given else [jax.ShapeDtypeStruct(sums_shape, F32)]),
        in_specs=[pl.BlockSpec(memory_space=pl.ANY)] * len(given) + [hbm] * 5,
        out_specs=[vmem] * (len(shapes) + 1 - len(given)),
        scratch_shapes=[
            pltpu.SMEM(log_table.shape, F32),
            pltpu.SMEM(obs_scale.shape, F32),
            pltpu.VMEM((states,) + block, F32),
            pltpu.VMEM((count,) + block, jnp.int32),
            pltpu.VMEM(block, F32),
            pltpu.VMEM((2, planes, 2, tiles, rows_y, 128), F32),
            pltpu.SemaphoreType.DMA((3, max(states, 3))),
        ],
        compiler_params=pltpu.CompilerParams(vmem_limit_bytes=6 * MIB),
        cost_estimate=pl.CostEstimate(flops=0, bytes_accessed=count * MIB, transcendentals=0),
        name="prepare",
    )(*given, log_table, obs_scale, state, target, rock_type)


def merge_far(mine, theirs, slots, size):
    tile = mine.shape[1:]

    def kernel(mine_ref, theirs_ref, sums_ref, *outs):
        core = lax.rem(team_place(), 2)
        for ref, at in ((mine_ref, core), (theirs_ref, 1 - core)):
            for slot in range(slots):
                for n in range(size):
                    outs[slot][at * size + n] = ref[slot * size + n]
        outs[0][2 * size] = sums_ref[...] + theirs_ref[slots * size]

    vmem = pl.BlockSpec(memory_space=pltpu.VMEM)

    def call(sums):
        return pl.pallas_call(
            kernel,
            out_shape=[
                jax.ShapeDtypeStruct((2 * size + (slot == 0),) + tile, F32) for slot in range(slots)
            ],
            in_specs=[vmem] * 3,
            out_specs=[vmem] * slots,
            compiler_params=pltpu.CompilerParams(vmem_limit_bytes=4 * MIB),
            name="merge_far",
        )(mine, theirs, sums)

    return call


def merge_near(mine, theirs, slots, size):
    tile = mine.shape[1:]

    def kernel(mine_ref, theirs_ref, out_ref):
        core = lax.rem(team_place(), 2)
        for ref, at in ((mine_ref, core), (theirs_ref, 1 - core)):
            for slot in range(slots):
                for n in range(size):
                    out_ref[at, slot, n] = ref[slot * size + n]

    vmem = pl.BlockSpec(memory_space=pltpu.VMEM)
    return pl.pallas_call(
        kernel,
        out_shape=jax.ShapeDtypeStruct((2, slots, size) + tile, F32),
        in_specs=[vmem] * 2,
        out_specs=vmem,
        compiler_params=pltpu.CompilerParams(vmem_limit_bytes=4 * MIB),
        name="merge_near",
    )(mine, theirs)


def reciprocal(x):
    guess = pl.reciprocal(x, approx=True)
    return guess * (2.0 - x * guess)


def harmonic(a, b):
    return (a * b) * (2.0 * reciprocal(a + b))


def each(start, stop, body, width):
    whole = (stop - start) // width

    def group(n, carry):
        for k in range(width):
            body(start + n * width + k)
        return carry

    lax.fori_loop(0, whole, group, 0)
    for p in range(start + whole * width, stop):
        body(p)


def solve(slot, near, far, near_halo, far_halo, planes):
    inputs = [near, near_halo, *far, *far_halo]
    half, columns = far[0].shape[-2:]
    part = 2 * planes
    halo = 2 * planes
    own = TEAM * planes
    span = own + 2 * halo
    centre, coefficients = chebyshev_constants(DEGREE)
    assert halo >= STEPS

    def kernel(*refs):
        ins, refs = refs[: len(inputs)], refs[len(inputs) :]
        outs, face_ref, refs = refs[:TEAM], refs[TEAM], refs[TEAM + 1 :]
        cond, u_a, u_b, s_a, s_b, zp, zm, yp, ym, xp, xm, t_a, t_b = refs
        place = team_place()
        side = place // 2
        upper, lower = halo + own, 0
        near_base = jnp.where(side == 0, upper, lower)
        far_base = jnp.where(side == 0, lower, upper)
        for core in range(2):
            for j in range(planes):
                for t in range(2):
                    n = 2 * j + t
                    own_base = halo + planes * core + j
                    for ref, base in ((ins[0], own_base + part * side), (ins[1], near_base + planes * core + j)):
                        cond[base, t] = jnp.maximum(ref[core, slot, n], 1e-30)
                        t_a[base, t] = ref[core, slot, part + n]
                    for i, base in ((0, own_base + part * (1 - side)), (1, far_base + planes * core + j)):
                        refs = ins[2 + i * len(far) : 2 + (i + 1) * len(far)]
                        if len(far) == 1:
                            first, second = refs[0][core * 2 * part + n], refs[0][(core * 2 + 1) * part + n]
                        else:
                            first, second = refs[0][core * part + n], refs[1][core * part + n]
                        cond[base, t] = jnp.maximum(first, 1e-30)
                        t_a[base, t] = second

        last_row = lax.broadcasted_iota(jnp.int32, (half, columns), 0) == half - 1
        last_column = lax.broadcasted_iota(jnp.int32, (half, columns), 1) == columns - 1

        def ahead_x(v):
            return pltpu.roll(v, columns - 1, 1)

        def behind_x(v):
            return pltpu.roll(v, 1, 1)

        def ahead_y(v):
            return pltpu.roll(v, half - 1, 0)

        def behind_y(v):
            return pltpu.roll(v, 1, 0)

        def setup(p):
            even, odd = cond[p, 0], cond[p, 1]
            w_pair = harmonic(even, odd)
            w_next = jnp.where(last_row, 0.0, harmonic(odd, ahead_y(even)))
            for t, here in enumerate((even, odd)):
                w_z = harmonic(here, cond[p + 1, t])
                w_z_behind = harmonic(here, cond[p - 1, t])
                w_y = w_next if t else w_pair
                w_y_behind = w_pair if t else behind_y(w_next)
                w_x = jnp.where(last_column, 0.0, harmonic(here, ahead_x(here)))
                w_x_behind = behind_x(w_x)
                diagonal = (w_z + w_z_behind) + (w_y + w_y_behind) + (w_x + w_x_behind) + STORAGE
                inverse = reciprocal(diagonal)
                zp[p, t] = w_z * inverse
                zm[p, t] = w_z_behind * inverse
                yp[p, t] = w_y * inverse
                ym[p, t] = w_y_behind * inverse
                xp[p, t] = w_x * inverse
                xm[p, t] = w_x_behind * inverse
                scaled = t_a[p, t] * inverse
                u_a[p, t] = scaled
                s_a[p, t] = scaled * (1.0 / centre)

        each(1, span - 1, setup, (span - 2) // 2)

        s_now, s_next, u_now, u_next, t_now, t_next = s_a, s_b, u_a, u_b, t_a, t_b
        for step in range(STEPS - 1):
            position = step % DEGREE
            if position + 1 < DEGREE:
                keep, mix = coefficients[position]
            else:
                keep, mix = 0.0, 1.0 / centre
            last = step == STEPS - 2

            def advance(p):
                even, odd = s_now[p, 0], s_now[p, 1]
                for t, s in enumerate((even, odd)):
                    ahead = ahead_y(even) if t else odd
                    behind = even if t else behind_y(odd)
                    moved = zp[p, t] * s_now[p + 1, t] + zm[p, t] * s_now[p - 1, t]
                    moved += yp[p, t] * ahead + ym[p, t] * behind
                    moved += xp[p, t] * ahead_x(s) + xm[p, t] * behind_x(s)
                    new_u = (u_now[p, t] - s) + moved
                    new_s = mix * new_u if keep == 0.0 else keep * s + mix * new_u
                    if not last:
                        u_next[p, t] = new_u
                        s_next[p, t] = new_s
                    if step == 0:
                        t_next[p, t] = s + new_s
                    elif step % 2 == 0:
                        t_next[p, t] = t_now[p, t] + (s + new_s)

            margin = halo - (STEPS - 2 - step)
            each(margin, span - margin, advance, span // 2 - margin)
            s_now, s_next, u_now, u_next = s_next, s_now, u_next, u_now
            if step % 2 == 0:
                t_now, t_next = t_next, t_now

        for m in range(TEAM):
            base = halo + planes * (place ^ m)
            for j in range(planes):
                for t in range(2):
                    outs[m][2 * j + t] = t_now[base + j, t]
        for p in range(own):
            face_ref[p : p + 1, :] = t_now[halo + p, 0, 0:1, :]

    vmem = pl.BlockSpec(memory_space=pltpu.VMEM)
    field = pltpu.VMEM((span, 2, half, columns), F32)
    return pl.pallas_call(
        kernel,
        out_shape=[jax.ShapeDtypeStruct((2 * planes, half, columns), F32)] * TEAM
        + [jax.ShapeDtypeStruct((own, columns), F32)],
        in_specs=[vmem] * len(inputs),
        out_specs=[vmem] * (TEAM + 1),
        scratch_shapes=[field] * 13,
        compiler_params=pltpu.CompilerParams(vmem_limit_bytes=16 * MIB),
        cost_estimate=pl.CostEstimate(flops=0, bytes_accessed=22 * MIB, transcendentals=0),
        name=f"solve{slot}",
    )(*inputs)


def weigh(sums, faces, cells, after):
    slots = len(faces)
    samples, columns = sums[0].shape

    def kernel(*refs):
        sum_refs, refs = refs[: len(sums)], refs[len(sums) :]
        face_refs, (out_ref, moments_ref, weights) = refs[:slots], refs[slots + len(after) :]
        place = team_place()
        summed = sum_refs[0][...]
        for ref in sum_refs[1:]:
            summed = summed + ref[...]
        misfit = summed * (1.0 / (2.0 * cells))
        mean = jnp.sum(misfit, axis=0, keepdims=True) * (1.0 / samples)
        deviation = misfit - mean
        variance = jnp.sum(deviation * deviation, axis=0, keepdims=True) * (1.0 / samples)
        lane = lax.broadcasted_iota(jnp.int32, (1, columns), 1)
        moments_ref[...] = jnp.where(lane == 0, mean, variance)
        weights[...] = 1.0 + 2.0 * BETA_RISK * deviation
        total = weights[pl.ds(slots * place, 1), :] * face_refs[0][...]
        for n in range(1, slots):
            total = total + weights[pl.ds(slots * place + n, 1), :] * face_refs[n][...]
        out_ref[...] = total

    vmem = pl.BlockSpec(memory_space=pltpu.VMEM)
    return pl.pallas_call(
        kernel,
        out_shape=[
            jax.ShapeDtypeStruct(faces[0].shape, F32),
            jax.ShapeDtypeStruct((1, columns), F32),
        ],
        in_specs=[vmem] * (len(sums) + slots)
        + [pl.BlockSpec(memory_space=pl.ANY)] * len(after),
        out_specs=[vmem, vmem],
        scratch_shapes=[pltpu.VMEM((samples, columns), F32)],
        compiler_params=pltpu.CompilerParams(vmem_limit_bytes=2 * MIB),
        name="weigh",
    )(*sums, *faces, *after)


def gather_adjoint(pieces, planes):
    slots = len(pieces)
    _, half, columns = pieces[0][0].shape
    tiles = columns // 128
    block = (planes, 2 * half, columns)

    def kernel(*refs):
        blocks, out, held, mixed, sems = refs[: slots * TEAM], *refs[slots * TEAM :]
        place = team_place()
        copies = []
        for slot in range(slots):
            for m in range(TEAM):
                i = slot * TEAM + m
                for j in range(planes):
                    for t in range(2):
                        for c in range(tiles):
                            mixed[i % 2, j, c, pl.ds(t, half, stride=2), :] = blocks[i][
                                2 * j + t, :, c * 128 : (c + 1) * 128
                            ]
                    for c in range(tiles):
                        held[i, j, :, c * 128 : (c + 1) * 128] = mixed[i % 2, j, c]
                copy = pltpu.make_async_copy(
                    held.at[i], out.at[slots * (place ^ m) + slot], sems.at[i]
                )
                copy.start()
                copies.append(copy)
        for copy in copies:
            copy.wait()

    return pl.pallas_call(
        kernel,
        out_shape=jax.ShapeDtypeStruct((slots * TEAM,) + block, F32),
        in_specs=[pl.BlockSpec(memory_space=pltpu.VMEM)] * (slots * TEAM),
        out_specs=pl.BlockSpec(memory_space=pltpu.HBM),
        scratch_shapes=[
            pltpu.VMEM((slots * TEAM,) + block, F32),
            pltpu.VMEM((2, planes, tiles, 2 * half, 128), F32),
            pltpu.SemaphoreType.DMA((slots * TEAM,)),
        ],
        compiler_params=pltpu.CompilerParams(vmem_limit_bytes=4 * MIB),
        cost_estimate=pl.CostEstimate(flops=0, bytes_accessed=4 * MIB, transcendentals=0),
        name="gather_adjoint",
    )(*[piece for group in pieces for piece in group])


def control(faces, radices, basis_z, basis_x):
    slabs, own_count, depth_total = basis_z.shape
    own, columns = faces[0].shape[1:]
    teams = depth_total // own

    def kernel(*refs):
        parts, (z_ref, x_ref, out_ref, whole) = refs[: len(faces)], refs[len(faces) :]
        rank = lax.axis_index("gz")
        team = rank // TEAM
        for n in range(teams):
            at, left, stride = 0, n, 1
            for radix in radices:
                digit = lax.rem(team // stride + left % radix, radix)
                at, left, stride = at + digit * stride, left // radix, stride * radix
            inner = teams // len(faces)
            whole[at] = parts[n // inner][n % inner]
        along_z = jnp.dot(
            z_ref[rank],
            whole[...].reshape(depth_total, columns),
            precision=lax.Precision.HIGHEST,
            preferred_element_type=F32,
        )
        out_ref[...] = jnp.dot(
            along_z, x_ref[...], precision=lax.Precision.HIGHEST, preferred_element_type=F32
        )

    vmem = pl.BlockSpec(memory_space=pltpu.VMEM)
    return pl.pallas_call(
        kernel,
        out_shape=jax.ShapeDtypeStruct((own_count, basis_x.shape[1]), F32),
        in_specs=[vmem] * (len(faces) + 2),
        out_specs=vmem,
        scratch_shapes=[pltpu.VMEM((teams, own, columns), F32)],
        compiler_params=pltpu.CompilerParams(vmem_limit_bytes=8 * MIB),
        name="control",
    )(*faces, basis_z, basis_x)


def radices_of(teams):
    radices = []
    while teams > 1:
        radix = next(r for r in (4, 2, 3, *range(5, teams + 1)) if teams % r == 0)
        radices.append(radix)
        teams //= radix
    return radices


def on_device(state, target, rock_type, log_table, obs_scale):
    samples, planes, rows_y, columns = state.shape
    slabs = lax.axis_size("gz")
    slots = samples // TEAM
    depth_total = planes * slabs
    radices = radices_of(slabs // TEAM)

    def swap(value, m):
        return lax.ppermute(value, "gz", [(i, i ^ m) for i in range(slabs)])

    def along(value, outward):
        pairs = []
        for i in range(slabs):
            side = (i % TEAM) // 2
            to = i + TEAM if (side == 1) == outward else i - TEAM
            if 0 <= to < slabs:
                pairs.append((i, to))
        return lax.ppermute(value, "gz", pairs)

    def from_teams(value, stride, radix):
        heard = []
        for k in range(1, radix):
            pairs = []
            for i in range(slabs):
                digit = i // (TEAM * stride) % radix
                pairs.append((i + ((digit + k) % radix - digit) * stride * TEAM, i))
            heard.append(lax.ppermute(value, "gz", pairs))
        return heard

    fields = [
        pltpu.with_memory_space_constraint(field, pltpu.HBM)
        for field in (state, target, rock_type, log_table, obs_scale)
    ]
    size = 4 * planes
    jobs = [[(slot, m) for slot in range(slots)] for m in range(TEAM)]
    mine, theirs, sums = prepare(jobs[2:], fields)
    across = merge_far(mine, swap(theirs, 1), slots, size)(sums)
    far = [[swap(value, 2)] for value in across]
    mine, theirs = prepare(jobs[:2], fields, sums)
    near = merge_near(mine, swap(theirs, 1), slots, size)
    near_halo = along(near, True)

    sums = across[0][2 * size] + far[0][0][2 * size]
    stride = 1
    while stride * TEAM < slabs:
        radix = next(r for r in range(2, slabs) if slabs // (stride * TEAM) % r == 0)
        sums = sum(from_teams(sums, stride, radix), sums)
        stride *= radix

    pieces, faces = [], []
    for slot in range(slots):
        far_halo = [along(block, False) for block in far[slot]]
        solved = solve(slot, near, far[slot], near_halo, far_halo, planes)
        pieces.append([solved[0]] + [swap(solved[m], m) for m in (1, 2, 3)])
        faces.append(solved[TEAM])

    face, moments = weigh([sums], faces, depth_total * rows_y * columns, pieces[0][1:])
    heard = [sum((swap(face, m) for m in (2, 3, 1)), face)[None]]
    stride = 1
    for radix in radices:
        held = heard[0] if len(heard) == 1 else jnp.concatenate(heard)
        heard = [held] + from_teams(held, stride, radix)
        stride *= radix
    adjoint = gather_adjoint(pieces, planes)
    own_count = MA // slabs
    gradient = control(
        heard,
        radices,
        jnp.asarray(cosine_basis(depth_total, MA).T.reshape(slabs, own_count, depth_total)),
        jnp.asarray(cosine_basis(columns, MB)),
    )
    return (adjoint, gradient, moments[0, :2])


def solution(mesh):
    return jax.shard_map(
        on_device,
        mesh=mesh,
        in_specs=(
            P("parts", "gz", None, None),
            P(("parts", "gz"), None, None),
            P("parts", "gz", None, None),
            P("parts", None),
            P("parts"),
        ),
        out_specs=(P("parts", "gz", None, None), P(("parts", "gz"), None), P("parts")),
        check_vma=False,
    )
```

```python
import math

import jax
import jax.numpy as jnp
import numpy as np
from jax import lax
from jax.experimental import pallas as pl
from jax.experimental.pallas import tpu as pltpu
from jax.sharding import PartitionSpec as P

NR = 8
DEGREE = 4
SWEEPS = 2
MA = 512
MB = 512

STORAGE = 0.05
BETA_RISK = 0.5
LOWER_EIGEN = 0.05
UPPER_EIGEN = 2.0

TEAM = 4
STEPS = DEGREE * SWEEPS
F32 = jnp.float32
MIB = 1024 * 1024
LANES = 128


def chebyshev_constants(number_steps):
    centre = (UPPER_EIGEN + LOWER_EIGEN) / 2
    spread = (UPPER_EIGEN - LOWER_EIGEN) / 2
    quotient = centre / spread
    rho_now = 1.0 / quotient
    coefficients = []
    for position in range(number_steps):
        rho_next = 1.0 / (2.0 * quotient - rho_now)
        coefficients.append((rho_next * rho_now, 2.0 * rho_next / spread))
        rho_now = rho_next
    return (centre, coefficients)


def cosine_basis(length_total, modes):
    positions = np.arange(length_total, dtype=np.int64)
    mode_index = np.arange(modes, dtype=np.int64)
    product_index = ((2 * positions[:, None] + 1) * (2 * mode_index[None, :] + 1)) % (
        8 * length_total
    )
    angle = product_index.astype(np.float64) * (math.pi / (4 * length_total))
    return (math.sqrt(2.0 / length_total) * np.cos(angle)).astype(np.float32)


def team_place():
    return lax.rem(lax.axis_index("gz"), TEAM)


def prepare(jobs, fields, sums=None):
    state, target, rock_type, log_table, obs_scale = fields
    samples, planes, rows_y, columns = state.shape
    slots = samples // TEAM
    block = (planes, rows_y, columns)
    half, tiles = rows_y // 2, columns // 128
    size = 2 * 2 * planes
    depth_total = planes * lax.axis_size("gz")
    flat = [(o, i, job) for o, group in enumerate(jobs) for i, job in enumerate(group)]
    count = len(flat)
    given = [] if sums is None else [sums]
    shapes = [(len(group) * size + 1 - len(given), half, columns) for group in jobs]
    states = count if given else samples

    def kernel(*refs):
        refs = refs[len(given) :]
        (table_ref, scale_ref, state_ref, target_ref, rock_ref), refs = refs[:5], refs[5:]
        outs, refs = refs[: len(jobs)], refs[len(jobs) :]
        if not given:
            sums_ref, refs = refs[0], refs[1:]
        table, scale, state_buf, rock_buf, target_buf, mixed, sems = refs
        place = team_place()
        first_plane = lax.axis_index("gz") * planes
        members = [slots * (place ^ m) + slot for _, _, (slot, m) in flat]
        small = [
            pltpu.make_async_copy(table_ref, table, sems.at[2, 0]),
            pltpu.make_async_copy(scale_ref, scale, sems.at[2, 1]),
            pltpu.make_async_copy(target_ref, target_buf, sems.at[2, 2]),
        ]
        for copy in small:
            copy.start()
        rocks = [
            pltpu.make_async_copy(rock_ref.at[member], rock_buf.at[n], sems.at[1, n])
            for n, member in enumerate(members)
        ]
        loads = [
            pltpu.make_async_copy(
                state_ref.at[members[n] if given else n], state_buf.at[n], sems.at[0, n]
            )
            for n in range(states)
        ]
        for copy in rocks + loads:
            copy.start()
        depth_weights = [
            1.0 + (2.0 / (depth_total - 1)) * (first_plane + p).astype(F32) for p in range(planes)
        ]
        for copy in small:
            copy.wait()
        if not given:
            for copy in loads:
                copy.wait()
            for n in range(samples):
                total = jnp.zeros((8, columns), F32)
                for p in range(planes):
                    part = jnp.zeros((8, columns), F32)
                    for first in range(0, rows_y, 8):
                        rows = slice(first, first + 8)
                        gap = state_buf[n, p, rows] - target_buf[p, rows]
                        part = part + gap * gap
                    total = total + (scale[n] * depth_weights[p]) * part
                summed = jnp.sum(total, keepdims=True)
                sums_ref[n : n + 1, :] = jnp.broadcast_to(summed, (1, columns))
        for n, (o, i, _) in enumerate(flat):
            rocks[n].wait()
            if given:
                loads[n].wait()
            member = members[n]
            own_state = n if given else member
            values = [
                jnp.exp(jnp.full((8, columns), table[member, code], F32)) for code in range(NR)
            ]
            for p in range(planes):
                factor = scale[member] * depth_weights[p]
                for first in range(0, rows_y, 8):
                    rows = slice(first, first + 8)
                    codes = rock_buf[n, p, rows]
                    low, mid, high = ((codes & bit) != 0 for bit in (1, 2, 4))
                    pairs = [
                        jnp.where(low, values[2 * k + 1], values[2 * k]) for k in range(NR // 2)
                    ]
                    halves = [jnp.where(mid, pairs[2 * k + 1], pairs[2 * k]) for k in range(2)]
                    gap = state_buf[own_state, p, rows] - target_buf[p, rows]
                    made = (jnp.where(high, halves[1], halves[0]), factor * gap)
                    for a in range(2):
                        for c in range(tiles):
                            mixed[n % 2, p, a, c, rows] = made[a][:, c * 128 : (c + 1) * 128]
                for a in range(2):
                    for t in range(2):
                        for c in range(tiles):
                            at = i * size + (a * planes + p) * 2 + t
                            outs[o][at, :, c * 128 : (c + 1) * 128] = mixed[
                                n % 2, p, a, c, pl.ds(t, half, stride=2), :
                            ]
        for o, group in enumerate([] if given else jobs):
            outs[o][len(group) * size] = sums_ref[...]

    hbm = pl.BlockSpec(memory_space=pltpu.HBM)
    vmem = pl.BlockSpec(memory_space=pltpu.VMEM)
    sums_shape = (samples, columns)
    return pl.pallas_call(
        kernel,
        out_shape=[jax.ShapeDtypeStruct(shape, F32) for shape in shapes]
        + ([] if given else [jax.ShapeDtypeStruct(sums_shape, F32)]),
        in_specs=[pl.BlockSpec(memory_space=pl.ANY)] * len(given) + [hbm] * 5,
        out_specs=[vmem] * (len(shapes) + 1 - len(given)),
        scratch_shapes=[
            pltpu.SMEM(log_table.shape, F32),
            pltpu.SMEM(obs_scale.shape, F32),
            pltpu.VMEM((states,) + block, F32),
            pltpu.VMEM((count,) + block, jnp.int32),
            pltpu.VMEM(block, F32),
            pltpu.VMEM((2, planes, 2, tiles, rows_y, 128), F32),
            pltpu.SemaphoreType.DMA((3, max(states, 3))),
        ],
        compiler_params=pltpu.CompilerParams(vmem_limit_bytes=6 * MIB),
        cost_estimate=pl.CostEstimate(flops=0, bytes_accessed=count * MIB, transcendentals=0),
        name="prepare",
    )(*given, log_table, obs_scale, state, target, rock_type)


def merge_far(mine, theirs, slots, size):
    tile = mine.shape[1:]

    def kernel(mine_ref, theirs_ref, sums_ref, *outs):
        core = lax.rem(team_place(), 2)
        for ref, at in ((mine_ref, core), (theirs_ref, 1 - core)):
            for slot in range(slots):
                for n in range(size):
                    outs[slot][at * size + n] = ref[slot * size + n]
        outs[0][2 * size] = sums_ref[...] + theirs_ref[slots * size]

    vmem = pl.BlockSpec(memory_space=pltpu.VMEM)

    def call(sums):
        return pl.pallas_call(
            kernel,
            out_shape=[
                jax.ShapeDtypeStruct((2 * size + (slot == 0),) + tile, F32) for slot in range(slots)
            ],
            in_specs=[vmem] * 3,
            out_specs=[vmem] * slots,
            compiler_params=pltpu.CompilerParams(vmem_limit_bytes=4 * MIB),
            name="merge_far",
        )(mine, theirs, sums)

    return call


def merge_near(mine, theirs, slots, size):
    tile = mine.shape[1:]

    def kernel(mine_ref, theirs_ref, out_ref):
        core = lax.rem(team_place(), 2)
        for ref, at in ((mine_ref, core), (theirs_ref, 1 - core)):
            for slot in range(slots):
                for n in range(size):
                    out_ref[at, slot, n] = ref[slot * size + n]

    vmem = pl.BlockSpec(memory_space=pltpu.VMEM)
    return pl.pallas_call(
        kernel,
        out_shape=jax.ShapeDtypeStruct((2, slots, size) + tile, F32),
        in_specs=[vmem] * 2,
        out_specs=vmem,
        compiler_params=pltpu.CompilerParams(vmem_limit_bytes=4 * MIB),
        name="merge_near",
    )(mine, theirs)


def reciprocal(x):
    guess = pl.reciprocal(x, approx=True)
    return guess * (2.0 - x * guess)


def harmonic(a, b):
    return (a * b) * (2.0 * reciprocal(a + b))


def each(start, stop, body, width):
    whole = (stop - start) // width

    def group(n, carry):
        for k in range(width):
            body(start + n * width + k)
        return carry

    lax.fori_loop(0, whole, group, 0)
    for p in range(start + whole * width, stop):
        body(p)


def solve(slot, near, far, near_halo, far_halo, planes):
    inputs = [near, near_halo, *far, *far_halo]
    half, columns = far[0].shape[-2:]
    part = 2 * planes
    halo = 2 * planes
    own = TEAM * planes
    span = own + 2 * halo
    centre, coefficients = chebyshev_constants(DEGREE)
    assert halo >= STEPS

    def kernel(*refs):
        ins, refs = refs[: len(inputs)], refs[len(inputs) :]
        outs, face_ref, refs = refs[:TEAM], refs[TEAM], refs[TEAM + 1 :]
        cond, u_a, u_b, s_a, s_b, zp, zm, yp, ym, xp, xm, t_a, t_b = refs
        place = team_place()
        side = place // 2
        upper, lower = halo + own, 0
        near_base = jnp.where(side == 0, upper, lower)
        far_base = jnp.where(side == 0, lower, upper)
        for core in range(2):
            for j in range(planes):
                for t in range(2):
                    n = 2 * j + t
                    own_base = halo + planes * core + j
                    for ref, base in ((ins[0], own_base + part * side), (ins[1], near_base + planes * core + j)):
                        cond[base, t] = jnp.maximum(ref[core, slot, n], 1e-30)
                        t_a[base, t] = ref[core, slot, part + n]
                    for i, base in ((0, own_base + part * (1 - side)), (1, far_base + planes * core + j)):
                        refs = ins[2 + i * len(far) : 2 + (i + 1) * len(far)]
                        if len(far) == 1:
                            first, second = refs[0][core * 2 * part + n], refs[0][(core * 2 + 1) * part + n]
                        else:
                            first, second = refs[0][core * part + n], refs[1][core * part + n]
                        cond[base, t] = jnp.maximum(first, 1e-30)
                        t_a[base, t] = second

        last_row = lax.broadcasted_iota(jnp.int32, (half, columns), 0) == half - 1
        last_column = lax.broadcasted_iota(jnp.int32, (half, columns), 1) == columns - 1

        def ahead_x(v):
            return pltpu.roll(v, columns - 1, 1)

        def behind_x(v):
            return pltpu.roll(v, 1, 1)

        def ahead_y(v):
            return pltpu.roll(v, half - 1, 0)

        def behind_y(v):
            return pltpu.roll(v, 1, 0)

        def setup(p):
            even, odd = cond[p, 0], cond[p, 1]
            w_pair = harmonic(even, odd)
            w_next = jnp.where(last_row, 0.0, harmonic(odd, ahead_y(even)))
            for t, here in enumerate((even, odd)):
                w_z = harmonic(here, cond[p + 1, t])
                w_z_behind = harmonic(here, cond[p - 1, t])
                w_y = w_next if t else w_pair
                w_y_behind = w_pair if t else behind_y(w_next)
                w_x = jnp.where(last_column, 0.0, harmonic(here, ahead_x(here)))
                w_x_behind = behind_x(w_x)
                diagonal = (w_z + w_z_behind) + (w_y + w_y_behind) + (w_x + w_x_behind) + STORAGE
                inverse = reciprocal(diagonal)
                zp[p, t] = w_z * inverse
                zm[p, t] = w_z_behind * inverse
                yp[p, t] = w_y * inverse
                ym[p, t] = w_y_behind * inverse
                xp[p, t] = w_x * inverse
                xm[p, t] = w_x_behind * inverse
                scaled = t_a[p, t] * inverse
                u_a[p, t] = scaled
                s_a[p, t] = scaled * (1.0 / centre)

        each(1, span - 1, setup, (span - 2) // 2)

        s_now, s_next, u_now, u_next, t_now, t_next = s_a, s_b, u_a, u_b, t_a, t_b
        for step in range(STEPS - 1):
            position = step % DEGREE
            if position + 1 < DEGREE:
                keep, mix = coefficients[position]
            else:
                keep, mix = 0.0, 1.0 / centre
            last = step == STEPS - 2

            def advance(p):
                even, odd = s_now[p, 0], s_now[p, 1]
                for t, s in enumerate((even, odd)):
                    ahead = ahead_y(even) if t else odd
                    behind = even if t else behind_y(odd)
                    moved = zp[p, t] * s_now[p + 1, t] + zm[p, t] * s_now[p - 1, t]
                    moved += yp[p, t] * ahead + ym[p, t] * behind
                    moved += xp[p, t] * ahead_x(s) + xm[p, t] * behind_x(s)
                    new_u = (u_now[p, t] - s) + moved
                    new_s = mix * new_u if keep == 0.0 else keep * s + mix * new_u
                    if not last:
                        u_next[p, t] = new_u
                        s_next[p, t] = new_s
                    if step == 0:
                        t_next[p, t] = s + new_s
                    elif step % 2 == 0:
                        t_next[p, t] = t_now[p, t] + (s + new_s)

            margin = halo - (STEPS - 2 - step)
            each(margin, span - margin, advance, span // 2 - margin)
            s_now, s_next, u_now, u_next = s_next, s_now, u_next, u_now
            if step % 2 == 0:
                t_now, t_next = t_next, t_now

        for m in range(TEAM):
            base = halo + planes * (place ^ m)
            for j in range(planes):
                for t in range(2):
                    outs[m][2 * j + t] = t_now[base + j, t]
        for p in range(own):
            face_ref[p : p + 1, :] = t_now[halo + p, 0, 0:1, :]

    vmem = pl.BlockSpec(memory_space=pltpu.VMEM)
    field = pltpu.VMEM((span, 2, half, columns), F32)
    return pl.pallas_call(
        kernel,
        out_shape=[jax.ShapeDtypeStruct((2 * planes, half, columns), F32)] * TEAM
        + [jax.ShapeDtypeStruct((own, columns), F32)],
        in_specs=[vmem] * len(inputs),
        out_specs=[vmem] * (TEAM + 1),
        scratch_shapes=[field] * 13,
        compiler_params=pltpu.CompilerParams(vmem_limit_bytes=16 * MIB),
        cost_estimate=pl.CostEstimate(flops=0, bytes_accessed=22 * MIB, transcendentals=0),
        name=f"solve{slot}",
    )(*inputs)


def hold(value, after):
    def kernel(value_ref, _, out_ref):
        for n in range(value.shape[0]):
            out_ref[n] = value_ref[n]

    vmem = pl.BlockSpec(memory_space=pltpu.VMEM)
    return pl.pallas_call(
        kernel,
        out_shape=jax.ShapeDtypeStruct(value.shape, F32),
        in_specs=[vmem, pl.BlockSpec(memory_space=pl.ANY)],
        out_specs=vmem,
        compiler_params=pltpu.CompilerParams(vmem_limit_bytes=2 * MIB),
        name="hold",
    )(value, after)


def weigh(sums, faces, cells, after):
    slots = len(faces)
    teams, samples, columns = sums.shape

    def kernel(sums_ref, *refs):
        face_refs, (out_ref, moments_ref, weights) = refs[:slots], refs[slots + len(after) :]
        place = team_place()
        summed = jnp.sum(sums_ref[...], axis=0)
        misfit = summed * (1.0 / (2.0 * cells))
        mean = jnp.sum(misfit, axis=0, keepdims=True) * (1.0 / samples)
        deviation = misfit - mean
        variance = jnp.sum(deviation * deviation, axis=0, keepdims=True) * (1.0 / samples)
        lane = lax.broadcasted_iota(jnp.int32, (1, columns), 1)
        moments_ref[...] = jnp.where(lane == 0, mean, variance)
        weights[...] = 1.0 + 2.0 * BETA_RISK * deviation
        total = weights[pl.ds(slots * place, 1), :] * face_refs[0][...]
        for n in range(1, slots):
            total = total + weights[pl.ds(slots * place + n, 1), :] * face_refs[n][...]
        out_ref[...] = total

    vmem = pl.BlockSpec(memory_space=pltpu.VMEM)
    return pl.pallas_call(
        kernel,
        out_shape=[
            jax.ShapeDtypeStruct(faces[0].shape, F32),
            jax.ShapeDtypeStruct((1, columns), F32),
        ],
        in_specs=[vmem] * (1 + slots)
        + [pl.BlockSpec(memory_space=pl.ANY)] * len(after),
        out_specs=[vmem, vmem],
        scratch_shapes=[pltpu.VMEM((samples, columns), F32)],
        compiler_params=pltpu.CompilerParams(vmem_limit_bytes=2 * MIB),
        name="weigh",
    )(sums, *faces, *after)


def gather_adjoint(pieces, planes):
    slots = len(pieces)
    _, half, columns = pieces[0][0].shape
    tiles = columns // 128
    block = (planes, 2 * half, columns)

    def kernel(*refs):
        blocks, out, held, mixed, sems = refs[: slots * TEAM], *refs[slots * TEAM :]
        place = team_place()
        copies = []
        for slot in range(slots):
            for m in range(TEAM):
                i = slot * TEAM + m
                for j in range(planes):
                    for t in range(2):
                        for c in range(tiles):
                            mixed[i % 2, j, c, pl.ds(t, half, stride=2), :] = blocks[i][
                                2 * j + t, :, c * 128 : (c + 1) * 128
                            ]
                    for c in range(tiles):
                        held[i, j, :, c * 128 : (c + 1) * 128] = mixed[i % 2, j, c]
                copy = pltpu.make_async_copy(
                    held.at[i], out.at[slots * (place ^ m) + slot], sems.at[i]
                )
                copy.start()
                copies.append(copy)
        for copy in copies:
            copy.wait()

    return pl.pallas_call(
        kernel,
        out_shape=jax.ShapeDtypeStruct((slots * TEAM,) + block, F32),
        in_specs=[pl.BlockSpec(memory_space=pltpu.VMEM)] * (slots * TEAM),
        out_specs=pl.BlockSpec(memory_space=pltpu.HBM),
        scratch_shapes=[
            pltpu.VMEM((slots * TEAM,) + block, F32),
            pltpu.VMEM((2, planes, tiles, 2 * half, 128), F32),
            pltpu.SemaphoreType.DMA((slots * TEAM,)),
        ],
        compiler_params=pltpu.CompilerParams(vmem_limit_bytes=4 * MIB),
        cost_estimate=pl.CostEstimate(flops=0, bytes_accessed=4 * MIB, transcendentals=0),
        name="gather_adjoint",
    )(*[piece for group in pieces for piece in group])


def control(faces, basis_z, basis_x):
    own_count = basis_z.shape[1]

    def kernel(face_ref, z_ref, x_ref, out_ref):
        along_z = jnp.dot(
            z_ref[lax.axis_index("gz")],
            face_ref[...],
            precision=lax.Precision.HIGHEST,
            preferred_element_type=F32,
        )
        out_ref[...] = jnp.dot(
            along_z, x_ref[...], precision=lax.Precision.HIGHEST, preferred_element_type=F32
        )

    vmem = pl.BlockSpec(memory_space=pltpu.VMEM)
    return pl.pallas_call(
        kernel,
        out_shape=jax.ShapeDtypeStruct((own_count, basis_x.shape[1]), F32),
        in_specs=[vmem] * 3,
        out_specs=vmem,
        compiler_params=pltpu.CompilerParams(vmem_limit_bytes=8 * MIB),
        name="control",
    )(faces, basis_z, basis_x)


def on_device(state, target, rock_type, log_table, obs_scale):
    samples, planes, rows_y, columns = state.shape
    slabs = lax.axis_size("gz")
    slots = samples // TEAM
    depth_total = planes * slabs

    def swap(value, m):
        return lax.ppermute(value, "gz", [(i, i ^ m) for i in range(slabs)])

    def along(value, outward):
        pairs = []
        for i in range(slabs):
            side = (i % TEAM) // 2
            to = i + TEAM if (side == 1) == outward else i - TEAM
            if 0 <= to < slabs:
                pairs.append((i, to))
        return lax.ppermute(value, "gz", pairs)

    def of_teams(value):
        columns_of_teams = [list(range(place, slabs, TEAM)) for place in range(TEAM)]
        repeated = jnp.broadcast_to(value[None], (slabs // TEAM,) + value.shape)
        return lax.all_to_all(
            repeated,
            "gz",
            split_axis=0,
            concat_axis=0,
            axis_index_groups=columns_of_teams,
            tiled=True,
        )

    fields = [
        pltpu.with_memory_space_constraint(field, pltpu.HBM)
        for field in (state, target, rock_type, log_table, obs_scale)
    ]
    size = 4 * planes
    jobs = [[(slot, m) for slot in range(slots)] for m in range(TEAM)]
    mine, theirs, sums = prepare(jobs[2:], fields)
    across = merge_far(mine, swap(theirs, 1), slots, size)(sums)
    far = [[swap(value, 2)] for value in across]
    mine, theirs = prepare(jobs[:2], fields, sums)
    near = merge_near(mine, swap(theirs, 1), slots, size)
    near_halo = along(near, True)

    sums = across[0][2 * size] + far[0][0][2 * size]
    sums = of_teams(sums)
    far[1:] = [[hold(value, sums) for value in values] for values in far[1:]]

    pieces, faces = [], []
    for slot in range(slots):
        far_halo = [along(block, False) for block in far[slot]]
        solved = solve(slot, near, far[slot], near_halo, far_halo, planes)
        pieces.append([solved[0]] + [swap(solved[m], m) for m in (1, 2, 3)])
        faces.append(solved[TEAM])

    face, moments = weigh(sums, faces, depth_total * rows_y * columns, pieces[0][1:])
    heard = of_teams(sum((swap(face, m) for m in (2, 3, 1)), face))
    adjoint = gather_adjoint(pieces, planes)
    own_count = MA // slabs
    gradient = control(
        heard.reshape(depth_total, columns),
        jnp.asarray(cosine_basis(depth_total, MA).T.reshape(slabs, own_count, depth_total)),
        jnp.asarray(cosine_basis(columns, MB)),
    )
    return (adjoint, gradient, moments[0, :2])


def solution(mesh):
    return jax.shard_map(
        on_device,
        mesh=mesh,
        in_specs=(
            P("parts", "gz", None, None),
            P(("parts", "gz"), None, None),
            P("parts", "gz", None, None),
            P("parts", None),
            P("parts"),
        ),
        out_specs=(P("parts", "gz", None, None), P(("parts", "gz"), None), P("parts")),
        check_vma=False,
    )
```

```python
import math

import jax
import jax.numpy as jnp
import numpy as np
from jax import lax
from jax.experimental import pallas as pl
from jax.experimental.pallas import tpu as pltpu
from jax.sharding import PartitionSpec as P

NR = 8
DEGREE = 4
SWEEPS = 2
MA = 512
MB = 512

STORAGE = 0.05
BETA_RISK = 0.5
LOWER_EIGEN = 0.05
UPPER_EIGEN = 2.0

TEAM = 4
STEPS = DEGREE * SWEEPS
F32 = jnp.float32
MIB = 1024 * 1024
LANES = 128


def chebyshev_constants(number_steps):
    centre = (UPPER_EIGEN + LOWER_EIGEN) / 2
    spread = (UPPER_EIGEN - LOWER_EIGEN) / 2
    quotient = centre / spread
    rho_now = 1.0 / quotient
    coefficients = []
    for position in range(number_steps):
        rho_next = 1.0 / (2.0 * quotient - rho_now)
        coefficients.append((rho_next * rho_now, 2.0 * rho_next / spread))
        rho_now = rho_next
    return (centre, coefficients)


def cosine_basis(length_total, modes):
    positions = np.arange(length_total, dtype=np.int64)
    mode_index = np.arange(modes, dtype=np.int64)
    product_index = ((2 * positions[:, None] + 1) * (2 * mode_index[None, :] + 1)) % (
        8 * length_total
    )
    angle = product_index.astype(np.float64) * (math.pi / (4 * length_total))
    return (math.sqrt(2.0 / length_total) * np.cos(angle)).astype(np.float32)


def team_place():
    return lax.rem(lax.axis_index("gz"), TEAM)


def prepare(jobs, fields, with_sums=False):
    state, target, rock_type, log_table, obs_scale = fields
    samples, planes, rows_y, columns = state.shape
    slots = samples // TEAM
    block = (planes, rows_y, columns)
    half, tiles = rows_y // 2, columns // 128
    size = 2 * 2 * planes
    depth_total = planes * lax.axis_size("gz")
    flat = [(o, i, job) for o, group in enumerate(jobs) for i, job in enumerate(group)]
    count = len(flat)
    shapes = [(len(group) * size + with_sums, half, columns) for group in jobs]
    states = samples if with_sums else count

    def kernel(*refs):
        (table_ref, scale_ref, state_ref, target_ref, rock_ref), refs = refs[:5], refs[5:]
        outs, refs = refs[: len(jobs)], refs[len(jobs) :]
        if with_sums:
            sums_ref, refs = refs[0], refs[1:]
        table, scale, state_buf, rock_buf, target_buf, mixed, sems = refs
        place = team_place()
        first_plane = lax.axis_index("gz") * planes
        members = [slots * (place ^ m) + slot for _, _, (slot, m) in flat]
        small = [
            pltpu.make_async_copy(table_ref, table, sems.at[2, 0]),
            pltpu.make_async_copy(scale_ref, scale, sems.at[2, 1]),
            pltpu.make_async_copy(target_ref, target_buf, sems.at[2, 2]),
        ]
        for copy in small:
            copy.start()
        rocks = [
            pltpu.make_async_copy(rock_ref.at[member], rock_buf.at[n], sems.at[1, n])
            for n, member in enumerate(members)
        ]
        loads = [
            pltpu.make_async_copy(
                state_ref.at[n if with_sums else members[n]], state_buf.at[n], sems.at[0, n]
            )
            for n in range(states)
        ]
        for copy in rocks + loads:
            copy.start()
        depth_weights = [
            1.0 + (2.0 / (depth_total - 1)) * (first_plane + p).astype(F32) for p in range(planes)
        ]
        for copy in small:
            copy.wait()
        if with_sums:
            for copy in loads:
                copy.wait()
            for n in range(samples):
                total = jnp.zeros((8, columns), F32)
                for p in range(planes):
                    part = jnp.zeros((8, columns), F32)
                    for first in range(0, rows_y, 8):
                        rows = slice(first, first + 8)
                        gap = state_buf[n, p, rows] - target_buf[p, rows]
                        part = part + gap * gap
                    total = total + (scale[n] * depth_weights[p]) * part
                summed = jnp.sum(total, keepdims=True)
                sums_ref[n : n + 1, :] = jnp.broadcast_to(summed, (1, columns))
        for n, (o, i, _) in enumerate(flat):
            rocks[n].wait()
            if not with_sums:
                loads[n].wait()
            member = members[n]
            own_state = member if with_sums else n
            values = [
                jnp.exp(jnp.full((8, columns), -table[member, code], F32)) for code in range(NR)
            ]
            for p in range(planes):
                factor = scale[member] * depth_weights[p]
                for first in range(0, rows_y, 8):
                    rows = slice(first, first + 8)
                    codes = rock_buf[n, p, rows]
                    low, mid, high = ((codes & bit) != 0 for bit in (1, 2, 4))
                    pairs = [
                        jnp.where(low, values[2 * k + 1], values[2 * k]) for k in range(NR // 2)
                    ]
                    halves = [jnp.where(mid, pairs[2 * k + 1], pairs[2 * k]) for k in range(2)]
                    gap = state_buf[own_state, p, rows] - target_buf[p, rows]
                    made = (jnp.where(high, halves[1], halves[0]), factor * gap)
                    for a in range(2):
                        for c in range(tiles):
                            mixed[n % 2, p, a, c, rows] = made[a][:, c * 128 : (c + 1) * 128]
                for a in range(2):
                    for t in range(2):
                        for c in range(tiles):
                            at = i * size + (a * planes + p) * 2 + t
                            outs[o][at, :, c * 128 : (c + 1) * 128] = mixed[
                                n % 2, p, a, c, pl.ds(t, half, stride=2), :
                            ]
        for o, group in enumerate(jobs if with_sums else []):
            outs[o][len(group) * size] = sums_ref[...]

    hbm = pl.BlockSpec(memory_space=pltpu.HBM)
    vmem = pl.BlockSpec(memory_space=pltpu.VMEM)
    return pl.pallas_call(
        kernel,
        out_shape=[jax.ShapeDtypeStruct(shape, F32) for shape in shapes]
        + [jax.ShapeDtypeStruct((samples, columns), F32)] * with_sums,
        in_specs=[hbm] * 5,
        out_specs=[vmem] * (len(shapes) + with_sums),
        scratch_shapes=[
            pltpu.SMEM(log_table.shape, F32),
            pltpu.SMEM(obs_scale.shape, F32),
            pltpu.VMEM((states,) + block, F32),
            pltpu.VMEM((count,) + block, jnp.int32),
            pltpu.VMEM(block, F32),
            pltpu.VMEM((2, planes, 2, tiles, rows_y, 128), F32),
            pltpu.SemaphoreType.DMA((3, max(states, 3))),
        ],
        compiler_params=pltpu.CompilerParams(vmem_limit_bytes=6 * MIB),
        cost_estimate=pl.CostEstimate(flops=0, bytes_accessed=count * MIB, transcendentals=0),
        name="prepare",
    )(log_table, obs_scale, state, target, rock_type)


def merge_far(mine, theirs, slot, size, sums=None, with_sums=None):
    given = [] if sums is None else [sums, with_sums]
    tile = mine.shape[1:]

    def kernel(mine_ref, theirs_ref, *refs):
        core = lax.rem(team_place(), 2)
        out_ref = refs[len(given)]
        for ref, at in ((mine_ref, core), (theirs_ref, 1 - core)):
            for n in range(size):
                out_ref[at * size + n] = ref[slot * size + n]
        if given:
            total = refs[0][...] + refs[1][with_sums.shape[0] - 1]
            out_ref[2 * size] = total
            refs[-1][...] = total

    vmem = pl.BlockSpec(memory_space=pltpu.VMEM)
    shapes = [(2 * size + 1,) + tile, tile] if given else [(2 * size,) + tile]
    outs = pl.pallas_call(
        kernel,
        out_shape=[jax.ShapeDtypeStruct(shape, F32) for shape in shapes],
        in_specs=[vmem] * (2 + len(given)),
        out_specs=[vmem] * len(shapes),
        compiler_params=pltpu.CompilerParams(vmem_limit_bytes=4 * MIB),
        name="merge_far",
    )(mine, theirs, *given)
    return outs if given else outs[0]


def team_sums(mine, theirs, count):
    def kernel(mine_ref, theirs_ref, out_ref):
        total = mine_ref[...] + theirs_ref[theirs.shape[0] - 1]
        for n in range(count):
            out_ref[n] = total

    vmem = pl.BlockSpec(memory_space=pltpu.VMEM)
    return pl.pallas_call(
        kernel,
        out_shape=jax.ShapeDtypeStruct((count,) + mine.shape, F32),
        in_specs=[vmem] * 2,
        out_specs=vmem,
        compiler_params=pltpu.CompilerParams(vmem_limit_bytes=4 * MIB),
        name="team_sums",
    )(mine, theirs)


def merge_near(mine, theirs, slots, size):
    tile = mine.shape[1:]

    def kernel(mine_ref, theirs_ref, out_ref):
        core = lax.rem(team_place(), 2)
        for ref, at in ((mine_ref, core), (theirs_ref, 1 - core)):
            for slot in range(slots):
                for n in range(size):
                    out_ref[at, slot, n] = ref[slot * size + n]

    vmem = pl.BlockSpec(memory_space=pltpu.VMEM)
    return pl.pallas_call(
        kernel,
        out_shape=jax.ShapeDtypeStruct((2, slots, size) + tile, F32),
        in_specs=[vmem] * 2,
        out_specs=vmem,
        compiler_params=pltpu.CompilerParams(vmem_limit_bytes=4 * MIB),
        name="merge_near",
    )(mine, theirs)


def reciprocal(x):
    guess = pl.reciprocal(x, approx=True)
    return guess * (2.0 - x * guess)


def harmonic(a, b):
    x = a + b
    guess = pl.reciprocal(x, approx=True)
    return guess * (4.0 - (2.0 * x) * guess)


def each(start, stop, body, width):
    whole = (stop - start) // width

    def group(n, carry):
        for k in range(width):
            body(start + n * width + k)
        return carry

    lax.fori_loop(0, whole, group, 0)
    for p in range(start + whole * width, stop):
        body(p)


def solve(slot, near, far, near_halo, far_halo, planes):
    inputs = [near, near_halo, *far, *far_halo]
    half, columns = far[0].shape[-2:]
    part = 2 * planes
    halo = 2 * planes
    own = TEAM * planes
    span = own + 2 * halo
    centre, coefficients = chebyshev_constants(DEGREE)
    assert halo >= STEPS

    def kernel(*refs):
        ins, refs = refs[: len(inputs)], refs[len(inputs) :]
        outs, face_ref, refs = refs[:TEAM], refs[TEAM], refs[TEAM + 1 :]
        cond, u_a, u_b, s_a, s_b, zp, zm, yp, ym, xp, xm, t_a, t_b = refs
        place = team_place()
        side = place // 2
        upper, lower = halo + own, 0
        near_base = jnp.where(side == 0, upper, lower)
        far_base = jnp.where(side == 0, lower, upper)
        def outside(v):
            return jnp.where(v > 0.0, v, 1e30)

        for core in range(2):
            for j in range(planes):
                for t in range(2):
                    n = 2 * j + t
                    own_base = halo + planes * core + j
                    for ref, base in ((ins[0], own_base + part * side), (ins[1], near_base + planes * core + j)):
                        cond[base, t] = outside(ref[core, slot, n])
                        t_a[base, t] = ref[core, slot, part + n]
                    for i, base in ((0, own_base + part * (1 - side)), (1, far_base + planes * core + j)):
                        refs = ins[2 + i * len(far) : 2 + (i + 1) * len(far)]
                        if len(far) == 1:
                            first, second = refs[0][core * 2 * part + n], refs[0][(core * 2 + 1) * part + n]
                        else:
                            first, second = refs[0][core * part + n], refs[1][core * part + n]
                        cond[base, t] = outside(first)
                        t_a[base, t] = second

        last_row = lax.broadcasted_iota(jnp.int32, (half, columns), 0) == half - 1
        last_column = lax.broadcasted_iota(jnp.int32, (half, columns), 1) == columns - 1

        def ahead_x(v):
            return pltpu.roll(v, columns - 1, 1)

        def behind_x(v):
            return pltpu.roll(v, 1, 1)

        def ahead_y(v):
            return pltpu.roll(v, half - 1, 0)

        def behind_y(v):
            return pltpu.roll(v, 1, 0)

        def setup(p, w_z_before):
            even, odd = cond[p, 0], cond[p, 1]
            w_pair = harmonic(even, odd)
            w_next = jnp.where(last_row, 0.0, harmonic(odd, ahead_y(even)))
            w_z_here = []
            for t, here in enumerate((even, odd)):
                w_z = harmonic(here, cond[p + 1, t])
                w_z_here.append(w_z)
                w_z_behind = w_z_before[t]
                w_y = w_next if t else w_pair
                w_y_behind = w_pair if t else behind_y(w_next)
                w_x = jnp.where(last_column, 0.0, harmonic(here, ahead_x(here)))
                w_x_behind = behind_x(w_x)
                diagonal = (w_z + w_z_behind) + (w_y + w_y_behind) + (w_x + w_x_behind) + STORAGE
                inverse = reciprocal(diagonal)
                zp[p, t] = w_z * inverse
                zm[p, t] = w_z_behind * inverse
                yp[p, t] = w_y * inverse
                ym[p, t] = w_y_behind * inverse
                xp[p, t] = w_x * inverse
                xm[p, t] = w_x_behind * inverse
                scaled = t_a[p, t] * inverse
                u_a[p, t] = scaled
                s_a[p, t] = scaled * (1.0 / centre)
            return w_z_here

        width = (span - 2) // 3

        def setup_group(n, carry):
            start = 1 + n * width
            w_z = [harmonic(cond[start - 1, t], cond[start, t]) for t in range(2)]
            for k in range(width):
                w_z = setup(start + k, w_z)
            return carry

        assert (span - 2) % width == 0
        lax.fori_loop(0, (span - 2) // width, setup_group, 0)

        s_now, s_next, u_now, u_next, t_now, t_next = s_a, s_b, u_a, u_b, t_a, t_b
        for step in range(STEPS - 1):
            position = step % DEGREE
            if position + 1 < DEGREE:
                keep, mix = coefficients[position]
            else:
                keep, mix = 0.0, 1.0 / centre
            last = step == STEPS - 2

            def advance(p):
                even, odd = s_now[p, 0], s_now[p, 1]
                for t, s in enumerate((even, odd)):
                    ahead = ahead_y(even) if t else odd
                    behind = even if t else behind_y(odd)
                    moved = zp[p, t] * s_now[p + 1, t] + zm[p, t] * s_now[p - 1, t]
                    moved += yp[p, t] * ahead + ym[p, t] * behind
                    moved += xp[p, t] * ahead_x(s) + xm[p, t] * behind_x(s)
                    new_u = (u_now[p, t] - s) + moved
                    new_s = mix * new_u if keep == 0.0 else keep * s + mix * new_u
                    if not last:
                        u_next[p, t] = new_u
                        s_next[p, t] = new_s
                    if step == 0:
                        t_next[p, t] = s + new_s
                    elif step % 2 == 0:
                        t_next[p, t] = t_now[p, t] + (s + new_s)

            margin = halo - (STEPS - 2 - step)
            each(margin, span - margin, advance, 8)
            s_now, s_next, u_now, u_next = s_next, s_now, u_next, u_now
            if step % 2 == 0:
                t_now, t_next = t_next, t_now

        for m in range(TEAM):
            base = halo + planes * (place ^ m)
            for j in range(planes):
                for t in range(2):
                    outs[m][2 * j + t] = t_now[base + j, t]
        for p in range(own):
            face_ref[p : p + 1, :] = t_now[halo + p, 0, 0:1, :]

    vmem = pl.BlockSpec(memory_space=pltpu.VMEM)
    field = pltpu.VMEM((span, 2, half, columns), F32)
    return pl.pallas_call(
        kernel,
        out_shape=[jax.ShapeDtypeStruct((2 * planes, half, columns), F32)] * TEAM
        + [jax.ShapeDtypeStruct((own, columns), F32)],
        in_specs=[vmem] * len(inputs),
        out_specs=[vmem] * (TEAM + 1),
        scratch_shapes=[field] * 13,
        compiler_params=pltpu.CompilerParams(vmem_limit_bytes=16 * MIB),
        cost_estimate=pl.CostEstimate(flops=0, bytes_accessed=22 * MIB, transcendentals=0),
        name=f"solve{slot}",
    )(*inputs)


def weigh(sums, faces, cells, after):
    slots = len(faces)
    teams, samples, columns = sums.shape

    def kernel(sums_ref, *refs):
        face_refs, (out_ref, moments_ref, weights) = refs[:slots], refs[slots + len(after) :]
        place = team_place()
        summed = jnp.sum(sums_ref[...], axis=0)
        misfit = summed * (1.0 / (2.0 * cells))
        mean = jnp.sum(misfit, axis=0, keepdims=True) * (1.0 / samples)
        deviation = misfit - mean
        variance = jnp.sum(deviation * deviation, axis=0, keepdims=True) * (1.0 / samples)
        lane = lax.broadcasted_iota(jnp.int32, (1, columns), 1)
        moments_ref[...] = jnp.where(lane == 0, mean, variance)
        weights[...] = 1.0 + 2.0 * BETA_RISK * deviation
        total = weights[pl.ds(slots * place, 1), :] * face_refs[0][...]
        for n in range(1, slots):
            total = total + weights[pl.ds(slots * place + n, 1), :] * face_refs[n][...]
        out_ref[...] = total

    vmem = pl.BlockSpec(memory_space=pltpu.VMEM)
    return pl.pallas_call(
        kernel,
        out_shape=[
            jax.ShapeDtypeStruct(faces[0].shape, F32),
            jax.ShapeDtypeStruct((1, columns), F32),
        ],
        in_specs=[vmem] * (1 + slots)
        + [pl.BlockSpec(memory_space=pl.ANY)] * len(after),
        out_specs=[vmem, vmem],
        scratch_shapes=[pltpu.VMEM((samples, columns), F32)],
        compiler_params=pltpu.CompilerParams(vmem_limit_bytes=2 * MIB),
        name="weigh",
    )(sums, *faces, *after)


def gather_adjoint(pieces, planes):
    slots = len(pieces)
    _, half, columns = pieces[0][0].shape
    tiles = columns // 128
    block = (planes, 2 * half, columns)

    def kernel(*refs):
        blocks, out, held, mixed, sems = refs[: slots * TEAM], *refs[slots * TEAM :]
        place = team_place()
        copies = []
        for slot in range(slots):
            for m in range(TEAM):
                i = slot * TEAM + m
                for j in range(planes):
                    for t in range(2):
                        for c in range(tiles):
                            mixed[i % 2, j, c, pl.ds(t, half, stride=2), :] = blocks[i][
                                2 * j + t, :, c * 128 : (c + 1) * 128
                            ]
                    for c in range(tiles):
                        held[i, j, :, c * 128 : (c + 1) * 128] = mixed[i % 2, j, c]
                copy = pltpu.make_async_copy(
                    held.at[i], out.at[slots * (place ^ m) + slot], sems.at[i]
                )
                copy.start()
                copies.append(copy)
        for copy in copies:
            copy.wait()

    return pl.pallas_call(
        kernel,
        out_shape=jax.ShapeDtypeStruct((slots * TEAM,) + block, F32),
        in_specs=[pl.BlockSpec(memory_space=pltpu.VMEM)] * (slots * TEAM),
        out_specs=pl.BlockSpec(memory_space=pltpu.HBM),
        scratch_shapes=[
            pltpu.VMEM((slots * TEAM,) + block, F32),
            pltpu.VMEM((2, planes, tiles, 2 * half, 128), F32),
            pltpu.SemaphoreType.DMA((slots * TEAM,)),
        ],
        compiler_params=pltpu.CompilerParams(vmem_limit_bytes=4 * MIB),
        cost_estimate=pl.CostEstimate(flops=0, bytes_accessed=4 * MIB, transcendentals=0),
        name="gather_adjoint",
    )(*[piece for group in pieces for piece in group])


def control(faces, radices, basis_z, basis_x):
    slabs, own_count, depth_total = basis_z.shape
    own, columns = faces[0].shape[1:]
    teams = depth_total // own

    def kernel(*refs):
        parts, (z_ref, x_ref, out_ref, whole) = refs[: len(faces)], refs[len(faces) :]
        rank = lax.axis_index("gz")
        team = rank // TEAM
        for n in range(teams):
            at, left, stride = 0, n, 1
            for radix in radices:
                digit = lax.rem(team // stride + left % radix, radix)
                at, left, stride = at + digit * stride, left // radix, stride * radix
            inner = teams // len(faces)
            whole[at] = parts[n // inner][n % inner]
        along_z = jnp.dot(
            z_ref[rank],
            whole[...].reshape(depth_total, columns),
            precision=lax.Precision.HIGHEST,
            preferred_element_type=F32,
        )
        out_ref[...] = jnp.dot(
            along_z, x_ref[...], precision=lax.Precision.HIGHEST, preferred_element_type=F32
        )

    vmem = pl.BlockSpec(memory_space=pltpu.VMEM)
    return pl.pallas_call(
        kernel,
        out_shape=jax.ShapeDtypeStruct((own_count, basis_x.shape[1]), F32),
        in_specs=[vmem] * (len(faces) + 2),
        out_specs=vmem,
        scratch_shapes=[pltpu.VMEM((teams, own, columns), F32)],
        compiler_params=pltpu.CompilerParams(vmem_limit_bytes=8 * MIB),
        name="control",
    )(*faces, basis_z, basis_x)


def radices_of(teams):
    radices = []
    while teams > 1:
        radix = next(r for r in (4, 2, 3, *range(5, teams + 1)) if teams % r == 0)
        radices.append(radix)
        teams //= radix
    return radices


def on_device(state, target, rock_type, log_table, obs_scale):
    samples, planes, rows_y, columns = state.shape
    slabs = lax.axis_size("gz")
    slots = samples // TEAM
    depth_total = planes * slabs
    radices = radices_of(slabs // TEAM)

    def swap(value, m):
        return lax.ppermute(value, "gz", [(i, i ^ m) for i in range(slabs)])

    def along(value, outward):
        pairs = []
        for i in range(slabs):
            side = (i % TEAM) // 2
            to = i + TEAM if (side == 1) == outward else i - TEAM
            if 0 <= to < slabs:
                pairs.append((i, to))
        return lax.ppermute(value, "gz", pairs)

    def from_teams(value, stride, radix):
        heard = []
        for k in range(1, radix):
            pairs = []
            for i in range(slabs):
                digit = i // (TEAM * stride) % radix
                pairs.append((i + ((digit + k) % radix - digit) * stride * TEAM, i))
            heard.append(lax.ppermute(value, "gz", pairs))
        return heard

    def of_teams(repeated):
        columns_of_teams = [list(range(place, slabs, TEAM)) for place in range(TEAM)]
        return lax.all_to_all(
            repeated,
            "gz",
            split_axis=0,
            concat_axis=0,
            axis_index_groups=columns_of_teams,
            tiled=True,
        )

    fields = [
        pltpu.with_memory_space_constraint(field, pltpu.HBM)
        for field in (state, target, rock_type, log_table, obs_scale)
    ]
    size = 4 * planes
    jobs = [[(slot, m) for slot in range(slots)] for m in range(TEAM)]
    mine, theirs = prepare(jobs[2:], fields)
    theirs = swap(theirs, 1)
    far = [[swap(merge_far(mine, theirs, slot, size), 2)] for slot in range(slots - 1)]
    mine_near, theirs_near, sums = prepare(jobs[:2], fields, with_sums=True)
    theirs_near = swap(theirs_near, 1)
    near = merge_near(mine_near, theirs_near, slots, size)
    near_halo = along(near, True)
    last, chip_sums = merge_far(mine, theirs, slots - 1, size, sums, theirs_near)
    far.append([swap(last, 2)])
    all_sums = of_teams(team_sums(chip_sums, far[-1][0], slabs // TEAM))

    pieces, faces = [], []
    for slot in range(slots):
        far_halo = [along(block, False) for block in far[slot]]
        solved = solve(slot, near, far[slot], near_halo, far_halo, planes)
        pieces.append([solved[0]] + [swap(solved[m], m) for m in (1, 2, 3)])
        faces.append(solved[TEAM])

    face, moments = weigh(all_sums, faces, depth_total * rows_y * columns, pieces[0][1:])
    heard = [sum((swap(face, m) for m in (2, 3, 1)), face)[None]]
    stride = 1
    for radix in radices:
        held = heard[0] if len(heard) == 1 else jnp.concatenate(heard)
        heard = [held] + from_teams(held, stride, radix)
        stride *= radix
    adjoint = gather_adjoint(pieces, planes)
    own_count = MA // slabs
    gradient = control(
        heard,
        radices,
        jnp.asarray(cosine_basis(depth_total, MA).T.reshape(slabs, own_count, depth_total)),
        jnp.asarray(cosine_basis(columns, MB)),
    )
    return (adjoint, gradient, moments[0, :2])


def solution(mesh):
    return jax.shard_map(
        on_device,
        mesh=mesh,
        in_specs=(
            P("parts", "gz", None, None),
            P(("parts", "gz"), None, None),
            P("parts", "gz", None, None),
            P("parts", None),
            P("parts"),
        ),
        out_specs=(P("parts", "gz", None, None), P(("parts", "gz"), None), P("parts")),
        check_vma=False,
    )
```

```python
import math

import jax
import jax.numpy as jnp
import numpy as np
from jax import lax
from jax.experimental import pallas as pl
from jax.experimental.pallas import tpu as pltpu
from jax.sharding import PartitionSpec as P

NR = 8
DEGREE = 4
SWEEPS = 2
MA = 512
MB = 512

STORAGE = 0.05
BETA_RISK = 0.5
LOWER_EIGEN = 0.05
UPPER_EIGEN = 2.0

TEAM = 4
STEPS = DEGREE * SWEEPS
F32 = jnp.float32
MIB = 1024 * 1024
LANES = 128


def chebyshev_constants(number_steps):
    centre = (UPPER_EIGEN + LOWER_EIGEN) / 2
    spread = (UPPER_EIGEN - LOWER_EIGEN) / 2
    quotient = centre / spread
    rho_now = 1.0 / quotient
    coefficients = []
    for position in range(number_steps):
        rho_next = 1.0 / (2.0 * quotient - rho_now)
        coefficients.append((rho_next * rho_now, 2.0 * rho_next / spread))
        rho_now = rho_next
    return (centre, coefficients)


def cosine_basis(length_total, modes):
    positions = np.arange(length_total, dtype=np.int64)
    mode_index = np.arange(modes, dtype=np.int64)
    product_index = ((2 * positions[:, None] + 1) * (2 * mode_index[None, :] + 1)) % (
        8 * length_total
    )
    angle = product_index.astype(np.float64) * (math.pi / (4 * length_total))
    return (math.sqrt(2.0 / length_total) * np.cos(angle)).astype(np.float32)


def team_place():
    return lax.rem(lax.axis_index("gz"), TEAM)


def prepare(jobs, fields, with_sums=False):
    state, target, rock_type, log_table, obs_scale = fields
    samples, planes, rows_y, columns = state.shape
    slots = samples // TEAM
    block = (planes, rows_y, columns)
    half, tiles = rows_y // 2, columns // 128
    size = 2 * 2 * planes
    depth_total = planes * lax.axis_size("gz")
    flat = [(o, i, job) for o, group in enumerate(jobs) for i, job in enumerate(group)]
    count = len(flat)
    shapes = [(len(group) * size + with_sums, half, columns) for group in jobs]
    states = samples if with_sums else count

    def kernel(*refs):
        (table_ref, scale_ref, state_ref, target_ref, rock_ref), refs = refs[:5], refs[5:]
        outs, refs = refs[: len(jobs)], refs[len(jobs) :]
        if with_sums:
            sums_ref, refs = refs[0], refs[1:]
        table, scale, state_buf, rock_buf, target_buf, mixed, sems = refs
        place = team_place()
        first_plane = lax.axis_index("gz") * planes
        members = [slots * (place ^ m) + slot for _, _, (slot, m) in flat]
        small = [
            pltpu.make_async_copy(table_ref, table, sems.at[2, 0]),
            pltpu.make_async_copy(scale_ref, scale, sems.at[2, 1]),
            pltpu.make_async_copy(target_ref, target_buf, sems.at[2, 2]),
        ]
        for copy in small:
            copy.start()
        rocks = [
            pltpu.make_async_copy(rock_ref.at[member], rock_buf.at[n], sems.at[1, n])
            for n, member in enumerate(members)
        ]
        loads = [
            pltpu.make_async_copy(
                state_ref.at[n if with_sums else members[n]], state_buf.at[n], sems.at[0, n]
            )
            for n in range(states)
        ]
        for copy in rocks + loads:
            copy.start()
        depth_weights = [
            1.0 + (2.0 / (depth_total - 1)) * (first_plane + p).astype(F32) for p in range(planes)
        ]
        for copy in small:
            copy.wait()
        if with_sums:
            for copy in loads:
                copy.wait()
            for n in range(samples):
                total = jnp.zeros((8, columns), F32)
                for p in range(planes):
                    part = jnp.zeros((8, columns), F32)
                    for first in range(0, rows_y, 8):
                        rows = slice(first, first + 8)
                        gap = state_buf[n, p, rows] - target_buf[p, rows]
                        part = part + gap * gap
                    total = total + (scale[n] * depth_weights[p]) * part
                summed = jnp.sum(total, keepdims=True)
                sums_ref[n : n + 1, :] = jnp.broadcast_to(summed, (1, columns))
        for n, (o, i, _) in enumerate(flat):
            rocks[n].wait()
            if not with_sums:
                loads[n].wait()
            member = members[n]
            own_state = member if with_sums else n
            values = [
                jnp.exp(jnp.full((8, columns), -table[member, code], F32)) for code in range(NR)
            ]
            for p in range(planes):
                factor = scale[member] * depth_weights[p]
                for first in range(0, rows_y, 8):
                    rows = slice(first, first + 8)
                    codes = rock_buf[n, p, rows]
                    low, mid, high = ((codes & bit) != 0 for bit in (1, 2, 4))
                    pairs = [
                        jnp.where(low, values[2 * k + 1], values[2 * k]) for k in range(NR // 2)
                    ]
                    halves = [jnp.where(mid, pairs[2 * k + 1], pairs[2 * k]) for k in range(2)]
                    gap = state_buf[own_state, p, rows] - target_buf[p, rows]
                    made = (jnp.where(high, halves[1], halves[0]), factor * gap)
                    for a in range(2):
                        for c in range(tiles):
                            mixed[n % 2, p, a, c, rows] = made[a][:, c * 128 : (c + 1) * 128]
                for a in range(2):
                    for t in range(2):
                        for c in range(tiles):
                            at = i * size + (a * planes + p) * 2 + t
                            outs[o][at, :, c * 128 : (c + 1) * 128] = mixed[
                                n % 2, p, a, c, pl.ds(t, half, stride=2), :
                            ]
        for o, group in enumerate(jobs if with_sums else []):
            outs[o][len(group) * size] = sums_ref[...]

    hbm = pl.BlockSpec(memory_space=pltpu.HBM)
    vmem = pl.BlockSpec(memory_space=pltpu.VMEM)
    return pl.pallas_call(
        kernel,
        out_shape=[jax.ShapeDtypeStruct(shape, F32) for shape in shapes]
        + [jax.ShapeDtypeStruct((samples, columns), F32)] * with_sums,
        in_specs=[hbm] * 5,
        out_specs=[vmem] * (len(shapes) + with_sums),
        scratch_shapes=[
            pltpu.SMEM(log_table.shape, F32),
            pltpu.SMEM(obs_scale.shape, F32),
            pltpu.VMEM((states,) + block, F32),
            pltpu.VMEM((count,) + block, jnp.int32),
            pltpu.VMEM(block, F32),
            pltpu.VMEM((2, planes, 2, tiles, rows_y, 128), F32),
            pltpu.SemaphoreType.DMA((3, max(states, 3))),
        ],
        compiler_params=pltpu.CompilerParams(vmem_limit_bytes=6 * MIB),
        cost_estimate=pl.CostEstimate(flops=0, bytes_accessed=count * MIB, transcendentals=0),
        name="prepare",
    )(log_table, obs_scale, state, target, rock_type)


def merge_far(mine, theirs, slot, size, sums=None):
    given = [] if sums is None else [sums]
    tile = mine.shape[1:]

    def kernel(mine_ref, theirs_ref, *refs):
        core = lax.rem(team_place(), 2)
        out_ref = refs[len(given)]
        for ref, at in ((mine_ref, core), (theirs_ref, 1 - core)):
            for n in range(size):
                out_ref[at * size + n] = ref[slot * size + n]
        if given:
            total = refs[0][...] + theirs_ref[theirs.shape[0] - 1]
            out_ref[2 * size] = total
            refs[-1][...] = total

    vmem = pl.BlockSpec(memory_space=pltpu.VMEM)
    shapes = [(2 * size + 1,) + tile, tile] if given else [(2 * size,) + tile]
    outs = pl.pallas_call(
        kernel,
        out_shape=[jax.ShapeDtypeStruct(shape, F32) for shape in shapes],
        in_specs=[vmem] * (2 + len(given)),
        out_specs=[vmem] * len(shapes),
        compiler_params=pltpu.CompilerParams(vmem_limit_bytes=4 * MIB),
        name="merge_far",
    )(mine, theirs, *given)
    return outs if given else outs[0]


def hold(value, after):
    def kernel(value_ref, _, out_ref):
        for n in range(value.shape[0]):
            out_ref[n] = value_ref[n]

    vmem = pl.BlockSpec(memory_space=pltpu.VMEM)
    return pl.pallas_call(
        kernel,
        out_shape=jax.ShapeDtypeStruct(value.shape, F32),
        in_specs=[vmem, pl.BlockSpec(memory_space=pl.ANY)],
        out_specs=vmem,
        compiler_params=pltpu.CompilerParams(vmem_limit_bytes=2 * MIB),
        name="hold",
    )(value, after)


def add_up(values, after):
    def kernel(*refs):
        total = refs[0][...]
        for ref in refs[1 : len(values)]:
            total = total + ref[...]
        refs[-1][...] = total

    vmem = pl.BlockSpec(memory_space=pltpu.VMEM)
    return pl.pallas_call(
        kernel,
        out_shape=jax.ShapeDtypeStruct(values[0].shape, F32),
        in_specs=[vmem] * len(values) + [pl.BlockSpec(memory_space=pl.ANY)],
        out_specs=vmem,
        compiler_params=pltpu.CompilerParams(vmem_limit_bytes=MIB),
        name="add_up",
    )(*values, after)


def merge_near(mine, theirs, slots, size):
    tile = mine.shape[1:]

    def kernel(mine_ref, theirs_ref, out_ref):
        core = lax.rem(team_place(), 2)
        for ref, at in ((mine_ref, core), (theirs_ref, 1 - core)):
            for slot in range(slots):
                for n in range(size):
                    out_ref[at, slot, n] = ref[slot * size + n]

    vmem = pl.BlockSpec(memory_space=pltpu.VMEM)
    return pl.pallas_call(
        kernel,
        out_shape=jax.ShapeDtypeStruct((2, slots, size) + tile, F32),
        in_specs=[vmem] * 2,
        out_specs=vmem,
        compiler_params=pltpu.CompilerParams(vmem_limit_bytes=4 * MIB),
        name="merge_near",
    )(mine, theirs)


def reciprocal(x):
    guess = pl.reciprocal(x, approx=True)
    return guess * (2.0 - x * guess)


def harmonic(a, b):
    x = a + b
    guess = pl.reciprocal(x, approx=True)
    return guess * (4.0 - (2.0 * x) * guess)


def each(start, stop, body, width):
    whole = (stop - start) // width

    def group(n, carry):
        for k in range(width):
            body(start + n * width + k)
        return carry

    lax.fori_loop(0, whole, group, 0)
    for p in range(start + whole * width, stop):
        body(p)


def solve(slot, near, far, near_halo, far_halo, planes):
    inputs = [near, near_halo, far, far_halo]
    half, columns = far.shape[-2:]
    part = 2 * planes
    halo = 2 * planes
    own = TEAM * planes
    span = own + 2 * halo
    centre, coefficients = chebyshev_constants(DEGREE)
    assert halo >= STEPS

    def kernel(*refs):
        ins, refs = refs[: len(inputs)], refs[len(inputs) :]
        outs, face_ref, refs = refs[:TEAM], refs[TEAM], refs[TEAM + 1 :]
        cond, u_a, u_b, s_a, s_b, zp, zm, yp, ym, xp, xm, t_a, t_b = refs
        place = team_place()
        side = place // 2
        upper, lower = halo + own, 0
        near_base = jnp.where(side == 0, upper, lower)
        far_base = jnp.where(side == 0, lower, upper)
        def outside(v):
            return jnp.where(v > 0.0, v, 1e30)

        for core in range(2):
            for j in range(planes):
                for t in range(2):
                    n = 2 * j + t
                    own_base = halo + planes * core + j
                    for ref, base in ((ins[0], own_base + part * side), (ins[1], near_base + planes * core + j)):
                        cond[base, t] = outside(ref[core, slot, n])
                        t_a[base, t] = ref[core, slot, part + n]
                    for i, base in ((0, own_base + part * (1 - side)), (1, far_base + planes * core + j)):
                        cond[base, t] = outside(ins[2 + i][core * 2 * part + n])
                        t_a[base, t] = ins[2 + i][(core * 2 + 1) * part + n]

        last_row = lax.broadcasted_iota(jnp.int32, (half, columns), 0) == half - 1
        last_column = lax.broadcasted_iota(jnp.int32, (half, columns), 1) == columns - 1

        def ahead_x(v):
            return pltpu.roll(v, columns - 1, 1)

        def behind_x(v):
            return pltpu.roll(v, 1, 1)

        def ahead_y(v):
            return pltpu.roll(v, half - 1, 0)

        def behind_y(v):
            return pltpu.roll(v, 1, 0)

        def setup(p, w_z_before):
            even, odd = cond[p, 0], cond[p, 1]
            w_pair = harmonic(even, odd)
            w_next = jnp.where(last_row, 0.0, harmonic(odd, ahead_y(even)))
            w_z_here = []
            for t, here in enumerate((even, odd)):
                w_z = harmonic(here, cond[p + 1, t])
                w_z_here.append(w_z)
                w_z_behind = w_z_before[t]
                w_y = w_next if t else w_pair
                w_y_behind = w_pair if t else behind_y(w_next)
                w_x = jnp.where(last_column, 0.0, harmonic(here, ahead_x(here)))
                w_x_behind = behind_x(w_x)
                diagonal = (w_z + w_z_behind) + (w_y + w_y_behind) + (w_x + w_x_behind) + STORAGE
                inverse = reciprocal(diagonal)
                zp[p, t] = w_z * inverse
                zm[p, t] = w_z_behind * inverse
                yp[p, t] = w_y * inverse
                ym[p, t] = w_y_behind * inverse
                xp[p, t] = w_x * inverse
                xm[p, t] = w_x_behind * inverse
                scaled = t_a[p, t] * inverse
                u_a[p, t] = scaled
                s_a[p, t] = scaled * (1.0 / centre)
            return w_z_here

        width = (span - 2) // 3

        def setup_group(n, carry):
            start = 1 + n * width
            w_z = [harmonic(cond[start - 1, t], cond[start, t]) for t in range(2)]
            for k in range(width):
                w_z = setup(start + k, w_z)
            return carry

        assert (span - 2) % width == 0
        lax.fori_loop(0, (span - 2) // width, setup_group, 0)

        s_now, s_next, u_now, u_next, t_now, t_next = s_a, s_b, u_a, u_b, t_a, t_b
        for step in range(STEPS - 1):
            position = step % DEGREE
            if position + 1 < DEGREE:
                keep, mix = coefficients[position]
            else:
                keep, mix = 0.0, 1.0 / centre
            last = step == STEPS - 2

            def advance(p):
                even, odd = s_now[p, 0], s_now[p, 1]
                for t, s in enumerate((even, odd)):
                    ahead = ahead_y(even) if t else odd
                    behind = even if t else behind_y(odd)
                    moved = zp[p, t] * s_now[p + 1, t] + zm[p, t] * s_now[p - 1, t]
                    moved += yp[p, t] * ahead + ym[p, t] * behind
                    moved += xp[p, t] * ahead_x(s) + xm[p, t] * behind_x(s)
                    new_u = (u_now[p, t] - s) + moved
                    new_s = mix * new_u if keep == 0.0 else keep * s + mix * new_u
                    if not last:
                        u_next[p, t] = new_u
                        s_next[p, t] = new_s
                    if step == 0:
                        t_next[p, t] = s + new_s
                    elif step % 2 == 0:
                        t_next[p, t] = t_now[p, t] + (s + new_s)

            margin = halo - (STEPS - 2 - step)
            each(margin, span - margin, advance, 8)
            s_now, s_next, u_now, u_next = s_next, s_now, u_next, u_now
            if step % 2 == 0:
                t_now, t_next = t_next, t_now

        for m in range(TEAM):
            base = halo + planes * (place ^ m)
            for j in range(planes):
                for t in range(2):
                    outs[m][2 * j + t] = t_now[base + j, t]
        for p in range(own):
            face_ref[p : p + 1, :] = t_now[halo + p, 0, 0:1, :]

    vmem = pl.BlockSpec(memory_space=pltpu.VMEM)
    field = pltpu.VMEM((span, 2, half, columns), F32)
    return pl.pallas_call(
        kernel,
        out_shape=[jax.ShapeDtypeStruct((2 * planes, half, columns), F32)] * TEAM
        + [jax.ShapeDtypeStruct((own, columns), F32)],
        in_specs=[vmem] * len(inputs),
        out_specs=[vmem] * (TEAM + 1),
        scratch_shapes=[field] * 13,
        compiler_params=pltpu.CompilerParams(vmem_limit_bytes=16 * MIB),
        cost_estimate=pl.CostEstimate(flops=0, bytes_accessed=22 * MIB, transcendentals=0),
        name=f"solve{slot}",
    )(*inputs)


def weigh(sums, faces, cells, after):
    slots = len(faces)
    samples, columns = sums[0].shape

    def kernel(*refs):
        sum_refs, refs = refs[: len(sums)], refs[len(sums) :]
        face_refs, (out_ref, moments_ref, weights) = refs[:slots], refs[slots + len(after) :]
        place = team_place()
        summed = sum_refs[0][...]
        for ref in sum_refs[1:]:
            summed = summed + ref[...]
        misfit = summed * (1.0 / (2.0 * cells))
        mean = jnp.sum(misfit, axis=0, keepdims=True) * (1.0 / samples)
        deviation = misfit - mean
        variance = jnp.sum(deviation * deviation, axis=0, keepdims=True) * (1.0 / samples)
        lane = lax.broadcasted_iota(jnp.int32, (1, columns), 1)
        moments_ref[...] = jnp.where(lane == 0, mean, variance)
        weights[...] = 1.0 + 2.0 * BETA_RISK * deviation
        total = weights[pl.ds(slots * place, 1), :] * face_refs[0][...]
        for n in range(1, slots):
            total = total + weights[pl.ds(slots * place + n, 1), :] * face_refs[n][...]
        out_ref[...] = total

    vmem = pl.BlockSpec(memory_space=pltpu.VMEM)
    return pl.pallas_call(
        kernel,
        out_shape=[
            jax.ShapeDtypeStruct(faces[0].shape, F32),
            jax.ShapeDtypeStruct((1, columns), F32),
        ],
        in_specs=[vmem] * (len(sums) + slots)
        + [pl.BlockSpec(memory_space=pl.ANY)] * len(after),
        out_specs=[vmem, vmem],
        scratch_shapes=[pltpu.VMEM((samples, columns), F32)],
        compiler_params=pltpu.CompilerParams(vmem_limit_bytes=2 * MIB),
        name="weigh",
    )(*sums, *faces, *after)


def gather_adjoint(pieces, planes):
    slots = len(pieces)
    _, half, columns = pieces[0][0].shape
    tiles = columns // 128
    block = (planes, 2 * half, columns)

    def kernel(*refs):
        blocks, out, held, mixed, sems = refs[: slots * TEAM], *refs[slots * TEAM :]
        place = team_place()
        copies = []
        for slot in range(slots):
            for m in range(TEAM):
                i = slot * TEAM + m
                for j in range(planes):
                    for t in range(2):
                        for c in range(tiles):
                            mixed[i % 2, j, c, pl.ds(t, half, stride=2), :] = blocks[i][
                                2 * j + t, :, c * 128 : (c + 1) * 128
                            ]
                    for c in range(tiles):
                        held[i, j, :, c * 128 : (c + 1) * 128] = mixed[i % 2, j, c]
                copy = pltpu.make_async_copy(
                    held.at[i], out.at[slots * (place ^ m) + slot], sems.at[i]
                )
                copy.start()
                copies.append(copy)
        for copy in copies:
            copy.wait()

    return pl.pallas_call(
        kernel,
        out_shape=jax.ShapeDtypeStruct((slots * TEAM,) + block, F32),
        in_specs=[pl.BlockSpec(memory_space=pltpu.VMEM)] * (slots * TEAM),
        out_specs=pl.BlockSpec(memory_space=pltpu.HBM),
        scratch_shapes=[
            pltpu.VMEM((slots * TEAM,) + block, F32),
            pltpu.VMEM((2, planes, tiles, 2 * half, 128), F32),
            pltpu.SemaphoreType.DMA((slots * TEAM,)),
        ],
        compiler_params=pltpu.CompilerParams(vmem_limit_bytes=4 * MIB),
        cost_estimate=pl.CostEstimate(flops=0, bytes_accessed=4 * MIB, transcendentals=0),
        name="gather_adjoint",
    )(*[piece for group in pieces for piece in group])


def control(faces, radices, basis_z, basis_x):
    slabs, own_count, depth_total = basis_z.shape
    own, columns = faces[0].shape[1:]
    teams = depth_total // own

    def kernel(*refs):
        parts, (z_ref, x_ref, out_ref, whole) = refs[: len(faces)], refs[len(faces) :]
        rank = lax.axis_index("gz")
        team = rank // TEAM
        for n in range(teams):
            at, left, stride = 0, n, 1
            for radix in radices:
                digit = lax.rem(team // stride + left % radix, radix)
                at, left, stride = at + digit * stride, left // radix, stride * radix
            inner = teams // len(faces)
            whole[at] = parts[n // inner][n % inner]
        along_z = jnp.dot(
            z_ref[rank],
            whole[...].reshape(depth_total, columns),
            precision=lax.Precision.HIGHEST,
            preferred_element_type=F32,
        )
        out_ref[...] = jnp.dot(
            along_z, x_ref[...], precision=lax.Precision.HIGHEST, preferred_element_type=F32
        )

    vmem = pl.BlockSpec(memory_space=pltpu.VMEM)
    return pl.pallas_call(
        kernel,
        out_shape=jax.ShapeDtypeStruct((own_count, basis_x.shape[1]), F32),
        in_specs=[vmem] * (len(faces) + 2),
        out_specs=vmem,
        scratch_shapes=[pltpu.VMEM((teams, own, columns), F32)],
        compiler_params=pltpu.CompilerParams(vmem_limit_bytes=8 * MIB),
        name="control",
    )(*faces, basis_z, basis_x)


def radices_of(teams):
    radices = []
    while teams > 1:
        radix = next(r for r in (4, 2, 3, *range(5, teams + 1)) if teams % r == 0)
        radices.append(radix)
        teams //= radix
    return radices


def on_device(state, target, rock_type, log_table, obs_scale):
    samples, planes, rows_y, columns = state.shape
    slabs = lax.axis_size("gz")
    slots = samples // TEAM
    depth_total = planes * slabs
    radices = radices_of(slabs // TEAM)

    def swap(value, m):
        return lax.ppermute(value, "gz", [(i, i ^ m) for i in range(slabs)])

    def along(value, outward):
        pairs = []
        for i in range(slabs):
            side = (i % TEAM) // 2
            to = i + TEAM if (side == 1) == outward else i - TEAM
            if 0 <= to < slabs:
                pairs.append((i, to))
        return lax.ppermute(value, "gz", pairs)

    def from_teams(value, stride, radix):
        heard = []
        for k in range(1, radix):
            pairs = []
            for i in range(slabs):
                digit = i // (TEAM * stride) % radix
                pairs.append((i + ((digit + k) % radix - digit) * stride * TEAM, i))
            heard.append(lax.ppermute(value, "gz", pairs))
        return heard

    fields = [
        pltpu.with_memory_space_constraint(field, pltpu.HBM)
        for field in (state, target, rock_type, log_table, obs_scale)
    ]
    size = 4 * planes
    jobs = [[(slot, m) for slot in range(slots)] for m in range(TEAM)]
    mine, theirs, sums = prepare(jobs[2:], fields, with_sums=True)
    theirs = swap(theirs, 1)
    first, chip_sums = merge_far(mine, theirs, 0, size, sums)
    far = [swap(first, 2)]
    mine_near, theirs_near = prepare(jobs[:2], fields)
    theirs_near = swap(theirs_near, 1)
    near = merge_near(mine_near, theirs_near, slots, size)
    near_halo = along(near, True)
    far += [swap(merge_far(mine, theirs, slot, size), 2) for slot in range(1, slots)]
    teams = slabs // TEAM
    rounds, stride = [], 1
    while stride < teams:
        radix = next(r for r in range(2, teams + 1) if teams // stride % r == 0)
        rounds.append((stride, radix))
        stride *= radix
    sums = [chip_sums + far[0][2 * size]]
    for stride, radix in rounds[:1]:
        sums = [sum(from_teams(sums[0], stride, radix), sums[0])]
    far[1:] = [hold(value, sums[0]) for value in far[1:]]

    pieces, faces = [], []
    for slot in range(slots):
        far_halo = along(far[slot], False)
        solved = solve(slot, near, far[slot], near_halo, far_halo, planes)
        pieces.append([solved[0]] + [swap(solved[m], m) for m in (1, 2, 3)])
        faces.append(solved[TEAM])
        if slot == 0:
            for stride, radix in rounds[1:]:
                sums = [add_up(sums, solved[TEAM])]
                sums += from_teams(sums[0], stride, radix)

    face, moments = weigh(sums, faces, depth_total * rows_y * columns, pieces[0][1:])
    heard = [sum((swap(face, m) for m in (2, 3, 1)), face)[None]]
    stride = 1
    for radix in radices:
        held = heard[0] if len(heard) == 1 else jnp.concatenate(heard)
        heard = [held] + from_teams(held, stride, radix)
        stride *= radix
    adjoint = gather_adjoint(pieces, planes)
    own_count = MA // slabs
    gradient = control(
        heard,
        radices,
        jnp.asarray(cosine_basis(depth_total, MA).T.reshape(slabs, own_count, depth_total)),
        jnp.asarray(cosine_basis(columns, MB)),
    )
    return (adjoint, gradient, moments[0, :2])


def solution(mesh):
    return jax.shard_map(
        on_device,
        mesh=mesh,
        in_specs=(
            P("parts", "gz", None, None),
            P(("parts", "gz"), None, None),
            P("parts", "gz", None, None),
            P("parts", None),
            P("parts"),
        ),
        out_specs=(P("parts", "gz", None, None), P(("parts", "gz"), None), P("parts")),
        check_vma=False,
    )
```

```python
import math

import jax
import jax.numpy as jnp
import numpy as np
from jax import lax
from jax.experimental import pallas as pl
from jax.experimental.pallas import tpu as pltpu
from jax.sharding import PartitionSpec as P

NR = 8
DEGREE = 4
SWEEPS = 2
MA = 512
MB = 512

STORAGE = 0.05
BETA_RISK = 0.5
LOWER_EIGEN = 0.05
UPPER_EIGEN = 2.0

TEAM = 4
STEPS = DEGREE * SWEEPS
F32 = jnp.float32
MIB = 1024 * 1024
LANES = 128


def chebyshev_constants(number_steps):
    centre = (UPPER_EIGEN + LOWER_EIGEN) / 2
    spread = (UPPER_EIGEN - LOWER_EIGEN) / 2
    quotient = centre / spread
    rho_now = 1.0 / quotient
    coefficients = []
    for position in range(number_steps):
        rho_next = 1.0 / (2.0 * quotient - rho_now)
        coefficients.append((rho_next * rho_now, 2.0 * rho_next / spread))
        rho_now = rho_next
    return (centre, coefficients)


def cosine_basis(length_total, modes):
    positions = np.arange(length_total, dtype=np.int64)
    mode_index = np.arange(modes, dtype=np.int64)
    product_index = ((2 * positions[:, None] + 1) * (2 * mode_index[None, :] + 1)) % (
        8 * length_total
    )
    angle = product_index.astype(np.float64) * (math.pi / (4 * length_total))
    return (math.sqrt(2.0 / length_total) * np.cos(angle)).astype(np.float32)


def team_place():
    return lax.rem(lax.axis_index("gz"), TEAM)


def prepare(jobs, fields, with_sums=False):
    state, target, rock_type, log_table, obs_scale = fields
    samples, planes, rows_y, columns = state.shape
    slots = samples // TEAM
    block = (planes, rows_y, columns)
    half, tiles = rows_y // 2, columns // 128
    size = 2 * 2 * planes
    depth_total = planes * lax.axis_size("gz")
    flat = [(o, i, job) for o, group in enumerate(jobs) for i, job in enumerate(group)]
    count = len(flat)
    shapes = [(len(group) * size + with_sums, half, columns) for group in jobs]
    states = samples if with_sums else count

    def kernel(*refs):
        (table_ref, scale_ref, state_ref, target_ref, rock_ref), refs = refs[:5], refs[5:]
        outs, refs = refs[: len(jobs)], refs[len(jobs) :]
        if with_sums:
            sums_ref, refs = refs[0], refs[1:]
        table, scale, state_buf, rock_buf, target_buf, mixed, sems = refs
        place = team_place()
        first_plane = lax.axis_index("gz") * planes
        members = [slots * (place ^ m) + slot for _, _, (slot, m) in flat]
        small = [
            pltpu.make_async_copy(table_ref, table, sems.at[2, 0]),
            pltpu.make_async_copy(scale_ref, scale, sems.at[2, 1]),
            pltpu.make_async_copy(target_ref, target_buf, sems.at[2, 2]),
        ]
        for copy in small:
            copy.start()
        rocks = [
            pltpu.make_async_copy(rock_ref.at[member], rock_buf.at[n], sems.at[1, n])
            for n, member in enumerate(members)
        ]
        loads = [
            pltpu.make_async_copy(
                state_ref.at[n if with_sums else members[n]], state_buf.at[n], sems.at[0, n]
            )
            for n in range(states)
        ]
        for copy in rocks + loads:
            copy.start()
        depth_weights = [
            1.0 + (2.0 / (depth_total - 1)) * (first_plane + p).astype(F32) for p in range(planes)
        ]
        for copy in small:
            copy.wait()
        if with_sums:
            for copy in loads:
                copy.wait()
            for n in range(samples):
                total = jnp.zeros((8, columns), F32)
                for p in range(planes):
                    part = jnp.zeros((8, columns), F32)
                    for first in range(0, rows_y, 8):
                        rows = slice(first, first + 8)
                        gap = state_buf[n, p, rows] - target_buf[p, rows]
                        part = part + gap * gap
                    total = total + (scale[n] * depth_weights[p]) * part
                summed = jnp.sum(total, keepdims=True)
                sums_ref[n : n + 1, :] = jnp.broadcast_to(summed, (1, columns))
        for n, (o, i, _) in enumerate(flat):
            rocks[n].wait()
            if not with_sums:
                loads[n].wait()
            member = members[n]
            own_state = member if with_sums else n
            values = [
                jnp.exp(jnp.full((8, columns), -table[member, code], F32)) for code in range(NR)
            ]
            for p in range(planes):
                factor = scale[member] * depth_weights[p]
                for first in range(0, rows_y, 8):
                    rows = slice(first, first + 8)
                    codes = rock_buf[n, p, rows]
                    low, mid, high = ((codes & bit) != 0 for bit in (1, 2, 4))
                    pairs = [
                        jnp.where(low, values[2 * k + 1], values[2 * k]) for k in range(NR // 2)
                    ]
                    halves = [jnp.where(mid, pairs[2 * k + 1], pairs[2 * k]) for k in range(2)]
                    gap = state_buf[own_state, p, rows] - target_buf[p, rows]
                    made = (jnp.where(high, halves[1], halves[0]), factor * gap)
                    for a in range(2):
                        for c in range(tiles):
                            mixed[n % 2, p, a, c, rows] = made[a][:, c * 128 : (c + 1) * 128]
                for a in range(2):
                    for t in range(2):
                        for c in range(tiles):
                            at = i * size + (a * planes + p) * 2 + t
                            outs[o][at, :, c * 128 : (c + 1) * 128] = mixed[
                                n % 2, p, a, c, pl.ds(t, half, stride=2), :
                            ]
        for o, group in enumerate(jobs if with_sums else []):
            outs[o][len(group) * size] = sums_ref[...]

    hbm = pl.BlockSpec(memory_space=pltpu.HBM)
    vmem = pl.BlockSpec(memory_space=pltpu.VMEM)
    return pl.pallas_call(
        kernel,
        out_shape=[jax.ShapeDtypeStruct(shape, F32) for shape in shapes]
        + [jax.ShapeDtypeStruct((samples, columns), F32)] * with_sums,
        in_specs=[hbm] * 5,
        out_specs=[vmem] * (len(shapes) + with_sums),
        scratch_shapes=[
            pltpu.SMEM(log_table.shape, F32),
            pltpu.SMEM(obs_scale.shape, F32),
            pltpu.VMEM((states,) + block, F32),
            pltpu.VMEM((count,) + block, jnp.int32),
            pltpu.VMEM(block, F32),
            pltpu.VMEM((2, planes, 2, tiles, rows_y, 128), F32),
            pltpu.SemaphoreType.DMA((3, max(states, 3))),
        ],
        compiler_params=pltpu.CompilerParams(vmem_limit_bytes=6 * MIB),
        cost_estimate=pl.CostEstimate(flops=0, bytes_accessed=count * MIB, transcendentals=0),
        name="prepare",
    )(log_table, obs_scale, state, target, rock_type)


def merge_far(mine, theirs, slot, size, sums, add=False):
    tile = mine.shape[1:]

    def kernel(mine_ref, theirs_ref, sums_ref, out_ref, *more):
        core = lax.rem(team_place(), 2)
        for ref, at in ((mine_ref, core), (theirs_ref, 1 - core)):
            for n in range(size):
                out_ref[at * size + n] = ref[slot * size + n]
        if add:
            more[0][...] = sums_ref[...] + theirs_ref[theirs.shape[0] - 1]
        else:
            out_ref[2 * size] = sums_ref[...]

    vmem = pl.BlockSpec(memory_space=pltpu.VMEM)
    shapes = [(2 * size,) + tile, tile] if add else [(2 * size + 1,) + tile]
    outs = pl.pallas_call(
        kernel,
        out_shape=[jax.ShapeDtypeStruct(shape, F32) for shape in shapes],
        in_specs=[vmem] * 3,
        out_specs=[vmem] * len(shapes),
        compiler_params=pltpu.CompilerParams(vmem_limit_bytes=4 * MIB),
        name="merge_far",
    )(mine, theirs, sums)
    return outs if add else outs[0]


def merge_near(mine, theirs, slot, size, sums):
    def kernel(mine_ref, theirs_ref, sums_ref, out_ref):
        core = lax.rem(team_place(), 2)
        for ref, at in ((mine_ref, core), (theirs_ref, 1 - core)):
            for n in range(size):
                out_ref[at * size + n] = ref[slot * size + n]
        out_ref[2 * size] = sums_ref[...]

    vmem = pl.BlockSpec(memory_space=pltpu.VMEM)
    return pl.pallas_call(
        kernel,
        out_shape=jax.ShapeDtypeStruct((2 * size + 1,) + mine.shape[1:], F32),
        in_specs=[vmem] * 3,
        out_specs=vmem,
        compiler_params=pltpu.CompilerParams(vmem_limit_bytes=4 * MIB),
        name="merge_near",
    )(mine, theirs, sums)


def reciprocal(x):
    guess = pl.reciprocal(x, approx=True)
    return guess * (2.0 - x * guess)


def harmonic(a, b):
    x = a + b
    guess = pl.reciprocal(x, approx=True)
    return guess * (4.0 - (2.0 * x) * guess)


def each(start, stop, body, width):
    whole = (stop - start) // width

    def group(n, carry):
        for k in range(width):
            body(start + n * width + k)
        return carry

    lax.fori_loop(0, whole, group, 0)
    for p in range(start + whole * width, stop):
        body(p)


def solve(near, far, near_halo, far_halo, planes):
    inputs = [near, near_halo, far, far_halo]
    half, columns = far.shape[-2:]
    part = 2 * planes
    halo = 2 * planes
    own = TEAM * planes
    span = own + 2 * halo
    centre, coefficients = chebyshev_constants(DEGREE)
    assert halo >= STEPS

    def kernel(*refs):
        ins, refs = refs[: len(inputs)], refs[len(inputs) :]
        outs, face_ref, refs = refs[:TEAM], refs[TEAM], refs[TEAM + 1 :]
        cond, u_a, u_b, s_a, s_b, zp, zm, yp, ym, xp, xm, t_a, t_b = refs
        place = team_place()
        side = place // 2
        upper, lower = halo + own, 0
        near_base = jnp.where(side == 0, upper, lower)
        far_base = jnp.where(side == 0, lower, upper)
        def outside(v):
            return jnp.where(v > 0.0, v, 1e30)

        for core in range(2):
            for j in range(planes):
                for t in range(2):
                    n = 2 * j + t
                    own_base = halo + planes * core + j
                    for ref, base in (
                        (ins[0], own_base + part * side),
                        (ins[1], near_base + planes * core + j),
                        (ins[2], own_base + part * (1 - side)),
                        (ins[3], far_base + planes * core + j),
                    ):
                        cond[base, t] = outside(ref[core * 2 * part + n])
                        t_a[base, t] = ref[(core * 2 + 1) * part + n]

        last_row = lax.broadcasted_iota(jnp.int32, (half, columns), 0) == half - 1
        last_column = lax.broadcasted_iota(jnp.int32, (half, columns), 1) == columns - 1

        def ahead_x(v):
            return pltpu.roll(v, columns - 1, 1)

        def behind_x(v):
            return pltpu.roll(v, 1, 1)

        def ahead_y(v):
            return pltpu.roll(v, half - 1, 0)

        def behind_y(v):
            return pltpu.roll(v, 1, 0)

        def setup(p, w_z_before):
            even, odd = cond[p, 0], cond[p, 1]
            w_pair = harmonic(even, odd)
            w_next = jnp.where(last_row, 0.0, harmonic(odd, ahead_y(even)))
            w_z_here = []
            for t, here in enumerate((even, odd)):
                w_z = harmonic(here, cond[p + 1, t])
                w_z_here.append(w_z)
                w_z_behind = w_z_before[t]
                w_y = w_next if t else w_pair
                w_y_behind = w_pair if t else behind_y(w_next)
                w_x = jnp.where(last_column, 0.0, harmonic(here, ahead_x(here)))
                w_x_behind = behind_x(w_x)
                diagonal = (w_z + w_z_behind) + (w_y + w_y_behind) + (w_x + w_x_behind) + STORAGE
                inverse = reciprocal(diagonal)
                zp[p, t] = w_z * inverse
                zm[p, t] = w_z_behind * inverse
                yp[p, t] = w_y * inverse
                ym[p, t] = w_y_behind * inverse
                xp[p, t] = w_x * inverse
                xm[p, t] = w_x_behind * inverse
                scaled = t_a[p, t] * inverse
                u_a[p, t] = scaled
                s_a[p, t] = scaled * (1.0 / centre)
            return w_z_here

        width = (span - 2) // 3

        def setup_group(n, carry):
            start = 1 + n * width
            w_z = [harmonic(cond[start - 1, t], cond[start, t]) for t in range(2)]
            for k in range(width):
                w_z = setup(start + k, w_z)
            return carry

        assert (span - 2) % width == 0
        lax.fori_loop(0, (span - 2) // width, setup_group, 0)

        s_now, s_next, u_now, u_next, t_now, t_next = s_a, s_b, u_a, u_b, t_a, t_b
        for step in range(STEPS - 1):
            position = step % DEGREE
            if position + 1 < DEGREE:
                keep, mix = coefficients[position]
            else:
                keep, mix = 0.0, 1.0 / centre
            last = step == STEPS - 2

            def advance(p):
                even, odd = s_now[p, 0], s_now[p, 1]
                for t, s in enumerate((even, odd)):
                    ahead = ahead_y(even) if t else odd
                    behind = even if t else behind_y(odd)
                    moved = zp[p, t] * s_now[p + 1, t] + zm[p, t] * s_now[p - 1, t]
                    moved += yp[p, t] * ahead + ym[p, t] * behind
                    moved += xp[p, t] * ahead_x(s) + xm[p, t] * behind_x(s)
                    new_u = (u_now[p, t] - s) + moved
                    new_s = mix * new_u if keep == 0.0 else keep * s + mix * new_u
                    if not last:
                        u_next[p, t] = new_u
                        s_next[p, t] = new_s
                    if step == 0:
                        t_next[p, t] = s + new_s
                    elif step % 2 == 0:
                        t_next[p, t] = t_now[p, t] + (s + new_s)

            margin = halo - (STEPS - 2 - step)
            each(margin, span - margin, advance, 8)
            s_now, s_next, u_now, u_next = s_next, s_now, u_next, u_now
            if step % 2 == 0:
                t_now, t_next = t_next, t_now

        for m in range(TEAM):
            base = halo + planes * (place ^ m)
            for j in range(planes):
                for t in range(2):
                    outs[m][2 * j + t] = t_now[base + j, t]
        for p in range(own):
            face_ref[p : p + 1, :] = t_now[halo + p, 0, 0:1, :]

    vmem = pl.BlockSpec(memory_space=pltpu.VMEM)
    field = pltpu.VMEM((span, 2, half, columns), F32)
    return pl.pallas_call(
        kernel,
        out_shape=[jax.ShapeDtypeStruct((2 * planes, half, columns), F32)] * TEAM
        + [jax.ShapeDtypeStruct((own, columns), F32)],
        in_specs=[vmem] * len(inputs),
        out_specs=[vmem] * (TEAM + 1),
        scratch_shapes=[field] * 13,
        compiler_params=pltpu.CompilerParams(vmem_limit_bytes=16 * MIB),
        cost_estimate=pl.CostEstimate(flops=0, bytes_accessed=22 * MIB, transcendentals=0),
        name="solve",
    )(*inputs)


def weigh(sums, faces, cells, after):
    slots = len(faces)
    samples, columns = sums[0].shape

    def kernel(*refs):
        sum_refs, refs = refs[: len(sums)], refs[len(sums) :]
        face_refs, (out_ref, moments_ref, weights) = refs[:slots], refs[slots + len(after) :]
        place = team_place()
        summed = sum_refs[0][...]
        for ref in sum_refs[1:]:
            summed = summed + ref[...]
        misfit = summed * (1.0 / (2.0 * cells))
        mean = jnp.sum(misfit, axis=0, keepdims=True) * (1.0 / samples)
        deviation = misfit - mean
        variance = jnp.sum(deviation * deviation, axis=0, keepdims=True) * (1.0 / samples)
        lane = lax.broadcasted_iota(jnp.int32, (1, columns), 1)
        moments_ref[...] = jnp.where(lane == 0, mean, variance)
        weights[...] = 1.0 + 2.0 * BETA_RISK * deviation
        total = weights[pl.ds(slots * place, 1), :] * face_refs[0][...]
        for n in range(1, slots):
            total = total + weights[pl.ds(slots * place + n, 1), :] * face_refs[n][...]
        out_ref[...] = total

    vmem = pl.BlockSpec(memory_space=pltpu.VMEM)
    return pl.pallas_call(
        kernel,
        out_shape=[
            jax.ShapeDtypeStruct(faces[0].shape, F32),
            jax.ShapeDtypeStruct((1, columns), F32),
        ],
        in_specs=[vmem] * (len(sums) + slots)
        + [pl.BlockSpec(memory_space=pl.ANY)] * len(after),
        out_specs=[vmem, vmem],
        scratch_shapes=[pltpu.VMEM((samples, columns), F32)],
        compiler_params=pltpu.CompilerParams(vmem_limit_bytes=2 * MIB),
        name="weigh",
    )(*sums, *faces, *after)


def gather_adjoint(pieces, planes):
    slots = len(pieces)
    _, half, columns = pieces[0][0].shape
    tiles = columns // 128
    block = (planes, 2 * half, columns)

    def kernel(*refs):
        blocks, out, mark, held, mixed, sems = refs[: slots * TEAM], *refs[slots * TEAM :]
        mark[...] = blocks[0][0, :, :LANES]
        place = team_place()
        copies = []
        for slot in range(slots):
            for m in range(TEAM):
                i = slot * TEAM + m
                for j in range(planes):
                    for t in range(2):
                        for c in range(tiles):
                            mixed[i % 2, j, c, pl.ds(t, half, stride=2), :] = blocks[i][
                                2 * j + t, :, c * 128 : (c + 1) * 128
                            ]
                    for c in range(tiles):
                        held[i, j, :, c * 128 : (c + 1) * 128] = mixed[i % 2, j, c]
                copy = pltpu.make_async_copy(
                    held.at[i], out.at[slots * (place ^ m) + slot], sems.at[i]
                )
                copy.start()
                copies.append(copy)
        for copy in copies:
            copy.wait()

    return pl.pallas_call(
        kernel,
        out_shape=[
            jax.ShapeDtypeStruct((slots * TEAM,) + block, F32),
            jax.ShapeDtypeStruct((half, LANES), F32),
        ],
        in_specs=[pl.BlockSpec(memory_space=pltpu.VMEM)] * (slots * TEAM),
        out_specs=[
            pl.BlockSpec(memory_space=pltpu.HBM),
            pl.BlockSpec(memory_space=pltpu.VMEM),
        ],
        scratch_shapes=[
            pltpu.VMEM((slots * TEAM,) + block, F32),
            pltpu.VMEM((2, planes, tiles, 2 * half, 128), F32),
            pltpu.SemaphoreType.DMA((slots * TEAM,)),
        ],
        compiler_params=pltpu.CompilerParams(vmem_limit_bytes=4 * MIB),
        cost_estimate=pl.CostEstimate(flops=0, bytes_accessed=4 * MIB, transcendentals=0),
        name="gather_adjoint",
    )(*[piece for group in pieces for piece in group])


def control(faces, radices, basis_z, basis_x, after):
    slabs, own_count, depth_total = basis_z.shape
    own, columns = faces[0].shape[1:]
    teams = depth_total // own

    def kernel(*refs):
        parts, (z_ref, x_ref, _, out_ref, whole) = refs[: len(faces)], refs[len(faces) :]
        rank = lax.axis_index("gz")
        team = rank // TEAM
        for n in range(teams):
            at, left, stride = 0, n, 1
            for radix in radices:
                digit = lax.rem(team // stride + left % radix, radix)
                at, left, stride = at + digit * stride, left // radix, stride * radix
            inner = teams // len(faces)
            whole[at] = parts[n // inner][n % inner]
        along_z = jnp.dot(
            z_ref[rank],
            whole[...].reshape(depth_total, columns),
            precision=lax.Precision.HIGHEST,
            preferred_element_type=F32,
        )
        out_ref[...] = jnp.dot(
            along_z, x_ref[...], precision=lax.Precision.HIGHEST, preferred_element_type=F32
        )

    vmem = pl.BlockSpec(memory_space=pltpu.VMEM)
    return pl.pallas_call(
        kernel,
        out_shape=jax.ShapeDtypeStruct((own_count, basis_x.shape[1]), F32),
        in_specs=[vmem] * (len(faces) + 2) + [pl.BlockSpec(memory_space=pl.ANY)],
        out_specs=vmem,
        scratch_shapes=[pltpu.VMEM((teams, own, columns), F32)],
        compiler_params=pltpu.CompilerParams(vmem_limit_bytes=8 * MIB),
        name="control",
    )(*faces, basis_z, basis_x, after)


def radices_of(teams):
    radices = []
    while teams > 1:
        radix = next(r for r in (4, 2, 3, *range(5, teams + 1)) if teams % r == 0)
        radices.append(radix)
        teams //= radix
    return radices


def on_device(state, target, rock_type, log_table, obs_scale):
    samples, planes, rows_y, columns = state.shape
    slabs = lax.axis_size("gz")
    slots = samples // TEAM
    depth_total = planes * slabs
    radices = radices_of(slabs // TEAM)

    def swap(value, m):
        return lax.ppermute(value, "gz", [(i, i ^ m) for i in range(slabs)])

    def along(value, outward):
        pairs = []
        for i in range(slabs):
            side = (i % TEAM) // 2
            to = i + TEAM if (side == 1) == outward else i - TEAM
            if 0 <= to < slabs:
                pairs.append((i, to))
        return lax.ppermute(value, "gz", pairs)

    def from_teams(value, stride, radix):
        heard = []
        for k in range(1, radix):
            pairs = []
            for i in range(slabs):
                digit = i // (TEAM * stride) % radix
                pairs.append((i + ((digit + k) % radix - digit) * stride * TEAM, i))
            heard.append(lax.ppermute(value, "gz", pairs))
        return heard

    fields = [
        pltpu.with_memory_space_constraint(field, pltpu.HBM)
        for field in (state, target, rock_type, log_table, obs_scale)
    ]
    size = 4 * planes
    jobs = [[(slot, m) for slot in range(slots)] for m in range(TEAM)]
    mine, theirs, sums = prepare(jobs[2:], fields, with_sums=True)
    theirs = swap(theirs, 1)
    first, sums = merge_far(mine, theirs, 0, size, sums, add=True)
    far = [swap(first, 2)]
    stride, teams = 1, slabs // TEAM
    while stride < teams:
        radix = next(r for r in range(2, teams + 1) if teams // stride % r == 0)
        sums = sum(from_teams(sums, stride, radix), sums)
        stride *= radix

    mine_near, theirs_near = prepare(jobs[:2], fields)
    theirs_near = swap(theirs_near, 1)
    near = [merge_near(mine_near, theirs_near, slot, size, sums) for slot in range(slots)]
    near_halo = [along(value, True) for value in near]
    far += [swap(merge_far(mine, theirs, slot, size, sums), 2) for slot in range(1, slots)]
    sums = [sums, far[-1][2 * size]]

    pieces, faces = [], []
    for slot in range(slots):
        far_halo = along(far[slot], False)
        solved = solve(near[slot], far[slot], near_halo[slot], far_halo, planes)
        pieces.append([solved[0]] + [swap(solved[m], m) for m in (1, 2, 3)])
        faces.append(solved[TEAM])

    face, moments = weigh(sums, faces, depth_total * rows_y * columns, pieces[0][1:])
    heard = [sum((swap(face, m) for m in (2, 3, 1)), face)[None]]
    stride = 1
    for radix in radices:
        held = heard[0] if len(heard) == 1 else jnp.concatenate(heard)
        heard = [held] + from_teams(held, stride, radix)
        stride *= radix
    adjoint, mark = gather_adjoint(pieces, planes)
    own_count = MA // slabs
    gradient = control(
        heard,
        radices,
        jnp.asarray(cosine_basis(depth_total, MA).T.reshape(slabs, own_count, depth_total)),
        jnp.asarray(cosine_basis(columns, MB)),
        mark,
    )
    return (adjoint, gradient, moments[0, :2])


def solution(mesh):
    return jax.shard_map(
        on_device,
        mesh=mesh,
        in_specs=(
            P("parts", "gz", None, None),
            P(("parts", "gz"), None, None),
            P("parts", "gz", None, None),
            P("parts", None),
            P("parts"),
        ),
        out_specs=(P("parts", "gz", None, None), P(("parts", "gz"), None), P("parts")),
        check_vma=False,
    )
```

```python
import math

import jax
import jax.numpy as jnp
import numpy as np
from jax import lax
from jax.experimental import pallas as pl
from jax.experimental.pallas import tpu as pltpu
from jax.sharding import PartitionSpec as P

NR = 8
DEGREE = 4
SWEEPS = 2
MA = 512
MB = 512

STORAGE = 0.05
BETA_RISK = 0.5
LOWER_EIGEN = 0.05
UPPER_EIGEN = 2.0

TEAM = 4
STEPS = DEGREE * SWEEPS
F32 = jnp.float32
MIB = 1024 * 1024
LANES = 128


def chebyshev_constants(number_steps):
    centre = (UPPER_EIGEN + LOWER_EIGEN) / 2
    spread = (UPPER_EIGEN - LOWER_EIGEN) / 2
    quotient = centre / spread
    rho_now = 1.0 / quotient
    coefficients = []
    for position in range(number_steps):
        rho_next = 1.0 / (2.0 * quotient - rho_now)
        coefficients.append((rho_next * rho_now, 2.0 * rho_next / spread))
        rho_now = rho_next
    return (centre, coefficients)


def cosine_basis(length_total, modes):
    positions = np.arange(length_total, dtype=np.int64)
    mode_index = np.arange(modes, dtype=np.int64)
    product_index = ((2 * positions[:, None] + 1) * (2 * mode_index[None, :] + 1)) % (
        8 * length_total
    )
    angle = product_index.astype(np.float64) * (math.pi / (4 * length_total))
    return (math.sqrt(2.0 / length_total) * np.cos(angle)).astype(np.float32)


def in_halves(values):
    high = values.astype(jnp.bfloat16)
    return high, (values - high.astype(F32)).astype(jnp.bfloat16)


def team_place():
    return lax.rem(lax.axis_index("gz"), TEAM)


def prepare(jobs, fields, with_sums=False):
    state, target, rock_type, log_table, obs_scale = fields
    samples, planes, rows_y, columns = state.shape
    slots = samples // TEAM
    block = (planes, rows_y, columns)
    half, tiles = rows_y // 2, columns // 128
    size = 2 * 2 * planes
    depth_total = planes * lax.axis_size("gz")
    flat = [(o, i, job) for o, group in enumerate(jobs) for i, job in enumerate(group)]
    count = len(flat)
    shapes = [(len(group) * size + with_sums, half, columns) for group in jobs]
    states = samples if with_sums else count

    def kernel(*refs):
        (table_ref, scale_ref, state_ref, target_ref, rock_ref), refs = refs[:5], refs[5:]
        outs, refs = refs[: len(jobs)], refs[len(jobs) :]
        if with_sums:
            sums_ref, refs = refs[0], refs[1:]
        table, scale, state_buf, rock_buf, target_buf, mixed, sems = refs
        place = team_place()
        first_plane = lax.axis_index("gz") * planes
        members = [slots * (place ^ m) + slot for _, _, (slot, m) in flat]
        small = [
            pltpu.make_async_copy(table_ref, table, sems.at[2, 0]),
            pltpu.make_async_copy(scale_ref, scale, sems.at[2, 1]),
            pltpu.make_async_copy(target_ref, target_buf, sems.at[2, 2]),
        ]
        for copy in small:
            copy.start()
        rocks = [
            pltpu.make_async_copy(rock_ref.at[member], rock_buf.at[n], sems.at[1, n])
            for n, member in enumerate(members)
        ]
        loads = [
            pltpu.make_async_copy(
                state_ref.at[n if with_sums else members[n]], state_buf.at[n], sems.at[0, n]
            )
            for n in range(states)
        ]
        for copy in rocks + loads:
            copy.start()
        depth_weights = [
            1.0 + (2.0 / (depth_total - 1)) * (first_plane + p).astype(F32) for p in range(planes)
        ]
        for copy in small:
            copy.wait()
        if with_sums:
            for copy in loads:
                copy.wait()
            for n in range(samples):
                total = jnp.zeros((8, columns), F32)
                for p in range(planes):
                    part = jnp.zeros((8, columns), F32)
                    for first in range(0, rows_y, 8):
                        rows = slice(first, first + 8)
                        gap = state_buf[n, p, rows] - target_buf[p, rows]
                        part = part + gap * gap
                    total = total + (scale[n] * depth_weights[p]) * part
                summed = jnp.sum(total, keepdims=True)
                sums_ref[n : n + 1, :] = jnp.broadcast_to(summed, (1, columns))
        for n, (o, i, _) in enumerate(flat):
            rocks[n].wait()
            if not with_sums:
                loads[n].wait()
            member = members[n]
            own_state = member if with_sums else n
            values = [
                jnp.exp(jnp.full((8, columns), -table[member, code], F32)) for code in range(NR)
            ]
            for p in range(planes):
                factor = scale[member] * depth_weights[p]
                for first in range(0, rows_y, 8):
                    rows = slice(first, first + 8)
                    codes = rock_buf[n, p, rows]
                    low, mid, high = ((codes & bit) != 0 for bit in (1, 2, 4))
                    pairs = [
                        jnp.where(low, values[2 * k + 1], values[2 * k]) for k in range(NR // 2)
                    ]
                    halves = [jnp.where(mid, pairs[2 * k + 1], pairs[2 * k]) for k in range(2)]
                    gap = state_buf[own_state, p, rows] - target_buf[p, rows]
                    made = (jnp.where(high, halves[1], halves[0]), factor * gap)
                    for a in range(2):
                        for c in range(tiles):
                            mixed[n % 2, p, a, c, rows] = made[a][:, c * 128 : (c + 1) * 128]
                for a in range(2):
                    for t in range(2):
                        for c in range(tiles):
                            at = i * size + (a * planes + p) * 2 + t
                            outs[o][at, :, c * 128 : (c + 1) * 128] = mixed[
                                n % 2, p, a, c, pl.ds(t, half, stride=2), :
                            ]
        for o, group in enumerate(jobs if with_sums else []):
            outs[o][len(group) * size] = sums_ref[...]

    hbm = pl.BlockSpec(memory_space=pltpu.HBM)
    vmem = pl.BlockSpec(memory_space=pltpu.VMEM)
    return pl.pallas_call(
        kernel,
        out_shape=[jax.ShapeDtypeStruct(shape, F32) for shape in shapes]
        + [jax.ShapeDtypeStruct((samples, columns), F32)] * with_sums,
        in_specs=[hbm] * 5,
        out_specs=[vmem] * (len(shapes) + with_sums),
        scratch_shapes=[
            pltpu.SMEM(log_table.shape, F32),
            pltpu.SMEM(obs_scale.shape, F32),
            pltpu.VMEM((states,) + block, F32),
            pltpu.VMEM((count,) + block, jnp.int32),
            pltpu.VMEM(block, F32),
            pltpu.VMEM((2, planes, 2, tiles, rows_y, 128), F32),
            pltpu.SemaphoreType.DMA((3, max(states, 3))),
        ],
        compiler_params=pltpu.CompilerParams(vmem_limit_bytes=6 * MIB),
        cost_estimate=pl.CostEstimate(flops=0, bytes_accessed=count * MIB, transcendentals=0),
        name="prepare",
    )(log_table, obs_scale, state, target, rock_type)


def merge(mine, theirs, slot, size, behind=None, add=None):
    given = [value for value in (behind, add) if value is not None]

    def kernel(mine_ref, theirs_ref, *refs):
        core = lax.rem(team_place(), 2)
        tail, (out_ref, *more) = refs[: len(given)], refs[len(given) :]
        for ref, at in ((mine_ref, core), (theirs_ref, 1 - core)):
            for n in range(size):
                out_ref[at * size + n] = ref[slot * size + n]
        if behind is not None:
            out_ref[2 * size] = tail[0][...]
        if add is not None:
            more[0][...] = tail[-1][...] + theirs_ref[theirs.shape[0] - 1]

    vmem = pl.BlockSpec(memory_space=pltpu.VMEM)
    tile = mine.shape[1:]
    outs = pl.pallas_call(
        kernel,
        out_shape=[jax.ShapeDtypeStruct((2 * size + (behind is not None),) + tile, F32)]
        + [jax.ShapeDtypeStruct(tile, F32)] * (add is not None),
        in_specs=[vmem] * (2 + len(given)),
        out_specs=[vmem] * (1 + (add is not None)),
        compiler_params=pltpu.CompilerParams(vmem_limit_bytes=4 * MIB),
        name="merge",
    )(mine, theirs, *given)
    return outs if add is not None else outs[0]


def copy_trimmed(ref, out_ref, size, below):
    part = size // 2
    for core in range(2):
        for n in range(part):
            out_ref[core * part + n] = ref[core * size + n]
    for n in range(size - 2):
        at = n + jnp.where(below, 2, 0)
        out_ref[size + n] = ref[(at // part) * size + part + lax.rem(at, part)]


def trim(blocks, size):
    def kernel(ref, out_ref):
        copy_trimmed(ref, out_ref, size, team_place() < 2)

    vmem = pl.BlockSpec(memory_space=pltpu.VMEM)
    return pl.pallas_call(
        kernel,
        out_shape=jax.ShapeDtypeStruct((2 * size - 2,) + blocks.shape[1:], F32),
        in_specs=[vmem],
        out_specs=vmem,
        compiler_params=pltpu.CompilerParams(vmem_limit_bytes=4 * MIB),
        name="trim",
    )(blocks)


def merge_near(mine, theirs, slot, size, after):
    tile = mine.shape[1:]

    def kernel(mine_ref, theirs_ref, _, out_ref, trimmed_ref):
        core = lax.rem(team_place(), 2)
        for ref, at in ((mine_ref, core), (theirs_ref, 1 - core)):
            for n in range(size):
                out_ref[at * size + n] = ref[slot * size + n]
        copy_trimmed(out_ref, trimmed_ref, size, team_place() >= 2)

    vmem = pl.BlockSpec(memory_space=pltpu.VMEM)
    return pl.pallas_call(
        kernel,
        out_shape=[
            jax.ShapeDtypeStruct((2 * size,) + tile, F32),
            jax.ShapeDtypeStruct((2 * size - 2,) + tile, F32),
        ],
        in_specs=[vmem] * 2 + [pl.BlockSpec(memory_space=pl.ANY)],
        out_specs=[vmem] * 2,
        compiler_params=pltpu.CompilerParams(vmem_limit_bytes=4 * MIB),
        name="merge_near",
    )(mine, theirs, after)


def reciprocal(x):
    guess = pl.reciprocal(x, approx=True)
    return guess * (2.0 - x * guess)


def harmonic(a, b):
    x = a + b
    guess = pl.reciprocal(x, approx=True)
    return guess * (4.0 - (2.0 * x) * guess)


def each(start, stop, body, width):
    whole = (stop - start) // width

    def group(n, carry):
        for k in range(width):
            body(start + n * width + k)
        return carry

    lax.fori_loop(0, whole, group, 0)
    for p in range(start + whole * width, stop):
        body(p)


def solve(near, far, near_halo, far_halo, planes):
    inputs = [near, near_halo, far, far_halo]
    half, columns = far.shape[-2:]
    part = 2 * planes
    halo = 2 * planes
    own = TEAM * planes
    span = own + 2 * halo
    centre, coefficients = chebyshev_constants(DEGREE)
    assert halo >= STEPS

    def kernel(*refs):
        ins, refs = refs[: len(inputs)], refs[len(inputs) :]
        outs, face_ref, refs = refs[:TEAM], refs[TEAM], refs[TEAM + 1 :]
        cond, u_a, u_b, s_a, s_b, zp, zm, yp, ym, xp, xm, t_a, t_b = refs
        place = team_place()
        side = place // 2
        upper, lower = halo + own, 0
        near_base = jnp.where(side == 0, upper, lower)
        far_base = jnp.where(side == 0, lower, upper)
        def outside(v):
            return jnp.where(v > 0.0, v, 1e30)

        for core in range(2):
            for n in range(part):
                base = halo + planes * core + n // 2
                for ref, at in ((ins[0], base + part * side), (ins[2], base + part * (1 - side))):
                    cond[at, n % 2] = outside(ref[core * 2 * part + n])
                    t_a[at, n % 2] = ref[(core * 2 + 1) * part + n]
        for ref, at in ((ins[1], near_base), (ins[3], far_base)):
            skip = jnp.where(at == lower, 1, 0)
            for n in range(2 * part):
                cond[at + n // 2, n % 2] = outside(ref[n])
            for n in range(2 * part - 2):
                t_a[at + skip + n // 2, n % 2] = ref[2 * part + n]

        last_row = lax.broadcasted_iota(jnp.int32, (half, columns), 0) == half - 1
        last_column = lax.broadcasted_iota(jnp.int32, (half, columns), 1) == columns - 1

        def ahead_x(v):
            return pltpu.roll(v, columns - 1, 1)

        def behind_x(v):
            return pltpu.roll(v, 1, 1)

        def ahead_y(v):
            return pltpu.roll(v, half - 1, 0)

        def behind_y(v):
            return pltpu.roll(v, 1, 0)

        def setup(p, w_z_before):
            even, odd = cond[p, 0], cond[p, 1]
            w_pair = harmonic(even, odd)
            w_next = jnp.where(last_row, 0.0, harmonic(odd, ahead_y(even)))
            w_z_here = []
            for t, here in enumerate((even, odd)):
                w_z = harmonic(here, cond[p + 1, t])
                w_z_here.append(w_z)
                w_z_behind = w_z_before[t]
                w_y = w_next if t else w_pair
                w_y_behind = w_pair if t else behind_y(w_next)
                w_x = jnp.where(last_column, 0.0, harmonic(here, ahead_x(here)))
                w_x_behind = behind_x(w_x)
                diagonal = (w_z + w_z_behind) + (w_y + w_y_behind) + (w_x + w_x_behind) + STORAGE
                inverse = reciprocal(diagonal)
                zp[p, t] = w_z * inverse
                zm[p, t] = w_z_behind * inverse
                yp[p, t] = w_y * inverse
                ym[p, t] = w_y_behind * inverse
                xp[p, t] = w_x * inverse
                xm[p, t] = w_x_behind * inverse
                scaled = t_a[p, t] * inverse
                u_a[p, t] = scaled
                s_a[p, t] = scaled * (1.0 / centre)
            return w_z_here

        width = (span - 2) // 3

        def setup_group(n, carry):
            start = 1 + n * width
            w_z = [harmonic(cond[start - 1, t], cond[start, t]) for t in range(2)]
            for k in range(width):
                w_z = setup(start + k, w_z)
            return carry

        assert (span - 2) % width == 0
        lax.fori_loop(0, (span - 2) // width, setup_group, 0)

        s_now, s_next, u_now, u_next, t_now, t_next = s_a, s_b, u_a, u_b, t_a, t_b
        for step in range(STEPS - 1):
            position = step % DEGREE
            if position + 1 < DEGREE:
                keep, mix = coefficients[position]
            else:
                keep, mix = 0.0, 1.0 / centre
            last = step == STEPS - 2

            def advance(p):
                even, odd = s_now[p, 0], s_now[p, 1]
                for t, s in enumerate((even, odd)):
                    ahead = ahead_y(even) if t else odd
                    behind = even if t else behind_y(odd)
                    moved = zp[p, t] * s_now[p + 1, t] + zm[p, t] * s_now[p - 1, t]
                    moved += yp[p, t] * ahead + ym[p, t] * behind
                    moved += xp[p, t] * ahead_x(s) + xm[p, t] * behind_x(s)
                    new_u = (u_now[p, t] - s) + moved
                    new_s = mix * new_u if keep == 0.0 else keep * s + mix * new_u
                    if not last:
                        u_next[p, t] = new_u
                        s_next[p, t] = new_s
                    if step == 0:
                        t_next[p, t] = s + new_s
                    elif step % 2 == 0:
                        t_next[p, t] = t_now[p, t] + (s + new_s)

            margin = halo - (STEPS - 2 - step)
            each(margin, span - margin, advance, 8)
            s_now, s_next, u_now, u_next = s_next, s_now, u_next, u_now
            if step % 2 == 0:
                t_now, t_next = t_next, t_now

        for m in range(TEAM):
            base = halo + planes * (place ^ m)
            for j in range(planes):
                for t in range(2):
                    outs[m][2 * j + t] = t_now[base + j, t]
        for p in range(own):
            face_ref[p : p + 1, :] = t_now[halo + p, 0, 0:1, :]

    vmem = pl.BlockSpec(memory_space=pltpu.VMEM)
    field = pltpu.VMEM((span, 2, half, columns), F32)
    return pl.pallas_call(
        kernel,
        out_shape=[jax.ShapeDtypeStruct((2 * planes, half, columns), F32)] * TEAM
        + [jax.ShapeDtypeStruct((own, columns), F32)],
        in_specs=[vmem] * len(inputs),
        out_specs=[vmem] * (TEAM + 1),
        scratch_shapes=[field] * 13,
        compiler_params=pltpu.CompilerParams(vmem_limit_bytes=16 * MIB),
        cost_estimate=pl.CostEstimate(flops=0, bytes_accessed=22 * MIB, transcendentals=0),
        name="solve",
    )(*inputs)


def weigh(sums, faces, cells, after):
    slots = len(faces)
    samples, columns = sums[0].shape

    def kernel(*refs):
        sum_refs, refs = refs[: len(sums)], refs[len(sums) :]
        face_refs, (out_ref, moments_ref, weights) = refs[:slots], refs[slots + len(after) :]
        place = team_place()
        summed = sum_refs[0][...]
        for ref in sum_refs[1:]:
            summed = summed + ref[...]
        misfit = summed * (1.0 / (2.0 * cells))
        mean = jnp.sum(misfit, axis=0, keepdims=True) * (1.0 / samples)
        deviation = misfit - mean
        variance = jnp.sum(deviation * deviation, axis=0, keepdims=True) * (1.0 / samples)
        lane = lax.broadcasted_iota(jnp.int32, (1, columns), 1)
        moments_ref[...] = jnp.where(lane == 0, mean, variance)
        weights[...] = 1.0 + 2.0 * BETA_RISK * deviation
        total = weights[pl.ds(slots * place, 1), :] * face_refs[0][...]
        for n in range(1, slots):
            total = total + weights[pl.ds(slots * place + n, 1), :] * face_refs[n][...]
        out_ref[...] = total

    vmem = pl.BlockSpec(memory_space=pltpu.VMEM)
    return pl.pallas_call(
        kernel,
        out_shape=[
            jax.ShapeDtypeStruct(faces[0].shape, F32),
            jax.ShapeDtypeStruct((1, columns), F32),
        ],
        in_specs=[vmem] * (len(sums) + slots)
        + [pl.BlockSpec(memory_space=pl.ANY)] * len(after),
        out_specs=[vmem, vmem],
        scratch_shapes=[pltpu.VMEM((samples, columns), F32)],
        compiler_params=pltpu.CompilerParams(vmem_limit_bytes=2 * MIB),
        name="weigh",
    )(*sums, *faces, *after)


def gather_adjoint(pieces, planes):
    slots = len(pieces)
    _, half, columns = pieces[0][0].shape
    tiles = columns // 128
    block = (planes, 2 * half, columns)

    def kernel(*refs):
        blocks, out, mark, held, mixed, sems = refs[: slots * TEAM], *refs[slots * TEAM :]
        mark[...] = blocks[0][0, :, :LANES]
        place = team_place()
        copies = []
        for slot in range(slots):
            for m in range(TEAM):
                i = slot * TEAM + m
                for j in range(planes):
                    for t in range(2):
                        for c in range(tiles):
                            mixed[i % 2, j, c, pl.ds(t, half, stride=2), :] = blocks[i][
                                2 * j + t, :, c * 128 : (c + 1) * 128
                            ]
                    for c in range(tiles):
                        held[i, j, :, c * 128 : (c + 1) * 128] = mixed[i % 2, j, c]
                copy = pltpu.make_async_copy(
                    held.at[i], out.at[slots * (place ^ m) + slot], sems.at[i]
                )
                copy.start()
                copies.append(copy)
        for copy in copies:
            copy.wait()

    return pl.pallas_call(
        kernel,
        out_shape=[
            jax.ShapeDtypeStruct((slots * TEAM,) + block, F32),
            jax.ShapeDtypeStruct((half, LANES), F32),
        ],
        in_specs=[pl.BlockSpec(memory_space=pltpu.VMEM)] * (slots * TEAM),
        out_specs=[
            pl.BlockSpec(memory_space=pltpu.HBM),
            pl.BlockSpec(memory_space=pltpu.VMEM),
        ],
        scratch_shapes=[
            pltpu.VMEM((slots * TEAM,) + block, F32),
            pltpu.VMEM((2, planes, tiles, 2 * half, 128), F32),
            pltpu.SemaphoreType.DMA((slots * TEAM,)),
        ],
        compiler_params=pltpu.CompilerParams(vmem_limit_bytes=4 * MIB),
        cost_estimate=pl.CostEstimate(flops=0, bytes_accessed=4 * MIB, transcendentals=0),
        name="gather_adjoint",
    )(*[piece for group in pieces for piece in group])


def control(faces, radices, basis_z, basis_x, after):
    slabs, own_count, depth_total = basis_z.shape
    own, columns = faces[0].shape[1:]
    teams = depth_total // own

    def kernel(*refs):
        parts, (z_ref, x_ref, _, out_ref, whole) = refs[: len(faces)], refs[len(faces) :]
        rank = lax.axis_index("gz")
        team = rank // TEAM
        for n in range(teams):
            at, left, stride = 0, n, 1
            for radix in radices:
                digit = lax.rem(team // stride + left % radix, radix)
                at, left, stride = at + digit * stride, left // radix, stride * radix
            inner = teams // len(faces)
            whole[at] = parts[n // inner][n % inner]
        along_z = jnp.dot(
            z_ref[rank],
            whole[...].reshape(depth_total, columns),
            precision=lax.Precision.HIGHEST,
            preferred_element_type=F32,
        )
        high, low = in_halves(along_z)
        x_high, x_low = in_halves(x_ref[...])
        both = jnp.concatenate([high, low], axis=0)
        first = jnp.dot(both, x_high, preferred_element_type=F32)
        second = jnp.dot(high, x_low, preferred_element_type=F32)
        out_ref[...] = (first[:own_count] + first[own_count:]) + second

    vmem = pl.BlockSpec(memory_space=pltpu.VMEM)
    return pl.pallas_call(
        kernel,
        out_shape=jax.ShapeDtypeStruct((own_count, basis_x.shape[1]), F32),
        in_specs=[vmem] * (len(faces) + 2) + [pl.BlockSpec(memory_space=pl.ANY)],
        out_specs=vmem,
        scratch_shapes=[pltpu.VMEM((teams, own, columns), F32)],
        compiler_params=pltpu.CompilerParams(vmem_limit_bytes=8 * MIB),
        name="control",
    )(*faces, basis_z, basis_x, after)


def radices_of(teams):
    radices = []
    while teams > 1:
        radix = next(r for r in (4, 2, 3, *range(5, teams + 1)) if teams % r == 0)
        radices.append(radix)
        teams //= radix
    return radices


def on_device(state, target, rock_type, log_table, obs_scale):
    samples, planes, rows_y, columns = state.shape
    slabs = lax.axis_size("gz")
    slots = samples // TEAM
    depth_total = planes * slabs
    radices = radices_of(slabs // TEAM)

    def swap(value, m):
        return lax.ppermute(value, "gz", [(i, i ^ m) for i in range(slabs)])

    def along(value, outward):
        pairs = []
        for i in range(slabs):
            side = (i % TEAM) // 2
            to = i + TEAM if (side == 1) == outward else i - TEAM
            if 0 <= to < slabs:
                pairs.append((i, to))
        return lax.ppermute(value, "gz", pairs)

    def from_teams(value, stride, radix):
        heard = []
        for k in range(1, radix):
            pairs = []
            for i in range(slabs):
                digit = i // (TEAM * stride) % radix
                pairs.append((i + ((digit + k) % radix - digit) * stride * TEAM, i))
            heard.append(lax.ppermute(value, "gz", pairs))
        return heard

    fields = [
        pltpu.with_memory_space_constraint(field, pltpu.HBM)
        for field in (state, target, rock_type, log_table, obs_scale)
    ]
    size = 4 * planes
    jobs = [[(slot, m) for slot in range(slots)] for m in range(TEAM)]
    mine, theirs, sums = prepare(jobs[2:], fields, with_sums=True)
    theirs = swap(theirs, 1)
    first, sums = merge(mine, theirs, 0, size, add=sums)
    far = [swap(first, 2)]
    stride, teams = 1, slabs // TEAM
    while stride < teams:
        radix = next(r for r in range(2, teams + 1) if teams // stride % r == 0)
        sums = sum(from_teams(sums, stride, radix), sums)
        stride *= radix

    mine_near, theirs_near = prepare(jobs[:2], fields)
    theirs_near = swap(theirs_near, 1)
    near, near_halo = [], []
    for slot in range(slots):
        blocks, trimmed = merge_near(mine_near, theirs_near, slot, size, sums)
        near.append(blocks)
        near_halo.append(along(trimmed, True))
    for slot in range(1, slots):
        far.append(swap(merge(mine, theirs, slot, size, sums), 2))
    sums = [sums, far[-1][2 * size]]

    pieces, faces = [], []
    for slot in range(slots):
        far_halo = along(trim(far[slot], size), False)
        solved = solve(near[slot], far[slot], near_halo[slot], far_halo, planes)
        pieces.append([solved[0]] + [swap(solved[m], m) for m in (1, 2, 3)])
        faces.append(solved[TEAM])

    face, moments = weigh(sums, faces, depth_total * rows_y * columns, pieces[0][1:])
    heard = [sum((swap(face, m) for m in (2, 3, 1)), face)[None]]
    stride = 1
    for radix in radices:
        held = heard[0] if len(heard) == 1 else jnp.concatenate(heard)
        heard = [held] + from_teams(held, stride, radix)
        stride *= radix
    adjoint, mark = gather_adjoint(pieces, planes)
    own_count = MA // slabs
    gradient = control(
        heard,
        radices,
        jnp.asarray(cosine_basis(depth_total, MA).T.reshape(slabs, own_count, depth_total)),
        jnp.asarray(cosine_basis(columns, MB)),
        mark,
    )
    return (adjoint, gradient, moments[0, :2])


def solution(mesh):
    return jax.shard_map(
        on_device,
        mesh=mesh,
        in_specs=(
            P("parts", "gz", None, None),
            P(("parts", "gz"), None, None),
            P("parts", "gz", None, None),
            P("parts", None),
            P("parts"),
        ),
        out_specs=(P("parts", "gz", None, None), P(("parts", "gz"), None), P("parts")),
        check_vma=False,
    )
```

```python
import math

import jax
import jax.numpy as jnp
import numpy as np
from jax import lax
from jax.experimental import pallas as pl
from jax.experimental.pallas import tpu as pltpu
from jax.sharding import PartitionSpec as P

NR = 8
DEGREE = 4
SWEEPS = 2
MA = 512
MB = 512

STORAGE = 0.05
BETA_RISK = 0.5
LOWER_EIGEN = 0.05
UPPER_EIGEN = 2.0

TEAM = 4
STEPS = DEGREE * SWEEPS
F32 = jnp.float32
MIB = 1024 * 1024
LANES = 128


def chebyshev_constants(number_steps):
    centre = (UPPER_EIGEN + LOWER_EIGEN) / 2
    spread = (UPPER_EIGEN - LOWER_EIGEN) / 2
    quotient = centre / spread
    rho_now = 1.0 / quotient
    coefficients = []
    for position in range(number_steps):
        rho_next = 1.0 / (2.0 * quotient - rho_now)
        coefficients.append((rho_next * rho_now, 2.0 * rho_next / spread))
        rho_now = rho_next
    return (centre, coefficients)


def cosine_basis(length_total, modes):
    positions = np.arange(length_total, dtype=np.int64)
    mode_index = np.arange(modes, dtype=np.int64)
    product_index = ((2 * positions[:, None] + 1) * (2 * mode_index[None, :] + 1)) % (
        8 * length_total
    )
    angle = product_index.astype(np.float64) * (math.pi / (4 * length_total))
    return (math.sqrt(2.0 / length_total) * np.cos(angle)).astype(np.float32)


def in_halves(values):
    high = values.astype(jnp.bfloat16)
    return high, (values - high.astype(F32)).astype(jnp.bfloat16)


def team_place():
    return lax.rem(lax.axis_index("gz"), TEAM)


def prepare(jobs, fields, with_sums=False):
    state, target, rock_type, log_table, obs_scale = fields
    samples, planes, rows_y, columns = state.shape
    slots = samples // TEAM
    block = (planes, rows_y, columns)
    half, tiles = rows_y // 2, columns // 128
    size = 2 * 2 * planes
    depth_total = planes * lax.axis_size("gz")
    flat = [(o, i, job) for o, group in enumerate(jobs) for i, job in enumerate(group)]
    count = len(flat)
    shapes = [(len(group) * size + with_sums, half, columns) for group in jobs]
    states = samples if with_sums else count

    def kernel(*refs):
        (table_ref, scale_ref, state_ref, target_ref, rock_ref), refs = refs[:5], refs[5:]
        outs, refs = refs[: len(jobs)], refs[len(jobs) :]
        if with_sums:
            sums_ref, refs = refs[0], refs[1:]
        table, scale, state_buf, rock_buf, target_buf, mixed, sems = refs
        place = team_place()
        first_plane = lax.axis_index("gz") * planes
        members = [slots * (place ^ m) + slot for _, _, (slot, m) in flat]
        small = [
            pltpu.make_async_copy(table_ref, table, sems.at[2, 0]),
            pltpu.make_async_copy(scale_ref, scale, sems.at[2, 1]),
            pltpu.make_async_copy(target_ref, target_buf, sems.at[2, 2]),
        ]
        for copy in small:
            copy.start()
        rocks = [
            pltpu.make_async_copy(rock_ref.at[member], rock_buf.at[n], sems.at[1, n])
            for n, member in enumerate(members)
        ]
        loads = [
            pltpu.make_async_copy(
                state_ref.at[n if with_sums else members[n]], state_buf.at[n], sems.at[0, n]
            )
            for n in range(states)
        ]
        for copy in rocks + loads:
            copy.start()
        depth_weights = [
            1.0 + (2.0 / (depth_total - 1)) * (first_plane + p).astype(F32) for p in range(planes)
        ]
        for copy in small:
            copy.wait()
        if with_sums:
            for copy in loads:
                copy.wait()
            for n in range(samples):
                total = jnp.zeros((8, columns), F32)
                for p in range(planes):
                    part = jnp.zeros((8, columns), F32)
                    for first in range(0, rows_y, 8):
                        rows = slice(first, first + 8)
                        gap = state_buf[n, p, rows] - target_buf[p, rows]
                        part = part + gap * gap
                    total = total + (scale[n] * depth_weights[p]) * part
                summed = jnp.sum(total, keepdims=True)
                sums_ref[n : n + 1, :] = jnp.broadcast_to(summed, (1, columns))
        for n, (o, i, _) in enumerate(flat):
            rocks[n].wait()
            if not with_sums:
                loads[n].wait()
            member = members[n]
            own_state = member if with_sums else n
            values = [
                jnp.exp(jnp.full((8, columns), -table[member, code], F32)) for code in range(NR)
            ]
            for p in range(planes):
                factor = scale[member] * depth_weights[p]
                for first in range(0, rows_y, 8):
                    rows = slice(first, first + 8)
                    codes = rock_buf[n, p, rows]
                    low, mid, high = ((codes & bit) != 0 for bit in (1, 2, 4))
                    pairs = [
                        jnp.where(low, values[2 * k + 1], values[2 * k]) for k in range(NR // 2)
                    ]
                    halves = [jnp.where(mid, pairs[2 * k + 1], pairs[2 * k]) for k in range(2)]
                    gap = state_buf[own_state, p, rows] - target_buf[p, rows]
                    made = (jnp.where(high, halves[1], halves[0]), factor * gap)
                    for a in range(2):
                        for c in range(tiles):
                            mixed[n % 2, p, a, c, rows] = made[a][:, c * 128 : (c + 1) * 128]
                for a in range(2):
                    for t in range(2):
                        for c in range(tiles):
                            at = i * size + (a * planes + p) * 2 + t
                            outs[o][at, :, c * 128 : (c + 1) * 128] = mixed[
                                n % 2, p, a, c, pl.ds(t, half, stride=2), :
                            ]
        for o, group in enumerate(jobs if with_sums else []):
            outs[o][len(group) * size] = sums_ref[...]

    hbm = pl.BlockSpec(memory_space=pltpu.HBM)
    vmem = pl.BlockSpec(memory_space=pltpu.VMEM)
    return pl.pallas_call(
        kernel,
        out_shape=[jax.ShapeDtypeStruct(shape, F32) for shape in shapes]
        + [jax.ShapeDtypeStruct((samples, columns), F32)] * with_sums,
        in_specs=[hbm] * 5,
        out_specs=[vmem] * (len(shapes) + with_sums),
        scratch_shapes=[
            pltpu.SMEM(log_table.shape, F32),
            pltpu.SMEM(obs_scale.shape, F32),
            pltpu.VMEM((states,) + block, F32),
            pltpu.VMEM((count,) + block, jnp.int32),
            pltpu.VMEM(block, F32),
            pltpu.VMEM((2, planes, 2, tiles, rows_y, 128), F32),
            pltpu.SemaphoreType.DMA((3, max(states, 3))),
        ],
        compiler_params=pltpu.CompilerParams(vmem_limit_bytes=6 * MIB),
        cost_estimate=pl.CostEstimate(flops=0, bytes_accessed=count * MIB, transcendentals=0),
        name="prepare",
    )(log_table, obs_scale, state, target, rock_type)


def merge(mine, theirs, slot, size, behind=None, add=None, spare=0):
    given = [value for value in (behind, add) if value is not None]

    def kernel(mine_ref, theirs_ref, *refs):
        core = lax.rem(team_place(), 2)
        tail, (out_ref, *more) = refs[: len(given)], refs[len(given) :]
        for ref, at in ((mine_ref, core), (theirs_ref, 1 - core)):
            for n in range(size):
                out_ref[at * size + n] = ref[slot * size + n]
        if behind is not None:
            out_ref[2 * size] = tail[0][...]
        for n in range(spare):
            out_ref[2 * size + n] = mine_ref[slot * size]
        if add is not None:
            more[0][...] = tail[-1][...] + theirs_ref[theirs.shape[0] - 1]

    vmem = pl.BlockSpec(memory_space=pltpu.VMEM)
    tile = mine.shape[1:]
    outs = pl.pallas_call(
        kernel,
        out_shape=[jax.ShapeDtypeStruct((2 * size + (behind is not None) + spare,) + tile, F32)]
        + [jax.ShapeDtypeStruct(tile, F32)] * (add is not None),
        in_specs=[vmem] * (2 + len(given)),
        out_specs=[vmem] * (1 + (add is not None)),
        compiler_params=pltpu.CompilerParams(vmem_limit_bytes=4 * MIB),
        name="merge",
    )(mine, theirs, *given)
    return outs if add is not None else outs[0]


def copy_trimmed(ref, out_ref, size, below):
    part = size // 2
    for core in range(2):
        for n in range(part):
            out_ref[core * part + n] = ref[core * size + n]
    for n in range(size - 2):
        at = n + jnp.where(below, 2, 0)
        out_ref[size + n] = ref[(at // part) * size + part + lax.rem(at, part)]


def trim(blocks, size):
    def kernel(ref, out_ref):
        copy_trimmed(ref, out_ref, size, team_place() < 2)

    vmem = pl.BlockSpec(memory_space=pltpu.VMEM)
    return pl.pallas_call(
        kernel,
        out_shape=jax.ShapeDtypeStruct((2 * size - 2,) + blocks.shape[1:], F32),
        in_specs=[vmem],
        out_specs=vmem,
        compiler_params=pltpu.CompilerParams(vmem_limit_bytes=4 * MIB),
        name="trim",
    )(blocks)


def merge_near(mine, theirs, slot, size, after):
    tile = mine.shape[1:]

    def kernel(mine_ref, theirs_ref, _, out_ref, trimmed_ref):
        core = lax.rem(team_place(), 2)
        for ref, at in ((mine_ref, core), (theirs_ref, 1 - core)):
            for n in range(size):
                out_ref[at * size + n] = ref[slot * size + n]
        copy_trimmed(out_ref, trimmed_ref, size, team_place() >= 2)

    vmem = pl.BlockSpec(memory_space=pltpu.VMEM)
    return pl.pallas_call(
        kernel,
        out_shape=[
            jax.ShapeDtypeStruct((2 * size,) + tile, F32),
            jax.ShapeDtypeStruct((2 * size - 2,) + tile, F32),
        ],
        in_specs=[vmem] * 2 + [pl.BlockSpec(memory_space=pl.ANY)],
        out_specs=[vmem] * 2,
        compiler_params=pltpu.CompilerParams(vmem_limit_bytes=4 * MIB),
        name="merge_near",
    )(mine, theirs, after)


def reciprocal(x):
    guess = pl.reciprocal(x, approx=True)
    return guess * (2.0 - x * guess)


def harmonic(a, b):
    x = a + b
    guess = pl.reciprocal(x, approx=True)
    return guess * (4.0 - (2.0 * x) * guess)


def each(start, stop, body, width, field):
    whole = (stop - start) // width

    def planes(first, count):
        window = [[field[first + n, t] for t in range(2)] for n in (-1, 0)]
        for k in range(count):
            window.append([field[first + k + 1, t] for t in range(2)])
            body(first + k, window)
            window.pop(0)

    def group(n, carry):
        planes(start + n * width, width)
        return carry

    lax.fori_loop(0, whole, group, 0)
    planes(start + whole * width, stop - start - whole * width)


def solve(near, far, near_halo, far_halo, planes):
    inputs = [near, near_halo, far, far_halo]
    half, columns = far.shape[-2:]
    part = 2 * planes
    halo = 2 * planes
    own = TEAM * planes
    span = own + 2 * halo
    centre, coefficients = chebyshev_constants(DEGREE)
    assert halo >= STEPS

    def kernel(*refs):
        ins, refs = refs[: len(inputs)], refs[len(inputs) :]
        outs, face_ref, refs = refs[:TEAM], refs[TEAM], refs[TEAM + 1 :]
        cond, u_a, u_b, s_a, s_b, zp, zm, yp, ym, xp, xm, t_a, t_b = refs
        place = team_place()
        side = place // 2
        upper, lower = halo + own, 0
        near_base = jnp.where(side == 0, upper, lower)
        far_base = jnp.where(side == 0, lower, upper)
        def outside(v):
            return jnp.where(v > 0.0, v, 1e30)

        for core in range(2):
            for n in range(part):
                base = halo + planes * core + n // 2
                for ref, at in ((ins[0], base + part * side), (ins[2], base + part * (1 - side))):
                    cond[at, n % 2] = outside(ref[core * 2 * part + n])
                    t_a[at, n % 2] = ref[(core * 2 + 1) * part + n]
        for ref, at in ((ins[1], near_base), (ins[3], far_base)):
            skip = jnp.where(at == lower, 1, 0)
            for n in range(2 * part):
                cond[at + n // 2, n % 2] = outside(ref[n])
            for n in range(2 * part - 2):
                t_a[at + skip + n // 2, n % 2] = ref[2 * part + n]

        last_row = lax.broadcasted_iota(jnp.int32, (half, columns), 0) == half - 1
        last_column = lax.broadcasted_iota(jnp.int32, (half, columns), 1) == columns - 1

        def ahead_x(v):
            return pltpu.roll(v, columns - 1, 1)

        def behind_x(v):
            return pltpu.roll(v, 1, 1)

        def ahead_y(v):
            return pltpu.roll(v, half - 1, 0)

        def behind_y(v):
            return pltpu.roll(v, 1, 0)

        def setup(p, w_z_before, window):
            even, odd = window[0]
            w_pair = harmonic(even, odd)
            w_next = jnp.where(last_row, 0.0, harmonic(odd, ahead_y(even)))
            w_z_here = []
            for t, here in enumerate((even, odd)):
                w_z = harmonic(here, window[1][t])
                w_z_here.append(w_z)
                w_z_behind = w_z_before[t]
                w_y = w_next if t else w_pair
                w_y_behind = w_pair if t else behind_y(w_next)
                w_x = jnp.where(last_column, 0.0, harmonic(here, ahead_x(here)))
                w_x_behind = behind_x(w_x)
                diagonal = (w_z + w_z_behind) + (w_y + w_y_behind) + (w_x + w_x_behind) + STORAGE
                inverse = reciprocal(diagonal)
                zp[p, t] = w_z * inverse
                zm[p, t] = w_z_behind * inverse
                yp[p, t] = w_y * inverse
                ym[p, t] = w_y_behind * inverse
                xp[p, t] = w_x * inverse
                xm[p, t] = w_x_behind * inverse
                scaled = t_a[p, t] * inverse
                u_a[p, t] = scaled
                s_a[p, t] = scaled * (1.0 / centre)
            return w_z_here

        width = (span - 2) // 3

        def setup_group(n, carry):
            start = 1 + n * width
            here = [cond[start, t] for t in range(2)]
            w_z = [harmonic(cond[start - 1, t], here[t]) for t in range(2)]
            for k in range(width):
                above = [cond[start + k + 1, t] for t in range(2)]
                w_z = setup(start + k, w_z, (here, above))
                here = above
            return carry

        assert (span - 2) % width == 0
        lax.fori_loop(0, (span - 2) // width, setup_group, 0)

        s_now, s_next, u_now, u_next, t_now, t_next = s_a, s_b, u_a, u_b, t_a, t_b
        for step in range(STEPS - 1):
            position = step % DEGREE
            if position + 1 < DEGREE:
                keep, mix = coefficients[position]
            else:
                keep, mix = 0.0, 1.0 / centre
            last = step == STEPS - 2

            def advance(p, window):
                below, (even, odd), above = window
                for t, s in enumerate((even, odd)):
                    ahead = ahead_y(even) if t else odd
                    behind = even if t else behind_y(odd)
                    moved = zp[p, t] * above[t] + zm[p, t] * below[t]
                    moved += yp[p, t] * ahead + ym[p, t] * behind
                    moved += xp[p, t] * ahead_x(s) + xm[p, t] * behind_x(s)
                    new_u = (u_now[p, t] - s) + moved
                    new_s = mix * new_u if keep == 0.0 else keep * s + mix * new_u
                    if not last:
                        u_next[p, t] = new_u
                        s_next[p, t] = new_s
                    if step == 0:
                        t_next[p, t] = s + new_s
                    elif step % 2 == 0:
                        t_next[p, t] = t_now[p, t] + (s + new_s)

            margin = halo - (STEPS - 2 - step)
            each(margin, span - margin, advance, 8, s_now)
            s_now, s_next, u_now, u_next = s_next, s_now, u_next, u_now
            if step % 2 == 0:
                t_now, t_next = t_next, t_now

        for m in range(TEAM):
            base = halo + planes * (place ^ m)
            for j in range(planes):
                for t in range(2):
                    outs[m][2 * j + t] = t_now[base + j, t]
        for p in range(own):
            face_ref[p : p + 1, :] = t_now[halo + p, 0, 0:1, :]

    vmem = pl.BlockSpec(memory_space=pltpu.VMEM)
    field = pltpu.VMEM((span, 2, half, columns), F32)
    return pl.pallas_call(
        kernel,
        out_shape=[jax.ShapeDtypeStruct((2 * planes, half, columns), F32)] * TEAM
        + [jax.ShapeDtypeStruct((own, columns), F32)],
        in_specs=[vmem] * len(inputs),
        out_specs=[vmem] * (TEAM + 1),
        scratch_shapes=[field] * 13,
        compiler_params=pltpu.CompilerParams(vmem_limit_bytes=16 * MIB),
        cost_estimate=pl.CostEstimate(flops=0, bytes_accessed=22 * MIB, transcendentals=0),
        name="solve",
    )(*inputs)


def weigh(sums, faces, cells, after):
    slots = len(faces)
    samples, columns = sums[0].shape

    def kernel(*refs):
        sum_refs, refs = refs[: len(sums)], refs[len(sums) :]
        face_refs, (out_ref, moments_ref, weights) = refs[:slots], refs[slots + len(after) :]
        place = team_place()
        summed = sum_refs[0][...]
        for ref in sum_refs[1:]:
            summed = summed + ref[...]
        misfit = summed * (1.0 / (2.0 * cells))
        mean = jnp.sum(misfit, axis=0, keepdims=True) * (1.0 / samples)
        deviation = misfit - mean
        variance = jnp.sum(deviation * deviation, axis=0, keepdims=True) * (1.0 / samples)
        lane = lax.broadcasted_iota(jnp.int32, (1, columns), 1)
        moments_ref[...] = jnp.where(lane == 0, mean, variance)
        weights[...] = 1.0 + 2.0 * BETA_RISK * deviation
        total = weights[pl.ds(slots * place, 1), :] * face_refs[0][...]
        for n in range(1, slots):
            total = total + weights[pl.ds(slots * place + n, 1), :] * face_refs[n][...]
        out_ref[...] = total

    vmem = pl.BlockSpec(memory_space=pltpu.VMEM)
    return pl.pallas_call(
        kernel,
        out_shape=[
            jax.ShapeDtypeStruct(faces[0].shape, F32),
            jax.ShapeDtypeStruct((1, columns), F32),
        ],
        in_specs=[vmem] * (len(sums) + slots)
        + [pl.BlockSpec(memory_space=pl.ANY)] * len(after),
        out_specs=[vmem, vmem],
        scratch_shapes=[pltpu.VMEM((samples, columns), F32)],
        compiler_params=pltpu.CompilerParams(vmem_limit_bytes=2 * MIB),
        name="weigh",
    )(*sums, *faces, *after)


def gather_adjoint(pieces, planes):
    slots = len(pieces)
    _, half, columns = pieces[0][0].shape
    tiles = columns // 128
    block = (planes, 2 * half, columns)

    def kernel(*refs):
        blocks, out, mark, held, mixed, sems = refs[: slots * TEAM], *refs[slots * TEAM :]
        mark[...] = blocks[0][0, :, :LANES]
        place = team_place()
        copies = []
        for slot in range(slots):
            for m in range(TEAM):
                i = slot * TEAM + m
                for j in range(planes):
                    for t in range(2):
                        for c in range(tiles):
                            mixed[i % 2, j, c, pl.ds(t, half, stride=2), :] = blocks[i][
                                2 * j + t, :, c * 128 : (c + 1) * 128
                            ]
                    for c in range(tiles):
                        held[i, j, :, c * 128 : (c + 1) * 128] = mixed[i % 2, j, c]
                copy = pltpu.make_async_copy(
                    held.at[i], out.at[slots * (place ^ m) + slot], sems.at[i]
                )
                copy.start()
                copies.append(copy)
        for copy in copies:
            copy.wait()

    return pl.pallas_call(
        kernel,
        out_shape=[
            jax.ShapeDtypeStruct((slots * TEAM,) + block, F32),
            jax.ShapeDtypeStruct((half, LANES), F32),
        ],
        in_specs=[pl.BlockSpec(memory_space=pltpu.VMEM)] * (slots * TEAM),
        out_specs=[
            pl.BlockSpec(memory_space=pltpu.HBM),
            pl.BlockSpec(memory_space=pltpu.VMEM),
        ],
        scratch_shapes=[
            pltpu.VMEM((slots * TEAM,) + block, F32),
            pltpu.VMEM((2, planes, tiles, 2 * half, 128), F32),
            pltpu.SemaphoreType.DMA((slots * TEAM,)),
        ],
        compiler_params=pltpu.CompilerParams(vmem_limit_bytes=4 * MIB),
        cost_estimate=pl.CostEstimate(flops=0, bytes_accessed=4 * MIB, transcendentals=0),
        name="gather_adjoint",
    )(*[piece for group in pieces for piece in group])


def control(faces, radices, basis_z, basis_x, after):
    slabs, own_count, depth_total = basis_z.shape
    own, columns = faces[0].shape[1:]
    teams = depth_total // own

    def kernel(*refs):
        parts, (z_ref, x_ref, _, out_ref, whole) = refs[: len(faces)], refs[len(faces) :]
        rank = lax.axis_index("gz")
        team = rank // TEAM
        for n in range(teams):
            at, left, stride = 0, n, 1
            for radix in radices:
                digit = lax.rem(team // stride + left % radix, radix)
                at, left, stride = at + digit * stride, left // radix, stride * radix
            inner = teams // len(faces)
            whole[at] = parts[n // inner][n % inner]
        along_z = jnp.dot(
            z_ref[rank],
            whole[...].reshape(depth_total, columns),
            precision=lax.Precision.HIGHEST,
            preferred_element_type=F32,
        )
        high, low = in_halves(along_z)
        x_high, x_low = in_halves(x_ref[...])
        both = jnp.concatenate([high, low], axis=0)
        first = jnp.dot(both, x_high, preferred_element_type=F32)
        second = jnp.dot(high, x_low, preferred_element_type=F32)
        out_ref[...] = (first[:own_count] + first[own_count:]) + second

    vmem = pl.BlockSpec(memory_space=pltpu.VMEM)
    return pl.pallas_call(
        kernel,
        out_shape=jax.ShapeDtypeStruct((own_count, basis_x.shape[1]), F32),
        in_specs=[vmem] * (len(faces) + 2) + [pl.BlockSpec(memory_space=pl.ANY)],
        out_specs=vmem,
        scratch_shapes=[pltpu.VMEM((teams, own, columns), F32)],
        compiler_params=pltpu.CompilerParams(vmem_limit_bytes=8 * MIB),
        name="control",
    )(*faces, basis_z, basis_x, after)


def radices_of(teams):
    radices = []
    while teams > 1:
        radix = next(r for r in (4, 2, 3, *range(5, teams + 1)) if teams % r == 0)
        radices.append(radix)
        teams //= radix
    return radices


def on_device(state, target, rock_type, log_table, obs_scale):
    samples, planes, rows_y, columns = state.shape
    slabs = lax.axis_size("gz")
    slots = samples // TEAM
    depth_total = planes * slabs
    radices = radices_of(slabs // TEAM)

    def swap(value, m):
        return lax.ppermute(value, "gz", [(i, i ^ m) for i in range(slabs)])

    def along(value, outward):
        pairs = []
        for i in range(slabs):
            side = (i % TEAM) // 2
            to = i + TEAM if (side == 1) == outward else i - TEAM
            if 0 <= to < slabs:
                pairs.append((i, to))
        return lax.ppermute(value, "gz", pairs)

    def from_teams(value, stride, radix):
        heard = []
        for k in range(1, radix):
            pairs = []
            for i in range(slabs):
                digit = i // (TEAM * stride) % radix
                pairs.append((i + ((digit + k) % radix - digit) * stride * TEAM, i))
            heard.append(lax.ppermute(value, "gz", pairs))
        return heard

    fields = [
        pltpu.with_memory_space_constraint(field, pltpu.HBM)
        for field in (state, target, rock_type, log_table, obs_scale)
    ]
    size = 4 * planes
    jobs = [[(slot, m) for slot in range(slots)] for m in range(TEAM)]
    mine, theirs, sums = prepare(jobs[2:], fields, with_sums=True)
    theirs = swap(theirs, 1)
    first, sums = merge(mine, theirs, 0, size, add=sums, spare=1)
    far = [swap(first, 2)]
    stride, teams = 1, slabs // TEAM
    while stride < teams:
        radix = next(r for r in range(2, teams + 1) if teams // stride % r == 0)
        sums = sum(from_teams(sums, stride, radix), sums)
        stride *= radix

    mine_near, theirs_near = prepare(jobs[:2], fields)
    theirs_near = swap(theirs_near, 1)
    near, near_halo = [], []
    for slot in range(slots):
        blocks, trimmed = merge_near(mine_near, theirs_near, slot, size, sums)
        near.append(blocks)
        near_halo.append(along(trimmed, True))
    for slot in range(1, slots):
        far.append(swap(merge(mine, theirs, slot, size, sums), 2))
    sums = [sums, far[-1][2 * size]]

    pieces, faces = [], []
    for slot in range(slots):
        far_halo = along(trim(far[slot], size), False)
        solved = solve(near[slot], far[slot], near_halo[slot], far_halo, planes)
        pieces.append([solved[0]] + [swap(solved[m], m) for m in (1, 2, 3)])
        faces.append(solved[TEAM])

    face, moments = weigh(sums, faces, depth_total * rows_y * columns, pieces[0][1:])
    heard = [sum((swap(face, m) for m in (2, 3, 1)), face)[None]]
    stride = 1
    for radix in radices:
        held = heard[0] if len(heard) == 1 else jnp.concatenate(heard)
        heard = [held] + from_teams(held, stride, radix)
        stride *= radix
    adjoint, mark = gather_adjoint(pieces, planes)
    own_count = MA // slabs
    gradient = control(
        heard,
        radices,
        jnp.asarray(cosine_basis(depth_total, MA).T.reshape(slabs, own_count, depth_total)),
        jnp.asarray(cosine_basis(columns, MB)),
        mark,
    )
    return (adjoint, gradient, moments[0, :2])


def solution(mesh):
    return jax.shard_map(
        on_device,
        mesh=mesh,
        in_specs=(
            P("parts", "gz", None, None),
            P(("parts", "gz"), None, None),
            P("parts", "gz", None, None),
            P("parts", None),
            P("parts"),
        ),
        out_specs=(P("parts", "gz", None, None), P(("parts", "gz"), None), P("parts")),
        check_vma=False,
    )
```

```python
import math

import jax
import jax.numpy as jnp
import numpy as np
from jax import lax
from jax.experimental import pallas as pl
from jax.experimental.pallas import tpu as pltpu
from jax.sharding import PartitionSpec as P

NR = 8
DEGREE = 4
SWEEPS = 2
MA = 512
MB = 512

STORAGE = 0.05
BETA_RISK = 0.5
LOWER_EIGEN = 0.05
UPPER_EIGEN = 2.0

TEAM = 4
STEPS = DEGREE * SWEEPS
F32 = jnp.float32
MIB = 1024 * 1024
LANES = 128


def chebyshev_constants(number_steps):
    centre = (UPPER_EIGEN + LOWER_EIGEN) / 2
    spread = (UPPER_EIGEN - LOWER_EIGEN) / 2
    quotient = centre / spread
    rho_now = 1.0 / quotient
    coefficients = []
    for position in range(number_steps):
        rho_next = 1.0 / (2.0 * quotient - rho_now)
        coefficients.append((rho_next * rho_now, 2.0 * rho_next / spread))
        rho_now = rho_next
    return (centre, coefficients)


def cosine_basis(length_total, modes):
    positions = np.arange(length_total, dtype=np.int64)
    mode_index = np.arange(modes, dtype=np.int64)
    product_index = ((2 * positions[:, None] + 1) * (2 * mode_index[None, :] + 1)) % (
        8 * length_total
    )
    angle = product_index.astype(np.float64) * (math.pi / (4 * length_total))
    return (math.sqrt(2.0 / length_total) * np.cos(angle)).astype(np.float32)


def in_halves(values):
    high = values.astype(jnp.bfloat16)
    return high, (values - high.astype(F32)).astype(jnp.bfloat16)


def team_place():
    return lax.rem(lax.axis_index("gz"), TEAM)


def prepare(jobs, fields, with_sums=False):
    state, target, rock_type, log_table, obs_scale = fields
    samples, planes, rows_y, columns = state.shape
    slots = samples // TEAM
    block = (planes, rows_y, columns)
    half, tiles = rows_y // 2, columns // 128
    size = 2 * 2 * planes
    depth_total = planes * lax.axis_size("gz")
    flat = [(o, i, job) for o, group in enumerate(jobs) for i, job in enumerate(group)]
    count = len(flat)
    shapes = [(len(group) * size + with_sums, half, columns) for group in jobs]
    states = samples if with_sums else count

    def kernel(*refs):
        (table_ref, scale_ref, state_ref, target_ref, rock_ref), refs = refs[:5], refs[5:]
        outs, refs = refs[: len(jobs)], refs[len(jobs) :]
        if with_sums:
            sums_ref, refs = refs[0], refs[1:]
        table, scale, state_buf, rock_buf, target_buf, mixed, sems = refs
        place = team_place()
        first_plane = lax.axis_index("gz") * planes
        members = [slots * (place ^ m) + slot for _, _, (slot, m) in flat]
        small = [
            pltpu.make_async_copy(table_ref, table, sems.at[2, 0]),
            pltpu.make_async_copy(scale_ref, scale, sems.at[2, 1]),
            pltpu.make_async_copy(target_ref, target_buf, sems.at[2, 2]),
        ]
        for copy in small:
            copy.start()
        rocks = [
            pltpu.make_async_copy(rock_ref.at[member], rock_buf.at[n], sems.at[1, n])
            for n, member in enumerate(members)
        ]
        loads = [
            pltpu.make_async_copy(
                state_ref.at[n if with_sums else members[n]], state_buf.at[n], sems.at[0, n]
            )
            for n in range(states)
        ]
        for copy in rocks + loads:
            copy.start()
        depth_weights = [
            1.0 + (2.0 / (depth_total - 1)) * (first_plane + p).astype(F32) for p in range(planes)
        ]
        for copy in small:
            copy.wait()
        if with_sums:
            for copy in loads:
                copy.wait()
            for n in range(samples):
                total = jnp.zeros((8, columns), F32)
                for p in range(planes):
                    part = jnp.zeros((8, columns), F32)
                    for first in range(0, rows_y, 8):
                        rows = slice(first, first + 8)
                        gap = state_buf[n, p, rows] - target_buf[p, rows]
                        part = part + gap * gap
                    total = total + (scale[n] * depth_weights[p]) * part
                summed = jnp.sum(total, keepdims=True)
                sums_ref[n : n + 1, :] = jnp.broadcast_to(summed, (1, columns))
        for n, (o, i, _) in enumerate(flat):
            rocks[n].wait()
            if not with_sums:
                loads[n].wait()
            member = members[n]
            own_state = member if with_sums else n
            values = [
                jnp.exp(jnp.full((8, columns), -table[member, code], F32)) for code in range(NR)
            ]
            for p in range(planes):
                factor = scale[member] * depth_weights[p]
                for first in range(0, rows_y, 8):
                    rows = slice(first, first + 8)
                    codes = rock_buf[n, p, rows]
                    low, mid, high = ((codes & bit) != 0 for bit in (1, 2, 4))
                    pairs = [
                        jnp.where(low, values[2 * k + 1], values[2 * k]) for k in range(NR // 2)
                    ]
                    halves = [jnp.where(mid, pairs[2 * k + 1], pairs[2 * k]) for k in range(2)]
                    gap = state_buf[own_state, p, rows] - target_buf[p, rows]
                    made = (jnp.where(high, halves[1], halves[0]), factor * gap)
                    for a in range(2):
                        for c in range(tiles):
                            mixed[n % 2, p, a, c, rows] = made[a][:, c * 128 : (c + 1) * 128]
                for a in range(2):
                    for t in range(2):
                        for c in range(tiles):
                            at = i * size + (a * planes + p) * 2 + t
                            outs[o][at, :, c * 128 : (c + 1) * 128] = mixed[
                                n % 2, p, a, c, pl.ds(t, half, stride=2), :
                            ]
        for o, group in enumerate(jobs if with_sums else []):
            outs[o][len(group) * size] = sums_ref[...]

    hbm = pl.BlockSpec(memory_space=pltpu.HBM)
    vmem = pl.BlockSpec(memory_space=pltpu.VMEM)
    return pl.pallas_call(
        kernel,
        out_shape=[jax.ShapeDtypeStruct(shape, F32) for shape in shapes]
        + [jax.ShapeDtypeStruct((samples, columns), F32)] * with_sums,
        in_specs=[hbm] * 5,
        out_specs=[vmem] * (len(shapes) + with_sums),
        scratch_shapes=[
            pltpu.SMEM(log_table.shape, F32),
            pltpu.SMEM(obs_scale.shape, F32),
            pltpu.VMEM((states,) + block, F32),
            pltpu.VMEM((count,) + block, jnp.int32),
            pltpu.VMEM(block, F32),
            pltpu.VMEM((2, planes, 2, tiles, rows_y, 128), F32),
            pltpu.SemaphoreType.DMA((3, max(states, 3))),
        ],
        compiler_params=pltpu.CompilerParams(vmem_limit_bytes=6 * MIB),
        cost_estimate=pl.CostEstimate(flops=0, bytes_accessed=count * MIB, transcendentals=0),
        name="prepare",
    )(log_table, obs_scale, state, target, rock_type)


def merge(mine, theirs, slot, size, behind=None, add=None):
    given = [value for value in (behind, add) if value is not None]

    def kernel(mine_ref, theirs_ref, *refs):
        core = lax.rem(team_place(), 2)
        tail, (out_ref, *more) = refs[: len(given)], refs[len(given) :]
        for ref, at in ((mine_ref, core), (theirs_ref, 1 - core)):
            for n in range(size):
                out_ref[at * size + n] = ref[slot * size + n]
        if behind is not None:
            out_ref[2 * size] = tail[0][...]
        if add is not None:
            more[0][...] = tail[-1][...] + theirs_ref[theirs.shape[0] - 1]

    vmem = pl.BlockSpec(memory_space=pltpu.VMEM)
    tile = mine.shape[1:]
    outs = pl.pallas_call(
        kernel,
        out_shape=[jax.ShapeDtypeStruct((2 * size + (behind is not None),) + tile, F32)]
        + [jax.ShapeDtypeStruct(tile, F32)] * (add is not None),
        in_specs=[vmem] * (2 + len(given)),
        out_specs=[vmem] * (1 + (add is not None)),
        compiler_params=pltpu.CompilerParams(vmem_limit_bytes=4 * MIB),
        name="merge",
    )(mine, theirs, *given)
    return outs if add is not None else outs[0]


def copy_trimmed(ref, out_ref, size, below):
    part = size // 2
    for core in range(2):
        for n in range(part):
            out_ref[core * part + n] = ref[core * size + n]
    for n in range(size - 2):
        at = n + jnp.where(below, 2, 0)
        out_ref[size + n] = ref[(at // part) * size + part + lax.rem(at, part)]


def trim(blocks, size):
    def kernel(ref, out_ref):
        copy_trimmed(ref, out_ref, size, team_place() < 2)

    vmem = pl.BlockSpec(memory_space=pltpu.VMEM)
    return pl.pallas_call(
        kernel,
        out_shape=jax.ShapeDtypeStruct((2 * size - 2,) + blocks.shape[1:], F32),
        in_specs=[vmem],
        out_specs=vmem,
        compiler_params=pltpu.CompilerParams(vmem_limit_bytes=4 * MIB),
        name="trim",
    )(blocks)


def merge_near(mine, theirs, slot, size, after):
    tile = mine.shape[1:]

    def kernel(mine_ref, theirs_ref, _, out_ref, trimmed_ref):
        core = lax.rem(team_place(), 2)
        for ref, at in ((mine_ref, core), (theirs_ref, 1 - core)):
            for n in range(size):
                out_ref[at * size + n] = ref[slot * size + n]
        copy_trimmed(out_ref, trimmed_ref, size, team_place() >= 2)

    vmem = pl.BlockSpec(memory_space=pltpu.VMEM)
    return pl.pallas_call(
        kernel,
        out_shape=[
            jax.ShapeDtypeStruct((2 * size,) + tile, F32),
            jax.ShapeDtypeStruct((2 * size - 2,) + tile, F32),
        ],
        in_specs=[vmem] * 2 + [pl.BlockSpec(memory_space=pl.ANY)],
        out_specs=[vmem] * 2,
        compiler_params=pltpu.CompilerParams(vmem_limit_bytes=4 * MIB),
        name="merge_near",
    )(mine, theirs, after)


def reciprocal(x):
    guess = pl.reciprocal(x, approx=True)
    return guess * (2.0 - x * guess)


def harmonic(a, b):
    x = a + b
    guess = pl.reciprocal(x, approx=True)
    return guess * (4.0 - (2.0 * x) * guess)


def each(start, stop, body, width):
    whole = (stop - start) // width

    def group(n, carry):
        for k in range(width):
            body(start + n * width + k)
        return carry

    lax.fori_loop(0, whole, group, 0)
    for p in range(start + whole * width, stop):
        body(p)


def solve(near, far, near_halo, far_halo, planes):
    inputs = [near, near_halo, far, far_halo]
    half, columns = far.shape[-2:]
    part = 2 * planes
    halo = 2 * planes
    own = TEAM * planes
    span = own + 2 * halo
    centre, coefficients = chebyshev_constants(DEGREE)
    assert halo >= STEPS

    def kernel(*refs):
        ins, refs = refs[: len(inputs)], refs[len(inputs) :]
        outs, face_ref, refs = refs[:TEAM], refs[TEAM], refs[TEAM + 1 :]
        cond, u_a, u_b, s_a, s_b, zp, zm, yp, ym, xp, xm, t_a, t_b = refs
        place = team_place()
        side = place // 2
        upper, lower = halo + own, 0
        near_base = jnp.where(side == 0, upper, lower)
        far_base = jnp.where(side == 0, lower, upper)
        def outside(v):
            return jnp.where(v > 0.0, v, 1e30)

        for core in range(2):
            for n in range(part):
                base = halo + planes * core + n // 2
                for ref, at in ((ins[0], base + part * side), (ins[2], base + part * (1 - side))):
                    cond[at, n % 2] = outside(ref[core * 2 * part + n])
                    t_a[at, n % 2] = ref[(core * 2 + 1) * part + n]
        for ref, at in ((ins[1], near_base), (ins[3], far_base)):
            skip = jnp.where(at == lower, 1, 0)
            for n in range(2 * part):
                cond[at + n // 2, n % 2] = outside(ref[n])
            for n in range(2 * part - 2):
                t_a[at + skip + n // 2, n % 2] = ref[2 * part + n]

        last_row = lax.broadcasted_iota(jnp.int32, (half, columns), 0) == half - 1
        last_column = lax.broadcasted_iota(jnp.int32, (half, columns), 1) == columns - 1

        def ahead_x(v):
            return pltpu.roll(v, columns - 1, 1)

        def behind_x(v):
            return pltpu.roll(v, 1, 1)

        def ahead_y(v):
            return pltpu.roll(v, half - 1, 0)

        def behind_y(v):
            return pltpu.roll(v, 1, 0)

        def setup(p, w_z_before):
            even, odd = cond[p, 0], cond[p, 1]
            w_pair = harmonic(even, odd)
            w_next = jnp.where(last_row, 0.0, harmonic(odd, ahead_y(even)))
            w_z_here = []
            for t, here in enumerate((even, odd)):
                w_z = harmonic(here, cond[p + 1, t])
                w_z_here.append(w_z)
                w_z_behind = w_z_before[t]
                w_y = w_next if t else w_pair
                w_y_behind = w_pair if t else behind_y(w_next)
                w_x = jnp.where(last_column, 0.0, harmonic(here, ahead_x(here)))
                w_x_behind = behind_x(w_x)
                diagonal = (w_z + w_z_behind) + (w_y + w_y_behind) + (w_x + w_x_behind) + STORAGE
                inverse = reciprocal(diagonal)
                zp[p, t] = w_z * inverse
                zm[p, t] = w_z_behind * inverse
                yp[p, t] = w_y * inverse
                ym[p, t] = w_y_behind * inverse
                xp[p, t] = w_x * inverse
                xm[p, t] = w_x_behind * inverse
                scaled = t_a[p, t] * inverse
                u_a[p, t] = scaled
                s_a[p, t] = scaled * (1.0 / centre)
            return w_z_here

        width = (span - 2) // 3

        def setup_group(n, carry):
            start = 1 + n * width
            w_z = [harmonic(cond[start - 1, t], cond[start, t]) for t in range(2)]
            for k in range(width):
                w_z = setup(start + k, w_z)
            return carry

        assert (span - 2) % width == 0
        lax.fori_loop(0, (span - 2) // width, setup_group, 0)

        s_now, s_next, u_now, u_next, t_now, t_next = s_a, s_b, u_a, u_b, t_a, t_b
        for step in range(STEPS - 1):
            position = step % DEGREE
            if position + 1 < DEGREE:
                keep, mix = coefficients[position]
            else:
                keep, mix = 0.0, 1.0 / centre
            last = step == STEPS - 2

            def advance(p):
                even, odd = s_now[p, 0], s_now[p, 1]
                for t, s in enumerate((even, odd)):
                    ahead = ahead_y(even) if t else odd
                    behind = even if t else behind_y(odd)
                    moved = zp[p, t] * s_now[p + 1, t] + zm[p, t] * s_now[p - 1, t]
                    moved += yp[p, t] * ahead + ym[p, t] * behind
                    moved += xp[p, t] * ahead_x(s) + xm[p, t] * behind_x(s)
                    new_u = (u_now[p, t] - s) + moved
                    new_s = mix * new_u if keep == 0.0 else keep * s + mix * new_u
                    if not last:
                        u_next[p, t] = new_u
                        s_next[p, t] = new_s
                    if step == 0:
                        t_next[p, t] = s + new_s
                    elif step % 2 == 0:
                        t_next[p, t] = t_now[p, t] + (s + new_s)

            margin = halo - (STEPS - 2 - step)
            each(margin, span - margin, advance, 8)
            s_now, s_next, u_now, u_next = s_next, s_now, u_next, u_now
            if step % 2 == 0:
                t_now, t_next = t_next, t_now

        for m in range(TEAM):
            base = halo + planes * (place ^ m)
            for j in range(planes):
                for t in range(2):
                    outs[m][2 * j + t] = t_now[base + j, t]
        for p in range(own):
            face_ref[p : p + 1, :] = t_now[halo + p, 0, 0:1, :]

    vmem = pl.BlockSpec(memory_space=pltpu.VMEM)
    field = pltpu.VMEM((span, 2, half, columns), F32)
    return pl.pallas_call(
        kernel,
        out_shape=[jax.ShapeDtypeStruct((2 * planes, half, columns), F32)] * TEAM
        + [jax.ShapeDtypeStruct((own, columns), F32)],
        in_specs=[vmem] * len(inputs),
        out_specs=[vmem] * (TEAM + 1),
        scratch_shapes=[field] * 13,
        compiler_params=pltpu.CompilerParams(vmem_limit_bytes=16 * MIB),
        cost_estimate=pl.CostEstimate(flops=0, bytes_accessed=22 * MIB, transcendentals=0),
        name="solve",
    )(*inputs)


def weigh(sums, faces, cells, after):
    slots = len(faces)
    samples, columns = sums[0].shape

    def kernel(*refs):
        sum_refs, refs = refs[: len(sums)], refs[len(sums) :]
        face_refs, (out_ref, moments_ref, weights) = refs[:slots], refs[slots + len(after) :]
        place = team_place()
        summed = sum_refs[0][...]
        for ref in sum_refs[1:]:
            summed = summed + ref[...]
        misfit = summed * (1.0 / (2.0 * cells))
        mean = jnp.sum(misfit, axis=0, keepdims=True) * (1.0 / samples)
        deviation = misfit - mean
        variance = jnp.sum(deviation * deviation, axis=0, keepdims=True) * (1.0 / samples)
        lane = lax.broadcasted_iota(jnp.int32, (1, columns), 1)
        moments_ref[...] = jnp.where(lane == 0, mean, variance)
        weights[...] = 1.0 + 2.0 * BETA_RISK * deviation
        total = weights[pl.ds(slots * place, 1), :] * face_refs[0][...]
        for n in range(1, slots):
            total = total + weights[pl.ds(slots * place + n, 1), :] * face_refs[n][...]
        out_ref[...] = total

    vmem = pl.BlockSpec(memory_space=pltpu.VMEM)
    return pl.pallas_call(
        kernel,
        out_shape=[
            jax.ShapeDtypeStruct(faces[0].shape, F32),
            jax.ShapeDtypeStruct((1, columns), F32),
        ],
        in_specs=[vmem] * (len(sums) + slots)
        + [pl.BlockSpec(memory_space=pl.ANY)] * len(after),
        out_specs=[vmem, vmem],
        scratch_shapes=[pltpu.VMEM((samples, columns), F32)],
        compiler_params=pltpu.CompilerParams(vmem_limit_bytes=2 * MIB),
        name="weigh",
    )(*sums, *faces, *after)


def gather_adjoint(pieces, slot, slots, planes, adjoint):
    _, half, columns = pieces[0].shape
    tiles = columns // 128
    block = (planes, 2 * half, columns)
    given = [] if adjoint is None else [adjoint]

    def kernel(*refs):
        blocks, refs = refs[:TEAM], refs[TEAM + len(given) :]
        out, mark, held, mixed, sems = refs
        mark[...] = blocks[0][0, :, :LANES]
        place = team_place()
        copies = []
        for m in range(TEAM):
            for j in range(planes):
                for t in range(2):
                    for c in range(tiles):
                        mixed[m, j, c, pl.ds(t, half, stride=2), :] = blocks[m][
                            2 * j + t, :, c * 128 : (c + 1) * 128
                        ]
                for c in range(tiles):
                    held[m, j, :, c * 128 : (c + 1) * 128] = mixed[m, j, c]
            copy = pltpu.make_async_copy(
                held.at[m], out.at[slots * (place ^ m) + slot], sems.at[m]
            )
            copy.start()
            copies.append(copy)
        for copy in copies:
            copy.wait()

    vmem = pl.BlockSpec(memory_space=pltpu.VMEM)
    hbm = pl.BlockSpec(memory_space=pltpu.HBM)
    return pl.pallas_call(
        kernel,
        out_shape=[
            jax.ShapeDtypeStruct((slots * TEAM,) + block, F32),
            jax.ShapeDtypeStruct((half, LANES), F32),
        ],
        in_specs=[vmem] * TEAM + [hbm] * len(given),
        out_specs=[hbm, vmem],
        scratch_shapes=[
            pltpu.VMEM((TEAM,) + block, F32),
            pltpu.VMEM((TEAM, planes, tiles, 2 * half, 128), F32),
            pltpu.SemaphoreType.DMA((TEAM,)),
        ],
        input_output_aliases={TEAM: 0} if given else {},
        compiler_params=pltpu.CompilerParams(vmem_limit_bytes=4 * MIB),
        cost_estimate=pl.CostEstimate(flops=0, bytes_accessed=2 * MIB, transcendentals=0),
        name="gather_adjoint",
    )(*pieces, *given)


def control(faces, radices, basis_z, basis_x, after):
    slabs, own_count, depth_total = basis_z.shape
    own, columns = faces[0].shape[1:]
    teams = depth_total // own

    def kernel(*refs):
        parts, (z_ref, x_ref, _, out_ref, whole) = refs[: len(faces)], refs[len(faces) :]
        rank = lax.axis_index("gz")
        team = rank // TEAM
        for n in range(teams):
            at, left, stride = 0, n, 1
            for radix in radices:
                digit = turned(lax.rem(team // stride, radix), left % radix, radix)
                at, left, stride = at + digit * stride, left // radix, stride * radix
            inner = teams // len(faces)
            whole[at] = parts[n // inner][n % inner]
        along_z = jnp.dot(
            z_ref[rank],
            whole[...].reshape(depth_total, columns),
            precision=lax.Precision.HIGHEST,
            preferred_element_type=F32,
        )
        high, low = in_halves(along_z)
        x_high, x_low = in_halves(x_ref[...])
        both = jnp.concatenate([high, low], axis=0)
        first = jnp.dot(both, x_high, preferred_element_type=F32)
        second = jnp.dot(high, x_low, preferred_element_type=F32)
        out_ref[...] = (first[:own_count] + first[own_count:]) + second

    vmem = pl.BlockSpec(memory_space=pltpu.VMEM)
    return pl.pallas_call(
        kernel,
        out_shape=jax.ShapeDtypeStruct((own_count, basis_x.shape[1]), F32),
        in_specs=[vmem] * (len(faces) + 2) + [pl.BlockSpec(memory_space=pl.ANY)],
        out_specs=vmem,
        scratch_shapes=[pltpu.VMEM((teams, own, columns), F32)],
        compiler_params=pltpu.CompilerParams(vmem_limit_bytes=8 * MIB),
        name="control",
    )(*faces, basis_z, basis_x, after)


def turned(digit, k, radix):
    return digit ^ k if radix in (2, 4) else (digit + k) % radix


def radices_of(teams):
    radices = []
    while teams > 1:
        radix = next(r for r in (4, 2, 3, *range(5, teams + 1)) if teams % r == 0)
        radices.append(radix)
        teams //= radix
    return radices


def on_device(state, target, rock_type, log_table, obs_scale):
    samples, planes, rows_y, columns = state.shape
    slabs = lax.axis_size("gz")
    slots = samples // TEAM
    depth_total = planes * slabs
    radices = radices_of(slabs // TEAM)

    def swap(value, m):
        return lax.ppermute(value, "gz", [(i, i ^ m) for i in range(slabs)])

    def along(value, outward):
        pairs = []
        for i in range(slabs):
            side = (i % TEAM) // 2
            to = i + TEAM if (side == 1) == outward else i - TEAM
            if 0 <= to < slabs:
                pairs.append((i, to))
        return lax.ppermute(value, "gz", pairs)

    def from_teams(value, stride, radix):
        heard = {}
        for k in reversed(range(1, radix)):
            pairs = []
            for i in range(slabs):
                digit = i // (TEAM * stride) % radix
                pairs.append((i + (turned(digit, k, radix) - digit) * stride * TEAM, i))
            heard[k] = lax.ppermute(value, "gz", pairs)
        return [heard[k] for k in range(1, radix)]

    fields = [
        pltpu.with_memory_space_constraint(field, pltpu.HBM)
        for field in (state, target, rock_type, log_table, obs_scale)
    ]
    size = 4 * planes
    jobs = [[(slot, m) for slot in range(slots)] for m in range(TEAM)]
    mine, theirs, sums = prepare(jobs[2:], fields, with_sums=True)
    theirs = swap(theirs, 1)
    first, sums = merge(mine, theirs, 0, size, add=sums)
    far = [swap(first, 2)]
    stride, teams = 1, slabs // TEAM
    while stride < teams:
        radix = next(r for r in range(2, teams + 1) if teams // stride % r == 0)
        sums = sum(from_teams(sums, stride, radix), sums)
        stride *= radix

    mine_near, theirs_near = prepare(jobs[:2], fields)
    theirs_near = swap(theirs_near, 1)
    near, near_halo = [], []
    for slot in range(slots):
        blocks, trimmed = merge_near(mine_near, theirs_near, slot, size, sums)
        near.append(blocks)
        near_halo.append(along(trimmed, True))
    for slot in range(1, slots):
        far.append(swap(merge(mine, theirs, slot, size, sums), 2))
    sums = [sums, far[-1][2 * size]]

    pieces, faces = [], []
    for slot in range(slots):
        far_halo = along(trim(far[slot], size), False)
        solved = solve(near[slot], far[slot], near_halo[slot], far_halo, planes)
        traded = {m: swap(solved[m], m) for m in (2, 3, 1)}
        pieces.append([solved[0]] + [traded[m] for m in (1, 2, 3)])
        faces.append(solved[TEAM])

    face, moments = weigh(sums, faces, depth_total * rows_y * columns, pieces[0][1:])
    heard = [sum((swap(face, m) for m in (2, 3, 1)), face)[None]]
    stride = 1
    for radix in radices:
        held = heard[0] if len(heard) == 1 else jnp.concatenate(heard)
        heard = [held] + from_teams(held, stride, radix)
        stride *= radix
    adjoint = None
    for slot in range(slots):
        adjoint, mark = gather_adjoint(pieces[slot], slot, slots, planes, adjoint)
    own_count = MA // slabs
    gradient = control(
        heard,
        radices,
        jnp.asarray(cosine_basis(depth_total, MA).T.reshape(slabs, own_count, depth_total)),
        jnp.asarray(cosine_basis(columns, MB)),
        mark,
    )
    return (adjoint, gradient, moments[0, :2])


def solution(mesh):
    return jax.shard_map(
        on_device,
        mesh=mesh,
        in_specs=(
            P("parts", "gz", None, None),
            P(("parts", "gz"), None, None),
            P("parts", "gz", None, None),
            P("parts", None),
            P("parts"),
        ),
        out_specs=(P("parts", "gz", None, None), P(("parts", "gz"), None), P("parts")),
        check_vma=False,
    )
```

```python
import math

import jax
import jax.numpy as jnp
import numpy as np
from jax import lax
from jax.experimental import pallas as pl
from jax.experimental.pallas import tpu as pltpu
from jax.sharding import PartitionSpec as P

NR = 8
DEGREE = 4
SWEEPS = 2
MA = 512
MB = 512

STORAGE = 0.05
BETA_RISK = 0.5
LOWER_EIGEN = 0.05
UPPER_EIGEN = 2.0

TEAM = 4
STEPS = DEGREE * SWEEPS
F32 = jnp.float32
MIB = 1024 * 1024
LANES = 128


def chebyshev_constants(number_steps):
    centre = (UPPER_EIGEN + LOWER_EIGEN) / 2
    spread = (UPPER_EIGEN - LOWER_EIGEN) / 2
    quotient = centre / spread
    rho_now = 1.0 / quotient
    coefficients = []
    for position in range(number_steps):
        rho_next = 1.0 / (2.0 * quotient - rho_now)
        coefficients.append((rho_next * rho_now, 2.0 * rho_next / spread))
        rho_now = rho_next
    return (centre, coefficients)


def cosine_basis(length_total, modes):
    positions = np.arange(length_total, dtype=np.int64)
    mode_index = np.arange(modes, dtype=np.int64)
    product_index = ((2 * positions[:, None] + 1) * (2 * mode_index[None, :] + 1)) % (
        8 * length_total
    )
    angle = product_index.astype(np.float64) * (math.pi / (4 * length_total))
    return (math.sqrt(2.0 / length_total) * np.cos(angle)).astype(np.float32)


def in_halves(values):
    high = values.astype(jnp.bfloat16)
    return high, (values - high.astype(F32)).astype(jnp.bfloat16)


def team_place():
    return lax.rem(lax.axis_index("gz"), TEAM)


def prepare(jobs, fields, with_sums=False):
    state, target, rock_type, log_table, obs_scale = fields
    samples, planes, rows_y, columns = state.shape
    slots = samples // TEAM
    block = (planes, rows_y, columns)
    half, tiles = rows_y // 2, columns // 128
    size = 2 * 2 * planes
    depth_total = planes * lax.axis_size("gz")
    flat = [(o, i, job) for o, group in enumerate(jobs) for i, job in enumerate(group)]
    count = len(flat)
    shapes = [(len(group) * size + with_sums, half, columns) for group in jobs]
    states = samples if with_sums else count

    def kernel(*refs):
        (table_ref, scale_ref, state_ref, target_ref, rock_ref), refs = refs[:5], refs[5:]
        outs, refs = refs[: len(jobs)], refs[len(jobs) :]
        if with_sums:
            sums_ref, refs = refs[0], refs[1:]
        table, scale, state_buf, rock_buf, target_buf, mixed, sems = refs
        place = team_place()
        first_plane = lax.axis_index("gz") * planes
        members = [slots * (place ^ m) + slot for _, _, (slot, m) in flat]
        small = [
            pltpu.make_async_copy(table_ref, table, sems.at[2, 0]),
            pltpu.make_async_copy(scale_ref, scale, sems.at[2, 1]),
            pltpu.make_async_copy(target_ref, target_buf, sems.at[2, 2]),
        ]
        for copy in small:
            copy.start()
        rocks = [
            pltpu.make_async_copy(rock_ref.at[member], rock_buf.at[n], sems.at[1, n])
            for n, member in enumerate(members)
        ]
        loads = [
            pltpu.make_async_copy(
                state_ref.at[n if with_sums else members[n]], state_buf.at[n], sems.at[0, n]
            )
            for n in range(states)
        ]
        for copy in rocks + loads:
            copy.start()
        depth_weights = [
            1.0 + (2.0 / (depth_total - 1)) * (first_plane + p).astype(F32) for p in range(planes)
        ]
        for copy in small:
            copy.wait()
        if with_sums:
            for copy in loads:
                copy.wait()
            for n in range(samples):
                total = jnp.zeros((8, columns), F32)
                for p in range(planes):
                    part = jnp.zeros((8, columns), F32)
                    for first in range(0, rows_y, 8):
                        rows = slice(first, first + 8)
                        gap = state_buf[n, p, rows] - target_buf[p, rows]
                        part = part + gap * gap
                    total = total + (scale[n] * depth_weights[p]) * part
                summed = jnp.sum(total, keepdims=True)
                sums_ref[n : n + 1, :] = jnp.broadcast_to(summed, (1, columns))
        for n, (o, i, _) in enumerate(flat):
            rocks[n].wait()
            if not with_sums:
                loads[n].wait()
            member = members[n]
            own_state = member if with_sums else n
            values = [
                jnp.exp(jnp.full((8, columns), -table[member, code], F32)) for code in range(NR)
            ]
            for p in range(planes):
                factor = scale[member] * depth_weights[p]
                for first in range(0, rows_y, 8):
                    rows = slice(first, first + 8)
                    codes = rock_buf[n, p, rows]
                    low, mid, high = ((codes & bit) != 0 for bit in (1, 2, 4))
                    pairs = [
                        jnp.where(low, values[2 * k + 1], values[2 * k]) for k in range(NR // 2)
                    ]
                    halves = [jnp.where(mid, pairs[2 * k + 1], pairs[2 * k]) for k in range(2)]
                    gap = state_buf[own_state, p, rows] - target_buf[p, rows]
                    made = (jnp.where(high, halves[1], halves[0]), factor * gap)
                    for a in range(2):
                        for c in range(tiles):
                            mixed[n % 2, p, a, c, rows] = made[a][:, c * 128 : (c + 1) * 128]
                for a in range(2):
                    for t in range(2):
                        for c in range(tiles):
                            at = i * size + (a * planes + p) * 2 + t
                            outs[o][at, :, c * 128 : (c + 1) * 128] = mixed[
                                n % 2, p, a, c, pl.ds(t, half, stride=2), :
                            ]
        for o, group in enumerate(jobs if with_sums else []):
            outs[o][len(group) * size] = sums_ref[...]

    hbm = pl.BlockSpec(memory_space=pltpu.HBM)
    vmem = pl.BlockSpec(memory_space=pltpu.VMEM)
    return pl.pallas_call(
        kernel,
        out_shape=[jax.ShapeDtypeStruct(shape, F32) for shape in shapes]
        + [jax.ShapeDtypeStruct((samples, columns), F32)] * with_sums,
        in_specs=[hbm] * 5,
        out_specs=[vmem] * (len(shapes) + with_sums),
        scratch_shapes=[
            pltpu.SMEM(log_table.shape, F32),
            pltpu.SMEM(obs_scale.shape, F32),
            pltpu.VMEM((states,) + block, F32),
            pltpu.VMEM((count,) + block, jnp.int32),
            pltpu.VMEM(block, F32),
            pltpu.VMEM((2, planes, 2, tiles, rows_y, 128), F32),
            pltpu.SemaphoreType.DMA((3, max(states, 3))),
        ],
        compiler_params=pltpu.CompilerParams(vmem_limit_bytes=6 * MIB),
        cost_estimate=pl.CostEstimate(flops=0, bytes_accessed=count * MIB, transcendentals=0),
        name="prepare",
    )(log_table, obs_scale, state, target, rock_type)


def merge(mine, theirs, slot, size, behind=None, add=None):
    given = [value for value in (behind, add) if value is not None]

    def kernel(mine_ref, theirs_ref, *refs):
        core = lax.rem(team_place(), 2)
        tail, (out_ref, *more) = refs[: len(given)], refs[len(given) :]
        for ref, at in ((mine_ref, core), (theirs_ref, 1 - core)):
            for n in range(size):
                out_ref[at * size + n] = ref[slot * size + n]
        if behind is not None:
            out_ref[2 * size] = tail[0][...]
        if add is not None:
            more[0][...] = tail[-1][...] + theirs_ref[theirs.shape[0] - 1]

    vmem = pl.BlockSpec(memory_space=pltpu.VMEM)
    tile = mine.shape[1:]
    outs = pl.pallas_call(
        kernel,
        out_shape=[jax.ShapeDtypeStruct((2 * size + (behind is not None),) + tile, F32)]
        + [jax.ShapeDtypeStruct(tile, F32)] * (add is not None),
        in_specs=[vmem] * (2 + len(given)),
        out_specs=[vmem] * (1 + (add is not None)),
        compiler_params=pltpu.CompilerParams(vmem_limit_bytes=4 * MIB),
        name="merge",
    )(mine, theirs, *given)
    return outs if add is not None else outs[0]


def copy_trimmed(ref, out_ref, size, below):
    part = size // 2
    for core in range(2):
        for n in range(part):
            out_ref[core * part + n] = ref[core * size + n]
    for n in range(size - 2):
        at = n + jnp.where(below, 2, 0)
        out_ref[size + n] = ref[(at // part) * size + part + lax.rem(at, part)]


def trim(blocks, size):
    def kernel(ref, out_ref):
        copy_trimmed(ref, out_ref, size, team_place() < 2)

    vmem = pl.BlockSpec(memory_space=pltpu.VMEM)
    return pl.pallas_call(
        kernel,
        out_shape=jax.ShapeDtypeStruct((2 * size - 2,) + blocks.shape[1:], F32),
        in_specs=[vmem],
        out_specs=vmem,
        compiler_params=pltpu.CompilerParams(vmem_limit_bytes=4 * MIB),
        name="trim",
    )(blocks)


def merge_near(mine, theirs, slot, size, after):
    tile = mine.shape[1:]

    def kernel(mine_ref, theirs_ref, _, out_ref, trimmed_ref):
        core = lax.rem(team_place(), 2)
        for ref, at in ((mine_ref, core), (theirs_ref, 1 - core)):
            for n in range(size):
                out_ref[at * size + n] = ref[slot * size + n]
        copy_trimmed(out_ref, trimmed_ref, size, team_place() >= 2)

    vmem = pl.BlockSpec(memory_space=pltpu.VMEM)
    return pl.pallas_call(
        kernel,
        out_shape=[
            jax.ShapeDtypeStruct((2 * size,) + tile, F32),
            jax.ShapeDtypeStruct((2 * size - 2,) + tile, F32),
        ],
        in_specs=[vmem] * 2 + [pl.BlockSpec(memory_space=pl.ANY)],
        out_specs=[vmem] * 2,
        compiler_params=pltpu.CompilerParams(vmem_limit_bytes=4 * MIB),
        name="merge_near",
    )(mine, theirs, after)


def reciprocal(x):
    guess = pl.reciprocal(x, approx=True)
    return guess * (2.0 - x * guess)


def harmonic(a, b):
    x = a + b
    guess = pl.reciprocal(x, approx=True)
    return guess * (4.0 - (2.0 * x) * guess)


def each(start, stop, body, width):
    whole = (stop - start) // width

    def group(n, carry):
        for k in range(width):
            body(start + n * width + k)
        return carry

    lax.fori_loop(0, whole, group, 0)
    for p in range(start + whole * width, stop):
        body(p)


def ahead_x(v):
    return pltpu.roll(v, v.shape[1] - 1, 1)


def behind_x(v):
    return pltpu.roll(v, 1, 1)


def ahead_y(v):
    return pltpu.roll(v, v.shape[0] - 1, 0)


def behind_y(v):
    return pltpu.roll(v, 1, 0)


def set_up(planes, conductance, source, store):
    centre, _ = chebyshev_constants(DEGREE)
    here = [conductance(planes[0], t) for t in range(2)]
    half, columns = here[0].shape
    last_row = lax.broadcasted_iota(jnp.int32, (half, columns), 0) == half - 1
    last_column = lax.broadcasted_iota(jnp.int32, (half, columns), 1) == columns - 1
    w_below = [harmonic(conductance(planes[0] - 1, t), here[t]) for t in range(2)]
    for p in planes:
        above = [conductance(p + 1, t) for t in range(2)]
        even, odd = here
        w_pair = harmonic(even, odd)
        w_next = jnp.where(last_row, 0.0, harmonic(odd, ahead_y(even)))
        w_above = [harmonic(here[t], above[t]) for t in range(2)]
        for t in range(2):
            w_y = w_next if t else w_pair
            w_y_behind = w_pair if t else behind_y(w_next)
            w_x = jnp.where(last_column, 0.0, harmonic(here[t], ahead_x(here[t])))
            w_x_behind = behind_x(w_x)
            diagonal = (w_above[t] + w_below[t]) + (w_y + w_y_behind) + (w_x + w_x_behind) + STORAGE
            inverse = reciprocal(diagonal)
            weights = (w_above[t], w_below[t], w_y, w_y_behind, w_x, w_x_behind)
            scaled = source(p, t) * inverse
            store(p, t, [w * inverse for w in weights] + [scaled, scaled * (1.0 / centre)])
        here, w_below = above, w_above


def outside(v):
    return jnp.where(v > 0.0, v, 1e30)


def prepare_planes(near, far, near_halo, planes, after):
    half, columns = far.shape[-2:]
    halo, own, part = 2 * planes, TEAM * planes, 2 * planes
    span = own + 2 * halo
    first, count = halo + 1, own + halo - 2

    def kernel(near_ref, halo_ref, far_ref, *refs):
        refs = refs[len(after) :]
        outs, edge_ref, (cond, start) = refs[:8], refs[8], refs[9:]
        side = team_place() // 2

        def place(natural):
            return jnp.where(side == 0, natural, span - 1 - natural) - halo

        for core in range(2):
            for n in range(part):
                base = halo + planes * core + n // 2
                for ref, at in ((near_ref, base + part * side), (far_ref, base + part * (1 - side))):
                    cond[place(at), n % 2] = ref[core * 2 * part + n]
                    start[place(at), n % 2] = ref[(core * 2 + 1) * part + n]
        near_base = jnp.where(side == 0, halo + own, 0)
        for n in range(2 * part):
            cond[place(near_base + n // 2), n % 2] = outside(halo_ref[n])
        for n in range(2 * part - 2):
            start[place(near_base + side + n // 2), n % 2] = halo_ref[2 * part + n]
        for p in range(2):
            for t in range(2):
                edge_ref[0, p, t] = cond[p, t]
                edge_ref[1, p, t] = start[p, t]

        width = count // 2

        def group(n, carry):
            begin = 1 + n * width

            def store(p, t, values):
                for ref, value in zip(outs, values):
                    ref[p - 1, t] = value

            set_up(
                [begin + k for k in range(width)],
                lambda p, t: cond[p, t],
                lambda p, t: start[p, t],
                store,
            )
            return carry

        lax.fori_loop(0, 2, group, 0)

    assert count % 2 == 0
    vmem = pl.BlockSpec(memory_space=pltpu.VMEM)
    results = pl.pallas_call(
        kernel,
        out_shape=[jax.ShapeDtypeStruct((count, 2, half, columns), F32)] * 8
        + [jax.ShapeDtypeStruct((2, 2, 2, half, columns), F32)],
        in_specs=[vmem] * 3 + [pl.BlockSpec(memory_space=pl.ANY)] * len(after),
        out_specs=[vmem] * 9,
        scratch_shapes=[pltpu.VMEM((own + halo, 2, half, columns), F32)] * 2,
        compiler_params=pltpu.CompilerParams(vmem_limit_bytes=4 * MIB),
        cost_estimate=pl.CostEstimate(flops=0, bytes_accessed=8 * MIB, transcendentals=0),
        name="prepare_planes",
    )(near, near_halo, far, *after)
    return results[:8], results[8]


def solve(made, edge, far_halo, planes):
    half, columns = far_halo.shape[-2:]
    halo, own, part = 2 * planes, TEAM * planes, 2 * planes
    span = own + 2 * halo
    cut = halo + 1
    centre, coefficients = chebyshev_constants(DEGREE)
    assert halo >= STEPS

    def kernel(*refs):
        high, (edge_ref, halo_ref), refs = refs[:8], refs[8:10], refs[10:]
        outs, face_ref, refs = refs[:TEAM], refs[TEAM], refs[TEAM + 1 :]
        low, (cond, start, u_a, u_b, s_a, s_b, t_a, t_b) = refs[:6], refs[6:]
        place = team_place()
        side = place // 2

        def at(natural):
            return jnp.where(side == 0, natural, span - 1 - natural)

        far_base = jnp.where(side == 0, 0, halo + own)
        for n in range(2 * part):
            cond[at(far_base + n // 2), n % 2] = outside(halo_ref[n])
        for n in range(2 * part - 2):
            start[at(far_base + (1 - side) + n // 2), n % 2] = halo_ref[2 * part + n]
        for p in range(2):
            for t in range(2):
                cond[halo + p, t] = edge_ref[0, p, t]
                start[halo + p, t] = edge_ref[1, p, t]

        def store(p, t, values):
            for ref, value in zip((*low, u_a, s_a), values):
                ref[p, t] = value

        set_up(range(1, cut), lambda p, t: cond[p, t], lambda p, t: start[p, t], store)
        for p in range(cut, span - 1):
            for t in range(2):
                u_a[p, t] = high[6][p - cut, t]
                s_a[p, t] = high[7][p - cut, t]

        s_now, s_next, u_now, u_next, t_now, t_next = s_a, s_b, u_a, u_b, t_a, t_b
        for step in range(STEPS - 1):
            position = step % DEGREE
            if position + 1 < DEGREE:
                keep, mix = coefficients[position]
            else:
                keep, mix = 0.0, 1.0 / centre
            last = step == STEPS - 2

            def advance(p, fields, first):
                zp, zm, yp, ym, xp, xm = fields
                q = p - first
                even, odd = s_now[p, 0], s_now[p, 1]
                for t, s in enumerate((even, odd)):
                    ahead = ahead_y(even) if t else odd
                    behind = even if t else behind_y(odd)
                    moved = zp[q, t] * s_now[p + 1, t] + zm[q, t] * s_now[p - 1, t]
                    moved += yp[q, t] * ahead + ym[q, t] * behind
                    moved += xp[q, t] * ahead_x(s) + xm[q, t] * behind_x(s)
                    new_u = (u_now[p, t] - s) + moved
                    new_s = mix * new_u if keep == 0.0 else keep * s + mix * new_u
                    if not last:
                        u_next[p, t] = new_u
                        s_next[p, t] = new_s
                    if step == 0:
                        t_next[p, t] = s + new_s
                    elif step % 2 == 0:
                        t_next[p, t] = t_now[p, t] + (s + new_s)

            margin = halo - (STEPS - 2 - step)
            each(cut, span - margin, lambda p: advance(p, high[:6], cut), 8)
            each(margin, cut, lambda p: advance(p, low, 0), 8)
            s_now, s_next, u_now, u_next = s_next, s_now, u_next, u_now
            if step % 2 == 0:
                t_now, t_next = t_next, t_now

        for m in range(TEAM):
            base = halo + planes * (place ^ m)
            for j in range(planes):
                for t in range(2):
                    outs[m][2 * j + t] = t_now[at(base + j), t]
        for p in range(own):
            face_ref[p : p + 1, :] = t_now[at(halo + p), 0, 0:1, :]

    vmem = pl.BlockSpec(memory_space=pltpu.VMEM)
    field = pltpu.VMEM((span, 2, half, columns), F32)
    small = pltpu.VMEM((halo + 2, 2, half, columns), F32)
    return pl.pallas_call(
        kernel,
        out_shape=[jax.ShapeDtypeStruct((2 * planes, half, columns), F32)] * TEAM
        + [jax.ShapeDtypeStruct((own, columns), F32)],
        in_specs=[vmem] * 10,
        out_specs=[vmem] * (TEAM + 1),
        scratch_shapes=[small] * 8 + [field] * 6,
        compiler_params=pltpu.CompilerParams(vmem_limit_bytes=10 * MIB),
        cost_estimate=pl.CostEstimate(flops=0, bytes_accessed=16 * MIB, transcendentals=0),
        name="solve",
    )(*made, edge, far_halo)


def weigh(sums, faces, cells, after):
    slots = len(faces)
    samples, columns = sums[0].shape

    def kernel(*refs):
        sum_refs, refs = refs[: len(sums)], refs[len(sums) :]
        face_refs, (out_ref, moments_ref, weights) = refs[:slots], refs[slots + len(after) :]
        place = team_place()
        summed = sum_refs[0][...]
        for ref in sum_refs[1:]:
            summed = summed + ref[...]
        misfit = summed * (1.0 / (2.0 * cells))
        mean = jnp.sum(misfit, axis=0, keepdims=True) * (1.0 / samples)
        deviation = misfit - mean
        variance = jnp.sum(deviation * deviation, axis=0, keepdims=True) * (1.0 / samples)
        lane = lax.broadcasted_iota(jnp.int32, (1, columns), 1)
        moments_ref[...] = jnp.where(lane == 0, mean, variance)
        weights[...] = 1.0 + 2.0 * BETA_RISK * deviation
        total = weights[pl.ds(slots * place, 1), :] * face_refs[0][...]
        for n in range(1, slots):
            total = total + weights[pl.ds(slots * place + n, 1), :] * face_refs[n][...]
        out_ref[...] = total

    vmem = pl.BlockSpec(memory_space=pltpu.VMEM)
    return pl.pallas_call(
        kernel,
        out_shape=[
            jax.ShapeDtypeStruct(faces[0].shape, F32),
            jax.ShapeDtypeStruct((1, columns), F32),
        ],
        in_specs=[vmem] * (len(sums) + slots)
        + [pl.BlockSpec(memory_space=pl.ANY)] * len(after),
        out_specs=[vmem, vmem],
        scratch_shapes=[pltpu.VMEM((samples, columns), F32)],
        compiler_params=pltpu.CompilerParams(vmem_limit_bytes=2 * MIB),
        name="weigh",
    )(*sums, *faces, *after)


def gather_adjoint(pieces, planes):
    slots = len(pieces)
    _, half, columns = pieces[0][0].shape
    tiles = columns // 128
    block = (planes, 2 * half, columns)

    def kernel(*refs):
        blocks, out, mark, held, mixed, sems = refs[: slots * TEAM], *refs[slots * TEAM :]
        mark[...] = blocks[0][0, :, :LANES]
        place = team_place()
        copies = []
        for slot in range(slots):
            for m in range(TEAM):
                i = slot * TEAM + m
                for j in range(planes):
                    for t in range(2):
                        for c in range(tiles):
                            mixed[i % 2, j, c, pl.ds(t, half, stride=2), :] = blocks[i][
                                2 * j + t, :, c * 128 : (c + 1) * 128
                            ]
                    for c in range(tiles):
                        held[i, j, :, c * 128 : (c + 1) * 128] = mixed[i % 2, j, c]
                copy = pltpu.make_async_copy(
                    held.at[i], out.at[slots * (place ^ m) + slot], sems.at[i]
                )
                copy.start()
                copies.append(copy)
        for copy in copies:
            copy.wait()

    return pl.pallas_call(
        kernel,
        out_shape=[
            jax.ShapeDtypeStruct((slots * TEAM,) + block, F32),
            jax.ShapeDtypeStruct((half, LANES), F32),
        ],
        in_specs=[pl.BlockSpec(memory_space=pltpu.VMEM)] * (slots * TEAM),
        out_specs=[
            pl.BlockSpec(memory_space=pltpu.HBM),
            pl.BlockSpec(memory_space=pltpu.VMEM),
        ],
        scratch_shapes=[
            pltpu.VMEM((slots * TEAM,) + block, F32),
            pltpu.VMEM((2, planes, tiles, 2 * half, 128), F32),
            pltpu.SemaphoreType.DMA((slots * TEAM,)),
        ],
        compiler_params=pltpu.CompilerParams(vmem_limit_bytes=4 * MIB),
        cost_estimate=pl.CostEstimate(flops=0, bytes_accessed=4 * MIB, transcendentals=0),
        name="gather_adjoint",
    )(*[piece for group in pieces for piece in group])


def control(faces, radices, basis_z, basis_x, after):
    slabs, own_count, depth_total = basis_z.shape
    own, columns = faces[0].shape[1:]
    teams = depth_total // own

    def kernel(*refs):
        parts, (z_ref, x_ref, _, out_ref, whole) = refs[: len(faces)], refs[len(faces) :]
        rank = lax.axis_index("gz")
        team = rank // TEAM
        for n in range(teams):
            at, left, stride = 0, n, 1
            for radix in radices:
                digit = lax.rem(team // stride + left % radix, radix)
                at, left, stride = at + digit * stride, left // radix, stride * radix
            inner = teams // len(faces)
            whole[at] = parts[n // inner][n % inner]
        along_z = jnp.dot(
            z_ref[rank],
            whole[...].reshape(depth_total, columns),
            precision=lax.Precision.HIGHEST,
            preferred_element_type=F32,
        )
        high, low = in_halves(along_z)
        x_high, x_low = in_halves(x_ref[...])
        both = jnp.concatenate([high, low], axis=0)
        first = jnp.dot(both, x_high, preferred_element_type=F32)
        second = jnp.dot(high, x_low, preferred_element_type=F32)
        out_ref[...] = (first[:own_count] + first[own_count:]) + second

    vmem = pl.BlockSpec(memory_space=pltpu.VMEM)
    return pl.pallas_call(
        kernel,
        out_shape=jax.ShapeDtypeStruct((own_count, basis_x.shape[1]), F32),
        in_specs=[vmem] * (len(faces) + 2) + [pl.BlockSpec(memory_space=pl.ANY)],
        out_specs=vmem,
        scratch_shapes=[pltpu.VMEM((teams, own, columns), F32)],
        compiler_params=pltpu.CompilerParams(vmem_limit_bytes=8 * MIB),
        name="control",
    )(*faces, basis_z, basis_x, after)


def radices_of(teams):
    radices = []
    while teams > 1:
        radix = next(r for r in (4, 2, 3, *range(5, teams + 1)) if teams % r == 0)
        radices.append(radix)
        teams //= radix
    return radices


def on_device(state, target, rock_type, log_table, obs_scale):
    samples, planes, rows_y, columns = state.shape
    slabs = lax.axis_size("gz")
    slots = samples // TEAM
    depth_total = planes * slabs
    radices = radices_of(slabs // TEAM)

    def swap(value, m):
        return lax.ppermute(value, "gz", [(i, i ^ m) for i in range(slabs)])

    def along(value, outward):
        pairs = []
        for i in range(slabs):
            side = (i % TEAM) // 2
            to = i + TEAM if (side == 1) == outward else i - TEAM
            if 0 <= to < slabs:
                pairs.append((i, to))
        return lax.ppermute(value, "gz", pairs)

    def from_teams(value, stride, radix):
        heard = []
        for k in range(1, radix):
            pairs = []
            for i in range(slabs):
                digit = i // (TEAM * stride) % radix
                pairs.append((i + ((digit + k) % radix - digit) * stride * TEAM, i))
            heard.append(lax.ppermute(value, "gz", pairs))
        return heard

    fields = [
        pltpu.with_memory_space_constraint(field, pltpu.HBM)
        for field in (state, target, rock_type, log_table, obs_scale)
    ]
    size = 4 * planes
    jobs = [[(slot, m) for slot in range(slots)] for m in range(TEAM)]
    mine, theirs, sums = prepare(jobs[2:], fields, with_sums=True)
    theirs = swap(theirs, 1)
    first, sums = merge(mine, theirs, 0, size, add=sums)
    far = [swap(first, 2)]
    stride, teams = 1, slabs // TEAM
    while stride < teams:
        radix = next(r for r in range(2, teams + 1) if teams // stride % r == 0)
        sums = sum(from_teams(sums, stride, radix), sums)
        stride *= radix

    mine_near, theirs_near = prepare(jobs[:2], fields)
    theirs_near = swap(theirs_near, 1)
    near, near_halo = [], []
    for slot in range(slots):
        blocks, trimmed = merge_near(mine_near, theirs_near, slot, size, sums)
        near.append(blocks)
        near_halo.append(along(trimmed, True))
    for slot in range(1, slots):
        far.append(swap(merge(mine, theirs, slot, size, sums), 2))
    sums = [sums, far[-1][2 * size]]

    pieces, faces = [], []
    for slot in range(slots):
        far_halo = along(trim(far[slot], size), False)
        made, edge = prepare_planes(near[slot], far[slot], near_halo[slot], planes, faces[-1:])
        solved = solve(made, edge, far_halo, planes)
        pieces.append([solved[0]] + [swap(solved[m], m) for m in (1, 2, 3)])
        faces.append(solved[TEAM])

    face, moments = weigh(sums, faces, depth_total * rows_y * columns, pieces[0][1:])
    heard = [sum((swap(face, m) for m in (2, 3, 1)), face)[None]]
    stride = 1
    for radix in radices:
        held = heard[0] if len(heard) == 1 else jnp.concatenate(heard)
        heard = [held] + from_teams(held, stride, radix)
        stride *= radix
    adjoint, mark = gather_adjoint(pieces, planes)
    own_count = MA // slabs
    gradient = control(
        heard,
        radices,
        jnp.asarray(cosine_basis(depth_total, MA).T.reshape(slabs, own_count, depth_total)),
        jnp.asarray(cosine_basis(columns, MB)),
        mark,
    )
    return (adjoint, gradient, moments[0, :2])


def solution(mesh):
    return jax.shard_map(
        on_device,
        mesh=mesh,
        in_specs=(
            P("parts", "gz", None, None),
            P(("parts", "gz"), None, None),
            P("parts", "gz", None, None),
            P("parts", None),
            P("parts"),
        ),
        out_specs=(P("parts", "gz", None, None), P(("parts", "gz"), None), P("parts")),
        check_vma=False,
    )
```

```python
import math

import jax
import jax.numpy as jnp
import numpy as np
from jax import lax
from jax.experimental import pallas as pl
from jax.experimental.pallas import tpu as pltpu
from jax.sharding import PartitionSpec as P

NR = 8
DEGREE = 4
SWEEPS = 2
MA = 512
MB = 512

STORAGE = 0.05
BETA_RISK = 0.5
LOWER_EIGEN = 0.05
UPPER_EIGEN = 2.0

TEAM = 4
STEPS = DEGREE * SWEEPS
F32 = jnp.float32
MIB = 1024 * 1024
LANES = 128
OUT_ORDER = (0, 2, 3, 1)


def chebyshev_constants(number_steps):
    centre = (UPPER_EIGEN + LOWER_EIGEN) / 2
    spread = (UPPER_EIGEN - LOWER_EIGEN) / 2
    quotient = centre / spread
    rho_now = 1.0 / quotient
    coefficients = []
    for position in range(number_steps):
        rho_next = 1.0 / (2.0 * quotient - rho_now)
        coefficients.append((rho_next * rho_now, 2.0 * rho_next / spread))
        rho_now = rho_next
    return (centre, coefficients)


def cosine_basis(length_total, modes):
    positions = np.arange(length_total, dtype=np.int64)
    mode_index = np.arange(modes, dtype=np.int64)
    product_index = ((2 * positions[:, None] + 1) * (2 * mode_index[None, :] + 1)) % (
        8 * length_total
    )
    angle = product_index.astype(np.float64) * (math.pi / (4 * length_total))
    return (math.sqrt(2.0 / length_total) * np.cos(angle)).astype(np.float32)


def in_halves(values):
    high = values.astype(jnp.bfloat16)
    return high, (values - high.astype(F32)).astype(jnp.bfloat16)


def team_place():
    return lax.rem(lax.axis_index("gz"), TEAM)


def prepare(jobs, fields, with_sums=False):
    state, target, rock_type, log_table, obs_scale = fields
    samples, planes, rows_y, columns = state.shape
    slots = samples // TEAM
    block = (planes, rows_y, columns)
    half, tiles = rows_y // 2, columns // 128
    size = 2 * 2 * planes
    depth_total = planes * lax.axis_size("gz")
    flat = [(o, i, job) for o, group in enumerate(jobs) for i, job in enumerate(group)]
    count = len(flat)
    shapes = [(len(group) * size + with_sums, half, columns) for group in jobs]
    states = samples if with_sums else count

    def kernel(*refs):
        (table_ref, scale_ref, state_ref, target_ref, rock_ref), refs = refs[:5], refs[5:]
        outs, refs = refs[: len(jobs)], refs[len(jobs) :]
        if with_sums:
            sums_ref, refs = refs[0], refs[1:]
        table, scale, state_buf, rock_buf, target_buf, mixed, sems = refs
        place = team_place()
        first_plane = lax.axis_index("gz") * planes
        members = [slots * (place ^ m) + slot for _, _, (slot, m) in flat]
        small = [
            pltpu.make_async_copy(table_ref, table, sems.at[2, 0]),
            pltpu.make_async_copy(scale_ref, scale, sems.at[2, 1]),
            pltpu.make_async_copy(target_ref, target_buf, sems.at[2, 2]),
        ]
        for copy in small:
            copy.start()
        rocks = [
            pltpu.make_async_copy(rock_ref.at[member], rock_buf.at[n], sems.at[1, n])
            for n, member in enumerate(members)
        ]
        loads = [
            pltpu.make_async_copy(
                state_ref.at[n if with_sums else members[n]], state_buf.at[n], sems.at[0, n]
            )
            for n in range(states)
        ]
        for copy in rocks + loads:
            copy.start()
        depth_weights = [
            1.0 + (2.0 / (depth_total - 1)) * (first_plane + p).astype(F32) for p in range(planes)
        ]
        for copy in small:
            copy.wait()
        if with_sums:
            for copy in loads:
                copy.wait()
            for n in range(samples):
                total = jnp.zeros((8, columns), F32)
                for p in range(planes):
                    part = jnp.zeros((8, columns), F32)
                    for first in range(0, rows_y, 8):
                        rows = slice(first, first + 8)
                        gap = state_buf[n, p, rows] - target_buf[p, rows]
                        part = part + gap * gap
                    total = total + (scale[n] * depth_weights[p]) * part
                summed = jnp.sum(total, keepdims=True)
                sums_ref[n : n + 1, :] = jnp.broadcast_to(summed, (1, columns))
        for n, (o, i, _) in enumerate(flat):
            rocks[n].wait()
            if not with_sums:
                loads[n].wait()
            member = members[n]
            own_state = member if with_sums else n
            values = [
                jnp.exp(jnp.full((8, columns), -table[member, code], F32)) for code in range(NR)
            ]
            for p in range(planes):
                factor = scale[member] * depth_weights[p]
                for first in range(0, rows_y, 8):
                    rows = slice(first, first + 8)
                    codes = rock_buf[n, p, rows]
                    low, mid, high = ((codes & bit) != 0 for bit in (1, 2, 4))
                    pairs = [
                        jnp.where(low, values[2 * k + 1], values[2 * k]) for k in range(NR // 2)
                    ]
                    halves = [jnp.where(mid, pairs[2 * k + 1], pairs[2 * k]) for k in range(2)]
                    gap = state_buf[own_state, p, rows] - target_buf[p, rows]
                    made = (jnp.where(high, halves[1], halves[0]), factor * gap)
                    for a in range(2):
                        for c in range(tiles):
                            mixed[n % 2, p, a, c, rows] = made[a][:, c * 128 : (c + 1) * 128]
                for a in range(2):
                    for t in range(2):
                        for c in range(tiles):
                            at = i * size + (a * planes + p) * 2 + t
                            outs[o][at, :, c * 128 : (c + 1) * 128] = mixed[
                                n % 2, p, a, c, pl.ds(t, half, stride=2), :
                            ]
        for o, group in enumerate(jobs if with_sums else []):
            outs[o][len(group) * size] = sums_ref[...]

    hbm = pl.BlockSpec(memory_space=pltpu.HBM)
    vmem = pl.BlockSpec(memory_space=pltpu.VMEM)
    return pl.pallas_call(
        kernel,
        out_shape=[jax.ShapeDtypeStruct(shape, F32) for shape in shapes]
        + [jax.ShapeDtypeStruct((samples, columns), F32)] * with_sums,
        in_specs=[hbm] * 5,
        out_specs=[vmem] * (len(shapes) + with_sums),
        scratch_shapes=[
            pltpu.SMEM(log_table.shape, F32),
            pltpu.SMEM(obs_scale.shape, F32),
            pltpu.VMEM((states,) + block, F32),
            pltpu.VMEM((count,) + block, jnp.int32),
            pltpu.VMEM(block, F32),
            pltpu.VMEM((2, planes, 2, tiles, rows_y, 128), F32),
            pltpu.SemaphoreType.DMA((3, max(states, 3))),
        ],
        compiler_params=pltpu.CompilerParams(vmem_limit_bytes=6 * MIB),
        cost_estimate=pl.CostEstimate(flops=0, bytes_accessed=count * MIB, transcendentals=0),
        name="prepare",
    )(log_table, obs_scale, state, target, rock_type)


def merge(mine, theirs, slot, size, behind=None, add=None):
    given = [value for value in (behind, add) if value is not None]

    def kernel(mine_ref, theirs_ref, *refs):
        core = lax.rem(team_place(), 2)
        tail, (out_ref, *more) = refs[: len(given)], refs[len(given) :]
        for ref, at in ((mine_ref, core), (theirs_ref, 1 - core)):
            for n in range(size):
                out_ref[at * size + n] = ref[slot * size + n]
        if behind is not None:
            out_ref[2 * size] = tail[0][...]
        if add is not None:
            more[0][...] = tail[-1][...] + theirs_ref[theirs.shape[0] - 1]

    vmem = pl.BlockSpec(memory_space=pltpu.VMEM)
    tile = mine.shape[1:]
    outs = pl.pallas_call(
        kernel,
        out_shape=[jax.ShapeDtypeStruct((2 * size + (behind is not None),) + tile, F32)]
        + [jax.ShapeDtypeStruct(tile, F32)] * (add is not None),
        in_specs=[vmem] * (2 + len(given)),
        out_specs=[vmem] * (1 + (add is not None)),
        compiler_params=pltpu.CompilerParams(vmem_limit_bytes=4 * MIB),
        name="merge",
    )(mine, theirs, *given)
    return outs if add is not None else outs[0]


def copy_trimmed(ref, out_ref, size, below):
    part = size // 2
    for core in range(2):
        for n in range(part):
            out_ref[core * part + n] = ref[core * size + n]
    for n in range(size - 2):
        at = n + jnp.where(below, 2, 0)
        out_ref[size + n] = ref[(at // part) * size + part + lax.rem(at, part)]


def trim(blocks, size):
    def kernel(ref, out_ref):
        copy_trimmed(ref, out_ref, size, team_place() < 2)

    vmem = pl.BlockSpec(memory_space=pltpu.VMEM)
    return pl.pallas_call(
        kernel,
        out_shape=jax.ShapeDtypeStruct((2 * size - 2,) + blocks.shape[1:], F32),
        in_specs=[vmem],
        out_specs=vmem,
        compiler_params=pltpu.CompilerParams(vmem_limit_bytes=4 * MIB),
        name="trim",
    )(blocks)


def merge_near(mine, theirs, slot, size, after):
    tile = mine.shape[1:]

    def kernel(mine_ref, theirs_ref, _, out_ref, trimmed_ref):
        core = lax.rem(team_place(), 2)
        for ref, at in ((mine_ref, core), (theirs_ref, 1 - core)):
            for n in range(size):
                out_ref[at * size + n] = ref[slot * size + n]
        copy_trimmed(out_ref, trimmed_ref, size, team_place() >= 2)

    vmem = pl.BlockSpec(memory_space=pltpu.VMEM)
    return pl.pallas_call(
        kernel,
        out_shape=[
            jax.ShapeDtypeStruct((2 * size,) + tile, F32),
            jax.ShapeDtypeStruct((2 * size - 2,) + tile, F32),
        ],
        in_specs=[vmem] * 2 + [pl.BlockSpec(memory_space=pl.ANY)],
        out_specs=[vmem] * 2,
        compiler_params=pltpu.CompilerParams(vmem_limit_bytes=4 * MIB),
        name="merge_near",
    )(mine, theirs, after)


def reciprocal(x):
    guess = pl.reciprocal(x, approx=True)
    return guess * (2.0 - x * guess)


def harmonic(a, b):
    x = a + b
    guess = pl.reciprocal(x, approx=True)
    return guess * (4.0 - (2.0 * x) * guess)


def each(start, stop, body, width):
    whole = (stop - start) // width

    def group(n, carry):
        for k in range(width):
            body(start + n * width + k)
        return carry

    lax.fori_loop(0, whole, group, 0)
    for p in range(start + whole * width, stop):
        body(p)


def ahead_x(v):
    return pltpu.roll(v, v.shape[1] - 1, 1)


def behind_x(v):
    return pltpu.roll(v, 1, 1)


def ahead_y(v):
    return pltpu.roll(v, v.shape[0] - 1, 0)


def behind_y(v):
    return pltpu.roll(v, 1, 0)


def set_up(planes, conductance, source, store):
    centre, _ = chebyshev_constants(DEGREE)
    here = [conductance(planes[0], t) for t in range(2)]
    half, columns = here[0].shape
    last_row = lax.broadcasted_iota(jnp.int32, (half, columns), 0) == half - 1
    last_column = lax.broadcasted_iota(jnp.int32, (half, columns), 1) == columns - 1
    w_below = [harmonic(conductance(planes[0] - 1, t), here[t]) for t in range(2)]
    for p in planes:
        above = [conductance(p + 1, t) for t in range(2)]
        even, odd = here
        w_pair = harmonic(even, odd)
        w_next = jnp.where(last_row, 0.0, harmonic(odd, ahead_y(even)))
        w_above = [harmonic(here[t], above[t]) for t in range(2)]
        for t in range(2):
            w_y = w_next if t else w_pair
            w_y_behind = w_pair if t else behind_y(w_next)
            w_x = jnp.where(last_column, 0.0, harmonic(here[t], ahead_x(here[t])))
            w_x_behind = behind_x(w_x)
            diagonal = (w_above[t] + w_below[t]) + (w_y + w_y_behind) + (w_x + w_x_behind) + STORAGE
            inverse = reciprocal(diagonal)
            weights = (w_above[t], w_below[t], w_y, w_y_behind, w_x, w_x_behind)
            scaled = source(p, t) * inverse
            store(p, t, [w * inverse for w in weights] + [scaled, scaled * (1.0 / centre)])
        here, w_below = above, w_above


def outside(v):
    return jnp.where(v > 0.0, v, 1e30)


def prepare_planes(near, far, near_halo, planes, after):
    half, columns = far.shape[-2:]
    halo, own, part = 2 * planes, TEAM * planes, 2 * planes
    span = own + 2 * halo
    first, count = halo + 1, own + halo - 2

    def kernel(near_ref, halo_ref, far_ref, *refs):
        refs = refs[len(after) :]
        outs, edge_ref, (cond, start) = refs[:8], refs[8], refs[9:]
        side = team_place() // 2

        def place(natural):
            return jnp.where(side == 0, natural, span - 1 - natural) - halo

        for core in range(2):
            for n in range(part):
                base = halo + planes * core + n // 2
                for ref, at in ((near_ref, base + part * side), (far_ref, base + part * (1 - side))):
                    cond[place(at), n % 2] = ref[core * 2 * part + n]
                    start[place(at), n % 2] = ref[(core * 2 + 1) * part + n]
        near_base = jnp.where(side == 0, halo + own, 0)
        for n in range(2 * part):
            cond[place(near_base + n // 2), n % 2] = outside(halo_ref[n])
        for n in range(2 * part - 2):
            start[place(near_base + side + n // 2), n % 2] = halo_ref[2 * part + n]
        for p in range(2):
            for t in range(2):
                edge_ref[0, p, t] = cond[p, t]
                edge_ref[1, p, t] = start[p, t]

        width = count // 2

        def group(n, carry):
            begin = 1 + n * width

            def store(p, t, values):
                for ref, value in zip(outs, values):
                    ref[p - 1, t] = value

            set_up(
                [begin + k for k in range(width)],
                lambda p, t: cond[p, t],
                lambda p, t: start[p, t],
                store,
            )
            return carry

        lax.fori_loop(0, 2, group, 0)

    assert count % 2 == 0
    vmem = pl.BlockSpec(memory_space=pltpu.VMEM)
    results = pl.pallas_call(
        kernel,
        out_shape=[jax.ShapeDtypeStruct((count, 2, half, columns), F32)] * 8
        + [jax.ShapeDtypeStruct((2, 2, 2, half, columns), F32)],
        in_specs=[vmem] * 3 + [pl.BlockSpec(memory_space=pl.ANY)] * len(after),
        out_specs=[vmem] * 9,
        scratch_shapes=[pltpu.VMEM((own + halo, 2, half, columns), F32)] * 2,
        compiler_params=pltpu.CompilerParams(vmem_limit_bytes=4 * MIB),
        cost_estimate=pl.CostEstimate(flops=0, bytes_accessed=8 * MIB, transcendentals=0),
        name="prepare_planes",
    )(near, near_halo, far, *after)
    return results[:8], results[8]


def solve(made, edge, far_halo, planes):
    half, columns = far_halo.shape[-2:]
    halo, own, part = 2 * planes, TEAM * planes, 2 * planes
    span = own + 2 * halo
    cut = halo + 1
    centre, coefficients = chebyshev_constants(DEGREE)
    assert halo >= STEPS

    def kernel(*refs):
        high, (edge_ref, halo_ref), refs = refs[:8], refs[8:10], refs[10:]
        outs, face_ref, refs = refs[:TEAM], refs[TEAM], refs[TEAM + 1 :]
        low, (cond, start, u_a, u_b, s_a, s_b, t_a, t_b) = refs[:6], refs[6:]
        place = team_place()
        side = place // 2

        def at(natural):
            return jnp.where(side == 0, natural, span - 1 - natural)

        far_base = jnp.where(side == 0, 0, halo + own)
        for n in range(2 * part):
            cond[at(far_base + n // 2), n % 2] = outside(halo_ref[n])
        for n in range(2 * part - 2):
            start[at(far_base + (1 - side) + n // 2), n % 2] = halo_ref[2 * part + n]
        for p in range(2):
            for t in range(2):
                cond[halo + p, t] = edge_ref[0, p, t]
                start[halo + p, t] = edge_ref[1, p, t]

        def store(p, t, values):
            for ref, value in zip((*low, u_a, s_a), values):
                ref[p, t] = value

        set_up(range(1, cut), lambda p, t: cond[p, t], lambda p, t: start[p, t], store)
        for p in range(cut, span - 1):
            for t in range(2):
                u_a[p, t] = high[6][p - cut, t]
                s_a[p, t] = high[7][p - cut, t]

        s_now, s_next, u_now, u_next, t_now, t_next = s_a, s_b, u_a, u_b, t_a, t_b
        for step in range(STEPS - 1):
            position = step % DEGREE
            if position + 1 < DEGREE:
                keep, mix = coefficients[position]
            else:
                keep, mix = 0.0, 1.0 / centre
            last = step == STEPS - 2

            def advance(p, fields, first):
                zp, zm, yp, ym, xp, xm = fields
                q = p - first
                even, odd = s_now[p, 0], s_now[p, 1]
                for t, s in enumerate((even, odd)):
                    ahead = ahead_y(even) if t else odd
                    behind = even if t else behind_y(odd)
                    moved = zp[q, t] * s_now[p + 1, t] + zm[q, t] * s_now[p - 1, t]
                    moved += yp[q, t] * ahead + ym[q, t] * behind
                    moved += xp[q, t] * ahead_x(s) + xm[q, t] * behind_x(s)
                    new_u = (u_now[p, t] - s) + moved
                    new_s = mix * new_u if keep == 0.0 else keep * s + mix * new_u
                    if not last:
                        u_next[p, t] = new_u
                        s_next[p, t] = new_s
                    if step == 0:
                        t_next[p, t] = s + new_s
                    elif step % 2 == 0:
                        t_next[p, t] = t_now[p, t] + (s + new_s)

            margin = halo - (STEPS - 2 - step)
            each(cut, span - margin, lambda p: advance(p, high[:6], cut), 8)
            each(margin, cut, lambda p: advance(p, low, 0), 8)
            s_now, s_next, u_now, u_next = s_next, s_now, u_next, u_now
            if step % 2 == 0:
                t_now, t_next = t_next, t_now

        for m in range(TEAM):
            base = halo + planes * (place ^ m)
            for j in range(planes):
                for t in range(2):
                    outs[m][2 * j + t] = t_now[at(base + j), t]
        for p in range(own):
            face_ref[p : p + 1, :] = t_now[at(halo + p), 0, 0:1, :]

    vmem = pl.BlockSpec(memory_space=pltpu.VMEM)
    field = pltpu.VMEM((span, 2, half, columns), F32)
    small = pltpu.VMEM((halo + 2, 2, half, columns), F32)
    return pl.pallas_call(
        kernel,
        out_shape=[jax.ShapeDtypeStruct((2 * planes, half, columns), F32)] * TEAM
        + [jax.ShapeDtypeStruct((own, columns), F32)],
        in_specs=[vmem] * 10,
        out_specs=[vmem] * (TEAM + 1),
        scratch_shapes=[small] * 8 + [field] * 6,
        compiler_params=pltpu.CompilerParams(vmem_limit_bytes=10 * MIB),
        cost_estimate=pl.CostEstimate(flops=0, bytes_accessed=16 * MIB, transcendentals=0),
        name="solve",
    )(*made, edge, far_halo)


def weigh(sums, faces, cells, after):
    slots = len(faces)
    samples, columns = sums[0].shape

    def kernel(*refs):
        sum_refs, refs = refs[: len(sums)], refs[len(sums) :]
        face_refs, (out_ref, moments_ref, weights) = refs[:slots], refs[slots + len(after) :]
        place = team_place()
        summed = sum_refs[0][...]
        for ref in sum_refs[1:]:
            summed = summed + ref[...]
        misfit = summed * (1.0 / (2.0 * cells))
        mean = jnp.sum(misfit, axis=0, keepdims=True) * (1.0 / samples)
        deviation = misfit - mean
        variance = jnp.sum(deviation * deviation, axis=0, keepdims=True) * (1.0 / samples)
        lane = lax.broadcasted_iota(jnp.int32, (1, columns), 1)
        moments_ref[...] = jnp.where(lane == 0, mean, variance)
        weights[...] = 1.0 + 2.0 * BETA_RISK * deviation
        total = weights[pl.ds(slots * place, 1), :] * face_refs[0][...]
        for n in range(1, slots):
            total = total + weights[pl.ds(slots * place + n, 1), :] * face_refs[n][...]
        out_ref[...] = total

    vmem = pl.BlockSpec(memory_space=pltpu.VMEM)
    return pl.pallas_call(
        kernel,
        out_shape=[
            jax.ShapeDtypeStruct(faces[0].shape, F32),
            jax.ShapeDtypeStruct((1, columns), F32),
        ],
        in_specs=[vmem] * (len(sums) + slots)
        + [pl.BlockSpec(memory_space=pl.ANY)] * len(after),
        out_specs=[vmem, vmem],
        scratch_shapes=[pltpu.VMEM((samples, columns), F32)],
        compiler_params=pltpu.CompilerParams(vmem_limit_bytes=2 * MIB),
        name="weigh",
    )(*sums, *faces, *after)


def gather_adjoint(pieces, planes):
    slots = len(pieces)
    _, half, columns = pieces[0][0].shape
    tiles = columns // 128
    block = (planes, 2 * half, columns)

    def kernel(*refs):
        blocks, out, mark, held, mixed, sems = refs[: slots * TEAM], *refs[slots * TEAM :]
        mark[...] = blocks[0][0, :, :LANES]
        place = team_place()
        copies = []
        for slot in range(slots):
            for n, m in enumerate(OUT_ORDER):
                i = slot * TEAM + n
                for j in range(planes):
                    for t in range(2):
                        for c in range(tiles):
                            mixed[i % 2, j, c, pl.ds(t, half, stride=2), :] = blocks[i][
                                2 * j + t, :, c * 128 : (c + 1) * 128
                            ]
                    for c in range(tiles):
                        held[i, j, :, c * 128 : (c + 1) * 128] = mixed[i % 2, j, c]
                copy = pltpu.make_async_copy(
                    held.at[i], out.at[slots * (place ^ m) + slot], sems.at[i]
                )
                copy.start()
                copies.append(copy)
        for copy in copies:
            copy.wait()

    return pl.pallas_call(
        kernel,
        out_shape=[
            jax.ShapeDtypeStruct((slots * TEAM,) + block, F32),
            jax.ShapeDtypeStruct((half, LANES), F32),
        ],
        in_specs=[pl.BlockSpec(memory_space=pltpu.VMEM)] * (slots * TEAM),
        out_specs=[
            pl.BlockSpec(memory_space=pltpu.HBM),
            pl.BlockSpec(memory_space=pltpu.VMEM),
        ],
        scratch_shapes=[
            pltpu.VMEM((slots * TEAM,) + block, F32),
            pltpu.VMEM((2, planes, tiles, 2 * half, 128), F32),
            pltpu.SemaphoreType.DMA((slots * TEAM,)),
        ],
        compiler_params=pltpu.CompilerParams(vmem_limit_bytes=4 * MIB),
        cost_estimate=pl.CostEstimate(flops=0, bytes_accessed=4 * MIB, transcendentals=0),
        name="gather_adjoint",
    )(*[group[m] for group in pieces for m in OUT_ORDER])


def control(faces, radices, basis_z, basis_x, after):
    slabs, own_count, depth_total = basis_z.shape
    own, columns = faces[0].shape[1:]
    teams = depth_total // own

    def kernel(*refs):
        parts, (z_ref, x_ref, _, out_ref, whole) = refs[: len(faces)], refs[len(faces) :]
        rank = lax.axis_index("gz")
        team = rank // TEAM
        for n in range(teams):
            at, left, stride = 0, n, 1
            for radix in radices:
                digit = lax.rem(team // stride + left % radix, radix)
                at, left, stride = at + digit * stride, left // radix, stride * radix
            inner = teams // len(faces)
            whole[at] = parts[n // inner][n % inner]
        along_z = jnp.dot(
            z_ref[rank],
            whole[...].reshape(depth_total, columns),
            precision=lax.Precision.HIGHEST,
            preferred_element_type=F32,
        )
        high, low = in_halves(along_z)
        x_high, x_low = in_halves(x_ref[...])
        both = jnp.concatenate([high, low], axis=0)
        first = jnp.dot(both, x_high, preferred_element_type=F32)
        second = jnp.dot(high, x_low, preferred_element_type=F32)
        out_ref[...] = (first[:own_count] + first[own_count:]) + second

    vmem = pl.BlockSpec(memory_space=pltpu.VMEM)
    return pl.pallas_call(
        kernel,
        out_shape=jax.ShapeDtypeStruct((own_count, basis_x.shape[1]), F32),
        in_specs=[vmem] * (len(faces) + 2) + [pl.BlockSpec(memory_space=pl.ANY)],
        out_specs=vmem,
        scratch_shapes=[pltpu.VMEM((teams, own, columns), F32)],
        compiler_params=pltpu.CompilerParams(vmem_limit_bytes=8 * MIB),
        name="control",
    )(*faces, basis_z, basis_x, after)


def radices_of(teams):
    radices = []
    while teams > 1:
        radix = next(r for r in (4, 2, 3, *range(5, teams + 1)) if teams % r == 0)
        radices.append(radix)
        teams //= radix
    return radices


def on_device(state, target, rock_type, log_table, obs_scale):
    samples, planes, rows_y, columns = state.shape
    slabs = lax.axis_size("gz")
    slots = samples // TEAM
    depth_total = planes * slabs
    radices = radices_of(slabs // TEAM)

    def swap(value, m):
        return lax.ppermute(value, "gz", [(i, i ^ m) for i in range(slabs)])

    def along(value, outward):
        pairs = []
        for i in range(slabs):
            side = (i % TEAM) // 2
            to = i + TEAM if (side == 1) == outward else i - TEAM
            if 0 <= to < slabs:
                pairs.append((i, to))
        return lax.ppermute(value, "gz", pairs)

    def from_teams(value, stride, radix):
        heard = []
        for k in range(1, radix):
            pairs = []
            for i in range(slabs):
                digit = i // (TEAM * stride) % radix
                pairs.append((i + ((digit + k) % radix - digit) * stride * TEAM, i))
            heard.append(lax.ppermute(value, "gz", pairs))
        return heard

    fields = [
        pltpu.with_memory_space_constraint(field, pltpu.HBM)
        for field in (state, target, rock_type, log_table, obs_scale)
    ]
    size = 4 * planes
    jobs = [[(slot, m) for slot in range(slots)] for m in range(TEAM)]
    mine, theirs, sums = prepare(jobs[2:], fields, with_sums=True)
    theirs = swap(theirs, 1)
    first, sums = merge(mine, theirs, 0, size, add=sums)
    far = [swap(first, 2)]
    stride, teams = 1, slabs // TEAM
    while stride < teams:
        radix = next(r for r in range(2, teams + 1) if teams // stride % r == 0)
        sums = sum(from_teams(sums, stride, radix), sums)
        stride *= radix

    mine_near, theirs_near = prepare(jobs[:2], fields)
    theirs_near = swap(theirs_near, 1)
    near, near_halo = [], []
    for slot in range(slots):
        blocks, trimmed = merge_near(mine_near, theirs_near, slot, size, sums)
        near.append(blocks)
        near_halo.append(along(trimmed, True))
    for slot in range(1, slots):
        far.append(swap(merge(mine, theirs, slot, size, sums), 2))
    sums = [sums, far[-1][2 * size]]

    pieces, faces = [], []
    for slot in range(slots):
        far_halo = along(trim(far[slot], size), False)
        made, edge = prepare_planes(near[slot], far[slot], near_halo[slot], planes, faces[-1:])
        solved = solve(made, edge, far_halo, planes)
        pieces.append([solved[0]] + [swap(solved[m], m) for m in (1, 2, 3)])
        faces.append(solved[TEAM])

    face, moments = weigh(sums, faces, depth_total * rows_y * columns, pieces[0][1:])
    heard = [sum((swap(face, m) for m in (2, 3, 1)), face)[None]]
    stride = 1
    for radix in radices:
        held = heard[0] if len(heard) == 1 else jnp.concatenate(heard)
        heard = [held] + from_teams(held, stride, radix)
        stride *= radix
    adjoint, mark = gather_adjoint(pieces, planes)
    own_count = MA // slabs
    gradient = control(
        heard,
        radices,
        jnp.asarray(cosine_basis(depth_total, MA).T.reshape(slabs, own_count, depth_total)),
        jnp.asarray(cosine_basis(columns, MB)),
        mark,
    )
    return (adjoint, gradient, moments[0, :2])


def solution(mesh):
    return jax.shard_map(
        on_device,
        mesh=mesh,
        in_specs=(
            P("parts", "gz", None, None),
            P(("parts", "gz"), None, None),
            P("parts", "gz", None, None),
            P("parts", None),
            P("parts"),
        ),
        out_specs=(P("parts", "gz", None, None), P(("parts", "gz"), None), P("parts")),
        check_vma=False,
    )
```

```python
import math

import jax
import jax.numpy as jnp
import numpy as np
from jax import lax
from jax.experimental import pallas as pl
from jax.experimental.pallas import tpu as pltpu
from jax.sharding import PartitionSpec as P

NR = 8
DEGREE = 4
SWEEPS = 2
MA = 512
MB = 512

STORAGE = 0.05
BETA_RISK = 0.5
LOWER_EIGEN = 0.05
UPPER_EIGEN = 2.0

TEAM = 4
STEPS = DEGREE * SWEEPS
F32 = jnp.float32
MIB = 1024 * 1024
LANES = 128


def chebyshev_constants(number_steps):
    centre = (UPPER_EIGEN + LOWER_EIGEN) / 2
    spread = (UPPER_EIGEN - LOWER_EIGEN) / 2
    quotient = centre / spread
    rho_now = 1.0 / quotient
    coefficients = []
    for position in range(number_steps):
        rho_next = 1.0 / (2.0 * quotient - rho_now)
        coefficients.append((rho_next * rho_now, 2.0 * rho_next / spread))
        rho_now = rho_next
    return (centre, coefficients)


def cosine_basis(length_total, modes):
    positions = np.arange(length_total, dtype=np.int64)
    mode_index = np.arange(modes, dtype=np.int64)
    product_index = ((2 * positions[:, None] + 1) * (2 * mode_index[None, :] + 1)) % (
        8 * length_total
    )
    angle = product_index.astype(np.float64) * (math.pi / (4 * length_total))
    return (math.sqrt(2.0 / length_total) * np.cos(angle)).astype(np.float32)


def in_halves(values):
    high = values.astype(jnp.bfloat16)
    return high, (values - high.astype(F32)).astype(jnp.bfloat16)


def team_place():
    return lax.rem(lax.axis_index("gz"), TEAM)


def prepare(jobs, fields, with_sums=False):
    state, target, rock_type, log_table, obs_scale = fields
    samples, planes, rows_y, columns = state.shape
    slots = samples // TEAM
    block = (planes, rows_y, columns)
    half, tiles = rows_y // 2, columns // 128
    size = 2 * 2 * planes
    depth_total = planes * lax.axis_size("gz")
    flat = [(o, i, job) for o, group in enumerate(jobs) for i, job in enumerate(group)]
    count = len(flat)
    shapes = [(len(group) * size + with_sums, half, columns) for group in jobs]
    states = samples if with_sums else count

    def kernel(*refs):
        (table_ref, scale_ref, state_ref, target_ref, rock_ref), refs = refs[:5], refs[5:]
        outs, refs = refs[: len(jobs)], refs[len(jobs) :]
        if with_sums:
            sums_ref, refs = refs[0], refs[1:]
        table, scale, state_buf, rock_buf, target_buf, mixed, sems = refs
        place = team_place()
        first_plane = lax.axis_index("gz") * planes
        members = [slots * (place ^ m) + slot for _, _, (slot, m) in flat]
        small = [
            pltpu.make_async_copy(table_ref, table, sems.at[2, 0]),
            pltpu.make_async_copy(scale_ref, scale, sems.at[2, 1]),
            pltpu.make_async_copy(target_ref, target_buf, sems.at[2, 2]),
        ]
        for copy in small:
            copy.start()
        rocks = [
            pltpu.make_async_copy(rock_ref.at[member], rock_buf.at[n], sems.at[1, n])
            for n, member in enumerate(members)
        ]
        loads = [
            pltpu.make_async_copy(
                state_ref.at[n if with_sums else members[n]], state_buf.at[n], sems.at[0, n]
            )
            for n in range(states)
        ]
        for copy in rocks + loads:
            copy.start()
        depth_weights = [
            1.0 + (2.0 / (depth_total - 1)) * (first_plane + p).astype(F32) for p in range(planes)
        ]
        for copy in small:
            copy.wait()
        if with_sums:
            for copy in loads:
                copy.wait()
            for n in range(samples):
                total = jnp.zeros((8, columns), F32)
                for p in range(planes):
                    part = jnp.zeros((8, columns), F32)
                    for first in range(0, rows_y, 8):
                        rows = slice(first, first + 8)
                        gap = state_buf[n, p, rows] - target_buf[p, rows]
                        part = part + gap * gap
                    total = total + (scale[n] * depth_weights[p]) * part
                summed = jnp.sum(total, keepdims=True)
                sums_ref[n : n + 1, :] = jnp.broadcast_to(summed, (1, columns))
        for n, (o, i, _) in enumerate(flat):
            rocks[n].wait()
            if not with_sums:
                loads[n].wait()
            member = members[n]
            own_state = member if with_sums else n
            values = [
                jnp.exp(jnp.full((8, columns), -table[member, code], F32)) for code in range(NR)
            ]
            for p in range(planes):
                factor = scale[member] * depth_weights[p]
                for first in range(0, rows_y, 8):
                    rows = slice(first, first + 8)
                    codes = rock_buf[n, p, rows]
                    low, mid, high = ((codes & bit) != 0 for bit in (1, 2, 4))
                    pairs = [
                        jnp.where(low, values[2 * k + 1], values[2 * k]) for k in range(NR // 2)
                    ]
                    halves = [jnp.where(mid, pairs[2 * k + 1], pairs[2 * k]) for k in range(2)]
                    gap = state_buf[own_state, p, rows] - target_buf[p, rows]
                    made = (jnp.where(high, halves[1], halves[0]), factor * gap)
                    for a in range(2):
                        for c in range(tiles):
                            mixed[n % 2, p, a, c, rows] = made[a][:, c * 128 : (c + 1) * 128]
                for a in range(2):
                    for t in range(2):
                        for c in range(tiles):
                            at = i * size + (a * planes + p) * 2 + t
                            outs[o][at, :, c * 128 : (c + 1) * 128] = mixed[
                                n % 2, p, a, c, pl.ds(t, half, stride=2), :
                            ]
        for o, group in enumerate(jobs if with_sums else []):
            outs[o][len(group) * size] = sums_ref[...]

    hbm = pl.BlockSpec(memory_space=pltpu.HBM)
    vmem = pl.BlockSpec(memory_space=pltpu.VMEM)
    return pl.pallas_call(
        kernel,
        out_shape=[jax.ShapeDtypeStruct(shape, F32) for shape in shapes]
        + [jax.ShapeDtypeStruct((samples, columns), F32)] * with_sums,
        in_specs=[hbm] * 5,
        out_specs=[vmem] * (len(shapes) + with_sums),
        scratch_shapes=[
            pltpu.SMEM(log_table.shape, F32),
            pltpu.SMEM(obs_scale.shape, F32),
            pltpu.VMEM((states,) + block, F32),
            pltpu.VMEM((count,) + block, jnp.int32),
            pltpu.VMEM(block, F32),
            pltpu.VMEM((2, planes, 2, tiles, rows_y, 128), F32),
            pltpu.SemaphoreType.DMA((3, max(states, 3))),
        ],
        compiler_params=pltpu.CompilerParams(vmem_limit_bytes=6 * MIB),
        cost_estimate=pl.CostEstimate(flops=0, bytes_accessed=count * MIB, transcendentals=0),
        name="prepare",
    )(log_table, obs_scale, state, target, rock_type)


def merge(mine, theirs, slot, size, behind=None, add=None):
    given = [value for value in (behind, add) if value is not None]

    def kernel(mine_ref, theirs_ref, *refs):
        core = lax.rem(team_place(), 2)
        tail, (out_ref, *more) = refs[: len(given)], refs[len(given) :]
        for ref, at in ((mine_ref, core), (theirs_ref, 1 - core)):
            for n in range(size):
                out_ref[at * size + n] = ref[slot * size + n]
        if behind is not None:
            out_ref[2 * size] = tail[0][...]
        if add is not None:
            more[0][...] = tail[-1][...] + theirs_ref[theirs.shape[0] - 1]

    vmem = pl.BlockSpec(memory_space=pltpu.VMEM)
    tile = mine.shape[1:]
    outs = pl.pallas_call(
        kernel,
        out_shape=[jax.ShapeDtypeStruct((2 * size + (behind is not None),) + tile, F32)]
        + [jax.ShapeDtypeStruct(tile, F32)] * (add is not None),
        in_specs=[vmem] * (2 + len(given)),
        out_specs=[vmem] * (1 + (add is not None)),
        compiler_params=pltpu.CompilerParams(vmem_limit_bytes=4 * MIB),
        name="merge",
    )(mine, theirs, *given)
    return outs if add is not None else outs[0]


def copy_trimmed(ref, out_ref, size, below):
    part = size // 2
    for core in range(2):
        for n in range(part):
            out_ref[core * part + n] = ref[core * size + n]
    for n in range(size - 2):
        at = n + jnp.where(below, 2, 0)
        out_ref[size + n] = ref[(at // part) * size + part + lax.rem(at, part)]


def trim(blocks, size):
    def kernel(ref, out_ref):
        copy_trimmed(ref, out_ref, size, team_place() < 2)

    vmem = pl.BlockSpec(memory_space=pltpu.VMEM)
    return pl.pallas_call(
        kernel,
        out_shape=jax.ShapeDtypeStruct((2 * size - 2,) + blocks.shape[1:], F32),
        in_specs=[vmem],
        out_specs=vmem,
        compiler_params=pltpu.CompilerParams(vmem_limit_bytes=4 * MIB),
        name="trim",
    )(blocks)


def merge_near(mine, theirs, slot, size, after):
    tile = mine.shape[1:]

    def kernel(mine_ref, theirs_ref, _, out_ref, trimmed_ref):
        core = lax.rem(team_place(), 2)
        for ref, at in ((mine_ref, core), (theirs_ref, 1 - core)):
            for n in range(size):
                out_ref[at * size + n] = ref[slot * size + n]
        copy_trimmed(out_ref, trimmed_ref, size, team_place() >= 2)

    vmem = pl.BlockSpec(memory_space=pltpu.VMEM)
    return pl.pallas_call(
        kernel,
        out_shape=[
            jax.ShapeDtypeStruct((2 * size,) + tile, F32),
            jax.ShapeDtypeStruct((2 * size - 2,) + tile, F32),
        ],
        in_specs=[vmem] * 2 + [pl.BlockSpec(memory_space=pl.ANY)],
        out_specs=[vmem] * 2,
        compiler_params=pltpu.CompilerParams(vmem_limit_bytes=4 * MIB),
        name="merge_near",
    )(mine, theirs, after)


def reciprocal(x):
    guess = pl.reciprocal(x, approx=True)
    return guess * (2.0 - x * guess)


def harmonic(a, b):
    x = a + b
    guess = pl.reciprocal(x, approx=True)
    return guess * (4.0 - (2.0 * x) * guess)


def each(start, stop, body, width):
    whole = (stop - start) // width

    def group(n, carry):
        for k in range(width):
            body(start + n * width + k)
        return carry

    lax.fori_loop(0, whole, group, 0)
    for p in range(start + whole * width, stop):
        body(p)


def ahead_x(v):
    return pltpu.roll(v, v.shape[1] - 1, 1)


def behind_x(v):
    return pltpu.roll(v, 1, 1)


def ahead_y(v):
    return pltpu.roll(v, v.shape[0] - 1, 0)


def behind_y(v):
    return pltpu.roll(v, 1, 0)


def set_up(planes, conductance, source, store):
    centre, _ = chebyshev_constants(DEGREE)
    here = [conductance(planes[0], t) for t in range(2)]
    half, columns = here[0].shape
    last_row = lax.broadcasted_iota(jnp.int32, (half, columns), 0) == half - 1
    last_column = lax.broadcasted_iota(jnp.int32, (half, columns), 1) == columns - 1
    w_below = [harmonic(conductance(planes[0] - 1, t), here[t]) for t in range(2)]
    for p in planes:
        above = [conductance(p + 1, t) for t in range(2)]
        even, odd = here
        w_pair = harmonic(even, odd)
        w_next = jnp.where(last_row, 0.0, harmonic(odd, ahead_y(even)))
        w_above = [harmonic(here[t], above[t]) for t in range(2)]
        for t in range(2):
            w_y = w_next if t else w_pair
            w_y_behind = w_pair if t else behind_y(w_next)
            w_x = jnp.where(last_column, 0.0, harmonic(here[t], ahead_x(here[t])))
            w_x_behind = behind_x(w_x)
            diagonal = (w_above[t] + w_below[t]) + (w_y + w_y_behind) + (w_x + w_x_behind) + STORAGE
            inverse = reciprocal(diagonal)
            weights = (w_above[t], w_below[t], w_y, w_y_behind, w_x, w_x_behind)
            scaled = source(p, t) * inverse
            store(p, t, [w * inverse for w in weights] + [scaled, scaled * (1.0 / centre)])
        here, w_below = above, w_above


def outside(v):
    return jnp.where(v > 0.0, v, 1e30)


def prepare_planes(near, far, near_halo, planes, after):
    half, columns = far.shape[-2:]
    halo, own, part = 2 * planes, TEAM * planes, 2 * planes
    span = own + 2 * halo
    first, count = halo + 1, own + halo - 2

    def kernel(near_ref, halo_ref, far_ref, *refs):
        refs = refs[len(after) :]
        outs, edge_ref, (cond, start) = refs[:8], refs[8], refs[9:]
        side = team_place() // 2

        def place(natural):
            return jnp.where(side == 0, natural, span - 1 - natural) - halo

        for core in range(2):
            for n in range(part):
                base = halo + planes * core + n // 2
                for ref, at in ((near_ref, base + part * side), (far_ref, base + part * (1 - side))):
                    cond[place(at), n % 2] = ref[core * 2 * part + n]
                    start[place(at), n % 2] = ref[(core * 2 + 1) * part + n]
        near_base = jnp.where(side == 0, halo + own, 0)
        for n in range(2 * part):
            cond[place(near_base + n // 2), n % 2] = outside(halo_ref[n])
        for n in range(2 * part - 2):
            start[place(near_base + side + n // 2), n % 2] = halo_ref[2 * part + n]
        for p in range(2):
            for t in range(2):
                edge_ref[0, p, t] = cond[p, t]
                edge_ref[1, p, t] = start[p, t]

        width = count // 2

        def group(n, carry):
            begin = 1 + n * width

            def store(p, t, values):
                for ref, value in zip(outs, values):
                    ref[p - 1, t] = value

            set_up(
                [begin + k for k in range(width)],
                lambda p, t: cond[p, t],
                lambda p, t: start[p, t],
                store,
            )
            return carry

        lax.fori_loop(0, 2, group, 0)

    assert count % 2 == 0
    vmem = pl.BlockSpec(memory_space=pltpu.VMEM)
    results = pl.pallas_call(
        kernel,
        out_shape=[jax.ShapeDtypeStruct((count, 2, half, columns), F32)] * 8
        + [jax.ShapeDtypeStruct((2, 2, 2, half, columns), F32)],
        in_specs=[vmem] * 3 + [pl.BlockSpec(memory_space=pl.ANY)] * len(after),
        out_specs=[vmem] * 9,
        scratch_shapes=[pltpu.VMEM((own + halo, 2, half, columns), F32)] * 2,
        compiler_params=pltpu.CompilerParams(vmem_limit_bytes=4 * MIB),
        cost_estimate=pl.CostEstimate(flops=0, bytes_accessed=8 * MIB, transcendentals=0),
        name="prepare_planes",
    )(near, near_halo, far, *after)
    return results[:8], results[8]


def solve(made, edge, far_halo, planes):
    half, columns = far_halo.shape[-2:]
    halo, own, part = 2 * planes, TEAM * planes, 2 * planes
    span = own + 2 * halo
    cut = halo + 1
    centre, coefficients = chebyshev_constants(DEGREE)
    assert halo >= STEPS

    def kernel(*refs):
        high, (edge_ref, halo_ref), refs = refs[:8], refs[8:10], refs[10:]
        outs, face_ref, refs = refs[:TEAM], refs[TEAM], refs[TEAM + 1 :]
        low, (cond, start, u_a, u_b, s_a, s_b, t_a, t_b) = refs[:6], refs[6:]
        place = team_place()
        side = place // 2

        def at(natural):
            return jnp.where(side == 0, natural, span - 1 - natural)

        far_base = jnp.where(side == 0, 0, halo + own)
        for n in range(2 * part):
            cond[at(far_base + n // 2), n % 2] = outside(halo_ref[n])
        for n in range(2 * part - 2):
            start[at(far_base + (1 - side) + n // 2), n % 2] = halo_ref[2 * part + n]
        for p in range(2):
            for t in range(2):
                cond[halo + p, t] = edge_ref[0, p, t]
                start[halo + p, t] = edge_ref[1, p, t]

        def store(p, t, values):
            for ref, value in zip((*low, u_a, s_a), values):
                ref[p, t] = value

        set_up(range(1, cut), lambda p, t: cond[p, t], lambda p, t: start[p, t], store)
        for p in range(cut, span - 1):
            for t in range(2):
                u_a[p, t] = high[6][p - cut, t]
                s_a[p, t] = high[7][p - cut, t]

        s_now, s_next, u_now, u_next, t_now, t_next = s_a, s_b, u_a, u_b, t_a, t_b
        for step in range(STEPS - 1):
            position = step % DEGREE
            if position + 1 < DEGREE:
                keep, mix = coefficients[position]
            else:
                keep, mix = 0.0, 1.0 / centre
            last = step == STEPS - 2

            def advance(p, fields, first):
                zp, zm, yp, ym, xp, xm = fields
                q = p - first
                even, odd = s_now[p, 0], s_now[p, 1]
                for t, s in enumerate((even, odd)):
                    ahead = ahead_y(even) if t else odd
                    behind = even if t else behind_y(odd)
                    moved = zp[q, t] * s_now[p + 1, t] + zm[q, t] * s_now[p - 1, t]
                    moved += yp[q, t] * ahead + ym[q, t] * behind
                    moved += xp[q, t] * ahead_x(s) + xm[q, t] * behind_x(s)
                    new_u = (u_now[p, t] - s) + moved
                    new_s = mix * new_u if keep == 0.0 else keep * s + mix * new_u
                    if not last:
                        u_next[p, t] = new_u
                        s_next[p, t] = new_s
                    if step == 0:
                        t_next[p, t] = s + new_s
                    elif step % 2 == 0:
                        t_next[p, t] = t_now[p, t] + (s + new_s)

            margin = halo - (STEPS - 2 - step)
            each(cut, span - margin, lambda p: advance(p, high[:6], cut), 8)
            each(margin, cut, lambda p: advance(p, low, 0), 8)
            s_now, s_next, u_now, u_next = s_next, s_now, u_next, u_now
            if step % 2 == 0:
                t_now, t_next = t_next, t_now

        for m in range(TEAM):
            base = halo + planes * (place ^ m)
            for j in range(planes):
                for t in range(2):
                    outs[m][2 * j + t] = t_now[at(base + j), t]
        for p in range(own):
            face_ref[p : p + 1, :] = t_now[at(halo + p), 0, 0:1, :]

    vmem = pl.BlockSpec(memory_space=pltpu.VMEM)
    field = pltpu.VMEM((span, 2, half, columns), F32)
    small = pltpu.VMEM((halo + 2, 2, half, columns), F32)
    return pl.pallas_call(
        kernel,
        out_shape=[jax.ShapeDtypeStruct((2 * planes, half, columns), F32)] * TEAM
        + [jax.ShapeDtypeStruct((own, columns), F32)],
        in_specs=[vmem] * 10,
        out_specs=[vmem] * (TEAM + 1),
        scratch_shapes=[small] * 8 + [field] * 6,
        compiler_params=pltpu.CompilerParams(vmem_limit_bytes=10 * MIB),
        cost_estimate=pl.CostEstimate(flops=0, bytes_accessed=16 * MIB, transcendentals=0),
        name="solve",
    )(*made, edge, far_halo)


def weigh(sums, faces, cells, after):
    slots = len(faces)
    samples, columns = sums[0].shape

    def kernel(*refs):
        sum_refs, refs = refs[: len(sums)], refs[len(sums) :]
        face_refs, (out_ref, moments_ref, weights) = refs[:slots], refs[slots + len(after) :]
        place = team_place()
        summed = sum_refs[0][...]
        for ref in sum_refs[1:]:
            summed = summed + ref[...]
        misfit = summed * (1.0 / (2.0 * cells))
        mean = jnp.sum(misfit, axis=0, keepdims=True) * (1.0 / samples)
        deviation = misfit - mean
        variance = jnp.sum(deviation * deviation, axis=0, keepdims=True) * (1.0 / samples)
        lane = lax.broadcasted_iota(jnp.int32, (1, columns), 1)
        moments_ref[...] = jnp.where(lane == 0, mean, variance)
        weights[...] = 1.0 + 2.0 * BETA_RISK * deviation
        total = weights[pl.ds(slots * place, 1), :] * face_refs[0][...]
        for n in range(1, slots):
            total = total + weights[pl.ds(slots * place + n, 1), :] * face_refs[n][...]
        out_ref[...] = total

    vmem = pl.BlockSpec(memory_space=pltpu.VMEM)
    return pl.pallas_call(
        kernel,
        out_shape=[
            jax.ShapeDtypeStruct(faces[0].shape, F32),
            jax.ShapeDtypeStruct((1, columns), F32),
        ],
        in_specs=[vmem] * (len(sums) + slots)
        + [pl.BlockSpec(memory_space=pl.ANY)] * len(after),
        out_specs=[vmem, vmem],
        scratch_shapes=[pltpu.VMEM((samples, columns), F32)],
        compiler_params=pltpu.CompilerParams(vmem_limit_bytes=2 * MIB),
        name="weigh",
    )(*sums, *faces, *after)


def gather_adjoint(pieces, planes):
    slots = len(pieces)
    _, half, columns = pieces[0][0].shape
    tiles = columns // 128
    block = (planes, 2 * half, columns)

    def kernel(*refs):
        blocks, out, mark, held, mixed, sems = refs[: slots * TEAM], *refs[slots * TEAM :]
        mark[...] = blocks[0][0, :, :LANES]
        place = team_place()
        copies = []
        for slot in range(slots):
            for m in range(TEAM):
                i = slot * TEAM + m
                for j in range(planes):
                    for t in range(2):
                        for c in range(tiles):
                            mixed[i % 2, j, c, pl.ds(t, half, stride=2), :] = blocks[i][
                                2 * j + t, :, c * 128 : (c + 1) * 128
                            ]
                    for c in range(tiles):
                        held[i, j, :, c * 128 : (c + 1) * 128] = mixed[i % 2, j, c]
                copy = pltpu.make_async_copy(
                    held.at[i], out.at[slots * (place ^ m) + slot], sems.at[i]
                )
                copy.start()
                copies.append(copy)
        for copy in copies:
            copy.wait()

    return pl.pallas_call(
        kernel,
        out_shape=[
            jax.ShapeDtypeStruct((slots * TEAM,) + block, F32),
            jax.ShapeDtypeStruct((half, LANES), F32),
        ],
        in_specs=[pl.BlockSpec(memory_space=pltpu.VMEM)] * (slots * TEAM),
        out_specs=[
            pl.BlockSpec(memory_space=pltpu.HBM),
            pl.BlockSpec(memory_space=pltpu.VMEM),
        ],
        scratch_shapes=[
            pltpu.VMEM((slots * TEAM,) + block, F32),
            pltpu.VMEM((2, planes, tiles, 2 * half, 128), F32),
            pltpu.SemaphoreType.DMA((slots * TEAM,)),
        ],
        compiler_params=pltpu.CompilerParams(vmem_limit_bytes=4 * MIB),
        cost_estimate=pl.CostEstimate(flops=0, bytes_accessed=4 * MIB, transcendentals=0),
        name="gather_adjoint",
    )(*[piece for group in pieces for piece in group])


def control(faces, radices, basis_z, basis_x, after):
    slabs, own_count, depth_total = basis_z.shape
    own, columns = faces[0].shape[1:]
    teams = depth_total // own

    def kernel(*refs):
        parts, (z_ref, x_ref, _, out_ref, whole) = refs[: len(faces)], refs[len(faces) :]
        rank = lax.axis_index("gz")
        team = rank // TEAM
        for n in range(teams):
            at, left, stride = 0, n, 1
            for radix in radices:
                digit = lax.rem(team // stride + left % radix, radix)
                at, left, stride = at + digit * stride, left // radix, stride * radix
            inner = teams // len(faces)
            whole[at] = parts[n // inner][n % inner]
        along_z = jnp.dot(
            z_ref[rank],
            whole[...].reshape(depth_total, columns),
            precision=lax.Precision.HIGHEST,
            preferred_element_type=F32,
        )
        high, low = in_halves(along_z)
        x_high, x_low = in_halves(x_ref[...])
        both = jnp.concatenate([high, low], axis=0)
        first = jnp.dot(both, x_high, preferred_element_type=F32)
        second = jnp.dot(high, x_low, preferred_element_type=F32)
        out_ref[...] = (first[:own_count] + first[own_count:]) + second

    vmem = pl.BlockSpec(memory_space=pltpu.VMEM)
    return pl.pallas_call(
        kernel,
        out_shape=jax.ShapeDtypeStruct((own_count, basis_x.shape[1]), F32),
        in_specs=[vmem] * (len(faces) + 2) + [pl.BlockSpec(memory_space=pl.ANY)],
        out_specs=vmem,
        scratch_shapes=[pltpu.VMEM((teams, own, columns), F32)],
        compiler_params=pltpu.CompilerParams(vmem_limit_bytes=8 * MIB),
        name="control",
    )(*faces, basis_z, basis_x, after)


def radices_of(teams):
    radices = []
    while teams > 1:
        radix = next(r for r in (4, 2, 3, *range(5, teams + 1)) if teams % r == 0)
        radices.append(radix)
        teams //= radix
    return radices


def on_device(state, target, rock_type, log_table, obs_scale):
    samples, planes, rows_y, columns = state.shape
    slabs = lax.axis_size("gz")
    slots = samples // TEAM
    depth_total = planes * slabs
    radices = radices_of(slabs // TEAM)

    def swap(value, m):
        return lax.ppermute(value, "gz", [(i, i ^ m) for i in range(slabs)])

    def along(value, outward):
        pairs = []
        for i in range(slabs):
            side = (i % TEAM) // 2
            to = i + TEAM if (side == 1) == outward else i - TEAM
            if 0 <= to < slabs:
                pairs.append((i, to))
        return lax.ppermute(value, "gz", pairs)

    def from_teams(value, stride, radix):
        heard = []
        for k in range(1, radix):
            pairs = []
            for i in range(slabs):
                digit = i // (TEAM * stride) % radix
                pairs.append((i + ((digit + k) % radix - digit) * stride * TEAM, i))
            heard.append(lax.ppermute(value, "gz", pairs))
        return heard

    fields = [
        pltpu.with_memory_space_constraint(field, pltpu.HBM)
        for field in (state, target, rock_type, log_table, obs_scale)
    ]
    size = 4 * planes
    jobs = [[(slot, m) for slot in range(slots)] for m in range(TEAM)]
    mine, theirs, sums = prepare(jobs[2:], fields, with_sums=True)
    theirs = swap(theirs, 1)
    first, sums = merge(mine, theirs, 0, size, add=sums)
    far = [swap(first, 2)]
    stride, teams = 1, slabs // TEAM
    while stride < teams:
        radix = next(r for r in range(2, teams + 1) if teams // stride % r == 0)
        sums = sum(from_teams(sums, stride, radix), sums)
        stride *= radix

    mine_near, theirs_near = prepare(jobs[:2], fields)
    theirs_near = swap(theirs_near, 1)
    near, near_halo = [], []
    for slot in range(slots):
        blocks, trimmed = merge_near(mine_near, theirs_near, slot, size, sums)
        near.append(blocks)
        near_halo.append(along(trimmed, True))
    for slot in range(1, slots):
        far.append(swap(merge(mine, theirs, slot, size, sums), 2))
    sums = [sums, far[-1][2 * size]]

    pieces, faces = [], []
    for slot in range(slots):
        far_halo = along(trim(far[slot], size), False)
        made, edge = prepare_planes(near[slot], far[slot], near_halo[slot], planes, faces[-1:])
        solved = solve(made, edge, far_halo, planes)
        pieces.append([solved[0]] + [swap(solved[m], m) for m in (1, 2, 3)])
        faces.append(solved[TEAM])

    face, moments = weigh(sums, faces, depth_total * rows_y * columns, pieces[0][1:])
    for m in (1, 2):
        face = face + swap(face, m)
    heard = [face[None]]
    stride = 1
    for radix in radices:
        held = heard[0] if len(heard) == 1 else jnp.concatenate(heard)
        heard = [held] + from_teams(held, stride, radix)
        stride *= radix
    adjoint, mark = gather_adjoint(pieces, planes)
    own_count = MA // slabs
    gradient = control(
        heard,
        radices,
        jnp.asarray(cosine_basis(depth_total, MA).T.reshape(slabs, own_count, depth_total)),
        jnp.asarray(cosine_basis(columns, MB)),
        mark,
    )
    return (adjoint, gradient, moments[0, :2])


def solution(mesh):
    return jax.shard_map(
        on_device,
        mesh=mesh,
        in_specs=(
            P("parts", "gz", None, None),
            P(("parts", "gz"), None, None),
            P("parts", "gz", None, None),
            P("parts", None),
            P("parts"),
        ),
        out_specs=(P("parts", "gz", None, None), P(("parts", "gz"), None), P("parts")),
        check_vma=False,
    )
```

```python
import math

import jax
import jax.numpy as jnp
import numpy as np
from jax import lax
from jax.experimental import pallas as pl
from jax.experimental.pallas import tpu as pltpu
from jax.sharding import PartitionSpec as P

NR = 8
DEGREE = 4
SWEEPS = 2
MA = 512
MB = 512

STORAGE = 0.05
BETA_RISK = 0.5
LOWER_EIGEN = 0.05
UPPER_EIGEN = 2.0

TEAM = 4
STEPS = DEGREE * SWEEPS
F32 = jnp.float32
MIB = 1024 * 1024
LANES = 128


def chebyshev_constants(number_steps):
    centre = (UPPER_EIGEN + LOWER_EIGEN) / 2
    spread = (UPPER_EIGEN - LOWER_EIGEN) / 2
    quotient = centre / spread
    rho_now = 1.0 / quotient
    coefficients = []
    for position in range(number_steps):
        rho_next = 1.0 / (2.0 * quotient - rho_now)
        coefficients.append((rho_next * rho_now, 2.0 * rho_next / spread))
        rho_now = rho_next
    return (centre, coefficients)


def cosine_basis(length_total, modes):
    positions = np.arange(length_total, dtype=np.int64)
    mode_index = np.arange(modes, dtype=np.int64)
    product_index = ((2 * positions[:, None] + 1) * (2 * mode_index[None, :] + 1)) % (
        8 * length_total
    )
    angle = product_index.astype(np.float64) * (math.pi / (4 * length_total))
    return (math.sqrt(2.0 / length_total) * np.cos(angle)).astype(np.float32)


def in_halves(values):
    high = values.astype(jnp.bfloat16)
    return high, (values - high.astype(F32)).astype(jnp.bfloat16)


def team_place():
    return lax.rem(lax.axis_index("gz"), TEAM)


def prepare(jobs, fields, with_sums=False):
    state, target, rock_type, log_table, obs_scale = fields
    samples, planes, rows_y, columns = state.shape
    slots = samples // TEAM
    block = (planes, rows_y, columns)
    half, tiles = rows_y // 2, columns // 128
    size = 2 * 2 * planes
    depth_total = planes * lax.axis_size("gz")
    flat = [(o, i, job) for o, group in enumerate(jobs) for i, job in enumerate(group)]
    count = len(flat)
    shapes = [(len(group) * size + with_sums, half, columns) for group in jobs]
    states = samples if with_sums else count

    def kernel(*refs):
        (table_ref, scale_ref, state_ref, target_ref, rock_ref), refs = refs[:5], refs[5:]
        outs, refs = refs[: len(jobs)], refs[len(jobs) :]
        if with_sums:
            sums_ref, refs = refs[0], refs[1:]
        table, scale, state_buf, rock_buf, target_buf, mixed, sems = refs
        place = team_place()
        first_plane = lax.axis_index("gz") * planes
        members = [slots * (place ^ m) + slot for _, _, (slot, m) in flat]
        small = [
            pltpu.make_async_copy(table_ref, table, sems.at[2, 0]),
            pltpu.make_async_copy(scale_ref, scale, sems.at[2, 1]),
            pltpu.make_async_copy(target_ref, target_buf, sems.at[2, 2]),
        ]
        for copy in small:
            copy.start()
        rocks = [
            pltpu.make_async_copy(rock_ref.at[member], rock_buf.at[n], sems.at[1, n])
            for n, member in enumerate(members)
        ]
        loads = [
            pltpu.make_async_copy(
                state_ref.at[n if with_sums else members[n]], state_buf.at[n], sems.at[0, n]
            )
            for n in range(states)
        ]
        for copy in rocks + loads:
            copy.start()
        depth_weights = [
            1.0 + (2.0 / (depth_total - 1)) * (first_plane + p).astype(F32) for p in range(planes)
        ]
        for copy in small:
            copy.wait()
        if with_sums:
            for copy in loads:
                copy.wait()
            for n in range(samples):
                total = jnp.zeros((8, columns), F32)
                for p in range(planes):
                    part = jnp.zeros((8, columns), F32)
                    for first in range(0, rows_y, 8):
                        rows = slice(first, first + 8)
                        gap = state_buf[n, p, rows] - target_buf[p, rows]
                        part = part + gap * gap
                    total = total + (scale[n] * depth_weights[p]) * part
                summed = jnp.sum(total, keepdims=True)
                sums_ref[n : n + 1, :] = jnp.broadcast_to(summed, (1, columns))
        for n, (o, i, _) in enumerate(flat):
            rocks[n].wait()
            if not with_sums:
                loads[n].wait()
            member = members[n]
            own_state = member if with_sums else n
            values = [
                jnp.exp(jnp.full((8, columns), -table[member, code], F32)) for code in range(NR)
            ]
            for p in range(planes):
                factor = scale[member] * depth_weights[p]
                for first in range(0, rows_y, 8):
                    rows = slice(first, first + 8)
                    codes = rock_buf[n, p, rows]
                    low, mid, high = ((codes & bit) != 0 for bit in (1, 2, 4))
                    pairs = [
                        jnp.where(low, values[2 * k + 1], values[2 * k]) for k in range(NR // 2)
                    ]
                    halves = [jnp.where(mid, pairs[2 * k + 1], pairs[2 * k]) for k in range(2)]
                    gap = state_buf[own_state, p, rows] - target_buf[p, rows]
                    made = (jnp.where(high, halves[1], halves[0]), factor * gap)
                    for a in range(2):
                        for c in range(tiles):
                            mixed[n % 2, p, a, c, rows] = made[a][:, c * 128 : (c + 1) * 128]
                for a in range(2):
                    for t in range(2):
                        for c in range(tiles):
                            at = i * size + (a * planes + p) * 2 + t
                            outs[o][at, :, c * 128 : (c + 1) * 128] = mixed[
                                n % 2, p, a, c, pl.ds(t, half, stride=2), :
                            ]
        for o, group in enumerate(jobs if with_sums else []):
            outs[o][len(group) * size] = sums_ref[...]

    hbm = pl.BlockSpec(memory_space=pltpu.HBM)
    vmem = pl.BlockSpec(memory_space=pltpu.VMEM)
    return pl.pallas_call(
        kernel,
        out_shape=[jax.ShapeDtypeStruct(shape, F32) for shape in shapes]
        + [jax.ShapeDtypeStruct((samples, columns), F32)] * with_sums,
        in_specs=[hbm] * 5,
        out_specs=[vmem] * (len(shapes) + with_sums),
        scratch_shapes=[
            pltpu.SMEM(log_table.shape, F32),
            pltpu.SMEM(obs_scale.shape, F32),
            pltpu.VMEM((states,) + block, F32),
            pltpu.VMEM((count,) + block, jnp.int32),
            pltpu.VMEM(block, F32),
            pltpu.VMEM((2, planes, 2, tiles, rows_y, 128), F32),
            pltpu.SemaphoreType.DMA((3, max(states, 3))),
        ],
        compiler_params=pltpu.CompilerParams(vmem_limit_bytes=6 * MIB),
        cost_estimate=pl.CostEstimate(flops=0, bytes_accessed=count * MIB, transcendentals=0),
        name="prepare",
    )(log_table, obs_scale, state, target, rock_type)


def merge(mine, theirs, slot, size, behind=None, add=None):
    given = [value for value in (behind, add) if value is not None]

    def kernel(mine_ref, theirs_ref, *refs):
        core = lax.rem(team_place(), 2)
        tail, (out_ref, *more) = refs[: len(given)], refs[len(given) :]
        for ref, at in ((mine_ref, core), (theirs_ref, 1 - core)):
            for n in range(size):
                out_ref[at * size + n] = ref[slot * size + n]
        if behind is not None:
            out_ref[2 * size] = tail[0][...]
        if add is not None:
            more[0][...] = tail[-1][...] + theirs_ref[theirs.shape[0] - 1]

    vmem = pl.BlockSpec(memory_space=pltpu.VMEM)
    tile = mine.shape[1:]
    outs = pl.pallas_call(
        kernel,
        out_shape=[jax.ShapeDtypeStruct((2 * size + (behind is not None),) + tile, F32)]
        + [jax.ShapeDtypeStruct(tile, F32)] * (add is not None),
        in_specs=[vmem] * (2 + len(given)),
        out_specs=[vmem] * (1 + (add is not None)),
        compiler_params=pltpu.CompilerParams(vmem_limit_bytes=4 * MIB),
        name="merge",
    )(mine, theirs, *given)
    return outs if add is not None else outs[0]


def copy_trimmed(ref, out_ref, size, below):
    part = size // 2
    for core in range(2):
        for n in range(part):
            out_ref[core * part + n] = ref[core * size + n]
    for n in range(size - 2):
        at = n + jnp.where(below, 2, 0)
        out_ref[size + n] = ref[(at // part) * size + part + lax.rem(at, part)]


def trim(blocks, size):
    def kernel(ref, out_ref):
        copy_trimmed(ref, out_ref, size, team_place() < 2)

    vmem = pl.BlockSpec(memory_space=pltpu.VMEM)
    return pl.pallas_call(
        kernel,
        out_shape=jax.ShapeDtypeStruct((2 * size - 2,) + blocks.shape[1:], F32),
        in_specs=[vmem],
        out_specs=vmem,
        compiler_params=pltpu.CompilerParams(vmem_limit_bytes=4 * MIB),
        name="trim",
    )(blocks)


def merge_near(mine, theirs, slot, size, after):
    tile = mine.shape[1:]

    def kernel(mine_ref, theirs_ref, _, out_ref, trimmed_ref):
        core = lax.rem(team_place(), 2)
        for ref, at in ((mine_ref, core), (theirs_ref, 1 - core)):
            for n in range(size):
                out_ref[at * size + n] = ref[slot * size + n]
        copy_trimmed(out_ref, trimmed_ref, size, team_place() >= 2)

    vmem = pl.BlockSpec(memory_space=pltpu.VMEM)
    return pl.pallas_call(
        kernel,
        out_shape=[
            jax.ShapeDtypeStruct((2 * size,) + tile, F32),
            jax.ShapeDtypeStruct((2 * size - 2,) + tile, F32),
        ],
        in_specs=[vmem] * 2 + [pl.BlockSpec(memory_space=pl.ANY)],
        out_specs=[vmem] * 2,
        compiler_params=pltpu.CompilerParams(vmem_limit_bytes=4 * MIB),
        name="merge_near",
    )(mine, theirs, after)


def reciprocal(x):
    guess = pl.reciprocal(x, approx=True)
    return guess * (2.0 - x * guess)


def harmonic(a, b):
    x = a + b
    guess = pl.reciprocal(x, approx=True)
    return guess * (4.0 - (2.0 * x) * guess)


def each(start, stop, body, width):
    whole = (stop - start) // width

    def group(n, carry):
        for k in range(width):
            body(start + n * width + k)
        return carry

    if whole > 0:
        lax.fori_loop(0, whole, group, 0)
    for p in range(start + whole * width, stop):
        body(p)


def ahead_x(v):
    return pltpu.roll(v, v.shape[1] - 1, 1)


def behind_x(v):
    return pltpu.roll(v, 1, 1)


def ahead_y(v):
    return pltpu.roll(v, v.shape[0] - 1, 0)


def behind_y(v):
    return pltpu.roll(v, 1, 0)


def set_up(planes, conductance, source, store):
    centre, _ = chebyshev_constants(DEGREE)
    here = [conductance(planes[0], t) for t in range(2)]
    half, columns = here[0].shape
    last_row = lax.broadcasted_iota(jnp.int32, (half, columns), 0) == half - 1
    last_column = lax.broadcasted_iota(jnp.int32, (half, columns), 1) == columns - 1
    w_below = [harmonic(conductance(planes[0] - 1, t), here[t]) for t in range(2)]
    for p in planes:
        above = [conductance(p + 1, t) for t in range(2)]
        even, odd = here
        w_pair = harmonic(even, odd)
        w_next = jnp.where(last_row, 0.0, harmonic(odd, ahead_y(even)))
        w_above = [harmonic(here[t], above[t]) for t in range(2)]
        for t in range(2):
            w_y = w_next if t else w_pair
            w_y_behind = w_pair if t else behind_y(w_next)
            w_x = jnp.where(last_column, 0.0, harmonic(here[t], ahead_x(here[t])))
            w_x_behind = behind_x(w_x)
            diagonal = (w_above[t] + w_below[t]) + (w_y + w_y_behind) + (w_x + w_x_behind) + STORAGE
            inverse = reciprocal(diagonal)
            weights = (w_above[t], w_below[t], w_y, w_y_behind, w_x, w_x_behind)
            scaled = source(p, t) * inverse
            store(p, t, [w * inverse for w in weights] + [scaled, scaled * (1.0 / centre)])
        here, w_below = above, w_above


def outside(v):
    return jnp.where(v > 0.0, v, 1e30)


def prepare_planes(near, far, near_halo, planes, after):
    half, columns = far.shape[-2:]
    halo, own, part = 2 * planes, TEAM * planes, 2 * planes
    span = own + 2 * halo
    first, count = halo + 1, own + halo - 2

    def kernel(near_ref, halo_ref, far_ref, *refs):
        refs = refs[len(after) :]
        outs, edge_ref, (cond, start) = refs[:8], refs[8], refs[9:]
        side = team_place() // 2

        def place(natural):
            return jnp.where(side == 0, natural, span - 1 - natural) - halo

        for core in range(2):
            for n in range(part):
                base = halo + planes * core + n // 2
                for ref, at in ((near_ref, base + part * side), (far_ref, base + part * (1 - side))):
                    cond[place(at), n % 2] = ref[core * 2 * part + n]
                    start[place(at), n % 2] = ref[(core * 2 + 1) * part + n]
        near_base = jnp.where(side == 0, halo + own, 0)
        for n in range(2 * part):
            cond[place(near_base + n // 2), n % 2] = outside(halo_ref[n])
        for n in range(2 * part - 2):
            start[place(near_base + side + n // 2), n % 2] = halo_ref[2 * part + n]
        for p in range(2):
            for t in range(2):
                edge_ref[0, p, t] = cond[p, t]
                edge_ref[1, p, t] = start[p, t]

        width = count // 2

        def group(n, carry):
            begin = 1 + n * width

            def store(p, t, values):
                for ref, value in zip(outs, values):
                    ref[p - 1, t] = value

            set_up(
                [begin + k for k in range(width)],
                lambda p, t: cond[p, t],
                lambda p, t: start[p, t],
                store,
            )
            return carry

        lax.fori_loop(0, 2, group, 0)

    assert count % 2 == 0
    vmem = pl.BlockSpec(memory_space=pltpu.VMEM)
    results = pl.pallas_call(
        kernel,
        out_shape=[jax.ShapeDtypeStruct((count, 2, half, columns), F32)] * 8
        + [jax.ShapeDtypeStruct((2, 2, 2, half, columns), F32)],
        in_specs=[vmem] * 3 + [pl.BlockSpec(memory_space=pl.ANY)] * len(after),
        out_specs=[vmem] * 9,
        scratch_shapes=[pltpu.VMEM((own + halo, 2, half, columns), F32)] * 2,
        compiler_params=pltpu.CompilerParams(vmem_limit_bytes=4 * MIB),
        cost_estimate=pl.CostEstimate(flops=0, bytes_accessed=8 * MIB, transcendentals=0),
        name="prepare_planes",
    )(near, near_halo, far, *after)
    return results[:8], results[8]


def solve(made, edge, far_halo, planes):
    half, columns = far_halo.shape[-2:]
    halo, own, part = 2 * planes, TEAM * planes, 2 * planes
    span = own + 2 * halo
    cut = halo + 1
    centre, coefficients = chebyshev_constants(DEGREE)
    assert halo >= STEPS

    def kernel(*refs):
        high, (edge_ref, halo_ref), refs = refs[:8], refs[8:10], refs[10:]
        outs, face_ref, refs = refs[:TEAM], refs[TEAM], refs[TEAM + 1 :]
        low, (cond, start, u_a, u_b, s_a, s_b, t_a, t_b) = refs[:6], refs[6:]
        place = team_place()
        side = place // 2

        def at(natural):
            return jnp.where(side == 0, natural, span - 1 - natural)

        far_base = jnp.where(side == 0, 0, halo + own)
        for n in range(2 * part):
            cond[at(far_base + n // 2), n % 2] = outside(halo_ref[n])
        for n in range(2 * part - 2):
            start[at(far_base + (1 - side) + n // 2), n % 2] = halo_ref[2 * part + n]
        for p in range(2):
            for t in range(2):
                cond[halo + p, t] = edge_ref[0, p, t]
                start[halo + p, t] = edge_ref[1, p, t]

        def store(p, t, values):
            for ref, value in zip((*low, u_a, s_a), values):
                ref[p, t] = value

        set_up(range(1, cut), lambda p, t: cond[p, t], lambda p, t: start[p, t], store)
        for p in range(cut, span - 1):
            for t in range(2):
                u_a[p, t] = high[6][p - cut, t]
                s_a[p, t] = high[7][p - cut, t]

        s_now, s_next, u_now, u_next, t_now, t_next = s_a, s_b, u_a, u_b, t_a, t_b
        for step in range(STEPS - 1):
            position = step % DEGREE
            if position + 1 < DEGREE:
                keep, mix = coefficients[position]
            else:
                keep, mix = 0.0, 1.0 / centre
            last = step == STEPS - 2

            def advance(p, fields, first):
                zp, zm, yp, ym, xp, xm = fields
                q = p - first
                even, odd = s_now[p, 0], s_now[p, 1]
                for t, s in enumerate((even, odd)):
                    ahead = ahead_y(even) if t else odd
                    behind = even if t else behind_y(odd)
                    moved = zp[q, t] * s_now[p + 1, t] + zm[q, t] * s_now[p - 1, t]
                    moved += yp[q, t] * ahead + ym[q, t] * behind
                    moved += xp[q, t] * ahead_x(s) + xm[q, t] * behind_x(s)
                    new_u = (u_now[p, t] - s) + moved
                    new_s = mix * new_u if keep == 0.0 else keep * s + mix * new_u
                    if not last:
                        u_next[p, t] = new_u
                        s_next[p, t] = new_s
                    if step == 0:
                        t_next[p, t] = s + new_s
                    elif step % 2 == 0:
                        t_next[p, t] = t_now[p, t] + (s + new_s)

            margin = halo - (STEPS - 2 - step)
            each(cut, span - margin, lambda p: advance(p, high[:6], cut), 8)
            each(margin, cut, lambda p: advance(p, low, 0), 8)
            s_now, s_next, u_now, u_next = s_next, s_now, u_next, u_now
            if step % 2 == 0:
                t_now, t_next = t_next, t_now

        for m in range(TEAM):
            base = halo + planes * (place ^ m)
            for j in range(planes):
                for t in range(2):
                    outs[m][2 * j + t] = t_now[at(base + j), t]
        for p in range(own):
            face_ref[p : p + 1, :] = t_now[at(halo + p), 0, 0:1, :]

    vmem = pl.BlockSpec(memory_space=pltpu.VMEM)
    field = pltpu.VMEM((span, 2, half, columns), F32)
    small = pltpu.VMEM((halo + 2, 2, half, columns), F32)
    return pl.pallas_call(
        kernel,
        out_shape=[jax.ShapeDtypeStruct((2 * planes, half, columns), F32)] * TEAM
        + [jax.ShapeDtypeStruct((own, columns), F32)],
        in_specs=[vmem] * 10,
        out_specs=[vmem] * (TEAM + 1),
        scratch_shapes=[small] * 8 + [field] * 6,
        compiler_params=pltpu.CompilerParams(vmem_limit_bytes=10 * MIB),
        cost_estimate=pl.CostEstimate(flops=0, bytes_accessed=16 * MIB, transcendentals=0),
        name="solve",
    )(*made, edge, far_halo)


def weigh(sums, faces, cells, after):
    slots = len(faces)
    samples, columns = sums[0].shape

    def kernel(*refs):
        sum_refs, refs = refs[: len(sums)], refs[len(sums) :]
        face_refs, (out_ref, moments_ref, weights) = refs[:slots], refs[slots + len(after) :]
        place = team_place()
        summed = sum_refs[0][...]
        for ref in sum_refs[1:]:
            summed = summed + ref[...]
        misfit = summed * (1.0 / (2.0 * cells))
        mean = jnp.sum(misfit, axis=0, keepdims=True) * (1.0 / samples)
        deviation = misfit - mean
        variance = jnp.sum(deviation * deviation, axis=0, keepdims=True) * (1.0 / samples)
        lane = lax.broadcasted_iota(jnp.int32, (1, columns), 1)
        moments_ref[...] = jnp.where(lane == 0, mean, variance)
        weights[...] = 1.0 + 2.0 * BETA_RISK * deviation
        total = weights[pl.ds(slots * place, 1), :] * face_refs[0][...]
        for n in range(1, slots):
            total = total + weights[pl.ds(slots * place + n, 1), :] * face_refs[n][...]
        out_ref[...] = total

    vmem = pl.BlockSpec(memory_space=pltpu.VMEM)
    return pl.pallas_call(
        kernel,
        out_shape=[
            jax.ShapeDtypeStruct(faces[0].shape, F32),
            jax.ShapeDtypeStruct((1, columns), F32),
        ],
        in_specs=[vmem] * (len(sums) + slots)
        + [pl.BlockSpec(memory_space=pl.ANY)] * len(after),
        out_specs=[vmem, vmem],
        scratch_shapes=[pltpu.VMEM((samples, columns), F32)],
        compiler_params=pltpu.CompilerParams(vmem_limit_bytes=2 * MIB),
        name="weigh",
    )(*sums, *faces, *after)


def gather_adjoint(pieces, planes):
    slots = len(pieces)
    _, half, columns = pieces[0][0].shape
    tiles = columns // 128
    block = (planes, 2 * half, columns)

    def kernel(*refs):
        blocks, out, mark, held, mixed, sems = refs[: slots * TEAM], *refs[slots * TEAM :]
        mark[...] = blocks[0][0, :, :LANES]
        place = team_place()
        copies = []
        for slot in range(slots):
            for m in range(TEAM):
                i = slot * TEAM + m
                for j in range(planes):
                    for t in range(2):
                        for c in range(tiles):
                            mixed[i % 2, j, c, pl.ds(t, half, stride=2), :] = blocks[i][
                                2 * j + t, :, c * 128 : (c + 1) * 128
                            ]
                    for c in range(tiles):
                        held[i, j, :, c * 128 : (c + 1) * 128] = mixed[i % 2, j, c]
                copy = pltpu.make_async_copy(
                    held.at[i], out.at[slots * (place ^ m) + slot], sems.at[i]
                )
                copy.start()
                copies.append(copy)
        for copy in copies:
            copy.wait()

    return pl.pallas_call(
        kernel,
        out_shape=[
            jax.ShapeDtypeStruct((slots * TEAM,) + block, F32),
            jax.ShapeDtypeStruct((half, LANES), F32),
        ],
        in_specs=[pl.BlockSpec(memory_space=pltpu.VMEM)] * (slots * TEAM),
        out_specs=[
            pl.BlockSpec(memory_space=pltpu.HBM),
            pl.BlockSpec(memory_space=pltpu.VMEM),
        ],
        scratch_shapes=[
            pltpu.VMEM((slots * TEAM,) + block, F32),
            pltpu.VMEM((2, planes, tiles, 2 * half, 128), F32),
            pltpu.SemaphoreType.DMA((slots * TEAM,)),
        ],
        compiler_params=pltpu.CompilerParams(vmem_limit_bytes=4 * MIB),
        cost_estimate=pl.CostEstimate(flops=0, bytes_accessed=4 * MIB, transcendentals=0),
        name="gather_adjoint",
    )(*[piece for group in pieces for piece in group])


def control(faces, radices, basis_z, basis_x, after):
    slabs, own_count, depth_total = basis_z.shape
    own, columns = faces[0].shape[1:]
    teams = depth_total // own

    def kernel(*refs):
        parts, (z_ref, x_ref, _, out_ref, whole) = refs[: len(faces)], refs[len(faces) :]
        rank = lax.axis_index("gz")
        team = rank // TEAM
        for n in range(teams):
            at, left, stride = 0, n, 1
            for radix in radices:
                digit = lax.rem(team // stride + left % radix, radix)
                at, left, stride = at + digit * stride, left // radix, stride * radix
            inner = teams // len(faces)
            whole[at] = parts[n // inner][n % inner]
        along_z = jnp.dot(
            z_ref[rank],
            whole[...].reshape(depth_total, columns),
            precision=lax.Precision.HIGHEST,
            preferred_element_type=F32,
        )
        high, low = in_halves(along_z)
        x_high, x_low = in_halves(x_ref[...])
        both = jnp.concatenate([high, low], axis=0)
        first = jnp.dot(both, x_high, preferred_element_type=F32)
        second = jnp.dot(high, x_low, preferred_element_type=F32)
        out_ref[...] = (first[:own_count] + first[own_count:]) + second

    vmem = pl.BlockSpec(memory_space=pltpu.VMEM)
    return pl.pallas_call(
        kernel,
        out_shape=jax.ShapeDtypeStruct((own_count, basis_x.shape[1]), F32),
        in_specs=[vmem] * (len(faces) + 2) + [pl.BlockSpec(memory_space=pl.ANY)],
        out_specs=vmem,
        scratch_shapes=[pltpu.VMEM((teams, own, columns), F32)],
        compiler_params=pltpu.CompilerParams(vmem_limit_bytes=8 * MIB),
        name="control",
    )(*faces, basis_z, basis_x, after)


def radices_of(teams):
    radices = []
    while teams > 1:
        radix = next(r for r in (4, 2, 3, *range(5, teams + 1)) if teams % r == 0)
        radices.append(radix)
        teams //= radix
    return radices


def on_device(state, target, rock_type, log_table, obs_scale):
    samples, planes, rows_y, columns = state.shape
    slabs = lax.axis_size("gz")
    slots = samples // TEAM
    depth_total = planes * slabs
    radices = radices_of(slabs // TEAM)

    def swap(value, m):
        return lax.ppermute(value, "gz", [(i, i ^ m) for i in range(slabs)])

    def along(value, outward):
        pairs = []
        for i in range(slabs):
            side = (i % TEAM) // 2
            to = i + TEAM if (side == 1) == outward else i - TEAM
            if 0 <= to < slabs:
                pairs.append((i, to))
        return lax.ppermute(value, "gz", pairs)

    def from_teams(value, stride, radix):
        heard = []
        for k in range(1, radix):
            pairs = []
            for i in range(slabs):
                digit = i // (TEAM * stride) % radix
                pairs.append((i + ((digit + k) % radix - digit) * stride * TEAM, i))
            heard.append(lax.ppermute(value, "gz", pairs))
        return heard

    fields = [
        pltpu.with_memory_space_constraint(field, pltpu.HBM)
        for field in (state, target, rock_type, log_table, obs_scale)
    ]
    size = 4 * planes
    jobs = [[(slot, m) for slot in range(slots)] for m in range(TEAM)]
    mine, theirs, sums = prepare(jobs[2:], fields, with_sums=True)
    theirs = swap(theirs, 1)
    first, sums = merge(mine, theirs, 0, size, add=sums)
    far = [swap(first, 2)]
    stride, teams = 1, slabs // TEAM
    while stride < teams:
        radix = next(r for r in range(2, teams + 1) if teams // stride % r == 0)
        sums = sum(from_teams(sums, stride, radix), sums)
        stride *= radix

    mine_near, theirs_near = prepare(jobs[:2], fields)
    theirs_near = swap(theirs_near, 1)
    near, near_halo = [], []
    for slot in range(slots):
        blocks, trimmed = merge_near(mine_near, theirs_near, slot, size, sums)
        near.append(blocks)
        near_halo.append(along(trimmed, True))
    for slot in range(1, slots):
        far.append(swap(merge(mine, theirs, slot, size, sums), 2))
    sums = [sums, far[-1][2 * size]]

    pieces, faces = [], []
    for slot in range(slots):
        far_halo = along(trim(far[slot], size), False)
        made, edge = prepare_planes(near[slot], far[slot], near_halo[slot], planes, faces[-1:])
        solved = solve(made, edge, far_halo, planes)
        pieces.append([solved[0]] + [swap(solved[m], m) for m in (1, 2, 3)])
        faces.append(solved[TEAM])

    face, moments = weigh(sums, faces, depth_total * rows_y * columns, pieces[0][1:])
    heard = [sum((swap(face, m) for m in (2, 3, 1)), face)[None]]
    stride = 1
    for radix in radices:
        held = heard[0] if len(heard) == 1 else jnp.concatenate(heard)
        heard = [held] + from_teams(held, stride, radix)
        stride *= radix
    adjoint, mark = gather_adjoint(pieces, planes)
    own_count = MA // slabs
    gradient = control(
        heard,
        radices,
        jnp.asarray(cosine_basis(depth_total, MA).T.reshape(slabs, own_count, depth_total)),
        jnp.asarray(cosine_basis(columns, MB)),
        mark,
    )
    return (adjoint, gradient, moments[0, :2])


def solution(mesh):
    return jax.shard_map(
        on_device,
        mesh=mesh,
        in_specs=(
            P("parts", "gz", None, None),
            P(("parts", "gz"), None, None),
            P("parts", "gz", None, None),
            P("parts", None),
            P("parts"),
        ),
        out_specs=(P("parts", "gz", None, None), P(("parts", "gz"), None), P("parts")),
        check_vma=False,
    )
```

```python
import math

import jax
import jax.numpy as jnp
import numpy as np
from jax import lax
from jax.experimental import pallas as pl
from jax.experimental.pallas import tpu as pltpu
from jax.sharding import PartitionSpec as P

NR = 8
DEGREE = 4
SWEEPS = 2
MA = 512
MB = 512

STORAGE = 0.05
BETA_RISK = 0.5
LOWER_EIGEN = 0.05
UPPER_EIGEN = 2.0

TEAM = 4
STEPS = DEGREE * SWEEPS
F32 = jnp.float32
MIB = 1024 * 1024
LANES = 128


def chebyshev_constants(number_steps):
    centre = (UPPER_EIGEN + LOWER_EIGEN) / 2
    spread = (UPPER_EIGEN - LOWER_EIGEN) / 2
    quotient = centre / spread
    rho_now = 1.0 / quotient
    coefficients = []
    for position in range(number_steps):
        rho_next = 1.0 / (2.0 * quotient - rho_now)
        coefficients.append((rho_next * rho_now, 2.0 * rho_next / spread))
        rho_now = rho_next
    return (centre, coefficients)


def cosine_basis(length_total, modes):
    positions = np.arange(length_total, dtype=np.int64)
    mode_index = np.arange(modes, dtype=np.int64)
    product_index = ((2 * positions[:, None] + 1) * (2 * mode_index[None, :] + 1)) % (
        8 * length_total
    )
    angle = product_index.astype(np.float64) * (math.pi / (4 * length_total))
    return (math.sqrt(2.0 / length_total) * np.cos(angle)).astype(np.float32)


def in_halves(values):
    high = values.astype(jnp.bfloat16)
    return high, (values - high.astype(F32)).astype(jnp.bfloat16)


def team_place():
    return lax.rem(lax.axis_index("gz"), TEAM)


def prepare(jobs, fields, with_sums=False):
    state, target, rock_type, log_table, obs_scale = fields
    samples, planes, rows_y, columns = state.shape
    slots = samples // TEAM
    block = (planes, rows_y, columns)
    half, tiles = rows_y // 2, columns // 128
    size = 2 * 2 * planes
    depth_total = planes * lax.axis_size("gz")
    flat = [(o, i, job) for o, group in enumerate(jobs) for i, job in enumerate(group)]
    count = len(flat)
    shapes = [(len(group) * size + with_sums, half, columns) for group in jobs]
    states = samples if with_sums else count

    def kernel(*refs):
        (table_ref, scale_ref, state_ref, target_ref, rock_ref), refs = refs[:5], refs[5:]
        outs, refs = refs[: len(jobs)], refs[len(jobs) :]
        if with_sums:
            sums_ref, refs = refs[0], refs[1:]
        table, scale, state_buf, rock_buf, target_buf, mixed, sems = refs
        place = team_place()
        first_plane = lax.axis_index("gz") * planes
        members = [slots * (place ^ m) + slot for _, _, (slot, m) in flat]
        small = [
            pltpu.make_async_copy(table_ref, table, sems.at[2, 0]),
            pltpu.make_async_copy(scale_ref, scale, sems.at[2, 1]),
            pltpu.make_async_copy(target_ref, target_buf, sems.at[2, 2]),
        ]
        for copy in small:
            copy.start()
        rocks = [
            pltpu.make_async_copy(rock_ref.at[member], rock_buf.at[n], sems.at[1, n])
            for n, member in enumerate(members)
        ]
        loads = [
            pltpu.make_async_copy(
                state_ref.at[n if with_sums else members[n]], state_buf.at[n], sems.at[0, n]
            )
            for n in range(states)
        ]
        for copy in rocks + loads:
            copy.start()
        depth_weights = [
            1.0 + (2.0 / (depth_total - 1)) * (first_plane + p).astype(F32) for p in range(planes)
        ]
        for copy in small:
            copy.wait()
        if with_sums:
            for copy in loads:
                copy.wait()
            for n in range(samples):
                total = jnp.zeros((8, columns), F32)
                for p in range(planes):
                    part = jnp.zeros((8, columns), F32)
                    for first in range(0, rows_y, 8):
                        rows = slice(first, first + 8)
                        gap = state_buf[n, p, rows] - target_buf[p, rows]
                        part = part + gap * gap
                    total = total + (scale[n] * depth_weights[p]) * part
                summed = jnp.sum(total, keepdims=True)
                sums_ref[n : n + 1, :] = jnp.broadcast_to(summed, (1, columns))
        for n, (o, i, _) in enumerate(flat):
            rocks[n].wait()
            if not with_sums:
                loads[n].wait()
            member = members[n]
            own_state = member if with_sums else n
            values = [
                jnp.exp(jnp.full((8, columns), -table[member, code], F32)) for code in range(NR)
            ]
            for p in range(planes):
                factor = scale[member] * depth_weights[p]
                for first in range(0, rows_y, 8):
                    rows = slice(first, first + 8)
                    codes = rock_buf[n, p, rows]
                    low, mid, high = ((codes & bit) != 0 for bit in (1, 2, 4))
                    pairs = [
                        jnp.where(low, values[2 * k + 1], values[2 * k]) for k in range(NR // 2)
                    ]
                    halves = [jnp.where(mid, pairs[2 * k + 1], pairs[2 * k]) for k in range(2)]
                    gap = state_buf[own_state, p, rows] - target_buf[p, rows]
                    made = (jnp.where(high, halves[1], halves[0]), factor * gap)
                    for a in range(2):
                        for c in range(tiles):
                            mixed[n % 2, p, a, c, rows] = made[a][:, c * 128 : (c + 1) * 128]
                for a in range(2):
                    for t in range(2):
                        for c in range(tiles):
                            at = i * size + (a * planes + p) * 2 + t
                            outs[o][at, :, c * 128 : (c + 1) * 128] = mixed[
                                n % 2, p, a, c, pl.ds(t, half, stride=2), :
                            ]
        for o, group in enumerate(jobs if with_sums else []):
            outs[o][len(group) * size] = sums_ref[...]

    hbm = pl.BlockSpec(memory_space=pltpu.HBM)
    vmem = pl.BlockSpec(memory_space=pltpu.VMEM)
    return pl.pallas_call(
        kernel,
        out_shape=[jax.ShapeDtypeStruct(shape, F32) for shape in shapes]
        + [jax.ShapeDtypeStruct((samples, columns), F32)] * with_sums,
        in_specs=[hbm] * 5,
        out_specs=[vmem] * (len(shapes) + with_sums),
        scratch_shapes=[
            pltpu.SMEM(log_table.shape, F32),
            pltpu.SMEM(obs_scale.shape, F32),
            pltpu.VMEM((states,) + block, F32),
            pltpu.VMEM((count,) + block, jnp.int32),
            pltpu.VMEM(block, F32),
            pltpu.VMEM((2, planes, 2, tiles, rows_y, 128), F32),
            pltpu.SemaphoreType.DMA((3, max(states, 3))),
        ],
        compiler_params=pltpu.CompilerParams(vmem_limit_bytes=6 * MIB),
        cost_estimate=pl.CostEstimate(flops=0, bytes_accessed=count * MIB, transcendentals=0),
        name="prepare",
    )(log_table, obs_scale, state, target, rock_type)


def merge(mine, theirs, slot, size, behind=None, add=None):
    given = [value for value in (behind, add) if value is not None]

    def kernel(mine_ref, theirs_ref, *refs):
        core = lax.rem(team_place(), 2)
        tail, (out_ref, *more) = refs[: len(given)], refs[len(given) :]
        for ref, at in ((mine_ref, core), (theirs_ref, 1 - core)):
            for n in range(size):
                out_ref[at * size + n] = ref[slot * size + n]
        if behind is not None:
            out_ref[2 * size] = tail[0][...]
        if add is not None:
            more[0][...] = tail[-1][...] + theirs_ref[theirs.shape[0] - 1]

    vmem = pl.BlockSpec(memory_space=pltpu.VMEM)
    tile = mine.shape[1:]
    outs = pl.pallas_call(
        kernel,
        out_shape=[jax.ShapeDtypeStruct((2 * size + (behind is not None),) + tile, F32)]
        + [jax.ShapeDtypeStruct(tile, F32)] * (add is not None),
        in_specs=[vmem] * (2 + len(given)),
        out_specs=[vmem] * (1 + (add is not None)),
        compiler_params=pltpu.CompilerParams(vmem_limit_bytes=4 * MIB),
        name="merge",
    )(mine, theirs, *given)
    return outs if add is not None else outs[0]


def copy_trimmed(ref, out_ref, size, below):
    part = size // 2
    for core in range(2):
        for n in range(part):
            out_ref[core * part + n] = ref[core * size + n]
    for n in range(size - 2):
        at = n + jnp.where(below, 2, 0)
        out_ref[size + n] = ref[(at // part) * size + part + lax.rem(at, part)]


def trim(blocks, size):
    def kernel(ref, out_ref):
        copy_trimmed(ref, out_ref, size, team_place() < 2)

    vmem = pl.BlockSpec(memory_space=pltpu.VMEM)
    return pl.pallas_call(
        kernel,
        out_shape=jax.ShapeDtypeStruct((2 * size - 2,) + blocks.shape[1:], F32),
        in_specs=[vmem],
        out_specs=vmem,
        compiler_params=pltpu.CompilerParams(vmem_limit_bytes=4 * MIB),
        name="trim",
    )(blocks)


def merge_near(mine, theirs, slot, size, after):
    tile = mine.shape[1:]

    def kernel(mine_ref, theirs_ref, _, out_ref, trimmed_ref):
        core = lax.rem(team_place(), 2)
        for ref, at in ((mine_ref, core), (theirs_ref, 1 - core)):
            for n in range(size):
                out_ref[at * size + n] = ref[slot * size + n]
        copy_trimmed(out_ref, trimmed_ref, size, team_place() >= 2)

    vmem = pl.BlockSpec(memory_space=pltpu.VMEM)
    return pl.pallas_call(
        kernel,
        out_shape=[
            jax.ShapeDtypeStruct((2 * size,) + tile, F32),
            jax.ShapeDtypeStruct((2 * size - 2,) + tile, F32),
        ],
        in_specs=[vmem] * 2 + [pl.BlockSpec(memory_space=pl.ANY)],
        out_specs=[vmem] * 2,
        compiler_params=pltpu.CompilerParams(vmem_limit_bytes=4 * MIB),
        name="merge_near",
    )(mine, theirs, after)


def reciprocal(x):
    guess = pl.reciprocal(x, approx=True)
    return guess * (2.0 - x * guess)


def harmonic(a, b):
    x = a + b
    guess = pl.reciprocal(x, approx=True)
    return guess * (4.0 - (2.0 * x) * guess)


def each(start, stop, body, width):
    whole = (stop - start) // width

    def group(n, carry):
        for k in range(width):
            body(start + n * width + k)
        return carry

    lax.fori_loop(0, whole, group, 0)
    for p in range(start + whole * width, stop):
        body(p)


def ahead_x(v):
    return pltpu.roll(v, v.shape[1] - 1, 1)


def behind_x(v):
    return pltpu.roll(v, 1, 1)


def ahead_y(v):
    return pltpu.roll(v, v.shape[0] - 1, 0)


def behind_y(v):
    return pltpu.roll(v, 1, 0)


def set_up(planes, conductance, source, store):
    centre, _ = chebyshev_constants(DEGREE)
    here = [conductance(planes[0], t) for t in range(2)]
    half, columns = here[0].shape
    last_row = lax.broadcasted_iota(jnp.int32, (half, columns), 0) == half - 1
    last_column = lax.broadcasted_iota(jnp.int32, (half, columns), 1) == columns - 1
    w_below = [harmonic(conductance(planes[0] - 1, t), here[t]) for t in range(2)]
    for p in planes:
        above = [conductance(p + 1, t) for t in range(2)]
        even, odd = here
        w_pair = harmonic(even, odd)
        w_next = jnp.where(last_row, 0.0, harmonic(odd, ahead_y(even)))
        w_above = [harmonic(here[t], above[t]) for t in range(2)]
        for t in range(2):
            w_y = w_next if t else w_pair
            w_y_behind = w_pair if t else behind_y(w_next)
            w_x = jnp.where(last_column, 0.0, harmonic(here[t], ahead_x(here[t])))
            w_x_behind = behind_x(w_x)
            diagonal = (w_above[t] + w_below[t]) + (w_y + w_y_behind) + (w_x + w_x_behind) + STORAGE
            inverse = reciprocal(diagonal)
            weights = (w_above[t], w_below[t], w_y, w_y_behind, w_x, w_x_behind)
            scaled = source(p, t) * inverse
            store(p, t, [w * inverse for w in weights] + [scaled, scaled * (1.0 / centre)])
        here, w_below = above, w_above


def outside(v):
    return jnp.where(v > 0.0, v, 1e30)


def prepare_planes(near, far, near_halo, planes, after):
    half, columns = far.shape[-2:]
    halo, own, part = 2 * planes, TEAM * planes, 2 * planes
    span = own + 2 * halo
    first, count = halo + 1, own + halo - 2

    def kernel(near_ref, halo_ref, far_ref, *refs):
        refs = refs[len(after) :]
        outs, edge_ref, (cond, start) = refs[:8], refs[8], refs[9:]
        side = team_place() // 2

        def place(natural):
            return jnp.where(side == 0, natural, span - 1 - natural) - halo

        for core in range(2):
            for n in range(part):
                base = halo + planes * core + n // 2
                for ref, at in ((near_ref, base + part * side), (far_ref, base + part * (1 - side))):
                    cond[place(at), n % 2] = ref[core * 2 * part + n]
                    start[place(at), n % 2] = ref[(core * 2 + 1) * part + n]
        near_base = jnp.where(side == 0, halo + own, 0)
        for n in range(2 * part):
            cond[place(near_base + n // 2), n % 2] = outside(halo_ref[n])
        for n in range(2 * part - 2):
            start[place(near_base + side + n // 2), n % 2] = halo_ref[2 * part + n]
        for p in range(2):
            for t in range(2):
                edge_ref[0, p, t] = cond[p, t]
                edge_ref[1, p, t] = start[p, t]

        width = count // 2

        def group(n, carry):
            begin = 1 + n * width

            def store(p, t, values):
                for ref, value in zip(outs, values):
                    ref[p - 1, t] = value

            set_up(
                [begin + k for k in range(width)],
                lambda p, t: cond[p, t],
                lambda p, t: start[p, t],
                store,
            )
            return carry

        lax.fori_loop(0, 2, group, 0)

    assert count % 2 == 0
    vmem = pl.BlockSpec(memory_space=pltpu.VMEM)
    results = pl.pallas_call(
        kernel,
        out_shape=[jax.ShapeDtypeStruct((count, 2, half, columns), F32)] * 8
        + [jax.ShapeDtypeStruct((2, 2, 2, half, columns), F32)],
        in_specs=[vmem] * 3 + [pl.BlockSpec(memory_space=pl.ANY)] * len(after),
        out_specs=[vmem] * 9,
        scratch_shapes=[pltpu.VMEM((own + halo, 2, half, columns), F32)] * 2,
        compiler_params=pltpu.CompilerParams(vmem_limit_bytes=4 * MIB),
        cost_estimate=pl.CostEstimate(flops=0, bytes_accessed=8 * MIB, transcendentals=0),
        name="prepare_planes",
    )(near, near_halo, far, *after)
    return results[:8], results[8]


def solve(made, edge, far_halo, planes):
    half, columns = far_halo.shape[-2:]
    halo, own, part = 2 * planes, TEAM * planes, 2 * planes
    span = own + 2 * halo
    cut = halo + 1
    centre, coefficients = chebyshev_constants(DEGREE)
    assert halo >= STEPS

    def kernel(*refs):
        high, (edge_ref, halo_ref), refs = refs[:8], refs[8:10], refs[10:]
        outs, face_ref, refs = refs[:TEAM], refs[TEAM], refs[TEAM + 1 :]
        low, (cond, start, u_a, u_b, s_a, s_b, t_a, t_b) = refs[:6], refs[6:]
        place = team_place()
        side = place // 2

        def at(natural):
            return jnp.where(side == 0, natural, span - 1 - natural)

        far_base = jnp.where(side == 0, 0, halo + own)
        for n in range(2 * part):
            cond[at(far_base + n // 2), n % 2] = outside(halo_ref[n])
        for n in range(2 * part - 2):
            start[at(far_base + (1 - side) + n // 2), n % 2] = halo_ref[2 * part + n]
        for p in range(2):
            for t in range(2):
                cond[halo + p, t] = edge_ref[0, p, t]
                start[halo + p, t] = edge_ref[1, p, t]

        def store(p, t, values):
            for ref, value in zip((*low, u_a, s_a), values):
                ref[p, t] = value

        set_up(range(1, cut), lambda p, t: cond[p, t], lambda p, t: start[p, t], store)
        for p in range(cut, span - 1):
            for t in range(2):
                u_a[p, t] = high[6][p - cut, t]
                s_a[p, t] = high[7][p - cut, t]

        s_now, s_next, u_now, u_next, t_now, t_next = s_a, s_b, u_a, u_b, t_a, t_b
        for step in range(STEPS - 1):
            position = step % DEGREE
            if position + 1 < DEGREE:
                keep, mix = coefficients[position]
            else:
                keep, mix = 0.0, 1.0 / centre
            last = step == STEPS - 2

            def advance(p, fields, first):
                zp, zm, yp, ym, xp, xm = fields
                q = p - first
                even, odd = s_now[p, 0], s_now[p, 1]
                for t, s in enumerate((even, odd)):
                    ahead = ahead_y(even) if t else odd
                    behind = even if t else behind_y(odd)
                    moved = zp[q, t] * s_now[p + 1, t] + zm[q, t] * s_now[p - 1, t]
                    moved += yp[q, t] * ahead + ym[q, t] * behind
                    moved += xp[q, t] * ahead_x(s) + xm[q, t] * behind_x(s)
                    new_u = (u_now[p, t] - s) + moved
                    new_s = mix * new_u if keep == 0.0 else keep * s + mix * new_u
                    if not last:
                        u_next[p, t] = new_u
                        s_next[p, t] = new_s
                    if step == 0:
                        t_next[p, t] = s + new_s
                    elif step % 2 == 0:
                        t_next[p, t] = t_now[p, t] + (s + new_s)

            margin = halo - (STEPS - 2 - step)
            each(cut, span - margin, lambda p: advance(p, high[:6], cut), 8)
            each(margin, cut, lambda p: advance(p, low, 0), 8)
            s_now, s_next, u_now, u_next = s_next, s_now, u_next, u_now
            if step % 2 == 0:
                t_now, t_next = t_next, t_now

        for m in range(TEAM):
            base = halo + planes * (place ^ m)
            for j in range(planes):
                for t in range(2):
                    outs[m][2 * j + t] = t_now[at(base + j), t]
        for p in range(own):
            face_ref[p : p + 1, :] = t_now[at(halo + p), 0, 0:1, :]

    vmem = pl.BlockSpec(memory_space=pltpu.VMEM)
    field = pltpu.VMEM((span, 2, half, columns), F32)
    small = pltpu.VMEM((halo + 2, 2, half, columns), F32)
    return pl.pallas_call(
        kernel,
        out_shape=[jax.ShapeDtypeStruct((2 * planes, half, columns), F32)] * TEAM
        + [jax.ShapeDtypeStruct((own, columns), F32)],
        in_specs=[vmem] * 10,
        out_specs=[vmem] * (TEAM + 1),
        scratch_shapes=[small] * 8 + [field] * 6,
        compiler_params=pltpu.CompilerParams(vmem_limit_bytes=10 * MIB),
        cost_estimate=pl.CostEstimate(flops=0, bytes_accessed=16 * MIB, transcendentals=0),
        name="solve",
    )(*made, edge, far_halo)


def weigh(sums, faces, cells, after):
    slots = len(faces)
    samples, columns = sums[0].shape

    def kernel(*refs):
        sum_refs, refs = refs[: len(sums)], refs[len(sums) :]
        face_refs, (out_ref, moments_ref, weights) = refs[:slots], refs[slots + len(after) :]
        place = team_place()
        summed = sum_refs[0][...]
        for ref in sum_refs[1:]:
            summed = summed + ref[...]
        misfit = summed * (1.0 / (2.0 * cells))
        mean = jnp.sum(misfit, axis=0, keepdims=True) * (1.0 / samples)
        deviation = misfit - mean
        variance = jnp.sum(deviation * deviation, axis=0, keepdims=True) * (1.0 / samples)
        lane = lax.broadcasted_iota(jnp.int32, (1, columns), 1)
        moments_ref[...] = jnp.where(lane == 0, mean, variance)
        weights[...] = 1.0 + 2.0 * BETA_RISK * deviation
        total = weights[pl.ds(slots * place, 1), :] * face_refs[0][...]
        for n in range(1, slots):
            total = total + weights[pl.ds(slots * place + n, 1), :] * face_refs[n][...]
        out_ref[...] = total

    vmem = pl.BlockSpec(memory_space=pltpu.VMEM)
    return pl.pallas_call(
        kernel,
        out_shape=[
            jax.ShapeDtypeStruct(faces[0].shape, F32),
            jax.ShapeDtypeStruct((1, columns), F32),
        ],
        in_specs=[vmem] * (len(sums) + slots)
        + [pl.BlockSpec(memory_space=pl.ANY)] * len(after),
        out_specs=[vmem, vmem],
        scratch_shapes=[pltpu.VMEM((samples, columns), F32)],
        compiler_params=pltpu.CompilerParams(vmem_limit_bytes=2 * MIB),
        name="weigh",
    )(*sums, *faces, *after)


def gather_adjoint(pieces, planes):
    slots = len(pieces)
    _, half, columns = pieces[0][0].shape
    tiles = columns // 128
    block = (planes, 2 * half, columns)

    def kernel(*refs):
        blocks, out, mark, held, mixed, sems = refs[: slots * TEAM], *refs[slots * TEAM :]
        mark[...] = blocks[0][0, :, :LANES]
        place = team_place()
        copies = []
        for slot in range(slots):
            for m in range(TEAM):
                i = slot * TEAM + m
                for j in range(planes):
                    for t in range(2):
                        for c in range(tiles):
                            mixed[i % 2, j, c, pl.ds(t, half, stride=2), :] = blocks[i][
                                2 * j + t, :, c * 128 : (c + 1) * 128
                            ]
                    for c in range(tiles):
                        held[i, j, :, c * 128 : (c + 1) * 128] = mixed[i % 2, j, c]
                copy = pltpu.make_async_copy(
                    held.at[i], out.at[slots * (place ^ m) + slot], sems.at[i]
                )
                copy.start()
                copies.append(copy)
        for copy in copies:
            copy.wait()

    return pl.pallas_call(
        kernel,
        out_shape=[
            jax.ShapeDtypeStruct((slots * TEAM,) + block, F32),
            jax.ShapeDtypeStruct((half, LANES), F32),
        ],
        in_specs=[pl.BlockSpec(memory_space=pltpu.VMEM)] * (slots * TEAM),
        out_specs=[
            pl.BlockSpec(memory_space=pltpu.HBM),
            pl.BlockSpec(memory_space=pltpu.VMEM),
        ],
        scratch_shapes=[
            pltpu.VMEM((slots * TEAM,) + block, F32),
            pltpu.VMEM((2, planes, tiles, 2 * half, 128), F32),
            pltpu.SemaphoreType.DMA((slots * TEAM,)),
        ],
        compiler_params=pltpu.CompilerParams(vmem_limit_bytes=4 * MIB),
        cost_estimate=pl.CostEstimate(flops=0, bytes_accessed=4 * MIB, transcendentals=0),
        name="gather_adjoint",
    )(*[piece for group in pieces for piece in group])


def split_basis(basis):
    def kernel(ref, high_ref, low_ref):
        high_ref[...], low_ref[...] = in_halves(ref[...])

    vmem = pl.BlockSpec(memory_space=pltpu.VMEM)
    return pl.pallas_call(
        kernel,
        out_shape=[jax.ShapeDtypeStruct(basis.shape, jnp.bfloat16)] * 2,
        in_specs=[vmem],
        out_specs=[vmem] * 2,
        compiler_params=pltpu.CompilerParams(vmem_limit_bytes=4 * MIB),
        name="split_basis",
    )(basis)


def control(faces, radices, basis_z, basis_x, after):
    slabs, own_count, depth_total = basis_z.shape
    own, columns = faces[0].shape[1:]
    teams = depth_total // own

    def kernel(*refs):
        parts, (z_ref, x_ref, low_ref, _, out_ref, whole) = refs[: len(faces)], refs[len(faces) :]
        rank = lax.axis_index("gz")
        team = rank // TEAM
        for n in range(teams):
            at, left, stride = 0, n, 1
            for radix in radices:
                digit = lax.rem(team // stride + left % radix, radix)
                at, left, stride = at + digit * stride, left // radix, stride * radix
            inner = teams // len(faces)
            whole[at] = parts[n // inner][n % inner]
        along_z = jnp.dot(
            z_ref[rank],
            whole[...].reshape(depth_total, columns),
            precision=lax.Precision.HIGHEST,
            preferred_element_type=F32,
        )
        high, low = in_halves(along_z)
        both = jnp.concatenate([high, low], axis=0)
        first = jnp.dot(both, x_ref[...], preferred_element_type=F32)
        second = jnp.dot(high, low_ref[...], preferred_element_type=F32)
        out_ref[...] = (first[:own_count] + first[own_count:]) + second

    vmem = pl.BlockSpec(memory_space=pltpu.VMEM)
    return pl.pallas_call(
        kernel,
        out_shape=jax.ShapeDtypeStruct((own_count, columns), F32),
        in_specs=[vmem] * (len(faces) + 3) + [pl.BlockSpec(memory_space=pl.ANY)],
        out_specs=vmem,
        scratch_shapes=[pltpu.VMEM((teams, own, columns), F32)],
        compiler_params=pltpu.CompilerParams(vmem_limit_bytes=8 * MIB),
        name="control",
    )(*faces, basis_z, *basis_x, after)


def radices_of(teams):
    radices = []
    while teams > 1:
        radix = next(r for r in (4, 2, 3, *range(5, teams + 1)) if teams % r == 0)
        radices.append(radix)
        teams //= radix
    return radices


def on_device(state, target, rock_type, log_table, obs_scale):
    samples, planes, rows_y, columns = state.shape
    slabs = lax.axis_size("gz")
    slots = samples // TEAM
    depth_total = planes * slabs
    radices = radices_of(slabs // TEAM)

    def swap(value, m):
        return lax.ppermute(value, "gz", [(i, i ^ m) for i in range(slabs)])

    def along(value, outward):
        pairs = []
        for i in range(slabs):
            side = (i % TEAM) // 2
            to = i + TEAM if (side == 1) == outward else i - TEAM
            if 0 <= to < slabs:
                pairs.append((i, to))
        return lax.ppermute(value, "gz", pairs)

    def from_teams(value, stride, radix):
        heard = []
        for k in range(1, radix):
            pairs = []
            for i in range(slabs):
                digit = i // (TEAM * stride) % radix
                pairs.append((i + ((digit + k) % radix - digit) * stride * TEAM, i))
            heard.append(lax.ppermute(value, "gz", pairs))
        return heard

    fields = [
        pltpu.with_memory_space_constraint(field, pltpu.HBM)
        for field in (state, target, rock_type, log_table, obs_scale)
    ]
    size = 4 * planes
    jobs = [[(slot, m) for slot in range(slots)] for m in range(TEAM)]
    mine, theirs, sums = prepare(jobs[2:], fields, with_sums=True)
    theirs = swap(theirs, 1)
    first, sums = merge(mine, theirs, 0, size, add=sums)
    far = [swap(first, 2)]
    stride, teams = 1, slabs // TEAM
    while stride < teams:
        radix = next(r for r in range(2, teams + 1) if teams // stride % r == 0)
        sums = sum(from_teams(sums, stride, radix), sums)
        stride *= radix

    mine_near, theirs_near = prepare(jobs[:2], fields)
    theirs_near = swap(theirs_near, 1)
    near, near_halo = [], []
    for slot in range(slots):
        blocks, trimmed = merge_near(mine_near, theirs_near, slot, size, sums)
        near.append(blocks)
        near_halo.append(along(trimmed, True))
    for slot in range(1, slots):
        far.append(swap(merge(mine, theirs, slot, size, sums), 2))
    sums = [sums, far[-1][2 * size]]

    basis_x = split_basis(jnp.asarray(cosine_basis(columns, MB)))
    pieces, faces = [], []
    for slot in range(slots):
        far_halo = along(trim(far[slot], size), False)
        made, edge = prepare_planes(near[slot], far[slot], near_halo[slot], planes, [*faces[-1:], basis_x[0]] if slot else [])
        solved = solve(made, edge, far_halo, planes)
        pieces.append([solved[0]] + [swap(solved[m], m) for m in (1, 2, 3)])
        faces.append(solved[TEAM])

    face, moments = weigh(sums, faces, depth_total * rows_y * columns, pieces[0][1:])
    heard = [sum((swap(face, m) for m in (2, 3, 1)), face)[None]]
    stride = 1
    for radix in radices:
        held = heard[0] if len(heard) == 1 else jnp.concatenate(heard)
        heard = [held] + from_teams(held, stride, radix)
        stride *= radix
    adjoint, mark = gather_adjoint(pieces, planes)
    own_count = MA // slabs
    gradient = control(
        heard,
        radices,
        jnp.asarray(cosine_basis(depth_total, MA).T.reshape(slabs, own_count, depth_total)),
        basis_x,
        mark,
    )
    return (adjoint, gradient, moments[0, :2])


def solution(mesh):
    return jax.shard_map(
        on_device,
        mesh=mesh,
        in_specs=(
            P("parts", "gz", None, None),
            P(("parts", "gz"), None, None),
            P("parts", "gz", None, None),
            P("parts", None),
            P("parts"),
        ),
        out_specs=(P("parts", "gz", None, None), P(("parts", "gz"), None), P("parts")),
        check_vma=False,
    )
```
